32 devices in a mesh: dp: 8 (over y, x, core), tensor: 4 (over z).
Axes of the slice: x: 2, y: 2, z: 4, core: 2. Of those that a mesh axis runs over, the one named last changes fastest.
Arguments:
- tokens_in: bfloat16 [8192, 1024], P(('dp', 'tensor')), may hold values from -6 to 6
- out_grad: bfloat16 [8192, 1024], P(('dp', 'tensor')), may hold values from -6 to 6
- attn_gain: bfloat16 [1024], P('dp'), may hold values from 0.5 to 1.5
- w_query: bfloat16 [1024, 1024], P('dp', 'tensor'), may hold values from -0.1875 to 0.1875
- w_key: bfloat16 [1024, 1024], P('dp', 'tensor'), may hold values from -0.1875 to 0.1875
- w_value: bfloat16 [1024, 1024], P('dp', 'tensor'), may hold values from -0.1875 to 0.1875
- w_output: bfloat16 [1024, 1024], P('tensor', 'dp'), may hold values from -0.75 to 0.75
- rel_table: float32 [16, 32], P('tensor'), may hold values from -4 to 4
- moe_gain: bfloat16 [1024], P('dp'), may hold values from 0.5 to 1.5
- w_router: bfloat16 [1024, 4], P('dp'), may hold values from -0.125 to 0.125
- w_gate: bfloat16 [4, 1024, 2816], P(None, 'dp', 'tensor'), may hold values from -0.1875 to 0.1875
- w_up: bfloat16 [4, 1024, 2816], P(None, 'dp', 'tensor'), may hold values from -0.1875 to 0.1875
- down_weight: bfloat16 [4, 2816, 1024], P(None, 'tensor', 'dp'), may hold values from -0.3125 to 0.3125
- expert_ids: int32 [8192, 2], P('dp'), may hold values from 0 to 3, as said below
- piece_starts: int32 [8, 2], P('dp'), may hold values from 0 to 768, as said below
Outputs:
- out_rows: bfloat16 [8192, 1024], P(('dp', 'tensor'))
- in_grad: float32 [8192, 1024], P(('dp', 'tensor'))
- grad_attn_gain: float32 [1024], P(('dp', 'tensor'))
- grad_w_query: float32 [1024, 1024], P('dp', 'tensor')
- grad_w_key: float32 [1024, 1024], P('dp', 'tensor')
- grad_w_value: float32 [1024, 1024], P('dp', 'tensor')
- grad_w_output: float32 [1024, 1024], P('tensor', 'dp')
- grad_rel_table: float32 [16, 32], P('tensor')
- grad_moe_gain: float32 [1024], P(('dp', 'tensor'))
- grad_w_router: float32 [1024, 4], P(('dp', 'tensor'))
- gate_weight_gradient: float32 [4, 1024, 2816], P(None, 'dp', 'tensor')
- grad_w_up: float32 [4, 1024, 2816], P(None, 'dp', 'tensor')
- grad_w_down: float32 [4, 2816, 1024], P(None, 'tensor', 'dp')
The draws below stay inside these ranges and needn't reach their ends.
Inputs may be any that keep to these rules, and one draw needn't show every extreme that they name: `expert_ids`: the two experts of a token differ. Within the tokens of each index of dp, one expert, which one drawn from the seed, is among the two choices of exactly 768 tokens. `piece_starts`: in each sequence the k-th of the 2 pieces lies wholly inside the k-th of 2 equal parts of the sequence; positions count from the sequence's start. Some sequence's first piece starts at position 0 and some sequence's last piece ends at the sequence's end.
All inputs are finite; a program needn't handle non-finite values.
Results may differ from the reference program's by a relative error of at most 0.02.
Values may be sent and summed in bfloat16 or wider, within the bound.
No kernel may reach another device: no remote copies, remote signals or barrier semaphores. Data moves between devices by JAX's collectives and lax.ppermute only.
A program may use at most 256 MiB of HBM per device.

```python
import jax
import jax.numpy as jnp
from jax import lax

D = 1024
HEADS = 16
HEAD = 64
FF = 2816
EXPERTS = 4
BUCKETS = 32
SEQ_LEN = 1024
PIECE = 256
PIECES = 2
SEQS = 1
GROUP = 1024
TOKENS = 8192
SEQUENCES = 8
HD = 1024
CAP = 640
N_DP = 8


def draw_piece_starts(key, part):
    key = jax.random.fold_in(key, 11)
    part_width = SEQ_LEN // PIECES
    pick_key, offset_key = jax.random.split(key)
    offsets = jax.random.randint(offset_key, (SEQUENCES, PIECES), 0, part_width - PIECE + 1)
    chosen = jax.random.randint(pick_key, (), 0, SEQUENCES)
    row_ids = jnp.arange(SEQUENCES, dtype=jnp.int32)[:, None]
    col_ids = jnp.arange(PIECES, dtype=jnp.int32)[None, :]
    is_chosen = row_ids == chosen
    offsets = jnp.where(is_chosen & (col_ids == 0), 0, offsets)
    offsets = jnp.where(is_chosen & (col_ids == PIECES - 1), part_width - PIECE, offsets)
    bases = col_ids * part_width
    return (offsets + bases).astype(jnp.int32)


def draw_expert_ids(key, part):
    key = jax.random.fold_in(key, 23)
    group_count = TOKENS // GROUP
    busy_key, rank_key, side_key, first_key, second_key = jax.random.split(key, 5)
    busy_one = jax.random.randint(busy_key, (group_count, 1), 0, EXPERTS)
    rank_keys = jax.random.split(rank_key, group_count)
    token_rank = jax.vmap(lambda one_key: jax.random.permutation(one_key, GROUP))(rank_keys)
    holds_busy = token_rank < 3 * GROUP // 4
    busy_first = jax.random.randint(side_key, (group_count, GROUP), 0, 2) == 0
    other_a = jax.random.randint(first_key, (group_count, GROUP), 0, EXPERTS - 1)
    other_b = (other_a + jax.random.randint(second_key, (group_count, GROUP), 1, EXPERTS - 1)) % (EXPERTS - 1)
    expert_a = (busy_one + 1 + other_a) % EXPERTS
    expert_b = (busy_one + 1 + other_b) % EXPERTS
    first_pick = jnp.where(holds_busy & busy_first, busy_one, expert_a)
    second_pick = jnp.where(holds_busy, jnp.where(busy_first, expert_a, busy_one), expert_b)
    return jnp.stack([first_pick, second_pick], axis=-1).reshape(TOKENS, 2).astype(jnp.int32)


def with_spikes(array, stream_key, source, target, blocks, factor):
    owner, partner = [(jnp.arange(array.shape[axis_at]) // (array.shape[axis_at] // blocks)).reshape([-1 if axis == axis_at else 1 for axis in range(array.ndim)]) for axis_at in (source, target)]
    chosen = jax.random.permutation(stream_key, blocks)[partner]
    strong = (owner == chosen) | (owner == (partner + blocks // 2) % blocks)
    return jnp.where(strong, factor * array, array)


def levels(key, extent, pieces, low, top_value):
    def one(position, shards_of):
        heights = jax.random.uniform(jax.random.fold_in(jax.random.fold_in(key, 6), position), (shards_of,), jnp.float32, low / len(pieces), top_value / len(pieces))
        return jnp.repeat(jnp.exp(heights), extent[position] // shards_of).reshape((-1,) + (1,) * (len(extent) - position - 1))

    level = one(*pieces[0])
    for cut in pieces[1:]:
        level = level * one(*cut)
    return level


def noise(stream_key, extent, deviation, reach, cuts=(), held_as=jnp.bfloat16):
    values = jax.random.normal(stream_key, extent, jnp.float32) * deviation
    if len(cuts) > 0:
        values = levels(stream_key, extent, cuts, -0.22, 0.18) * values
    return jnp.clip(values, min=-reach, max=reach).astype(held_as)


def heavy_noise(key, shape, spread, most, pieces, heavy, kind=jnp.bfloat16):
    array = spread * jax.random.normal(key, shape, jnp.float32)
    if pieces:
        array = array * levels(key, shape, pieces, -0.22, 0.18)
    return jnp.clip(with_spikes(array, jax.random.fold_in(key, 3), *heavy), -most, most).astype(kind)


def setup_inputs(seed: int = 0) -> dict:
    key_list = jax.random.split(jax.random.key(seed), 16)
    return {
        "tokens_in": heavy_noise(key_list[0], (TOKENS, D), 1.0, 6.0, ((0, 32),), (0, 1, 32, 2.75)),
        "out_grad": heavy_noise(key_list[1], (TOKENS, D), 1.0, 6.0, ((0, 32),), (0, 1, 32, 2.75)),
        "attn_gain": jnp.clip(1.0 + 0.1 * jax.random.normal(key_list[2], (D,), jnp.float32), 0.5, 1.5).astype(jnp.bfloat16),
        "w_query": noise(key_list[3], (D, HD), D ** -0.5, 0.1875, ((0, 8), (1, 4))),
        "w_key": noise(key_list[4], (D, HD), D ** -0.5, 0.1875, ((0, 8), (1, 4))),
        "w_value": noise(key_list[5], (D, HD), D ** -0.5, 0.1875, ((0, 8), (1, 4))),
        "w_output": noise(key_list[6], (HD, D), (HD // 16) ** -0.5, 0.75, ((0, 4), (1, 8))),
        "rel_table": noise(key_list[7], (HEADS, BUCKETS), 1.0, 4.0, ((0, 4),), jnp.float32),
        "moe_gain": jnp.clip(1.0 + 0.1 * jax.random.normal(key_list[8], (D,), jnp.float32), 0.5, 1.5).astype(jnp.bfloat16),
        "w_router": noise(key_list[9], (D, EXPERTS), (2 * D) ** -0.5, 0.125, ((0, 8),)),
        "w_gate": noise(key_list[10], (EXPERTS, D, FF), D ** -0.5, 0.1875, ((1, 8), (2, 4))),
        "w_up": noise(key_list[11], (EXPERTS, D, FF), D ** -0.5, 0.1875, ((1, 8), (2, 4))),
        "down_weight": noise(key_list[12], (EXPERTS, FF, D), (FF // 8) ** -0.5, 0.3125, ((1, 4), (2, 8))),
        "expert_ids": draw_expert_ids(jax.random.fold_in(key_list[15], 71), 0),
        "piece_starts": draw_piece_starts(jax.random.fold_in(key_list[15], 71), 0),
    }


@jax.custom_vjp
def low(v):
    return lax.optimization_barrier(v.astype(jnp.bfloat16)).astype(jnp.float32)

@jax.custom_vjp
def low_back(v):
    return v

def low_keep(v):
    return (low(v), None)

def low_pass(kept, grad):
    return (grad,)

def back_keep(v):
    return (v, None)

def back_low(kept, grad):
    return (low(grad),)
low.defvjp(low_keep, low_pass)
low_back.defvjp(back_keep, back_low)
EPSILON = 1e-06
PRECISE = lax.Precision.HIGHEST
LIMITS = (12, 16, 23, 32, 46, 64, 91)
MASKED = -1e+30

def bucket_of(offsets):
    distance = jnp.abs(offsets)
    far_bucket = jnp.full_like(distance, 8)
    for bound_value in LIMITS:
        far_bucket = far_bucket + (distance >= bound_value).astype(jnp.int32)
    near_bucket = jnp.where(distance < 8, distance, far_bucket)
    return near_bucket + jnp.where(offsets > 0, 16, 0).astype(jnp.int32)

def piece_labels(starts_in, row_total):
    token_positions = jnp.arange(row_total, dtype=jnp.int32)
    seq_ids = token_positions // SEQ_LEN
    inner_pos = token_positions % SEQ_LEN
    own_starts = jnp.take(starts_in, seq_ids, axis=0)
    inside = (inner_pos[:, None] >= own_starts) & (inner_pos[:, None] < own_starts + PIECE)
    numbers = seq_ids[:, None] * PIECES + jnp.arange(PIECES, dtype=jnp.int32)[None, :]
    labels = lax.optimization_barrier(jnp.max(jnp.where(inside, numbers, -1), axis=1))
    return (seq_ids, labels)

def block_mask(seq_ids, labels, first_row, block_rows):
    query_pos = first_row + jnp.arange(block_rows, dtype=jnp.int32)
    key_pos = jnp.arange(seq_ids.shape[0], dtype=jnp.int32)
    query_seq = lax.dynamic_slice_in_dim(seq_ids, first_row, block_rows)
    query_label = lax.dynamic_slice_in_dim(labels, first_row, block_rows)
    same_seq = query_seq[:, None] == seq_ids[None, :]
    causal = key_pos[None, :] <= query_pos[:, None]
    joint = (query_label[:, None] == labels[None, :]) & (query_label[:, None] >= 0)
    return (same_seq & (causal | joint), key_pos[None, :] - query_pos[:, None])

def route_slots(ids_in):
    row_total = ids_in.shape[0]
    expert_range = jnp.arange(EXPERTS, dtype=jnp.int32)
    first_hot = (ids_in[:, 0:1] == expert_range[None, :]).astype(jnp.int32)
    second_hot = (ids_in[:, 1:2] == expert_range[None, :]).astype(jnp.int32)
    first_run = jnp.cumsum(first_hot, axis=0)
    second_run = jnp.cumsum(second_hot, axis=0) + first_run[-1][None, :]
    first_place = lax.optimization_barrier(jnp.sum(first_run * first_hot, axis=1)) - 1
    second_place = lax.optimization_barrier(jnp.sum(second_run * second_hot, axis=1)) - 1
    dump_slot = EXPERTS * CAP
    first_slot = jnp.where(first_place < CAP, ids_in[:, 0] * CAP + first_place, dump_slot).astype(jnp.int32)
    second_slot = jnp.where(second_place < CAP, ids_in[:, 1] * CAP + second_place, dump_slot).astype(jnp.int32)
    row_ids = jnp.arange(row_total, dtype=jnp.int32)
    slot_owner = jnp.full((dump_slot + 1,), row_total, jnp.int32).at[first_slot].set(row_ids).at[second_slot].set(row_ids)
    return (first_slot, second_slot, slot_owner[:dump_slot])

def rms_scale(values, gain_vec):
    return values * lax.rsqrt(lax.optimization_barrier(jnp.mean(values * values, axis=-1, keepdims=True)) + EPSILON) * gain_vec

def geglu_unit(gate_pre, up_pre):
    return jax.nn.gelu(gate_pre, approximate=True) * up_pre

def softmax_rows(logits):
    row_max = lax.optimization_barrier(jnp.max(logits, axis=-1, keepdims=True))
    exponent = jnp.exp(logits - row_max)
    return exponent / lax.optimization_barrier(jnp.sum(exponent, axis=-1, keepdims=True))

def block_layer(resid_in, gain_one, query_w, key_w, value_w, output_w, table_w, gain_two, router_w, gate_w, up_w, down_w, ids_in, starts_in):
    group_rows = resid_in.shape[0]
    model_width = resid_in.shape[1]
    normed_one = low(rms_scale(resid_in, gain_one))
    queries = low(low_back(jnp.dot(normed_one, query_w, precision=PRECISE))).reshape(group_rows, HEADS, HEAD)
    keys_all = low(low_back(jnp.dot(normed_one, key_w, precision=PRECISE))).reshape(group_rows, HEADS, HEAD)
    values_all = low(low_back(jnp.dot(normed_one, value_w, precision=PRECISE))).reshape(group_rows, HEADS, HEAD)
    seq_ids, labels = piece_labels(starts_in, group_rows)
    block_rows = min(512, group_rows)
    block_total = group_rows // block_rows

    def attend_block(block_index):
        first_row = (block_index * block_rows).astype(jnp.int32)
        visible, offsets = block_mask(seq_ids, labels, first_row, block_rows)
        query_rows = lax.dynamic_slice_in_dim(queries, first_row, block_rows, 0)
        raw_scores = jnp.einsum('qhd,khd->hqk', query_rows, keys_all, precision=PRECISE) * 0.125
        raw_scores = raw_scores + jnp.take(table_w, bucket_of(offsets), axis=1)
        scores = jnp.where(visible[None], low_back(raw_scores), MASKED)
        row_max = lax.optimization_barrier(jnp.max(scores, axis=2, keepdims=True))
        exponent = jnp.exp(scores - row_max)
        chances = low(exponent / lax.optimization_barrier(jnp.sum(exponent, axis=2, keepdims=True)))
        return jnp.einsum('hqk,khd->qhd', chances, values_all, precision=PRECISE)
    mixed_rows = lax.map(jax.checkpoint(attend_block), jnp.arange(block_total, dtype=jnp.int32))
    attended = low(low_back(mixed_rows.reshape(group_rows, HEADS * HEAD)))
    resid_mid = resid_in + low_back(jnp.dot(attended, output_w, precision=PRECISE))
    normed_two = low(rms_scale(resid_mid, gain_two))
    route_probs = softmax_rows(jnp.dot(normed_two, router_w, precision=PRECISE))
    gate_vals = jnp.take_along_axis(route_probs, ids_in, axis=1)
    first_slot, second_slot, slot_owner = route_slots(ids_in)
    zero_row = jnp.zeros((1, model_width), normed_two.dtype)
    routed = jnp.concatenate([normed_two, zero_row], 0)[slot_owner].reshape(EXPERTS, CAP, model_width)
    gate_pre = low_back(jnp.einsum('ecd,edf->ecf', routed, gate_w, precision=PRECISE))
    up_pre = low_back(jnp.einsum('ecd,edf->ecf', routed, up_w, precision=PRECISE))
    hidden = low(geglu_unit(gate_pre, up_pre))
    expert_out = low_back(jnp.einsum('ecf,efd->ecd', hidden, down_w, precision=PRECISE))
    out_pad = jnp.concatenate([expert_out.reshape(EXPERTS * CAP, model_width), zero_row], 0)
    moe_rows = gate_vals[:, 0:1] * out_pad[first_slot] + gate_vals[:, 1:2] * out_pad[second_slot]
    return resid_mid + low_back(moe_rows)

def reference(tokens_in, out_grad, attn_gain, w_query, w_key, w_value, w_output, rel_table, moe_gain, w_router, w_gate, w_up, down_weight, expert_ids, piece_starts):
    weights = tuple((item.astype(jnp.float32) for item in (attn_gain, w_query, w_key, w_value, w_output, rel_table, moe_gain, w_router, w_gate, w_up, down_weight)))
    inputs_all = tokens_in.reshape(N_DP, GROUP, D)
    grads_all = out_grad.reshape(N_DP, GROUP, D)
    ids_all = expert_ids.reshape(N_DP, GROUP, 2)
    starts_all = piece_starts.reshape(N_DP, SEQS, PIECES)

    def scan_step(summed, inputs_now):
        resid_group, grad_group, ids_group, starts_group = inputs_now

        def forward(resid_value, *params):
            return block_layer(resid_value, *params, ids_group, starts_group)
        result, pull_back = jax.vjp(forward, resid_group.astype(jnp.float32), *weights)
        gradients = pull_back(grad_group.astype(jnp.float32))
        summed = tuple((left + right for left, right in zip(summed, gradients[1:])))
        return (summed, (result.astype(jnp.bfloat16), gradients[0]))
    zero_sums = tuple((jnp.zeros_like(item) for item in weights))
    summed, (outputs, input_grads) = lax.scan(scan_step, zero_sums, (inputs_all, grads_all, ids_all, starts_all))
    return (outputs.reshape(TOKENS, D), input_grads.reshape(TOKENS, D), summed[0], summed[1], summed[2], summed[3], summed[4], summed[5], summed[6], summed[7], summed[8], summed[9], summed[10])
```

```python
import functools

import jax
import jax.numpy as jnp
import numpy as np
from jax import lax
from jax.experimental import pallas as pl
from jax.experimental.pallas import tpu as pltpu
from jax.sharding import PartitionSpec as P

EXPERTS = 4
PIECE = 256
CAP = 640
BUCKETS = 32
EPSILON = 1e-06
PRECISE = lax.Precision.HIGHEST
LIMITS = (12, 16, 23, 32, 46, 64, 91)
MASKED = -1e30
BF = jnp.bfloat16
F32 = jnp.float32
BLOCK = 256
VMEM_LIMIT = 56 * 1024 * 1024


def params(semantics=None):
    return pltpu.CompilerParams(dimension_semantics=semantics, vmem_limit_bytes=VMEM_LIMIT)


def dot_nn(a, b):
    return lax.dot_general(a, b, (((1,), (0,)), ((), ())), preferred_element_type=F32)


def dot_nt(a, b):
    return lax.dot_general(a, b, (((1,), (1,)), ((), ())), preferred_element_type=F32)


def dot_tn(a, b):
    return lax.dot_general(a, b, (((0,), (0,)), ((), ())), preferred_element_type=F32)


def bucket_of(offsets):
    distance = np.abs(offsets)
    far = np.full_like(distance, 8)
    for bound in LIMITS:
        far = far + (distance >= bound)
    return np.where(distance < 8, distance, far) + np.where(offsets > 0, 16, 0)


def onehot_of(offsets):
    return (bucket_of(offsets)[..., None] == np.arange(BUCKETS)).astype(np.float32)


def cost(flops, nbytes):
    return pl.CostEstimate(flops=int(flops), bytes_accessed=int(nbytes), transcendentals=0)


def vspec():
    return pl.BlockSpec(memory_space=pltpu.VMEM)


def sspec():
    return pl.BlockSpec(memory_space=pltpu.SMEM)


def z_swap(x, mask, size):
    return lax.ppermute(x, "tensor", [(i, i ^ mask) for i in range(size)])


def z_gather(x, size):
    return [x] + [z_swap(x, mask, size) for mask in range(1, size)]


def dp_slots(size):
    if size == 8:
        return np.array([((k >> 1) & 3) | ((k & 1) << 2) for k in range(8)], np.int32)
    return None


def dp_gather(x):
    for bit in (2, 4, 1):
        other = lax.ppermute(x, "dp", [(i, i ^ bit) for i in range(8)])
        x = jnp.concatenate([x, other], 0)
    return x


def dp_scatter_slots():
    return np.array([((k & 1) << 2) | (((k >> 1) & 1) << 1) | ((k >> 2) & 1) for k in range(8)], np.int32)


def dp_scatter(x):
    for bit in (1, 2, 4):
        half = x.shape[0] // 2
        other = lax.ppermute(x[half:], "dp", [(i, i ^ bit) for i in range(8)])
        x = (x[:half].astype(F32) + other.astype(F32)).astype(x.dtype)
    return x[0]


def join_rows(ref, index_ref, count, rows):
    if count == 1:
        return ref[0, 0:rows, :]
    return jnp.concatenate([ref[index_ref[c], 0:rows, :] for c in range(count)], 0)


def qkv_body(count, chunks, rows, index_ref, place_ref, *refs):
    toks = refs[:chunks]
    pack_ref, gain_ref = refs[chunks : chunks + 2]
    n1_ref, q_ref, k_ref, v_ref, kt_ref, vt_ref = refs[chunks + 2 :]
    depth = n1_ref.shape[1] // count
    weights = join_rows(pack_ref, index_ref, count, depth)
    width = q_ref.shape[1]
    gain = gain_ref[0:1, :]
    for c in range(chunks):
        at = pl.ds(pl.multiple_of(place_ref[c] * rows, rows), rows)
        x = toks[c][...].astype(F32)
        scale = lax.rsqrt(jnp.mean(x * x, axis=1, keepdims=True) + EPSILON)
        normed = (x * scale * gain).astype(BF)
        n1_ref[at, :] = normed
        out = dot_nn(normed, weights)
        q_ref[at, :] = (out[:, :width].astype(BF).astype(F32) * 0.125).astype(BF)
        key = out[:, width : 2 * width]
        value = out[:, 2 * width :]
        k_ref[at, :] = key.astype(BF)
        v_ref[at, :] = value.astype(BF)
        kt_ref[:, at] = jnp.transpose(key).astype(BF)
        vt_ref[:, at] = jnp.transpose(value).astype(BF)


def qkv_call(index, place, toks, pack, gain, width):
    chunks, rows, depth = len(toks), toks[0].shape[0], toks[0].shape[1]
    total = chunks * rows
    shapes = [(total, depth)] + [(total, width)] * 3 + [(width, total)] * 2
    return pl.pallas_call(
        functools.partial(qkv_body, pack.shape[0], chunks, rows),
        in_specs=[sspec(), sspec()] + [vspec()] * (chunks + 2),
        out_specs=[vspec()] * 6,
        out_shape=[jax.ShapeDtypeStruct(s, BF) for s in shapes],
        compiler_params=params(),
        cost_estimate=cost(2 * total * depth * 3 * width, 8 * total * depth),
        name="norm_qkv",
    )(index, place, *toks, pack, gain)


def extents(total):
    blocks = total // BLOCK
    return [(i, min(BLOCK * (i + 2), total)) for i in range(blocks)]


def fwd_body(total, starts_ref, q_ref, k_ref, vt_ref, line_ref, p_ref, ot_ref, att_ref, attt_ref, strip_ref, mask_ref):
    head = pl.program_id(0)
    heads = pl.num_programs(0)
    blocks = total // BLOCK
    width = q_ref.shape[1]
    dim = width // 4

    @pl.when(head == 0)
    def _():
        def label(pos):
            first = (pos >= starts_ref[0, 0]) & (pos < starts_ref[0, 0] + PIECE)
            second = (pos >= starts_ref[0, 1]) & (pos < starts_ref[0, 1] + PIECE)
            return first, second

        for i in range(blocks):
            for j in (i, i + 1):
                if j >= blocks:
                    continue
                kpos = lax.broadcasted_iota(jnp.int32, (BLOCK, BLOCK), 0) + BLOCK * j
                qpos = lax.broadcasted_iota(jnp.int32, (BLOCK, BLOCK), 1) + BLOCK * i
                k1, k2 = label(kpos)
                q1, q2 = label(qpos)
                seen = (kpos <= qpos) | (k1 & q1) | (k2 & q2)
                mask_ref[2 * i + j - i] = jnp.where(seen, 0.0, MASKED)

    for beta in range(blocks + 1):
        start = BLOCK * (blocks - beta)
        window = line_ref[0, 0:1, start : start + 2 * BLOCK]
        spread = jnp.broadcast_to(window, (BLOCK, 2 * BLOCK))
        rolled = pltpu.roll(spread, BLOCK + 1, 1, stride=1, stride_axis=0)
        strip_ref[BLOCK * beta : BLOCK * (beta + 1), :] = rolled[:, :BLOCK]

    lanes = lax.broadcasted_iota(jnp.int32, (BLOCK, width), 1)
    own = (lanes >= head * dim) & (lanes < (head + 1) * dim)
    at_head = pl.ds(pl.multiple_of(head * dim, dim), dim)
    for i, extent in extents(total):
        q_rows = q_ref[BLOCK * i : BLOCK * (i + 1), :]
        q_own = jnp.where(own, q_rows, jnp.zeros_like(q_rows))
        base = BLOCK * (blocks - 1 - i)
        scores = dot_nt(k_ref[0:extent, :], q_own) + strip_ref[base : base + extent, :]
        parts = [scores[BLOCK * j : BLOCK * (j + 1)] for j in range(extent // BLOCK)]
        for j in (i, i + 1):
            if j < blocks:
                parts[j] = parts[j] + mask_ref[2 * i + j - i]
        top = functools.reduce(jnp.maximum, parts)
        top = jnp.max(top, axis=0, keepdims=True)
        parts = [jnp.exp(part - top) for part in parts]
        total_sum = jnp.sum(functools.reduce(jnp.add, parts), axis=0, keepdims=True)
        inverse = 1.0 / total_sum
        chances = jnp.concatenate([(part * inverse).astype(BF) for part in parts], 0)
        p_ref[0, 0:extent, BLOCK * i : BLOCK * (i + 1)] = chances
        ot_ref[at_head, BLOCK * i : BLOCK * (i + 1)] = dot_nn(vt_ref[at_head, 0:extent], chances)

    @pl.when(head == heads - 1)
    def _():
        mixed = ot_ref[...]
        attt_ref[...] = mixed.astype(BF)
        att_ref[...] = jnp.transpose(mixed).astype(BF)


def attn_fwd(starts, q, k, vt, line):
    total, width = q.shape
    heads = line.shape[0]
    blocks = total // BLOCK
    whole = lambda shape: pl.BlockSpec(shape, lambda h: (0,) * len(shape))
    return pl.pallas_call(
        functools.partial(fwd_body, total),
        grid=(heads,),
        in_specs=[
            sspec(),
            whole((total, width)),
            whole((total, width)),
            whole((width, total)),
            pl.BlockSpec((1, 1, line.shape[2]), lambda h: (h, 0, 0)),
        ],
        out_specs=[
            pl.BlockSpec((1, total, total), lambda h: (h, 0, 0)),
            whole((width, total)),
            whole((total, width)),
            whole((width, total)),
        ],
        out_shape=[
            jax.ShapeDtypeStruct((heads, total, total), BF),
            jax.ShapeDtypeStruct((width, total), F32),
            jax.ShapeDtypeStruct((total, width), BF),
            jax.ShapeDtypeStruct((width, total), BF),
        ],
        scratch_shapes=[
            pltpu.VMEM((BLOCK * (blocks + 1), BLOCK), F32),
            pltpu.VMEM((2 * blocks, BLOCK, BLOCK), F32),
        ],
        compiler_params=params(("arbitrary",)),
        cost_estimate=cost(heads * 4 * total * total * width, 10 * total * total),
        name="attn_forward",
    )(starts, q, k, vt, line)


def diagonal_sums(acc):
    half = BLOCK // 2
    low, high = acc[:half], acc[half:]
    rows = jnp.concatenate(
        [high[:, :half], high[:, half:] + low[:, :half], low[:, half:], jnp.zeros((half, half), F32)], 1
    )
    step = half // 2
    while step >= 8:
        rows = rows[step:] + pltpu.roll(rows[:step], step, 1)
        step //= 2
    index = lax.broadcasted_iota(jnp.int32, rows.shape, 0)
    for step in (4, 2, 1):
        rows = jnp.where((index & step) == 0, pltpu.roll(rows, step, 1), rows)
    return jnp.sum(rows, axis=0, keepdims=True)


def bwd_body(total, chunks, place_ref, *refs):
    grads = refs[:chunks]
    p_ref, q_ref, k_ref, v_ref, kt_ref, ot_ref = refs[chunks : chunks + 6]
    dq_ref, dk_ref, dv_ref, diag_ref = refs[chunks + 6 : chunks + 10]
    do_ref, dot_ref, dqt_ref, dka_ref, dva_ref, ds_ref, acc_ref = refs[chunks + 10 :]
    head = pl.program_id(0)
    heads = pl.num_programs(0)
    blocks = total // BLOCK
    rows = total // chunks
    width = q_ref.shape[1]
    dim = width // 4

    @pl.when(head == 0)
    def _():
        for c in range(chunks):
            at = pl.ds(pl.multiple_of(place_ref[c] * rows, rows), rows)
            do_ref[at, :] = grads[c][...]
        dot_ref[...] = jnp.transpose(do_ref[...].astype(F32))
        dka_ref[...] = jnp.zeros_like(dka_ref)
        dva_ref[...] = jnp.zeros_like(dva_ref)

    at_head = pl.ds(pl.multiple_of(head * dim, dim), dim)
    inner = jnp.sum(dot_ref[at_head, :] * ot_ref[at_head, :], axis=0, keepdims=True)
    lanes = lax.broadcasted_iota(jnp.int32, (total, width), 1)
    own = (lanes >= head * dim) & (lanes < (head + 1) * dim)
    q_own = jnp.where(own, q_ref[...], jnp.zeros_like(q_ref))
    do_own = jnp.where(own, do_ref[...], jnp.zeros_like(do_ref))
    written = 0
    for i, extent in reversed(extents(total)):
        cols = slice(BLOCK * i, BLOCK * (i + 1))
        chance_grad = dot_nt(v_ref[0:extent, :], do_own[cols, :])
        chances = p_ref[0, 0:extent, cols].astype(F32)
        score_grad = (chances * (chance_grad - inner[:, cols])).astype(BF)
        ds_ref[0:extent, cols] = score_grad
        dqt_ref[at_head, cols] = dot_nn(kt_ref[at_head, 0:extent], score_grad)
        base = BLOCK * (blocks - 1 - i)
        wide = score_grad.astype(F32)
        if i == blocks - 1:
            acc_ref[0:extent, :] = wide
            written = extent
        else:
            old = written - base
            acc_ref[base:written, :] += wide[:old]
            if base + extent > written:
                acc_ref[written : base + extent, :] = wide[old:]
                written = base + extent
    for j in range(blocks):
        first = max(0, BLOCK * (j - 1))
        keys = slice(BLOCK * j, BLOCK * (j + 1))
        dka_ref[keys, :] += dot_nn(ds_ref[keys, first:], q_own[first:, :])
        dva_ref[keys, :] += dot_nn(p_ref[0, keys, first:], do_own[first:, :])
    for beta in range(blocks + 1):
        diag_ref[0, beta : beta + 1, :] = diagonal_sums(acc_ref[BLOCK * beta : BLOCK * (beta + 1), :])

    @pl.when(head == heads - 1)
    def _():
        dq_ref[...] = (jnp.transpose(dqt_ref[...]) * 0.125).astype(BF)
        dk_ref[...] = dka_ref[...].astype(BF)
        dv_ref[...] = dva_ref[...].astype(BF)


def attn_bwd(place, grads, chances, q, k, v, kt, ot):
    total, width = q.shape
    heads = chances.shape[0]
    blocks = total // BLOCK
    chunks = len(grads)
    whole = lambda shape: pl.BlockSpec(shape, lambda h: (0,) * len(shape))
    return pl.pallas_call(
        functools.partial(bwd_body, total, chunks),
        grid=(heads,),
        in_specs=[sspec()]
        + [whole(grads[0].shape)] * chunks
        + [pl.BlockSpec((1, total, total), lambda h: (h, 0, 0))]
        + [whole((total, width))] * 3
        + [whole((width, total))] * 2,
        out_specs=[whole((total, width))] * 3 + [pl.BlockSpec((1, blocks + 1, 2 * BLOCK), lambda h: (h, 0, 0))],
        out_shape=[jax.ShapeDtypeStruct((total, width), BF)] * 3
        + [jax.ShapeDtypeStruct((heads, blocks + 1, 2 * BLOCK), F32)],
        scratch_shapes=[
            pltpu.VMEM((total, width), BF),
            pltpu.VMEM((width, total), F32),
            pltpu.VMEM((width, total), F32),
            pltpu.VMEM((total, width), F32),
            pltpu.VMEM((total, width), F32),
            pltpu.VMEM((total, total), BF),
            pltpu.VMEM((BLOCK * (blocks + 1), BLOCK), F32),
        ],
        compiler_params=params(("arbitrary",)),
        cost_estimate=cost(heads * 8 * total * total * width, 10 * total * total),
        name="attn_backward",
    )(place, *grads, chances, q, k, v, kt, ot)


def join_lanes(ref, index_ref, count, slot):
    if count == 1:
        return ref[0, slot]
    return jnp.concatenate([ref[index_ref[c], slot] for c in range(count)], 1)


def mid_body(count, chunks, index_ref, *refs):
    atts = refs[:chunks]
    w_ref, tok_ref, gain_ref, mid_ref, n2_ref = refs[chunks:]
    u = tok_ref[...].astype(F32)
    for c in range(chunks):
        u = u + dot_nn(atts[c][...], join_lanes(w_ref, index_ref, count, c))
    mid_ref[...] = u
    scale = lax.rsqrt(jnp.mean(u * u, axis=1, keepdims=True) + EPSILON)
    n2_ref[...] = (u * scale * gain_ref[1:2, :]).astype(BF)


def mid_call(index, atts, w_out, tok, gains):
    chunks = len(atts)
    return pl.pallas_call(
        functools.partial(mid_body, w_out.shape[0], chunks),
        in_specs=[sspec()] + [vspec()] * (chunks + 3),
        out_specs=[vspec()] * 2,
        out_shape=[jax.ShapeDtypeStruct(tok.shape, F32), jax.ShapeDtypeStruct(tok.shape, BF)],
        compiler_params=params(),
        cost_estimate=cost(2 * tok.shape[0] * tok.shape[1] ** 2, 4 * tok.shape[1] ** 2),
        name="out_projection_norm",
    )(index, *atts, w_out, tok, gains)


def split_dot(a, b, dot):
    high = a.astype(BF)
    low = (a - high.astype(F32)).astype(BF)
    return dot(high, b) + dot(low, b)


def moe_body(count, chunks, unit, place_ref, *refs):
    n2s = refs[:chunks]
    gs = refs[chunks : 2 * chunks]
    sel_ref, rout_ref, w_ref = refs[2 * chunks : 2 * chunks + 3]
    rest = refs[2 * chunks + 3 :]
    outs = rest[:chunks]
    ngs = rest[chunks : 2 * chunks]
    hg_ref, gg_ref, ug_ref, rpart_ref = rest[2 * chunks : 2 * chunks + 4]
    out_acc, ng_acc, gate_ref, sum_ref, prob_ref = rest[2 * chunks + 4 :]
    step = pl.program_id(0)
    steps = pl.num_programs(0)
    rows = n2s[0].shape[0]
    fb = hg_ref.shape[1]
    lane = lax.broadcasted_iota(jnp.int32, (rows, 128), 1)

    @pl.when(step == 0)
    def _():
        out_acc[...] = jnp.zeros_like(out_acc)
        ng_acc[...] = jnp.zeros_like(ng_acc)
        sum_ref[...] = jnp.zeros_like(sum_ref)
        for c in range(chunks):
            logits = dot_nt(n2s[c][...], rout_ref[...])
            logits = jnp.where(lane < EXPERTS, logits, MASKED)
            raised = jnp.exp(logits - jnp.max(logits, axis=1, keepdims=True))
            probs = raised / jnp.sum(raised, axis=1, keepdims=True)
            prob_ref[c] = probs
            at = pl.ds(pl.multiple_of(place_ref[c] * rows, rows), rows)
            gates = probs * sel_ref[at, :]
            for e in range(EXPERTS):
                one = jnp.sum(jnp.where(lane == e, gates, 0.0), axis=1, keepdims=True)
                gate_ref[e, c] = jnp.broadcast_to(one, (rows, 128))

    def joined(which):
        if count == 1:
            return w_ref[0, which]
        return jnp.concatenate([w_ref[d, which] for d in range(count)], 1)

    wg, wu, wd = joined(0), joined(1), joined(2)
    for c in range(chunks):
        n2 = n2s[c][...]
        gate_pre = dot_nt(n2, wg)
        up_pre = dot_nt(n2, wu)
        raw = dot_nt(gs[c][...], wd)
        square = gate_pre * gate_pre
        c0 = float(np.sqrt(2.0 / np.pi))
        th = jnp.tanh(gate_pre * (c0 + (c0 * 0.044715) * square))
        half = 0.5 + 0.5 * th
        act = gate_pre * half
        slope = half + gate_pre * (0.5 * c0 + (1.5 * c0 * 0.044715) * square) * (1.0 - th * th)
        hidden = act * up_pre
        prod = raw * hidden
        hgs, ggs, ugs = [], [], []
        for m in range(fb // 128):
            col = step * (fb // 128) + m
            e_low = (col * 128) // unit
            e_high = (col * 128 + 127) // unit
            bound = jnp.where(e_high > e_low, unit * e_high - col * 128, 128)
            is_low = lane < bound
            part = slice(128 * m, 128 * (m + 1))
            gate = jnp.where(is_low, gate_ref[e_low, c], gate_ref[e_high, c])
            sum_ref[e_low, c] += jnp.where(is_low, prod[:, part], 0.0)
            sum_ref[e_high, c] += jnp.where(is_low, 0.0, prod[:, part])
            hgs.append((gate * hidden[:, part]).astype(BF))
            hidden_grad = gate * raw[:, part]
            ggs.append((hidden_grad * up_pre[:, part] * slope[:, part]).astype(BF))
            ugs.append((hidden_grad * act[:, part]).astype(BF))
        hg, gg, ug = [jnp.concatenate(x, 1) for x in (hgs, ggs, ugs)]
        at = slice(rows * c, rows * (c + 1))
        hg_ref[at, :] = hg
        gg_ref[at, :] = gg
        ug_ref[at, :] = ug
        out_acc[c] += dot_nn(hg, wd)
        ng_acc[c] += dot_nn(gg, wg) + dot_nn(ug, wu)

    @pl.when(step == steps - 1)
    def _():
        router_grad = jnp.zeros((128, n2s[0].shape[1]), F32)
        for c in range(chunks):
            outs[c][...] = out_acc[c].astype(BF)
            at = pl.ds(pl.multiple_of(place_ref[c] * rows, rows), rows)
            grad = jnp.zeros((rows, 128), F32)
            for e in range(EXPERTS):
                grad = grad + jnp.where(lane == e, jnp.sum(sum_ref[e, c], axis=1, keepdims=True), 0.0)
            grad = grad * sel_ref[at, :]
            probs = prob_ref[c]
            logit_grad = probs * (grad - jnp.sum(probs * grad, axis=1, keepdims=True))
            ngs[c][...] = (ng_acc[c] + split_dot(logit_grad, rout_ref[...], dot_nn)).astype(BF)
            router_grad = router_grad + split_dot(logit_grad, n2s[c][...], dot_tn)
        rpart_ref[...] = router_grad[0:8, :]


def moe_call(place, n2s, gs, sel, router, weights, unit):
    chunks, rows, depth = len(n2s), n2s[0].shape[0], n2s[0].shape[1]
    count, _, ff, part = weights.shape
    tokens = chunks * rows
    whole = lambda shape: pl.BlockSpec(shape, lambda s: (0,) * len(shape))
    kept = [jax.ShapeDtypeStruct((tokens, ff), BF)] * 3
    return pl.pallas_call(
        functools.partial(moe_body, count, chunks, unit),
        grid=(ff // BLOCK,),
        in_specs=[sspec()]
        + [whole((rows, depth))] * (2 * chunks)
        + [whole(sel.shape), whole(router.shape), pl.BlockSpec((count, 3, BLOCK, part), lambda s: (0, 0, s, 0))],
        out_specs=[whole((rows, depth))] * (2 * chunks)
        + [pl.BlockSpec((tokens, BLOCK), lambda s: (0, s))] * 3
        + [whole((8, depth))],
        out_shape=[jax.ShapeDtypeStruct((rows, depth), BF)] * (2 * chunks)
        + kept
        + [jax.ShapeDtypeStruct((8, depth), F32)],
        scratch_shapes=[
            pltpu.VMEM((chunks, rows, depth), F32),
            pltpu.VMEM((chunks, rows, depth), F32),
            pltpu.VMEM((EXPERTS, chunks, rows, 128), F32),
            pltpu.VMEM((EXPERTS, chunks, rows, 128), F32),
            pltpu.VMEM((chunks, rows, 128), F32),
        ],
        compiler_params=params(("arbitrary",)),
        cost_estimate=cost(12 * tokens * depth * ff, 6 * depth * ff + 12 * tokens * depth),
        name="experts",
    )(place, *n2s, *gs, sel, router, weights)


def wgrad_body(count, groups, chunks, *refs):
    kept = refs[: 3 * groups]
    n2s = refs[3 * groups : 3 * groups + chunks]
    gs = refs[3 * groups + chunks : 3 * groups + 2 * chunks]
    out_ref = refs[-1]
    part = out_ref.shape[3]
    rows = n2s[0].shape[0]
    per = chunks // groups
    for which, (pick, sides) in enumerate(((1, n2s), (2, n2s), (0, gs))):
        total = None
        for c in range(chunks):
            at = slice(rows * (c % per), rows * (c % per + 1))
            term = dot_tn(kept[3 * (c // per) + pick][at, :], sides[c][...])
            total = term if total is None else total + term
        total = total.astype(BF)
        for d in range(count):
            out_ref[d, which] = total[:, part * d : part * (d + 1)]


def wgrad_call(count, kept, n2s, gs):
    groups = len(kept) // 3
    tokens, ff = kept[0].shape
    chunks, rows, depth = len(n2s), n2s[0].shape[0], n2s[0].shape[1]
    whole = lambda shape: pl.BlockSpec(shape, lambda s: (0,) * len(shape))
    return pl.pallas_call(
        functools.partial(wgrad_body, count, groups, chunks),
        grid=(ff // BLOCK,),
        in_specs=[pl.BlockSpec((tokens, BLOCK), lambda s: (0, s))] * (3 * groups)
        + [whole((rows, depth))] * (2 * chunks),
        out_specs=pl.BlockSpec((count, 3, BLOCK, depth // count), lambda s: (0, 0, s, 0)),
        out_shape=jax.ShapeDtypeStruct((count, 3, ff, depth // count), BF),
        compiler_params=params(("arbitrary",)),
        cost_estimate=cost(6 * chunks * rows * depth * ff, 12 * depth * ff),
        name="expert_weight_grads",
    )(*kept, *n2s, *gs)


def norm_back(grad, u, gain):
    scale = lax.rsqrt(jnp.mean(u * u, axis=1, keepdims=True) + EPSILON)
    m = grad * gain
    back = scale * m - u * (scale * scale * scale) * jnp.mean(u * m, axis=1, keepdims=True)
    return back, jnp.sum(grad * u * scale, axis=0, keepdims=True)


def resid_body(count, chunks, index_ref, *refs):
    parts = refs[:chunks]
    mid_ref, g_ref, gains_ref, w_ref = refs[chunks : chunks + 4]
    rest = refs[chunks + 4 :]
    resid_ref, aog_ref, gain_ref = rest[:3]
    dos = rest[3:]
    grad = functools.reduce(jnp.add, [p[...].astype(F32) for p in parts])
    back, gain_part = norm_back(grad, mid_ref[...], gains_ref[1:2, :])
    resid = g_ref[...].astype(F32) + back
    resid_ref[...] = resid
    low = resid.astype(BF)
    aog_ref[...] = low
    gain_ref[...] = jnp.broadcast_to(gain_part, gain_ref.shape)
    for c in range(chunks):
        dos[c][...] = dot_nt(low, join_lanes(w_ref, index_ref, count, c)).astype(BF)


def resid_call(index, parts, mid, grad, gains, w_out):
    chunks = len(parts)
    shape = mid.shape
    width = w_out.shape[2]
    return pl.pallas_call(
        functools.partial(resid_body, w_out.shape[0], chunks),
        in_specs=[sspec()] + [vspec()] * (chunks + 4),
        out_specs=[vspec()] * (3 + chunks),
        out_shape=[
            jax.ShapeDtypeStruct(shape, F32),
            jax.ShapeDtypeStruct(shape, BF),
            jax.ShapeDtypeStruct((8, shape[1]), F32),
        ]
        + [jax.ShapeDtypeStruct((shape[0], width), BF)] * chunks,
        compiler_params=params(),
        cost_estimate=cost(2 * shape[0] * shape[1] ** 2, 4 * shape[1] ** 2),
        name="resid_grad",
    )(index, *parts, mid, grad, gains, w_out)


def final_body(chunks, *refs):
    parts = refs[:chunks]
    tok_ref, resid_ref, gains_ref, out_ref = refs[chunks:]
    grad = functools.reduce(jnp.add, [p[...].astype(F32) for p in parts])
    back, _ = norm_back(grad, tok_ref[...].astype(F32), gains_ref[0:1, :])
    out_ref[...] = resid_ref[...] + back


def final_call(parts, tok, resid, gains):
    return pl.pallas_call(
        functools.partial(final_body, len(parts)),
        in_specs=[vspec()] * (len(parts) + 3),
        out_specs=vspec(),
        out_shape=jax.ShapeDtypeStruct(tok.shape, F32),
        compiler_params=params(),
        cost_estimate=cost(20 * tok.size, 12 * tok.size),
        name="in_grad",
    )(*parts, tok, resid, gains)


def proj_body(count, chunks, rows, index_ref, place_ref, dq_ref, dk_ref, dv_ref, pack_ref, *refs):
    toks = refs[:chunks]
    outs = refs[chunks : 2 * chunks]
    gain_ref = refs[2 * chunks]
    depth = outs[0].shape[1]
    width = dq_ref.shape[1]
    weights = join_rows(pack_ref, index_ref, count, depth // count)
    gain = jnp.zeros((1, depth), F32)
    for c in range(chunks):
        at = pl.ds(pl.multiple_of(place_ref[c] * rows, rows), rows)
        grad = dot_nt(dq_ref[at, :], weights[:, :width])
        grad = grad + dot_nt(dk_ref[at, :], weights[:, width : 2 * width])
        grad = grad + dot_nt(dv_ref[at, :], weights[:, 2 * width :])
        outs[c][...] = grad.astype(BF)
        x = toks[c][...].astype(F32)
        scale = lax.rsqrt(jnp.mean(x * x, axis=1, keepdims=True) + EPSILON)
        gain = gain + jnp.sum(grad * x * scale, axis=0, keepdims=True)
    gain_ref[...] = jnp.broadcast_to(gain, gain_ref.shape)


def proj_call(index, place, dq, dk, dv, pack, toks):
    chunks, rows, depth = len(toks), toks[0].shape[0], toks[0].shape[1]
    return pl.pallas_call(
        functools.partial(proj_body, pack.shape[0], chunks, rows),
        in_specs=[sspec(), sspec()] + [vspec()] * (4 + chunks),
        out_specs=[vspec()] * (chunks + 1),
        out_shape=[jax.ShapeDtypeStruct((rows, depth), BF)] * chunks + [jax.ShapeDtypeStruct((8, depth), F32)],
        compiler_params=params(),
        cost_estimate=cost(6 * chunks * rows * depth * dq.shape[1], 8 * chunks * rows * depth),
        name="projection_grads",
    )(index, place, dq, dk, dv, pack, *toks)


def attn_weights_body(count, chunks, rows, slot_ref, place_ref, n1_ref, dq_ref, dk_ref, dv_ref, attt_ref, *refs):
    aogs = refs[:chunks]
    out_ref = refs[chunks]
    depth = n1_ref.shape[1]
    width = dq_ref.shape[1]
    part = depth // count
    normed = n1_ref[...]
    for m, ref in enumerate((dq_ref, dk_ref, dv_ref)):
        grad = dot_tn(normed, ref[...]).astype(BF)
        for d in range(count):
            slot = slot_ref[d]
            for half in range(width // 128):
                at = (m * (width // 128) + half) * part
                out_ref[slot, at : at + part, :] = grad[part * d : part * (d + 1), 128 * half : 128 * (half + 1)]
    grad = None
    for c in range(chunks):
        at = pl.ds(pl.multiple_of(place_ref[c] * rows, rows), rows)
        term = dot_nn(attt_ref[:, at], aogs[c][...])
        grad = term if grad is None else grad + term
    grad = grad.astype(BF)
    for d in range(count):
        at = 3 * (width // 128) * part
        out_ref[slot_ref[d], at : at + width, :] = grad[:, part * d : part * (d + 1)]


def attn_weights_call(slots, place, n1, dq, dk, dv, attt, aogs, count):
    total, depth = n1.shape
    width = dq.shape[1]
    part = depth // count
    chunks, rows = len(aogs), aogs[0].shape[0]
    out = (count, 3 * width * part // 128 + width, 128)
    return pl.pallas_call(
        functools.partial(attn_weights_body, count, chunks, rows),
        in_specs=[sspec(), sspec()] + [vspec()] * (5 + chunks),
        out_specs=vspec(),
        out_shape=jax.ShapeDtypeStruct(out, BF),
        compiler_params=params(),
        cost_estimate=cost(8 * total * depth * width, 8 * total * depth),
        name="attn_weight_grads",
    )(slots, place, n1, dq, dk, dv, attt, *aogs)


def kept_choices(ids):
    lanes = jnp.arange(128, dtype=jnp.int32)[None, :]
    expert_range = jnp.arange(EXPERTS, dtype=jnp.int32)[None, :]
    first = (ids[:, 0:1] == expert_range).astype(jnp.int32)
    second = (ids[:, 1:2] == expert_range).astype(jnp.int32)
    runs = jnp.cumsum(jnp.concatenate([first, second], 1), axis=0)
    first_run = runs[:, :EXPERTS]
    second_run = runs[:, EXPERTS:] + first_run[-1][None, :]
    place_one = jnp.sum(first_run * first, axis=1, keepdims=True) - 1
    place_two = jnp.sum(second_run * second, axis=1, keepdims=True) - 1
    kept = ((ids[:, 0:1] == lanes) & (place_one < CAP)) | ((ids[:, 1:2] == lanes) & (place_two < CAP))
    return kept.astype(F32)


def on_device(
    tokens_in,
    out_grad,
    attn_gain,
    w_query,
    w_key,
    w_value,
    w_output,
    rel_table,
    moe_gain,
    w_router,
    w_gate,
    w_up,
    down_weight,
    expert_ids,
    piece_starts,
):
    rows, depth = tokens_in.shape
    width = w_query.shape[1]
    z_size = lax.axis_size("tensor")
    dp_size = lax.axis_size("dp")
    z_rank = lax.axis_index("tensor").astype(jnp.int32)
    dp_rank = lax.axis_index("dp").astype(jnp.int32)
    total = rows * z_size
    share = depth // dp_size
    unit = w_gate.shape[2]
    ff = EXPERTS * unit
    heads = rel_table.shape[0]
    direct = dp_size == 8 and share == 128
    place = z_rank ^ jnp.arange(z_size, dtype=jnp.int32)

    local = jnp.stack(
        [
            jnp.swapaxes(w_gate, 1, 2).reshape(ff, share),
            jnp.swapaxes(w_up, 1, 2).reshape(ff, share),
            down_weight.reshape(ff, share),
        ]
    )
    if direct:
        experts_w = lax.all_gather(local, "dp", axis=0)
    else:
        experts_w = lax.all_gather(local, "dp", axis=2, tiled=True)[None]

    toks = z_gather(tokens_in, z_size)
    small = jnp.concatenate([attn_gain, moe_gain, w_router.T.reshape(-1)])[None, :]
    packed = jnp.concatenate([w_query, w_key, w_value], 1)
    wo_slots = jnp.stack(z_gather(w_output, z_size))
    if direct:
        index = jnp.asarray(dp_slots(8))[dp_rank ^ jnp.arange(8, dtype=jnp.int32)]
        pad = jnp.zeros((15, packed.shape[1]), BF)
        pack = dp_gather(jnp.concatenate([packed, small, pad], 0)[None])
        wo_all = dp_gather(wo_slots[None])
        small_all = pack[:, share, :][index]
    else:
        index = jnp.zeros((1,), jnp.int32)
        pack = lax.all_gather(packed, "dp", axis=0, tiled=True)[None]
        small_all = lax.all_gather(small[0], "dp", axis=0)
        wo_all = lax.all_gather(wo_slots, "dp", axis=2, tiled=True)[None]
    small_all = small_all.reshape(dp_size, 2 + EXPERTS, share)
    small_all = jnp.swapaxes(small_all, 0, 1).reshape(2 + EXPERTS, depth)
    gains = jnp.concatenate([small_all[:2].astype(F32), jnp.zeros((6, depth), F32)], 0)
    router = jnp.concatenate([small_all[2:], jnp.zeros((128 - EXPERTS, depth), BF)], 0)

    line_at = 2 * BLOCK - 1 - np.arange(total + 2 * BLOCK)
    line = jnp.dot(rel_table, jnp.asarray(onehot_of(line_at).T), precision=PRECISE)[:, None, :]
    sel = kept_choices(expert_ids)

    n1, q, k, v, kt, vt = qkv_call(index, place, toks, pack, gains, width)
    chances, ot, att, attt = attn_fwd(piece_starts, q, k, vt, line)

    atts = []
    for mask in range(z_size):
        piece = lax.dynamic_slice_in_dim(att, place[mask] * rows, rows, 0)
        atts.append(piece if mask == 0 else z_swap(piece, mask, z_size))
    mid, n2 = mid_call(index, atts, wo_all, tokens_in, gains)

    gs = z_gather(out_grad, z_size)
    n2s = z_gather(n2, z_size)
    moe = moe_call(place, n2s, gs, sel, router, experts_w, unit)
    outs, ngs = moe[:z_size], moe[z_size : 2 * z_size]
    kept = moe[2 * z_size : 2 * z_size + 3]
    router_part = moe[2 * z_size + 3]

    ng_parts = [ngs[0]] + [z_swap(ngs[m], m, z_size) for m in range(1, z_size)]
    weight_grads = wgrad_call(experts_w.shape[0], kept, n2s, gs)
    if direct:
        expert_grads = lax.psum_scatter(weight_grads, "dp", scatter_dimension=0, tiled=False)
    else:
        expert_grads = lax.psum_scatter(weight_grads[0], "dp", scatter_dimension=2, tiled=True)

    resid = resid_call(index, ng_parts, mid, out_grad, gains, wo_all)
    resid_grad, aog, gain_two = resid[:3]
    dos = [resid[3]] + [z_swap(resid[3 + m], m, z_size) for m in range(1, z_size)]
    dq, dk, dv, diag = attn_bwd(place, dos, chances, q, k, v, kt, ot)
    out_parts = [outs[0]] + [z_swap(outs[m], m, z_size) for m in range(1, z_size)]
    out_rows = (mid + functools.reduce(jnp.add, [p.astype(F32) for p in out_parts])).astype(BF)
    aogs = z_gather(aog, z_size)

    proj = proj_call(index, place, dq, dk, dv, pack, toks)
    n1_parts = [proj[0]] + [z_swap(proj[m], m, z_size) for m in range(1, z_size)]
    gain_one = proj[z_size]
    in_grad = final_call(n1_parts, tokens_in, resid_grad, gains)

    if direct:
        slots = jnp.asarray(dp_scatter_slots())[dp_rank ^ jnp.arange(8, dtype=jnp.int32)]
        attn_grads = dp_scatter(attn_weights_call(slots, place, n1, dq, dk, dv, attt, aogs, 8)).astype(F32)
        per = width // 128
        cut = attn_grads[: 3 * per * share].reshape(3, per, share, 128)
        cut = jnp.swapaxes(cut, 1, 2).reshape(3, share, width)
        grad_wo = attn_grads[3 * per * share :]
    else:
        ordered = lax.all_gather(aog, "tensor", axis=0, tiled=True)
        cut = jnp.stack([jnp.dot(n1.T, d, preferred_element_type=F32) for d in (dq, dk, dv)])
        cut = lax.psum_scatter(cut, "dp", scatter_dimension=1, tiled=True)
        grad_wo = jnp.dot(attt, ordered, preferred_element_type=F32)
        grad_wo = lax.psum_scatter(grad_wo, "dp", scatter_dimension=1, tiled=True)

    diag_at = (
        BLOCK * np.arange(total // BLOCK + 1)[:, None] - (BLOCK * (total // BLOCK - 2) + 1) - np.arange(2 * BLOCK)[None, :]
    )
    table = jnp.einsum("hbt,btk->hk", diag, jnp.asarray(onehot_of(diag_at)), precision=PRECISE)

    smalls = jnp.concatenate([gain_one[:1], gain_two[:1], router_part[:EXPERTS]], 0)
    table_row = jnp.pad(table.reshape(1, -1), ((0, 0), (0, depth - heads * BUCKETS)))
    if direct:
        for bit in (1, 2):
            smalls = smalls + z_swap(smalls, bit, z_size)
        smalls = jnp.concatenate([smalls, table_row], 0)
        for bit in (1, 2, 4):
            smalls = smalls + lax.ppermute(smalls, "dp", [(i, i ^ bit) for i in range(8)])
        table_row = smalls[2 + EXPERTS :]
    else:
        smalls = lax.psum(smalls, ("dp", "tensor"))
        table_row = lax.psum(table_row, "dp")
    grad_table = table_row[0, : heads * BUCKETS].reshape(heads, BUCKETS)
    per_device = depth // (dp_size * z_size)
    own = lax.dynamic_slice_in_dim(smalls, (dp_rank * z_size + z_rank) * per_device, per_device, 1)

    wide = expert_grads.astype(F32).reshape(3, EXPERTS, unit, share)
    return (
        out_rows,
        in_grad,
        own[0],
        cut[0],
        cut[1],
        cut[2],
        grad_wo,
        grad_table,
        own[1],
        own[2 : 2 + EXPERTS].T,
        jnp.swapaxes(wide[0], 1, 2),
        jnp.swapaxes(wide[1], 1, 2),
        wide[2],
    )


def solution(mesh):
    rows = P(("dp", "tensor"), None)
    grid = P("dp", "tensor")
    flat = P(("dp", "tensor"))
    weights = (P(None, "dp", "tensor"), P(None, "dp", "tensor"), P(None, "tensor", "dp"))
    in_specs = (rows, rows, P("dp"), grid, grid, grid, P("tensor", "dp"), P("tensor", None), P("dp"), P("dp", None))
    out_specs = (rows, rows, flat, grid, grid, grid, P("tensor", "dp"), P("tensor", None), flat, rows)
    return jax.shard_map(
        on_device,
        mesh=mesh,
        in_specs=in_specs + weights + (P("dp", None), P("dp", None)),
        out_specs=out_specs + weights,
        check_vma=False,
    )
```

```python
import functools

import jax
import jax.numpy as jnp
import numpy as np
from jax import lax
from jax.experimental import pallas as pl
from jax.experimental.pallas import tpu as pltpu
from jax.sharding import PartitionSpec as P

EXPERTS = 4
PIECE = 256
CAP = 640
BUCKETS = 32
EPSILON = 1e-06
PRECISE = lax.Precision.HIGHEST
LIMITS = (12, 16, 23, 32, 46, 64, 91)
MASKED = -1e30
BF = jnp.bfloat16
F32 = jnp.float32
BLOCK = 256
VMEM_LIMIT = 56 * 1024 * 1024


def params(semantics=None):
    return pltpu.CompilerParams(dimension_semantics=semantics, vmem_limit_bytes=VMEM_LIMIT)


def dot_nn(a, b):
    return lax.dot_general(a, b, (((1,), (0,)), ((), ())), preferred_element_type=F32)


def dot_nt(a, b):
    return lax.dot_general(a, b, (((1,), (1,)), ((), ())), preferred_element_type=F32)


def dot_tn(a, b):
    return lax.dot_general(a, b, (((0,), (0,)), ((), ())), preferred_element_type=F32)


def bucket_of(offsets):
    distance = np.abs(offsets)
    far = np.full_like(distance, 8)
    for bound in LIMITS:
        far = far + (distance >= bound)
    return np.where(distance < 8, distance, far) + np.where(offsets > 0, 16, 0)


def onehot_of(offsets):
    return (bucket_of(offsets)[..., None] == np.arange(BUCKETS)).astype(np.float32)


def cost(flops, nbytes):
    return pl.CostEstimate(flops=int(flops), bytes_accessed=int(nbytes), transcendentals=0)


def vspec():
    return pl.BlockSpec(memory_space=pltpu.VMEM)


def sspec():
    return pl.BlockSpec(memory_space=pltpu.SMEM)


def z_swap(x, mask, size):
    return lax.ppermute(x, "tensor", [(i, i ^ mask) for i in range(size)])


def z_gather(x, size):
    near = z_swap(x, 1, size)
    far = z_swap(x, 2, size)
    return [x, near, far, z_swap(far, 1, size)]


def z_direct(parts, size):
    return [parts[0]] + [z_swap(parts[mask], mask, size) for mask in range(1, size)]


def z_reduce(parts, size):
    passed = z_swap(parts[3], 1, size)
    far = z_swap((parts[2].astype(F32) + passed.astype(F32)).astype(BF), 2, size)
    return [parts[0], z_swap(parts[1], 1, size), far]


def after(x, *others):
    return lax.optimization_barrier((x,) + others)[0]


def dp_slots(ranks):
    return ((ranks >> 1) & 3) | ((ranks & 1) << 2)


def dp_step(x, bit):
    other = lax.ppermute(x, "dp", [(i, i ^ bit) for i in range(8)])
    return jnp.concatenate([x, other], 0)


def dp_fold(x, bit):
    half = x.shape[0] // 2
    other = lax.ppermute(x[half:], "dp", [(i, i ^ bit) for i in range(8)])
    return (x[:half].astype(F32) + other.astype(F32)).astype(x.dtype)


def dp_scatter_slots(ranks):
    return ((ranks & 1) << 2) | (((ranks >> 1) & 1) << 1) | ((ranks >> 2) & 1)


def join_rows(ref, index_ref, count, rows):
    if count == 1:
        return ref[0, 0:rows, :]
    return jnp.concatenate([ref[index_ref[c], 0:rows, :] for c in range(count)], 0)


def qkv_body(count, chunks, rows, index_ref, place_ref, *refs):
    toks = refs[:chunks]
    pack_ref, small_ref = refs[chunks : chunks + 2]
    n1_ref, q_ref, k_ref, v_ref, kt_ref, vt_ref, gains_ref, router_ref = refs[chunks + 2 :]
    depth = n1_ref.shape[1] // count
    weights = join_rows(pack_ref, index_ref, count, depth)
    width = q_ref.shape[1]
    if count == 1:
        small = [small_ref[r : r + 1, :] for r in range(2 + EXPERTS)]
    else:
        lines = [small_ref[index_ref[d], depth : depth + 1, :].astype(F32) for d in range(count)]
        small = [
            jnp.concatenate([x[:, depth * r : depth * (r + 1)] for x in lines], 1) for r in range(2 + EXPERTS)
        ]
    small = jnp.concatenate([x.astype(F32) for x in small] + [jnp.zeros((2, depth * count), F32)], 0)
    gains_ref[...] = small
    routers = jnp.concatenate([small[2:], jnp.zeros((10, depth * count), F32)], 0)
    router_ref[...] = jnp.zeros_like(router_ref)
    router_ref[0:16, :] = routers.astype(BF)
    gain = small[0:1, :]
    for c in range(chunks):
        at = pl.ds(pl.multiple_of(place_ref[c] * rows, rows), rows)
        x = toks[c][...].astype(F32)
        scale = lax.rsqrt(jnp.mean(x * x, axis=1, keepdims=True) + EPSILON)
        normed = (x * scale * gain).astype(BF)
        n1_ref[at, :] = normed
        out = dot_nn(normed, weights)
        q_ref[at, :] = (out[:, :width].astype(BF).astype(F32) * 0.125).astype(BF)
        key = out[:, width : 2 * width]
        value = out[:, 2 * width :]
        k_ref[at, :] = key.astype(BF)
        v_ref[at, :] = value.astype(BF)
        kt_ref[:, at] = jnp.transpose(key).astype(BF)
        vt_ref[:, at] = jnp.transpose(value).astype(BF)


def qkv_call(index, place, toks, pack, small, width):
    chunks, rows, depth = len(toks), toks[0].shape[0], toks[0].shape[1]
    total = chunks * rows
    shapes = [(total, depth)] + [(total, width)] * 3 + [(width, total)] * 2
    return pl.pallas_call(
        functools.partial(qkv_body, pack.shape[0], chunks, rows),
        in_specs=[sspec(), sspec()] + [vspec()] * (chunks + 2),
        out_specs=[vspec()] * 8,
        out_shape=[jax.ShapeDtypeStruct(s, BF) for s in shapes]
        + [jax.ShapeDtypeStruct((8, depth), F32), jax.ShapeDtypeStruct((128, depth), BF)],
        compiler_params=params(),
        cost_estimate=cost(2 * total * depth * 3 * width, 8 * total * depth),
        name="norm_qkv",
    )(index, place, *toks, pack, small)


def extents(total):
    blocks = total // BLOCK
    return [(i, min(BLOCK * (i + 2), total)) for i in range(blocks)]


def fwd_body(total, starts_ref, q_ref, k_ref, vt_ref, line_ref, p_ref, ot_ref, att_ref, strip_ref, mask_ref):
    head = pl.program_id(0)
    heads = pl.num_programs(0)
    blocks = total // BLOCK
    width = q_ref.shape[1]
    dim = width // 4

    @pl.when(head == 0)
    def _():
        def label(pos):
            first = (pos >= starts_ref[0, 0]) & (pos < starts_ref[0, 0] + PIECE)
            second = (pos >= starts_ref[0, 1]) & (pos < starts_ref[0, 1] + PIECE)
            return first, second

        for i in range(blocks):
            for j in (i, i + 1):
                if j >= blocks:
                    continue
                kpos = lax.broadcasted_iota(jnp.int32, (BLOCK, BLOCK), 0) + BLOCK * j
                qpos = lax.broadcasted_iota(jnp.int32, (BLOCK, BLOCK), 1) + BLOCK * i
                k1, k2 = label(kpos)
                q1, q2 = label(qpos)
                seen = (kpos <= qpos) | (k1 & q1) | (k2 & q2)
                mask_ref[2 * i + j - i] = jnp.where(seen, 0.0, MASKED)

    for beta in range(blocks + 1):
        start = BLOCK * (blocks - beta)
        window = line_ref[0, 0:1, start : start + 2 * BLOCK]
        spread = jnp.broadcast_to(window, (BLOCK, 2 * BLOCK))
        rolled = pltpu.roll(spread, BLOCK + 1, 1, stride=1, stride_axis=0)
        strip_ref[BLOCK * beta : BLOCK * (beta + 1), :] = rolled[:, :BLOCK]

    lanes = lax.broadcasted_iota(jnp.int32, (BLOCK, width), 1)
    own = (lanes >= head * dim) & (lanes < (head + 1) * dim)
    at_head = pl.ds(pl.multiple_of(head * dim, dim), dim)
    for i, extent in extents(total):
        q_rows = q_ref[BLOCK * i : BLOCK * (i + 1), :]
        q_own = jnp.where(own, q_rows, jnp.zeros_like(q_rows))
        base = BLOCK * (blocks - 1 - i)
        scores = dot_nt(k_ref[0:extent, :], q_own) + strip_ref[base : base + extent, :]
        parts = [scores[BLOCK * j : BLOCK * (j + 1)] for j in range(extent // BLOCK)]
        for j in (i, i + 1):
            if j < blocks:
                parts[j] = parts[j] + mask_ref[2 * i + j - i]
        top = functools.reduce(jnp.maximum, parts)
        top = jnp.max(top, axis=0, keepdims=True)
        parts = [jnp.exp(part - top) for part in parts]
        total_sum = jnp.sum(functools.reduce(jnp.add, parts), axis=0, keepdims=True)
        inverse = 1.0 / total_sum
        chances = jnp.concatenate([(part * inverse).astype(BF) for part in parts], 0)
        p_ref[0, 0:extent, BLOCK * i : BLOCK * (i + 1)] = chances
        ot_ref[at_head, BLOCK * i : BLOCK * (i + 1)] = dot_nn(vt_ref[at_head, 0:extent], chances)

    @pl.when(head == heads - 1)
    def _():
        mixed = ot_ref[...]
        att_ref[...] = jnp.transpose(mixed).astype(BF)


def attn_fwd(starts, q, k, vt, line):
    total, width = q.shape
    heads = line.shape[0]
    blocks = total // BLOCK
    whole = lambda shape: pl.BlockSpec(shape, lambda h: (0,) * len(shape))
    return pl.pallas_call(
        functools.partial(fwd_body, total),
        grid=(heads,),
        in_specs=[
            sspec(),
            whole((total, width)),
            whole((total, width)),
            whole((width, total)),
            pl.BlockSpec((1, 1, line.shape[2]), lambda h: (h, 0, 0)),
        ],
        out_specs=[
            pl.BlockSpec((1, total, total), lambda h: (h, 0, 0)),
            whole((width, total)),
            whole((total, width)),
        ],
        out_shape=[
            jax.ShapeDtypeStruct((heads, total, total), BF),
            jax.ShapeDtypeStruct((width, total), F32),
            jax.ShapeDtypeStruct((total, width), BF),
        ],
        scratch_shapes=[
            pltpu.VMEM((BLOCK * (blocks + 1), BLOCK), F32),
            pltpu.VMEM((2 * blocks, BLOCK, BLOCK), F32),
        ],
        compiler_params=params(("arbitrary",)),
        cost_estimate=cost(heads * 4 * total * total * width, 10 * total * total),
        name="attn_forward",
    )(starts, q, k, vt, line)


def diagonal_sums(acc):
    half = BLOCK // 2
    low, high = acc[:half], acc[half:]
    rows = jnp.concatenate(
        [high[:, :half], high[:, half:] + low[:, :half], low[:, half:], jnp.zeros((half, half), F32)], 1
    )
    step = half // 2
    while step >= 8:
        rows = rows[step:] + pltpu.roll(rows[:step], step, 1)
        step //= 2
    index = lax.broadcasted_iota(jnp.int32, rows.shape, 0)
    for step in (4, 2, 1):
        rows = jnp.where((index & step) == 0, pltpu.roll(rows, step, 1), rows)
    return jnp.sum(rows, axis=0, keepdims=True)


def bwd_body(total, chunks, place_ref, *refs):
    grads = refs[:chunks]
    p_ref, q_ref, k_ref, v_ref, kt_ref, ot_ref = refs[chunks : chunks + 6]
    dq_ref, dk_ref, dv_ref, diag_ref = refs[chunks + 6 : chunks + 10]
    do_ref, dot_ref, dqt_ref, dka_ref, dva_ref, ds_ref, acc_ref = refs[chunks + 10 :]
    head = pl.program_id(0)
    heads = pl.num_programs(0)
    blocks = total // BLOCK
    rows = total // chunks
    width = q_ref.shape[1]
    dim = width // 4

    @pl.when(head == 0)
    def _():
        for c in range(chunks):
            at = pl.ds(pl.multiple_of(place_ref[c] * rows, rows), rows)
            do_ref[at, :] = grads[c][...]
        dot_ref[...] = jnp.transpose(do_ref[...].astype(F32))
        dka_ref[...] = jnp.zeros_like(dka_ref)
        dva_ref[...] = jnp.zeros_like(dva_ref)

    at_head = pl.ds(pl.multiple_of(head * dim, dim), dim)
    inner = jnp.sum(dot_ref[at_head, :] * ot_ref[at_head, :], axis=0, keepdims=True)
    lanes = lax.broadcasted_iota(jnp.int32, (total, width), 1)
    own = (lanes >= head * dim) & (lanes < (head + 1) * dim)
    q_own = jnp.where(own, q_ref[...], jnp.zeros_like(q_ref))
    do_own = jnp.where(own, do_ref[...], jnp.zeros_like(do_ref))
    written = 0
    for i, extent in reversed(extents(total)):
        cols = slice(BLOCK * i, BLOCK * (i + 1))
        chance_grad = dot_nt(v_ref[0:extent, :], do_own[cols, :])
        chances = p_ref[0, 0:extent, cols].astype(F32)
        score_grad = (chances * (chance_grad - inner[:, cols])).astype(BF)
        ds_ref[0:extent, cols] = score_grad
        dqt_ref[at_head, cols] = dot_nn(kt_ref[at_head, 0:extent], score_grad)
        base = BLOCK * (blocks - 1 - i)
        wide = score_grad.astype(F32)
        if i == blocks - 1:
            acc_ref[0:extent, :] = wide
            written = extent
        else:
            old = written - base
            acc_ref[base:written, :] += wide[:old]
            if base + extent > written:
                acc_ref[written : base + extent, :] = wide[old:]
                written = base + extent
    for j in range(blocks):
        first = max(0, BLOCK * (j - 1))
        keys = slice(BLOCK * j, BLOCK * (j + 1))
        dka_ref[keys, :] += dot_nn(ds_ref[keys, first:], q_own[first:, :])
        dva_ref[keys, :] += dot_nn(p_ref[0, keys, first:], do_own[first:, :])
    for beta in range(blocks + 1):
        diag_ref[0, beta : beta + 1, :] = diagonal_sums(acc_ref[BLOCK * beta : BLOCK * (beta + 1), :])

    @pl.when(head == heads - 1)
    def _():
        dq_ref[...] = (jnp.transpose(dqt_ref[...]) * 0.125).astype(BF)
        dk_ref[...] = dka_ref[...].astype(BF)
        dv_ref[...] = dva_ref[...].astype(BF)


def attn_bwd(place, grads, chances, q, k, v, kt, ot):
    total, width = q.shape
    heads = chances.shape[0]
    blocks = total // BLOCK
    chunks = len(grads)
    whole = lambda shape: pl.BlockSpec(shape, lambda h: (0,) * len(shape))
    return pl.pallas_call(
        functools.partial(bwd_body, total, chunks),
        grid=(heads,),
        in_specs=[sspec()]
        + [whole(grads[0].shape)] * chunks
        + [pl.BlockSpec((1, total, total), lambda h: (h, 0, 0))]
        + [whole((total, width))] * 3
        + [whole((width, total))] * 2,
        out_specs=[whole((total, width))] * 3 + [pl.BlockSpec((1, blocks + 1, 2 * BLOCK), lambda h: (h, 0, 0))],
        out_shape=[jax.ShapeDtypeStruct((total, width), BF)] * 3
        + [jax.ShapeDtypeStruct((heads, blocks + 1, 2 * BLOCK), F32)],
        scratch_shapes=[
            pltpu.VMEM((total, width), BF),
            pltpu.VMEM((width, total), F32),
            pltpu.VMEM((width, total), F32),
            pltpu.VMEM((total, width), F32),
            pltpu.VMEM((total, width), F32),
            pltpu.VMEM((total, total), BF),
            pltpu.VMEM((BLOCK * (blocks + 1), BLOCK), F32),
        ],
        compiler_params=params(("arbitrary",)),
        cost_estimate=cost(heads * 160 * total * total * width, 10 * total * total),
        name="attn_backward",
    )(place, *grads, chances, q, k, v, kt, ot)


def join_lanes(ref, index_ref, count, slot):
    if count == 1:
        return ref[0, slot]
    return jnp.concatenate([ref[index_ref[c], slot] for c in range(count)], 1)


def mid_body(count, chunks, index_ref, *refs):
    atts = refs[:chunks]
    w_ref, tok_ref, gain_ref, mid_ref, n2_ref = refs[chunks:]
    u = tok_ref[...].astype(F32)
    for c in range(chunks):
        u = u + dot_nn(atts[c][...], join_lanes(w_ref, index_ref, count, c))
    mid_ref[...] = u
    scale = lax.rsqrt(jnp.mean(u * u, axis=1, keepdims=True) + EPSILON)
    n2_ref[...] = (u * scale * gain_ref[1:2, :]).astype(BF)


def mid_call(index, atts, w_out, tok, gains):
    chunks = len(atts)
    return pl.pallas_call(
        functools.partial(mid_body, w_out.shape[0], chunks),
        in_specs=[sspec()] + [vspec()] * (chunks + 3),
        out_specs=[vspec()] * 2,
        out_shape=[jax.ShapeDtypeStruct(tok.shape, F32), jax.ShapeDtypeStruct(tok.shape, BF)],
        compiler_params=params(),
        cost_estimate=cost(2 * tok.shape[0] * tok.shape[1] ** 2, 4 * tok.shape[1] ** 2),
        name="out_projection_norm",
    )(index, *atts, w_out, tok, gains)


def split_dot(a, b, dot):
    high = a.astype(BF)
    low = (a - high.astype(F32)).astype(BF)
    return dot(high, b) + dot(low, b)


def joined(ref, which):
    if ref.shape[0] == 1:
        return ref[0, which]
    return jnp.concatenate([ref[d, which] for d in range(ref.shape[0])], 1)


def units_body(chunks, unit, place_ref, *refs):
    n2s = refs[:chunks]
    gs = refs[chunks : 2 * chunks]
    sel_ref, rout_ref, w_ref = refs[2 * chunks : 2 * chunks + 3]
    hg_ref, gg_ref, ug_ref, lg_ref, rpart_ref = refs[2 * chunks + 3 : 2 * chunks + 8]
    n2_ref, g_ref, gate_ref, sum_ref, prob_ref, pick_ref = refs[2 * chunks + 8 :]
    step = pl.program_id(0)
    steps = pl.num_programs(0)
    rows = n2s[0].shape[0]
    tokens = chunks * rows
    lane = lax.broadcasted_iota(jnp.int32, (tokens, 128), 1)

    @pl.when(step == 0)
    def _():
        for c in range(chunks):
            n2_ref[rows * c : rows * (c + 1), :] = n2s[c][...]
            g_ref[rows * c : rows * (c + 1), :] = gs[c][...]
        logits = dot_nt(n2_ref[...], rout_ref[...])
        logits = jnp.where(lane < EXPERTS, logits, MASKED)
        raised = jnp.exp(logits - jnp.max(logits, axis=1, keepdims=True))
        prob_ref[...] = raised / jnp.sum(raised, axis=1, keepdims=True)
        for c in range(chunks):
            at = pl.ds(pl.multiple_of(place_ref[c] * rows, rows), rows)
            pick_ref[rows * c : rows * (c + 1), :] = sel_ref[at, :]
        gates = prob_ref[...] * pick_ref[...]
        for e in range(EXPERTS):
            one = jnp.sum(jnp.where(lane == e, gates, 0.0), axis=1, keepdims=True)
            gate_ref[e] = jnp.broadcast_to(one, (tokens, 128))
        sum_ref[...] = jnp.zeros_like(sum_ref)

    wg, wu, wd = joined(w_ref, 0), joined(w_ref, 1), joined(w_ref, 2)
    gate_pre = dot_nt(n2_ref[...], wg)
    up_pre = dot_nt(n2_ref[...], wu)
    raw = dot_nt(g_ref[...], wd)
    c0 = float(np.sqrt(2.0 / np.pi))
    square = gate_pre * gate_pre
    th = jnp.tanh(gate_pre * (c0 + (c0 * 0.044715) * square))
    half = 0.5 + 0.5 * th
    act = gate_pre * half
    slope = half + gate_pre * (0.5 * c0 + (1.5 * c0 * 0.044715) * square) * (1.0 - th * th)
    hidden = act * up_pre
    prod = raw * hidden
    for m in range(hg_ref.shape[1] // 128):
        col = step * (hg_ref.shape[1] // 128) + m
        e_low = (col * 128) // unit
        e_high = (col * 128 + 127) // unit
        is_low = lane < jnp.where(e_high > e_low, unit * e_high - col * 128, 128)
        part = slice(128 * m, 128 * (m + 1))
        gate = jnp.where(is_low, gate_ref[e_low], gate_ref[e_high])
        sum_ref[e_low] += jnp.where(is_low, prod[:, part], 0.0)
        sum_ref[e_high] += jnp.where(is_low, 0.0, prod[:, part])
        hg_ref[:, part] = (gate * hidden[:, part]).astype(BF)
        hidden_grad = gate * raw[:, part]
        gg_ref[:, part] = (hidden_grad * up_pre[:, part] * slope[:, part]).astype(BF)
        ug_ref[:, part] = (hidden_grad * act[:, part]).astype(BF)

    @pl.when(step == steps - 1)
    def _():
        grad = jnp.zeros((tokens, 128), F32)
        for e in range(EXPERTS):
            grad = grad + jnp.where(lane == e, jnp.sum(sum_ref[e], axis=1, keepdims=True), 0.0)
        grad = grad * pick_ref[...]
        probs = prob_ref[...]
        logit_grad = probs * (grad - jnp.sum(probs * grad, axis=1, keepdims=True))
        lg_ref[...] = logit_grad
        rpart_ref[...] = split_dot(logit_grad, n2_ref[...], dot_tn)[0:8, :]


def units_call(place, n2s, gs, sel, router, weights, unit):
    chunks, rows, depth = len(n2s), n2s[0].shape[0], n2s[0].shape[1]
    count, _, ff, part = weights.shape
    tokens = chunks * rows
    whole = lambda shape: pl.BlockSpec(shape, lambda s: (0,) * len(shape))
    return pl.pallas_call(
        functools.partial(units_body, chunks, unit),
        grid=(ff // BLOCK,),
        in_specs=[sspec()]
        + [whole((rows, depth))] * (2 * chunks)
        + [whole(sel.shape), whole(router.shape), pl.BlockSpec((count, 3, BLOCK, part), lambda s: (0, 0, s, 0))],
        out_specs=[pl.BlockSpec((tokens, BLOCK), lambda s: (0, s))] * 3 + [whole((tokens, 128)), whole((8, depth))],
        out_shape=[jax.ShapeDtypeStruct((tokens, ff), BF)] * 3
        + [jax.ShapeDtypeStruct((tokens, 128), F32), jax.ShapeDtypeStruct((8, depth), F32)],
        scratch_shapes=[
            pltpu.VMEM((tokens, depth), BF),
            pltpu.VMEM((tokens, depth), BF),
            pltpu.VMEM((EXPERTS, tokens, 128), F32),
            pltpu.VMEM((EXPERTS, tokens, 128), F32),
            pltpu.VMEM((tokens, 128), F32),
            pltpu.VMEM((tokens, 128), F32),
        ],
        compiler_params=params(("arbitrary",)),
        cost_estimate=cost(6 * tokens * depth * ff, 6 * depth * ff + 12 * tokens * depth),
        name="expert_units",
    )(place, *n2s, *gs, sel, router, weights)


def product_body(terms, chunks, extra, *refs):
    xs = refs[:terms]
    ws = refs[terms : 2 * terms]
    at = 2 * terms + (2 if extra else 0)
    outs = refs[at : at + chunks]
    total = None
    for x, w in zip(xs, ws):
        term = dot_nn(x[...], joined(w, 0))
        total = term if total is None else total + term
    if extra:
        lg_ref, rout_ref = refs[2 * terms : 2 * terms + 2]
        total = total + split_dot(lg_ref[...], rout_ref[...], dot_nn)
    rows = outs[0].shape[0]
    for c in range(chunks):
        outs[c][...] = total[rows * c : rows * (c + 1)].astype(BF)


def product_call(xs, picks, weights, chunks, extra, name):
    tokens, ff = xs[0].shape
    count, _, _, part = weights.shape
    depth = count * part
    rows = tokens // chunks
    per = max(1, BLOCK // part)
    wide = min(part * per, BLOCK)
    whole = lambda shape: pl.BlockSpec(shape, lambda s: (0,) * len(shape))
    place_at = (lambda i, s: (s, i, 0, 0)) if count > 1 else (lambda i, s: (0, i, 0, s))
    w_specs = [pl.BlockSpec((min(per, count), 1, ff, wide // min(per, count)), functools.partial(place_at, i)) for i in picks]
    return pl.pallas_call(
        functools.partial(product_body, len(xs), chunks, bool(extra)),
        grid=(depth // wide,),
        in_specs=[whole((tokens, ff))] * len(xs)
        + w_specs
        + ([whole(extra[0].shape), pl.BlockSpec((128, wide), lambda s: (0, s))] if extra else []),
        out_specs=[pl.BlockSpec((rows, wide), lambda s: (0, s))] * chunks,
        out_shape=[jax.ShapeDtypeStruct((rows, depth), BF)] * chunks,
        compiler_params=params(("arbitrary",)),
        cost_estimate=cost(2 * len(xs) * tokens * depth * ff, 4 * len(xs) * depth * ff),
        name=name,
    )(*xs, *([weights] * len(xs)), *extra)


def wgrad_body(count, chunks, *refs):
    hg_ref, gg_ref, ug_ref = refs[:3]
    n2s = refs[3 : 3 + chunks]
    gs = refs[3 + chunks : 3 + 2 * chunks]
    out_ref, n2_ref, g_ref = refs[3 + 2 * chunks :]
    part = out_ref.shape[3]
    rows = n2s[0].shape[0]

    @pl.when(pl.program_id(0) == 0)
    def _():
        for c in range(chunks):
            n2_ref[rows * c : rows * (c + 1), :] = n2s[c][...]
            g_ref[rows * c : rows * (c + 1), :] = gs[c][...]

    for which, (kept, side) in enumerate(((gg_ref, n2_ref), (ug_ref, n2_ref), (hg_ref, g_ref))):
        total = dot_tn(kept[...], side[...]).astype(BF)
        for d in range(count):
            out_ref[d, which] = total[:, part * d : part * (d + 1)]


def wgrad_call(count, kept, n2s, gs):
    tokens, ff = kept[0].shape
    chunks, rows, depth = len(n2s), n2s[0].shape[0], n2s[0].shape[1]
    whole = lambda shape: pl.BlockSpec(shape, lambda s: (0,) * len(shape))
    return pl.pallas_call(
        functools.partial(wgrad_body, count, chunks),
        grid=(ff // BLOCK,),
        in_specs=[pl.BlockSpec((tokens, BLOCK), lambda s: (0, s))] * 3 + [whole((rows, depth))] * (2 * chunks),
        out_specs=pl.BlockSpec((count, 3, BLOCK, depth // count), lambda s: (0, 0, s, 0)),
        out_shape=jax.ShapeDtypeStruct((count, 3, ff, depth // count), BF),
        scratch_shapes=[pltpu.VMEM((tokens, depth), BF), pltpu.VMEM((tokens, depth), BF)],
        compiler_params=params(("arbitrary",)),
        cost_estimate=cost(6 * tokens * depth * ff, 12 * depth * ff),
        name="expert_weight_grads",
    )(*kept, *n2s, *gs)


def norm_back(grad, u, gain):
    scale = lax.rsqrt(jnp.mean(u * u, axis=1, keepdims=True) + EPSILON)
    m = grad * gain
    back = scale * m - u * (scale * scale * scale) * jnp.mean(u * m, axis=1, keepdims=True)
    return back, jnp.sum(grad * u * scale, axis=0, keepdims=True)


def resid_body(count, chunks, terms, index_ref, *refs):
    parts = refs[:terms]
    mid_ref, g_ref, gains_ref, w_ref = refs[terms : terms + 4]
    rest = refs[terms + 4 :]
    resid_ref, aog_ref, gain_ref = rest[:3]
    dos = rest[3:]
    grad = functools.reduce(jnp.add, [p[...].astype(F32) for p in parts])
    back, gain_part = norm_back(grad, mid_ref[...], gains_ref[1:2, :])
    resid = g_ref[...].astype(F32) + back
    resid_ref[...] = resid
    low = resid.astype(BF)
    aog_ref[...] = low
    gain_ref[...] = jnp.broadcast_to(gain_part, gain_ref.shape)
    for c in range(chunks):
        dos[c][...] = dot_nt(low, join_lanes(w_ref, index_ref, count, c)).astype(BF)


def resid_call(index, parts, mid, grad, gains, w_out):
    chunks, terms = w_out.shape[1], len(parts)
    shape = mid.shape
    width = w_out.shape[2]
    return pl.pallas_call(
        functools.partial(resid_body, w_out.shape[0], chunks, terms),
        in_specs=[sspec()] + [vspec()] * (terms + 4),
        out_specs=[vspec()] * (3 + chunks),
        out_shape=[
            jax.ShapeDtypeStruct(shape, F32),
            jax.ShapeDtypeStruct(shape, BF),
            jax.ShapeDtypeStruct((8, shape[1]), F32),
        ]
        + [jax.ShapeDtypeStruct((shape[0], width), BF)] * chunks,
        compiler_params=params(),
        cost_estimate=cost(2 * shape[0] * shape[1] ** 2, 4 * shape[1] ** 2),
        name="resid_grad",
    )(index, *parts, mid, grad, gains, w_out)


def final_body(chunks, *refs):
    parts = refs[:chunks]
    tok_ref, resid_ref, gains_ref, out_ref = refs[chunks:]
    grad = functools.reduce(jnp.add, [p[...].astype(F32) for p in parts])
    back, _ = norm_back(grad, tok_ref[...].astype(F32), gains_ref[0:1, :])
    out_ref[...] = resid_ref[...] + back


def final_call(parts, tok, resid, gains):
    return pl.pallas_call(
        functools.partial(final_body, len(parts)),
        in_specs=[vspec()] * (len(parts) + 3),
        out_specs=vspec(),
        out_shape=jax.ShapeDtypeStruct(tok.shape, F32),
        compiler_params=params(),
        cost_estimate=cost(20 * tok.size, 12 * tok.size),
        name="in_grad",
    )(*parts, tok, resid, gains)


def proj_body(count, chunks, rows, index_ref, place_ref, dq_ref, dk_ref, dv_ref, pack_ref, *refs):
    toks = refs[:chunks]
    outs = refs[chunks : 2 * chunks]
    gain_ref = refs[2 * chunks]
    depth = outs[0].shape[1]
    width = dq_ref.shape[1]
    weights = join_rows(pack_ref, index_ref, count, depth // count)
    gain = jnp.zeros((1, depth), F32)
    for c in range(chunks):
        at = pl.ds(pl.multiple_of(place_ref[c] * rows, rows), rows)
        grad = dot_nt(dq_ref[at, :], weights[:, :width])
        grad = grad + dot_nt(dk_ref[at, :], weights[:, width : 2 * width])
        grad = grad + dot_nt(dv_ref[at, :], weights[:, 2 * width :])
        outs[c][...] = grad.astype(BF)
        x = toks[c][...].astype(F32)
        scale = lax.rsqrt(jnp.mean(x * x, axis=1, keepdims=True) + EPSILON)
        gain = gain + jnp.sum(grad * x * scale, axis=0, keepdims=True)
    gain_ref[...] = jnp.broadcast_to(gain, gain_ref.shape)


def proj_call(index, place, dq, dk, dv, pack, toks):
    chunks, rows, depth = len(toks), toks[0].shape[0], toks[0].shape[1]
    return pl.pallas_call(
        functools.partial(proj_body, pack.shape[0], chunks, rows),
        in_specs=[sspec(), sspec()] + [vspec()] * (4 + chunks),
        out_specs=[vspec()] * (chunks + 1),
        out_shape=[jax.ShapeDtypeStruct((rows, depth), BF)] * chunks + [jax.ShapeDtypeStruct((8, depth), F32)],
        compiler_params=params(),
        cost_estimate=cost(6 * chunks * rows * depth * dq.shape[1], 8 * chunks * rows * depth),
        name="projection_grads",
    )(index, place, dq, dk, dv, pack, *toks)


def attn_weights_body(count, slot_ref, n1_ref, dq_ref, dk_ref, dv_ref, small_ref, table_ref, out_ref):
    depth = n1_ref.shape[1]
    width = dq_ref.shape[1]
    part = depth // count
    normed = n1_ref[...]
    pieces = width // 128
    for m, ref in enumerate((dq_ref, dk_ref, dv_ref)):
        grad = dot_tn(normed, ref[...]).astype(BF)
        for d in range(count):
            slot = slot_ref[d]
            for half in range(pieces):
                at = (m * pieces + half) * part
                out_ref[slot, at : at + part, :] = grad[part * d : part * (d + 1), 128 * half : 128 * (half + 1)]
    at = 3 * pieces * part
    for d in range(count):
        rows = jnp.concatenate([small_ref[:, part * d : part * (d + 1)], table_ref[...]], 0)
        out_ref[slot_ref[d], at : at + 16, :] = rows.astype(BF)


def attn_weights_call(slots, n1, dq, dk, dv, small, table, count):
    total, depth = n1.shape
    width = dq.shape[1]
    part = depth // count
    return pl.pallas_call(
        functools.partial(attn_weights_body, count),
        in_specs=[sspec()] + [vspec()] * 6,
        out_specs=vspec(),
        out_shape=jax.ShapeDtypeStruct((count, 3 * width * part // 128 + 16, 128), BF),
        compiler_params=params(),
        cost_estimate=cost(6 * total * depth * width, 8 * total * depth),
        name="attn_weight_grads",
    )(slots, n1, dq, dk, dv, small, table)


def wo_grad_body(count, chunks, slot_ref, *refs):
    atts = refs[:chunks]
    aog_ref, out_ref = refs[chunks:]
    width = atts[0].shape[1]
    for c in range(chunks):
        grad = dot_tn(atts[c][...], aog_ref[...]).astype(BF)
        part = grad.shape[1] // count
        for d in range(count):
            out_ref[slot_ref[d], c * width : (c + 1) * width, :] = grad[:, part * d : part * (d + 1)]


def wo_grad_call(slots, atts, aog, count):
    chunks, width = len(atts), atts[0].shape[1]
    rows, depth = aog.shape
    return pl.pallas_call(
        functools.partial(wo_grad_body, count, chunks),
        in_specs=[sspec()] + [vspec()] * (chunks + 1),
        out_specs=vspec(),
        out_shape=jax.ShapeDtypeStruct((count, chunks * width, depth // count), BF),
        compiler_params=params(),
        cost_estimate=cost(2 * rows * depth * chunks * width, 4 * depth * chunks * width),
        name="w_output_grad",
    )(slots, *atts, aog)


def kept_choices(ids):
    lanes = jnp.arange(128, dtype=jnp.int32)[None, :]
    expert_range = jnp.arange(EXPERTS, dtype=jnp.int32)[None, :]
    first = (ids[:, 0:1] == expert_range).astype(jnp.int32)
    second = (ids[:, 1:2] == expert_range).astype(jnp.int32)
    runs = jnp.cumsum(jnp.concatenate([first, second], 1), axis=0)
    first_run = runs[:, :EXPERTS]
    second_run = runs[:, EXPERTS:] + first_run[-1][None, :]
    place_one = jnp.sum(first_run * first, axis=1, keepdims=True) - 1
    place_two = jnp.sum(second_run * second, axis=1, keepdims=True) - 1
    kept = ((ids[:, 0:1] == lanes) & (place_one < CAP)) | ((ids[:, 1:2] == lanes) & (place_two < CAP))
    return kept.astype(F32)


def on_device(
    tokens_in,
    out_grad,
    attn_gain,
    w_query,
    w_key,
    w_value,
    w_output,
    rel_table,
    moe_gain,
    w_router,
    w_gate,
    w_up,
    down_weight,
    expert_ids,
    piece_starts,
):
    rows, depth = tokens_in.shape
    width = w_query.shape[1]
    z_size = lax.axis_size("tensor")
    dp_size = lax.axis_size("dp")
    z_rank = lax.axis_index("tensor").astype(jnp.int32)
    dp_rank = lax.axis_index("dp").astype(jnp.int32)
    total = rows * z_size
    share = depth // dp_size
    unit = w_gate.shape[2]
    ff = EXPERTS * unit
    heads = rel_table.shape[0]
    direct = dp_size == 8 and share == 128
    place = z_rank ^ jnp.arange(z_size, dtype=jnp.int32)

    near = z_swap(tokens_in, 1, z_size)
    far = z_swap(tokens_in, 2, z_size)
    line_at = 2 * BLOCK - 1 - np.arange(total + 2 * BLOCK)
    line = jnp.dot(rel_table, jnp.asarray(onehot_of(line_at).T), precision=PRECISE)[:, None, :]
    sel = kept_choices(expert_ids)
    toks = [tokens_in, near, far, z_swap(after(far, near, sel, line), 1, z_size)]
    small = jnp.concatenate([attn_gain, moe_gain, w_router.T.reshape(-1)])[None, :]
    packed = jnp.concatenate([w_query, w_key, w_value], 1)
    wo_slots = jnp.stack(z_direct([w_output] * z_size, z_size))[None]
    ranks = dp_rank ^ jnp.arange(8, dtype=jnp.int32)
    if direct:
        index, slots = dp_slots(ranks), dp_scatter_slots(ranks)
        pad = jnp.zeros((15, packed.shape[1]), BF)
        pack = dp_step(jnp.concatenate([packed, small, pad], 0)[None], 2)
        pack = dp_step(after(pack, near, far), 4)
        wo_half = dp_step(after(wo_slots, near, far), 2)
        pack = dp_step(pack, 1)
        small_all = pack
    else:
        index = slots = jnp.zeros((1,), jnp.int32)
        pack = lax.all_gather(packed, "dp", axis=0, tiled=True)[None]
        small_all = lax.all_gather(small[0], "dp", axis=0).reshape(dp_size, 2 + EXPERTS, share)
        small_all = jnp.swapaxes(small_all, 0, 1).reshape(2 + EXPERTS, depth)
        small_all = jnp.concatenate([small_all, jnp.zeros((2, depth), BF)], 0)
        wo_all = lax.all_gather(wo_slots[0], "dp", axis=2, tiled=True)[None]

    local = jnp.stack(
        [
            jnp.swapaxes(w_gate, 1, 2).reshape(ff, share),
            jnp.swapaxes(w_up, 1, 2).reshape(ff, share),
            down_weight.reshape(ff, share),
        ]
    )
    if direct:
        experts_w = lax.all_gather(local, "dp", axis=0)
    else:
        experts_w = lax.all_gather(local, "dp", axis=2, tiled=True)[None]

    n1, q, k, v, kt, vt, gains, router = qkv_call(index, place, toks, pack, small_all, width)
    g_near = z_swap(after(out_grad, toks[3]), 1, z_size)
    g_far = z_swap(after(out_grad, toks[3]), 2, z_size)
    chances, ot, att = attn_fwd(piece_starts, q, k, vt, line)

    att = after(att, g_near, g_far)
    if direct:
        wo_all = dp_step(after(dp_step(after(wo_half, n1), 4), att), 1)
    pieces = [lax.dynamic_slice_in_dim(att, place[mask] * rows, rows, 0) for mask in range(z_size)]
    atts = z_direct(pieces, z_size)
    gs = [out_grad, g_near, g_far, z_swap(after(g_far, att), 1, z_size)]
    mid, n2 = mid_call(index, [after(atts[0], gs[3])] + atts[1:], wo_all, tokens_in, gains)

    n2_near = z_swap(n2, 1, z_size)
    n2_far = z_swap(n2, 2, z_size)
    n2s = [n2, n2_near, n2_far, z_swap(after(n2_far, n2_near), 1, z_size)]
    hg, gg, ug, logit_grad, router_part = units_call(place, n2s, gs, sel, router, experts_w, unit)
    ngs = product_call([gg, ug], (0, 1), experts_w, z_size, [logit_grad, router], "normed_two_grads")
    passed = z_swap(ngs[3], 1, z_size)
    outs = product_call([after(hg, ngs[0])], (2,), experts_w, z_size, [], "expert_out")
    both = (ngs[2].astype(F32) + after(passed, outs[0]).astype(F32)).astype(BF)
    far = z_swap(both, 2, z_size)
    ng_near = z_swap(after(ngs[1], passed), 1, z_size)
    weight_grads = wgrad_call(experts_w.shape[0], [after(hg, both, *outs), gg, ug], n2s, gs)
    resid = resid_call(index, [after(ngs[0], weight_grads), ng_near, far], mid, out_grad, gains, wo_all)
    resid_grad, aog, gain_two = resid[:3]
    weight_grads = after(weight_grads, aog)
    if direct:
        expert_grads = lax.psum_scatter(weight_grads, "dp", scatter_dimension=0, tiled=False)
    else:
        expert_grads = lax.psum_scatter(weight_grads[0], "dp", scatter_dimension=2, tiled=True)
    dos = z_direct(resid[3:], z_size)
    count = experts_w.shape[0]
    wo_grads = wo_grad_call(slots, atts, aog, count)
    dos[0] = after(dos[0], wo_grads)
    if direct:
        wo_grads = dp_fold(after(wo_grads, *dos), 1)
    dq, dk, dv, diag = attn_bwd(place, dos, chances, q, k, v, kt, ot)
    out_passed = z_swap(after(outs[3], *dos), 1, z_size)
    out_near = z_swap(after(outs[1], *dos), 1, z_size)
    if direct:
        wo_grads = dp_fold(wo_grads, 2)
        dq = after(dq, wo_grads, out_passed, out_near)
    out_far = z_swap((outs[2].astype(F32) + after(out_passed, dq).astype(F32)).astype(BF), 2, z_size)
    proj = proj_call(index, place, dq, dk, dv, pack, toks)
    gain_one = proj[z_size]
    diag_at = (
        BLOCK * np.arange(total // BLOCK + 1)[:, None] - (BLOCK * (total // BLOCK - 2) + 1) - np.arange(2 * BLOCK)[None, :]
    )
    table = jnp.einsum("hbt,btk->hk", diag, jnp.asarray(onehot_of(diag_at)), precision=PRECISE)
    smalls = jnp.concatenate([gain_one[:1], gain_two[:1], router_part[:EXPERTS], jnp.zeros((2, depth), F32)], 0)
    n1_passed = z_swap(proj[3], 1, z_size)
    n1_near = z_swap(proj[1], 1, z_size)
    if direct:
        table_rows = jnp.pad(table.reshape(1, -1), ((0, 7), (0, 0)))
        attn_grads = attn_weights_call(slots, n1, dq, dk, dv, smalls, table_rows, 8)
        wo_grads = dp_fold(wo_grads, 4)[0]
        n1_passed = after(n1_passed, attn_grads, out_far, wo_grads)
    n1_both = (proj[2].astype(F32) + n1_passed.astype(F32)).astype(BF)
    n1_far = z_swap(n1_both, 2, z_size)
    in_grad = final_call([proj[0], n1_near, n1_far], tokens_in, resid_grad, gains)
    out_parts = [outs[0], out_near, out_far]
    out_rows = (mid + functools.reduce(jnp.add, [p.astype(F32) for p in out_parts])).astype(BF)

    if direct:
        attn_grads = dp_fold(after(attn_grads, n1_both), 1)
        attn_grads = dp_fold(after(attn_grads, n1_near), 2)
        attn_grads = dp_fold(attn_grads, 4)
        attn_grads = attn_grads[0].astype(F32)
        per = width // 128
        cut = attn_grads[: 3 * per * share].reshape(3, per, share, 128)
        cut = jnp.swapaxes(cut, 1, 2).reshape(3, share, width)
        smalls = attn_grads[3 * per * share :]
        grad_table = smalls[8, : heads * BUCKETS].reshape(heads, BUCKETS)
        smalls = smalls[:8]
        for bit in (1, 2):
            smalls = smalls + z_swap(smalls, bit, z_size)
        mine = z_rank
        grad_wo = wo_grads
    else:
        cut = jnp.stack([jnp.dot(n1.T, d, preferred_element_type=F32) for d in (dq, dk, dv)])
        cut = lax.psum_scatter(cut, "dp", scatter_dimension=1, tiled=True)
        smalls = lax.psum(smalls, ("dp", "tensor"))
        grad_table = lax.psum(table, "dp")
        mine = dp_rank * z_size + z_rank
        grad_wo = lax.psum_scatter(wo_grads[0], "dp", scatter_dimension=1, tiled=True)
    wo_parts = z_direct([grad_wo[width * c : width * (c + 1)] for c in range(z_size)], z_size)
    grad_wo = functools.reduce(jnp.add, [p.astype(F32) for p in wo_parts])
    per_device = depth // (dp_size * z_size)
    own = lax.dynamic_slice_in_dim(smalls, mine * per_device, per_device, 1)

    wide = expert_grads.astype(F32).reshape(3, EXPERTS, unit, share)
    return (
        out_rows,
        in_grad,
        own[0],
        cut[0],
        cut[1],
        cut[2],
        grad_wo,
        grad_table,
        own[1],
        own[2 : 2 + EXPERTS].T,
        jnp.swapaxes(wide[0], 1, 2),
        jnp.swapaxes(wide[1], 1, 2),
        wide[2],
    )


def solution(mesh):
    rows = P(("dp", "tensor"), None)
    grid = P("dp", "tensor")
    flat = P(("dp", "tensor"))
    weights = (P(None, "dp", "tensor"), P(None, "dp", "tensor"), P(None, "tensor", "dp"))
    in_specs = (rows, rows, P("dp"), grid, grid, grid, P("tensor", "dp"), P("tensor", None), P("dp"), P("dp", None))
    out_specs = (rows, rows, flat, grid, grid, grid, P("tensor", "dp"), P("tensor", None), flat, rows)
    return jax.shard_map(
        on_device,
        mesh=mesh,
        in_specs=in_specs + weights + (P("dp", None), P("dp", None)),
        out_specs=out_specs + weights,
        check_vma=False,
    )
```

```python
import functools

import jax
import jax.numpy as jnp
import numpy as np
from jax import lax
from jax.experimental import pallas as pl
from jax.experimental.pallas import tpu as pltpu
from jax.sharding import PartitionSpec as P

EXPERTS = 4
PIECE = 256
CAP = 640
BUCKETS = 32
EPSILON = 1e-06
PRECISE = lax.Precision.HIGHEST
LIMITS = (12, 16, 23, 32, 46, 64, 91)
MASKED = -1e30
BF = jnp.bfloat16
F32 = jnp.float32
BLOCK = 256
VMEM_LIMIT = 56 * 1024 * 1024


def params(semantics=None):
    return pltpu.CompilerParams(dimension_semantics=semantics, vmem_limit_bytes=VMEM_LIMIT)


def dot_nn(a, b):
    return lax.dot_general(a, b, (((1,), (0,)), ((), ())), preferred_element_type=F32)


def dot_nt(a, b):
    return lax.dot_general(a, b, (((1,), (1,)), ((), ())), preferred_element_type=F32)


def dot_tn(a, b):
    return lax.dot_general(a, b, (((0,), (0,)), ((), ())), preferred_element_type=F32)


def bucket_of(offsets):
    distance = np.abs(offsets)
    far = np.full_like(distance, 8)
    for bound in LIMITS:
        far = far + (distance >= bound)
    return np.where(distance < 8, distance, far) + np.where(offsets > 0, 16, 0)


def onehot_of(offsets):
    return (bucket_of(offsets)[..., None] == np.arange(BUCKETS)).astype(np.float32)


def cost(flops, nbytes):
    return pl.CostEstimate(flops=int(flops), bytes_accessed=int(nbytes), transcendentals=0)


def vspec():
    return pl.BlockSpec(memory_space=pltpu.VMEM)


def sspec():
    return pl.BlockSpec(memory_space=pltpu.SMEM)


def z_swap(x, mask, size):
    return lax.ppermute(x, "tensor", [(i, i ^ mask) for i in range(size)])


def z_gather(x, size):
    near = z_swap(x, 1, size)
    far = z_swap(x, 2, size)
    return [x, near, far, z_swap(far, 1, size)]


def z_direct(parts, size):
    return [parts[0]] + [z_swap(parts[mask], mask, size) for mask in range(1, size)]


def z_reduce(parts, size):
    passed = z_swap(parts[3], 1, size)
    far = z_swap((parts[2].astype(F32) + passed.astype(F32)).astype(BF), 2, size)
    return [parts[0], z_swap(parts[1], 1, size), far]


def after(x, *others):
    return lax.optimization_barrier((x,) + others)[0]


def dp_slots(ranks):
    return ((ranks >> 1) & 3) | ((ranks & 1) << 2)


def dp_step(x, bit):
    other = lax.ppermute(x, "dp", [(i, i ^ bit) for i in range(8)])
    return jnp.concatenate([x, other], 0)


def dp_fold(keep, send, bit):
    other = lax.ppermute(send, "dp", [(i, i ^ bit) for i in range(8)])
    return (keep.astype(F32) + other.astype(F32)).astype(keep.dtype)


def halves(x):
    return x[: x.shape[0] // 2], x[x.shape[0] // 2 :]


def dp_scatter_slots(ranks):
    return ((ranks & 1) << 2) | (((ranks >> 1) & 1) << 1) | ((ranks >> 2) & 1)


def join_rows(ref, index_ref, count, rows):
    if count == 1:
        return ref[0, 0:rows, :]
    return jnp.concatenate([ref[index_ref[c], 0:rows, :] for c in range(count)], 0)


def qkv_body(count, chunks, rows, index_ref, place_ref, *refs):
    toks = refs[:chunks]
    pack_ref, small_ref = refs[chunks : chunks + 2]
    n1_ref, q_ref, k_ref, v_ref, kt_ref, vt_ref, gains_ref, router_ref = refs[chunks + 2 :]
    depth = n1_ref.shape[1] // count
    weights = join_rows(pack_ref, index_ref, count, depth)
    width = q_ref.shape[1]
    if count == 1:
        small = [small_ref[r : r + 1, :] for r in range(2 + EXPERTS)]
    else:
        lines = [small_ref[index_ref[d], depth : depth + 1, :].astype(F32) for d in range(count)]
        small = [
            jnp.concatenate([x[:, depth * r : depth * (r + 1)] for x in lines], 1) for r in range(2 + EXPERTS)
        ]
    small = jnp.concatenate([x.astype(F32) for x in small] + [jnp.zeros((2, depth * count), F32)], 0)
    gains_ref[...] = small
    routers = jnp.concatenate([small[2:], jnp.zeros((10, depth * count), F32)], 0)
    router_ref[...] = jnp.zeros_like(router_ref)
    router_ref[0:16, :] = routers.astype(BF)
    gain = small[0:1, :]
    for c in range(chunks):
        at = pl.ds(pl.multiple_of(place_ref[c] * rows, rows), rows)
        x = toks[c][...].astype(F32)
        scale = lax.rsqrt(jnp.mean(x * x, axis=1, keepdims=True) + EPSILON)
        normed = (x * scale * gain).astype(BF)
        n1_ref[at, :] = normed
        out = dot_nn(normed, weights)
        q_ref[at, :] = (out[:, :width].astype(BF).astype(F32) * 0.125).astype(BF)
        key = out[:, width : 2 * width]
        value = out[:, 2 * width :]
        k_ref[at, :] = key.astype(BF)
        v_ref[at, :] = value.astype(BF)
        kt_ref[:, at] = jnp.transpose(key).astype(BF)
        vt_ref[:, at] = jnp.transpose(value).astype(BF)


def qkv_call(index, place, toks, pack, small, width):
    chunks, rows, depth = len(toks), toks[0].shape[0], toks[0].shape[1]
    total = chunks * rows
    shapes = [(total, depth)] + [(total, width)] * 3 + [(width, total)] * 2
    return pl.pallas_call(
        functools.partial(qkv_body, pack.shape[0], chunks, rows),
        in_specs=[sspec(), sspec()] + [vspec()] * (chunks + 2),
        out_specs=[vspec()] * 8,
        out_shape=[jax.ShapeDtypeStruct(s, BF) for s in shapes]
        + [jax.ShapeDtypeStruct((8, depth), F32), jax.ShapeDtypeStruct((128, depth), BF)],
        compiler_params=params(),
        cost_estimate=cost(2 * total * depth * 3 * width, 8 * total * depth),
        name="norm_qkv",
    )(index, place, *toks, pack, small)


def extents(total):
    blocks = total // BLOCK
    return [(i, min(BLOCK * (i + 2), total)) for i in range(blocks)]


def fwd_body(total, chunks, starts_ref, place_ref, q_ref, k_ref, vt_ref, line_ref, p_ref, ot_ref, *refs):
    atts = refs[:chunks]
    strip_ref, mask_ref, all_ref = refs[chunks:]
    head = pl.program_id(0)
    heads = pl.num_programs(0)
    blocks = total // BLOCK
    width = q_ref.shape[1]
    dim = width // 4

    @pl.when(head == 0)
    def _():
        def label(pos):
            first = (pos >= starts_ref[0, 0]) & (pos < starts_ref[0, 0] + PIECE)
            second = (pos >= starts_ref[0, 1]) & (pos < starts_ref[0, 1] + PIECE)
            return first, second

        for i in range(blocks):
            for j in (i, i + 1):
                if j >= blocks:
                    continue
                kpos = lax.broadcasted_iota(jnp.int32, (BLOCK, BLOCK), 0) + BLOCK * j
                qpos = lax.broadcasted_iota(jnp.int32, (BLOCK, BLOCK), 1) + BLOCK * i
                k1, k2 = label(kpos)
                q1, q2 = label(qpos)
                seen = (kpos <= qpos) | (k1 & q1) | (k2 & q2)
                mask_ref[2 * i + j - i] = jnp.where(seen, 0.0, MASKED)

    for beta in range(blocks + 1):
        start = BLOCK * (blocks - beta)
        window = line_ref[0, 0:1, start : start + 2 * BLOCK]
        spread = jnp.broadcast_to(window, (BLOCK, 2 * BLOCK))
        rolled = pltpu.roll(spread, BLOCK + 1, 1, stride=1, stride_axis=0)
        strip_ref[BLOCK * beta : BLOCK * (beta + 1), :] = rolled[:, :BLOCK]

    lanes = lax.broadcasted_iota(jnp.int32, (BLOCK, width), 1)
    own = (lanes >= head * dim) & (lanes < (head + 1) * dim)
    at_head = pl.ds(pl.multiple_of(head * dim, dim), dim)
    for i, extent in extents(total):
        q_rows = q_ref[BLOCK * i : BLOCK * (i + 1), :]
        q_own = jnp.where(own, q_rows, jnp.zeros_like(q_rows))
        base = BLOCK * (blocks - 1 - i)
        scores = dot_nt(k_ref[0:extent, :], q_own) + strip_ref[base : base + extent, :]
        parts = [scores[BLOCK * j : BLOCK * (j + 1)] for j in range(extent // BLOCK)]
        for j in (i, i + 1):
            if j < blocks:
                parts[j] = parts[j] + mask_ref[2 * i + j - i]
        top = functools.reduce(jnp.maximum, parts)
        top = jnp.max(top, axis=0, keepdims=True)
        parts = [jnp.exp(part - top) for part in parts]
        total_sum = jnp.sum(functools.reduce(jnp.add, parts), axis=0, keepdims=True)
        inverse = 1.0 / total_sum
        chances = jnp.concatenate([(part * inverse).astype(BF) for part in parts], 0)
        p_ref[0, 0:extent, BLOCK * i : BLOCK * (i + 1)] = chances
        ot_ref[at_head, BLOCK * i : BLOCK * (i + 1)] = dot_nn(vt_ref[at_head, 0:extent], chances)

    @pl.when(head == heads - 1)
    def _():
        mixed = ot_ref[...]
        all_ref[...] = jnp.transpose(mixed).astype(BF)
        rows = total // chunks
        for c in range(chunks):
            at = pl.ds(pl.multiple_of(place_ref[c] * rows, rows), rows)
            atts[c][...] = all_ref[at, :]


def attn_fwd(starts, place, chunks, q, k, vt, line):
    total, width = q.shape
    heads = line.shape[0]
    blocks = total // BLOCK
    whole = lambda shape: pl.BlockSpec(shape, lambda h: (0,) * len(shape))
    return pl.pallas_call(
        functools.partial(fwd_body, total, chunks),
        grid=(heads,),
        in_specs=[
            sspec(),
            sspec(),
            whole((total, width)),
            whole((total, width)),
            whole((width, total)),
            pl.BlockSpec((1, 1, line.shape[2]), lambda h: (h, 0, 0)),
        ],
        out_specs=[
            pl.BlockSpec((1, total, total), lambda h: (h, 0, 0)),
            whole((width, total)),
        ]
        + [whole((total // chunks, width))] * chunks,
        out_shape=[
            jax.ShapeDtypeStruct((heads, total, total), BF),
            jax.ShapeDtypeStruct((width, total), F32),
        ]
        + [jax.ShapeDtypeStruct((total // chunks, width), BF)] * chunks,
        scratch_shapes=[
            pltpu.VMEM((BLOCK * (blocks + 1), BLOCK), F32),
            pltpu.VMEM((2 * blocks, BLOCK, BLOCK), F32),
            pltpu.VMEM((total, width), BF),
        ],
        compiler_params=params(("arbitrary",)),
        cost_estimate=cost(heads * 4 * total * total * width, 10 * total * total),
        name="attn_forward",
    )(starts, place, q, k, vt, line)


def diagonal_sums(acc):
    half = BLOCK // 2
    low, high = acc[:half], acc[half:]
    rows = jnp.concatenate(
        [high[:, :half], high[:, half:] + low[:, :half], low[:, half:], jnp.zeros((half, half), F32)], 1
    )
    step = half // 2
    while step >= 8:
        rows = rows[step:] + pltpu.roll(rows[:step], step, 1)
        step //= 2
    index = lax.broadcasted_iota(jnp.int32, rows.shape, 0)
    for step in (4, 2, 1):
        rows = jnp.where((index & step) == 0, pltpu.roll(rows, step, 1), rows)
    return jnp.sum(rows, axis=0, keepdims=True)


def bwd_body(total, chunks, place_ref, *refs):
    grads = refs[:chunks]
    p_ref, q_ref, k_ref, v_ref, kt_ref, ot_ref = refs[chunks : chunks + 6]
    dq_ref, dk_ref, dv_ref, diag_ref = refs[chunks + 6 : chunks + 10]
    do_ref, dot_ref, dqt_ref, dka_ref, dva_ref, ds_ref, acc_ref = refs[chunks + 10 :]
    head = pl.program_id(0)
    heads = pl.num_programs(0)
    blocks = total // BLOCK
    rows = total // chunks
    width = q_ref.shape[1]
    dim = width // 4

    @pl.when(head == 0)
    def _():
        for c in range(chunks):
            at = pl.ds(pl.multiple_of(place_ref[c] * rows, rows), rows)
            do_ref[at, :] = grads[c][...]
        dot_ref[...] = jnp.transpose(do_ref[...].astype(F32))
        dka_ref[...] = jnp.zeros_like(dka_ref)
        dva_ref[...] = jnp.zeros_like(dva_ref)

    at_head = pl.ds(pl.multiple_of(head * dim, dim), dim)
    inner = jnp.sum(dot_ref[at_head, :] * ot_ref[at_head, :], axis=0, keepdims=True)
    lanes = lax.broadcasted_iota(jnp.int32, (total, width), 1)
    own = (lanes >= head * dim) & (lanes < (head + 1) * dim)
    q_own = jnp.where(own, q_ref[...], jnp.zeros_like(q_ref))
    do_own = jnp.where(own, do_ref[...], jnp.zeros_like(do_ref))
    written = 0
    for i, extent in reversed(extents(total)):
        cols = slice(BLOCK * i, BLOCK * (i + 1))
        chance_grad = dot_nt(v_ref[0:extent, :], do_own[cols, :])
        chances = p_ref[0, 0:extent, cols].astype(F32)
        score_grad = (chances * (chance_grad - inner[:, cols])).astype(BF)
        ds_ref[0:extent, cols] = score_grad
        dqt_ref[at_head, cols] = dot_nn(kt_ref[at_head, 0:extent], score_grad)
        base = BLOCK * (blocks - 1 - i)
        wide = score_grad.astype(F32)
        if i == blocks - 1:
            acc_ref[0:extent, :] = wide
            written = extent
        else:
            old = written - base
            acc_ref[base:written, :] += wide[:old]
            if base + extent > written:
                acc_ref[written : base + extent, :] = wide[old:]
                written = base + extent
    for j in range(blocks):
        first = max(0, BLOCK * (j - 1))
        keys = slice(BLOCK * j, BLOCK * (j + 1))
        dka_ref[keys, :] += dot_nn(ds_ref[keys, first:], q_own[first:, :])
        dva_ref[keys, :] += dot_nn(p_ref[0, keys, first:], do_own[first:, :])
    for beta in range(blocks + 1):
        diag_ref[0, beta : beta + 1, :] = diagonal_sums(acc_ref[BLOCK * beta : BLOCK * (beta + 1), :])

    @pl.when(head == heads - 1)
    def _():
        dq_ref[...] = (jnp.transpose(dqt_ref[...]) * 0.125).astype(BF)
        dk_ref[...] = dka_ref[...].astype(BF)
        dv_ref[...] = dva_ref[...].astype(BF)


def attn_bwd(place, grads, chances, q, k, v, kt, ot):
    total, width = q.shape
    heads = chances.shape[0]
    blocks = total // BLOCK
    chunks = len(grads)
    whole = lambda shape: pl.BlockSpec(shape, lambda h: (0,) * len(shape))
    return pl.pallas_call(
        functools.partial(bwd_body, total, chunks),
        grid=(heads,),
        in_specs=[sspec()]
        + [whole(grads[0].shape)] * chunks
        + [pl.BlockSpec((1, total, total), lambda h: (h, 0, 0))]
        + [whole((total, width))] * 3
        + [whole((width, total))] * 2,
        out_specs=[whole((total, width))] * 3 + [pl.BlockSpec((1, blocks + 1, 2 * BLOCK), lambda h: (h, 0, 0))],
        out_shape=[jax.ShapeDtypeStruct((total, width), BF)] * 3
        + [jax.ShapeDtypeStruct((heads, blocks + 1, 2 * BLOCK), F32)],
        scratch_shapes=[
            pltpu.VMEM((total, width), BF),
            pltpu.VMEM((width, total), F32),
            pltpu.VMEM((width, total), F32),
            pltpu.VMEM((total, width), F32),
            pltpu.VMEM((total, width), F32),
            pltpu.VMEM((total, total), BF),
            pltpu.VMEM((BLOCK * (blocks + 1), BLOCK), F32),
        ],
        compiler_params=params(("arbitrary",)),
        cost_estimate=cost(heads * 160 * total * total * width, 10 * total * total),
        name="attn_backward",
    )(place, *grads, chances, q, k, v, kt, ot)


def join_lanes(ref, index_ref, count, slot):
    if count == 1:
        return ref[0, slot]
    return jnp.concatenate([ref[index_ref[c], slot] for c in range(count)], 1)


def mid_body(count, chunks, index_ref, *refs):
    atts = refs[:chunks]
    w_ref, tok_ref, gain_ref, mid_ref, n2_ref = refs[chunks:]
    u = tok_ref[...].astype(F32)
    for c in range(chunks):
        u = u + dot_nn(atts[c][...], join_lanes(w_ref, index_ref, count, c))
    mid_ref[...] = u
    scale = lax.rsqrt(jnp.mean(u * u, axis=1, keepdims=True) + EPSILON)
    n2_ref[...] = (u * scale * gain_ref[1:2, :]).astype(BF)


def mid_call(index, atts, w_out, tok, gains):
    chunks = len(atts)
    return pl.pallas_call(
        functools.partial(mid_body, w_out.shape[0], chunks),
        in_specs=[sspec()] + [vspec()] * (chunks + 3),
        out_specs=[vspec()] * 2,
        out_shape=[jax.ShapeDtypeStruct(tok.shape, F32), jax.ShapeDtypeStruct(tok.shape, BF)],
        compiler_params=params(),
        cost_estimate=cost(2 * tok.shape[0] * tok.shape[1] ** 2, 4 * tok.shape[1] ** 2),
        name="out_projection_norm",
    )(index, *atts, w_out, tok, gains)


def split_dot(a, b, dot):
    high = a.astype(BF)
    low = (a - high.astype(F32)).astype(BF)
    return dot(high, b) + dot(low, b)


def joined(ref, which):
    if ref.shape[0] == 1:
        return ref[0, which]
    return jnp.concatenate([ref[d, which] for d in range(ref.shape[0])], 1)


def units_body(chunks, unit, place_ref, *refs):
    n2s = refs[:chunks]
    gs = refs[chunks : 2 * chunks]
    sel_ref, rout_ref, w_ref = refs[2 * chunks : 2 * chunks + 3]
    hg_ref, gg_ref, ug_ref, lg_ref, rpart_ref = refs[2 * chunks + 3 : 2 * chunks + 8]
    n2_ref, g_ref, gate_ref, sum_ref, prob_ref, pick_ref = refs[2 * chunks + 8 :]
    step = pl.program_id(0)
    steps = pl.num_programs(0)
    rows = n2s[0].shape[0]
    tokens = chunks * rows
    lane = lax.broadcasted_iota(jnp.int32, (tokens, 128), 1)

    @pl.when(step == 0)
    def _():
        for c in range(chunks):
            n2_ref[rows * c : rows * (c + 1), :] = n2s[c][...]
            g_ref[rows * c : rows * (c + 1), :] = gs[c][...]
        logits = dot_nt(n2_ref[...], rout_ref[...])
        logits = jnp.where(lane < EXPERTS, logits, MASKED)
        raised = jnp.exp(logits - jnp.max(logits, axis=1, keepdims=True))
        prob_ref[...] = raised / jnp.sum(raised, axis=1, keepdims=True)
        for c in range(chunks):
            at = pl.ds(pl.multiple_of(place_ref[c] * rows, rows), rows)
            pick_ref[rows * c : rows * (c + 1), :] = sel_ref[at, :]
        gates = prob_ref[...] * pick_ref[...]
        for e in range(EXPERTS):
            one = jnp.sum(jnp.where(lane == e, gates, 0.0), axis=1, keepdims=True)
            gate_ref[e] = jnp.broadcast_to(one, (tokens, 128))
        sum_ref[...] = jnp.zeros_like(sum_ref)

    wg, wu, wd = joined(w_ref, 0), joined(w_ref, 1), joined(w_ref, 2)
    gate_pre = dot_nt(n2_ref[...], wg)
    up_pre = dot_nt(n2_ref[...], wu)
    raw = dot_nt(g_ref[...], wd)
    c0 = float(np.sqrt(2.0 / np.pi))
    square = gate_pre * gate_pre
    th = jnp.tanh(gate_pre * (c0 + (c0 * 0.044715) * square))
    half = 0.5 + 0.5 * th
    act = gate_pre * half
    slope = half + gate_pre * (0.5 * c0 + (1.5 * c0 * 0.044715) * square) * (1.0 - th * th)
    hidden = act * up_pre
    prod = raw * hidden
    for m in range(hg_ref.shape[1] // 128):
        col = step * (hg_ref.shape[1] // 128) + m
        e_low = (col * 128) // unit
        e_high = (col * 128 + 127) // unit
        is_low = lane < jnp.where(e_high > e_low, unit * e_high - col * 128, 128)
        part = slice(128 * m, 128 * (m + 1))
        gate = jnp.where(is_low, gate_ref[e_low], gate_ref[e_high])
        sum_ref[e_low] += jnp.where(is_low, prod[:, part], 0.0)
        sum_ref[e_high] += jnp.where(is_low, 0.0, prod[:, part])
        hg_ref[:, part] = (gate * hidden[:, part]).astype(BF)
        hidden_grad = gate * raw[:, part]
        gg_ref[:, part] = (hidden_grad * up_pre[:, part] * slope[:, part]).astype(BF)
        ug_ref[:, part] = (hidden_grad * act[:, part]).astype(BF)

    @pl.when(step == steps - 1)
    def _():
        grad = jnp.zeros((tokens, 128), F32)
        for e in range(EXPERTS):
            grad = grad + jnp.where(lane == e, jnp.sum(sum_ref[e], axis=1, keepdims=True), 0.0)
        grad = grad * pick_ref[...]
        probs = prob_ref[...]
        logit_grad = probs * (grad - jnp.sum(probs * grad, axis=1, keepdims=True))
        lg_ref[...] = logit_grad
        rpart_ref[...] = split_dot(logit_grad, n2_ref[...], dot_tn)[0:8, :]


def units_call(place, n2s, gs, sel, router, weights, unit):
    chunks, rows, depth = len(n2s), n2s[0].shape[0], n2s[0].shape[1]
    count, _, ff, part = weights.shape
    tokens = chunks * rows
    whole = lambda shape: pl.BlockSpec(shape, lambda s: (0,) * len(shape))
    return pl.pallas_call(
        functools.partial(units_body, chunks, unit),
        grid=(ff // BLOCK,),
        in_specs=[sspec()]
        + [whole((rows, depth))] * (2 * chunks)
        + [whole(sel.shape), whole(router.shape), pl.BlockSpec((count, 3, BLOCK, part), lambda s: (0, 0, s, 0))],
        out_specs=[pl.BlockSpec((tokens, BLOCK), lambda s: (0, s))] * 3 + [whole((tokens, 128)), whole((8, depth))],
        out_shape=[jax.ShapeDtypeStruct((tokens, ff), BF)] * 3
        + [jax.ShapeDtypeStruct((tokens, 128), F32), jax.ShapeDtypeStruct((8, depth), F32)],
        scratch_shapes=[
            pltpu.VMEM((tokens, depth), BF),
            pltpu.VMEM((tokens, depth), BF),
            pltpu.VMEM((EXPERTS, tokens, 128), F32),
            pltpu.VMEM((EXPERTS, tokens, 128), F32),
            pltpu.VMEM((tokens, 128), F32),
            pltpu.VMEM((tokens, 128), F32),
        ],
        compiler_params=params(("arbitrary",)),
        cost_estimate=cost(6 * tokens * depth * ff, 6 * depth * ff + 12 * tokens * depth),
        name="expert_units",
    )(place, *n2s, *gs, sel, router, weights)


def product_body(terms, chunks, extra, *refs):
    xs = refs[:terms]
    ws = refs[terms : 2 * terms]
    at = 2 * terms + (2 if extra else 0)
    outs = refs[at : at + chunks]
    total = None
    for x, w in zip(xs, ws):
        term = dot_nn(x[...], joined(w, 0))
        total = term if total is None else total + term
    if extra:
        lg_ref, rout_ref = refs[2 * terms : 2 * terms + 2]
        total = total + split_dot(lg_ref[...], rout_ref[...], dot_nn)
    rows = outs[0].shape[0]
    for c in range(chunks):
        outs[c][...] = total[rows * c : rows * (c + 1)].astype(BF)


def product_call(xs, picks, weights, chunks, extra, name):
    tokens, ff = xs[0].shape
    count, _, _, part = weights.shape
    depth = count * part
    rows = tokens // chunks
    per = max(1, BLOCK // part)
    wide = min(part * per, BLOCK)
    whole = lambda shape: pl.BlockSpec(shape, lambda s: (0,) * len(shape))
    place_at = (lambda i, s: (s, i, 0, 0)) if count > 1 else (lambda i, s: (0, i, 0, s))
    w_specs = [pl.BlockSpec((min(per, count), 1, ff, wide // min(per, count)), functools.partial(place_at, i)) for i in picks]
    return pl.pallas_call(
        functools.partial(product_body, len(xs), chunks, bool(extra)),
        grid=(depth // wide,),
        in_specs=[whole((tokens, ff))] * len(xs)
        + w_specs
        + ([whole(extra[0].shape), pl.BlockSpec((128, wide), lambda s: (0, s))] if extra else []),
        out_specs=[pl.BlockSpec((rows, wide), lambda s: (0, s))] * chunks,
        out_shape=[jax.ShapeDtypeStruct((rows, depth), BF)] * chunks,
        compiler_params=params(("arbitrary",)),
        cost_estimate=cost(2 * len(xs) * tokens * depth * ff, 4 * len(xs) * depth * ff),
        name=name,
    )(*xs, *([weights] * len(xs)), *extra)


def wgrad_body(count, chunks, *refs):
    hg_ref, gg_ref, ug_ref = refs[:3]
    n2s = refs[3 : 3 + chunks]
    gs = refs[3 + chunks : 3 + 2 * chunks]
    out_ref, n2_ref, g_ref = refs[3 + 2 * chunks :]
    part = out_ref.shape[3]
    rows = n2s[0].shape[0]

    @pl.when(pl.program_id(0) == 0)
    def _():
        for c in range(chunks):
            n2_ref[rows * c : rows * (c + 1), :] = n2s[c][...]
            g_ref[rows * c : rows * (c + 1), :] = gs[c][...]

    for which, (kept, side) in enumerate(((gg_ref, n2_ref), (ug_ref, n2_ref), (hg_ref, g_ref))):
        total = dot_tn(kept[...], side[...]).astype(BF)
        for d in range(count):
            out_ref[d, which] = total[:, part * d : part * (d + 1)]


def wgrad_call(count, kept, n2s, gs):
    tokens, ff = kept[0].shape
    chunks, rows, depth = len(n2s), n2s[0].shape[0], n2s[0].shape[1]
    whole = lambda shape: pl.BlockSpec(shape, lambda s: (0,) * len(shape))
    return pl.pallas_call(
        functools.partial(wgrad_body, count, chunks),
        grid=(ff // BLOCK,),
        in_specs=[pl.BlockSpec((tokens, BLOCK), lambda s: (0, s))] * 3 + [whole((rows, depth))] * (2 * chunks),
        out_specs=pl.BlockSpec((count, 3, BLOCK, depth // count), lambda s: (0, 0, s, 0)),
        out_shape=jax.ShapeDtypeStruct((count, 3, ff, depth // count), BF),
        scratch_shapes=[pltpu.VMEM((tokens, depth), BF), pltpu.VMEM((tokens, depth), BF)],
        compiler_params=params(("arbitrary",)),
        cost_estimate=cost(6 * tokens * depth * ff, 12 * depth * ff),
        name="expert_weight_grads",
    )(*kept, *n2s, *gs)


def norm_back(grad, u, gain):
    scale = lax.rsqrt(jnp.mean(u * u, axis=1, keepdims=True) + EPSILON)
    m = grad * gain
    back = scale * m - u * (scale * scale * scale) * jnp.mean(u * m, axis=1, keepdims=True)
    return back, jnp.sum(grad * u * scale, axis=0, keepdims=True)


def resid_body(count, chunks, terms, index_ref, *refs):
    parts = refs[:terms]
    mid_ref, g_ref, gains_ref, w_ref = refs[terms : terms + 4]
    rest = refs[terms + 4 :]
    resid_ref, aog_ref, gain_ref = rest[:3]
    dos = rest[3:]
    grad = functools.reduce(jnp.add, [p[...].astype(F32) for p in parts])
    back, gain_part = norm_back(grad, mid_ref[...], gains_ref[1:2, :])
    resid = g_ref[...].astype(F32) + back
    resid_ref[...] = resid
    low = resid.astype(BF)
    aog_ref[...] = low
    gain_ref[...] = jnp.broadcast_to(gain_part, gain_ref.shape)
    for c in range(chunks):
        dos[c][...] = dot_nt(low, join_lanes(w_ref, index_ref, count, c)).astype(BF)


def resid_call(index, parts, mid, grad, gains, w_out):
    chunks, terms = w_out.shape[1], len(parts)
    shape = mid.shape
    width = w_out.shape[2]
    return pl.pallas_call(
        functools.partial(resid_body, w_out.shape[0], chunks, terms),
        in_specs=[sspec()] + [vspec()] * (terms + 4),
        out_specs=[vspec()] * (3 + chunks),
        out_shape=[
            jax.ShapeDtypeStruct(shape, F32),
            jax.ShapeDtypeStruct(shape, BF),
            jax.ShapeDtypeStruct((8, shape[1]), F32),
        ]
        + [jax.ShapeDtypeStruct((shape[0], width), BF)] * chunks,
        compiler_params=params(),
        cost_estimate=cost(2 * shape[0] * shape[1] ** 2, 4 * shape[1] ** 2),
        name="resid_grad",
    )(index, *parts, mid, grad, gains, w_out)


def final_body(chunks, *refs):
    parts = refs[:chunks]
    tok_ref, resid_ref, gains_ref, out_ref = refs[chunks:]
    grad = functools.reduce(jnp.add, [p[...].astype(F32) for p in parts])
    back, _ = norm_back(grad, tok_ref[...].astype(F32), gains_ref[0:1, :])
    out_ref[...] = resid_ref[...] + back


def final_call(parts, tok, resid, gains):
    return pl.pallas_call(
        functools.partial(final_body, len(parts)),
        in_specs=[vspec()] * (len(parts) + 3),
        out_specs=vspec(),
        out_shape=jax.ShapeDtypeStruct(tok.shape, F32),
        compiler_params=params(),
        cost_estimate=cost(20 * tok.size, 12 * tok.size),
        name="in_grad",
    )(*parts, tok, resid, gains)


def proj_body(count, chunks, rows, index_ref, place_ref, dq_ref, dk_ref, dv_ref, pack_ref, two_ref, router_ref, *refs):
    toks = refs[:chunks]
    outs = refs[chunks : 2 * chunks]
    gain_ref = refs[2 * chunks]
    depth = outs[0].shape[1]
    width = dq_ref.shape[1]
    weights = join_rows(pack_ref, index_ref, count, depth // count)
    gain = jnp.zeros((1, depth), F32)
    for c in range(chunks):
        at = pl.ds(pl.multiple_of(place_ref[c] * rows, rows), rows)
        grad = dot_nt(dq_ref[at, :], weights[:, :width])
        grad = grad + dot_nt(dk_ref[at, :], weights[:, width : 2 * width])
        grad = grad + dot_nt(dv_ref[at, :], weights[:, 2 * width :])
        outs[c][...] = grad.astype(BF)
        x = toks[c][...].astype(F32)
        scale = lax.rsqrt(jnp.mean(x * x, axis=1, keepdims=True) + EPSILON)
        gain = gain + jnp.sum(grad * x * scale, axis=0, keepdims=True)
    blank = jnp.zeros((6 - EXPERTS, depth), F32)
    gain_ref[...] = jnp.concatenate([gain, two_ref[0:1, :], router_ref[0:EXPERTS, :], blank], 0)


def proj_call(index, place, dq, dk, dv, pack, gain_two, router_part, toks):
    chunks, rows, depth = len(toks), toks[0].shape[0], toks[0].shape[1]
    return pl.pallas_call(
        functools.partial(proj_body, pack.shape[0], chunks, rows),
        in_specs=[sspec(), sspec()] + [vspec()] * (6 + chunks),
        out_specs=[vspec()] * (chunks + 1),
        out_shape=[jax.ShapeDtypeStruct((rows, depth), BF)] * chunks + [jax.ShapeDtypeStruct((8, depth), F32)],
        compiler_params=params(),
        cost_estimate=cost(6 * chunks * rows * depth * dq.shape[1], 8 * chunks * rows * depth),
        name="projection_grads",
    )(index, place, dq, dk, dv, pack, gain_two, router_part, *toks)


def put(keep_ref, send_ref, slot, at, value):
    half = keep_ref.shape[0]

    @pl.when(slot < half)
    def _():
        keep_ref[slot, at, :] = value

    @pl.when(slot >= half)
    def _():
        send_ref[slot - half, at, :] = value


def attn_weights_body(count, smalls, slot_ref, n1_ref, dq_ref, dk_ref, dv_ref, table_ref, *refs):
    keep_ref, send_ref = refs[smalls:]
    small = functools.reduce(jnp.add, [r[...] for r in refs[:smalls]])
    depth = n1_ref.shape[1]
    width = dq_ref.shape[1]
    part = depth // count
    normed = n1_ref[...]
    pieces = width // 128
    for m, ref in enumerate((dq_ref, dk_ref, dv_ref)):
        grad = dot_tn(normed, ref[...]).astype(BF)
        for d in range(count):
            slot = slot_ref[d]
            for half in range(pieces):
                at = (m * pieces + half) * part
                value = grad[part * d : part * (d + 1), 128 * half : 128 * (half + 1)]
                put(keep_ref, send_ref, slot, slice(at, at + part), value)
    at = 3 * pieces * part
    for d in range(count):
        value = jnp.concatenate([small[:, part * d : part * (d + 1)], table_ref[...]], 0).astype(BF)
        put(keep_ref, send_ref, slot_ref[d], slice(at, at + 16), value)


def attn_weights_call(slots, n1, dq, dk, dv, table, smalls, count):
    total, depth = n1.shape
    width = dq.shape[1]
    part = depth // count
    return pl.pallas_call(
        functools.partial(attn_weights_body, count, len(smalls)),
        in_specs=[sspec()] + [vspec()] * (5 + len(smalls)),
        out_specs=[vspec()] * 2,
        out_shape=[jax.ShapeDtypeStruct((count // 2, 3 * width * part // 128 + 16, 128), BF)] * 2,
        compiler_params=params(),
        cost_estimate=cost(6 * total * depth * width, 8 * total * depth),
        name="attn_weight_grads",
    )(slots, n1, dq, dk, dv, table, *smalls)


def wo_grad_body(count, chunks, slot_ref, *refs):
    atts = refs[:chunks]
    aog_ref, keep_ref, send_ref = refs[chunks:]
    width = atts[0].shape[1]
    for c in range(chunks):
        grad = dot_tn(atts[c][...], aog_ref[...]).astype(BF)
        part = grad.shape[1] // count
        for d in range(count):
            put(keep_ref, send_ref, slot_ref[d], slice(c * width, (c + 1) * width), grad[:, part * d : part * (d + 1)])


def wo_grad_call(slots, atts, aog, count):
    chunks, width = len(atts), atts[0].shape[1]
    rows, depth = aog.shape
    return pl.pallas_call(
        functools.partial(wo_grad_body, count, chunks),
        in_specs=[sspec()] + [vspec()] * (chunks + 1),
        out_specs=[vspec()] * 2,
        out_shape=[jax.ShapeDtypeStruct((max(1, count // 2), chunks * width, depth // count), BF)] * 2,
        compiler_params=params(),
        cost_estimate=cost(2 * rows * depth * chunks * width, 4 * depth * chunks * width),
        name="w_output_grad",
    )(slots, *atts, aog)


def kept_choices(ids):
    lanes = jnp.arange(128, dtype=jnp.int32)[None, :]
    expert_range = jnp.arange(EXPERTS, dtype=jnp.int32)[None, :]
    first = (ids[:, 0:1] == expert_range).astype(jnp.int32)
    second = (ids[:, 1:2] == expert_range).astype(jnp.int32)
    runs = jnp.cumsum(jnp.concatenate([first, second], 1), axis=0)
    first_run = runs[:, :EXPERTS]
    second_run = runs[:, EXPERTS:] + first_run[-1][None, :]
    place_one = jnp.sum(first_run * first, axis=1, keepdims=True) - 1
    place_two = jnp.sum(second_run * second, axis=1, keepdims=True) - 1
    kept = ((ids[:, 0:1] == lanes) & (place_one < CAP)) | ((ids[:, 1:2] == lanes) & (place_two < CAP))
    return kept.astype(F32)


def on_device(
    tokens_in,
    out_grad,
    attn_gain,
    w_query,
    w_key,
    w_value,
    w_output,
    rel_table,
    moe_gain,
    w_router,
    w_gate,
    w_up,
    down_weight,
    expert_ids,
    piece_starts,
):
    rows, depth = tokens_in.shape
    width = w_query.shape[1]
    z_size = lax.axis_size("tensor")
    dp_size = lax.axis_size("dp")
    z_rank = lax.axis_index("tensor").astype(jnp.int32)
    dp_rank = lax.axis_index("dp").astype(jnp.int32)
    total = rows * z_size
    share = depth // dp_size
    unit = w_gate.shape[2]
    ff = EXPERTS * unit
    heads = rel_table.shape[0]
    direct = dp_size == 8 and share == 128
    place = z_rank ^ jnp.arange(z_size, dtype=jnp.int32)

    near = z_swap(tokens_in, 1, z_size)
    far = z_swap(tokens_in, 2, z_size)
    line_at = 2 * BLOCK - 1 - np.arange(total + 2 * BLOCK)
    line = jnp.dot(rel_table, jnp.asarray(onehot_of(line_at).T), precision=PRECISE)[:, None, :]
    sel = kept_choices(expert_ids)
    toks = [tokens_in, near, far, z_swap(after(far, near, sel, line), 1, z_size)]
    w_output_late = after(w_output, far)
    small = jnp.concatenate([attn_gain, moe_gain, w_router.T.reshape(-1)])[None, :]
    packed = jnp.concatenate([w_query, w_key, w_value], 1)
    wo_slots = jnp.stack(z_direct([w_output_late] * z_size, z_size))[None]
    ranks = dp_rank ^ jnp.arange(8, dtype=jnp.int32)
    if direct:
        index, slots = dp_slots(ranks), dp_scatter_slots(ranks)
        pad = jnp.zeros((15, packed.shape[1]), BF)
        pack = dp_step(jnp.concatenate([packed, small, pad], 0)[None], 2)
        pack = dp_step(after(pack, near, far), 4)
        wo_half = dp_step(after(wo_slots, near, far), 2)
        pack = dp_step(after(pack, toks[3], wo_half), 1)
        small_all = pack
    else:
        index = slots = jnp.zeros((1,), jnp.int32)
        pack = lax.all_gather(packed, "dp", axis=0, tiled=True)[None]
        small_all = lax.all_gather(small[0], "dp", axis=0).reshape(dp_size, 2 + EXPERTS, share)
        small_all = jnp.swapaxes(small_all, 0, 1).reshape(2 + EXPERTS, depth)
        small_all = jnp.concatenate([small_all, jnp.zeros((2, depth), BF)], 0)
        wo_all = lax.all_gather(wo_slots[0], "dp", axis=2, tiled=True)[None]

    local = jnp.stack(
        [
            jnp.swapaxes(w_gate, 1, 2).reshape(ff, share),
            jnp.swapaxes(w_up, 1, 2).reshape(ff, share),
            down_weight.reshape(ff, share),
        ]
    )
    if direct:
        experts_w = lax.all_gather(local, "dp", axis=0)
    else:
        experts_w = lax.all_gather(local, "dp", axis=2, tiled=True)[None]

    n1, q, k, v, kt, vt, gains, router = qkv_call(index, place, toks, pack, small_all, width)
    g_near = z_swap(after(out_grad, toks[3]), 1, z_size)
    g_far = z_swap(after(out_grad, toks[3]), 2, z_size)
    fwd = attn_fwd(piece_starts, place, z_size, q, k, vt, line)
    chances, ot = fwd[:2]
    atts = z_direct([after(fwd[2], g_near, g_far)] + [after(x, g_near, g_far) for x in fwd[3:]], z_size)
    if direct:
        wo_all = dp_step(after(dp_step(after(wo_half, n1), 4), atts[1]), 1)
    gs = [out_grad, g_near, g_far, z_swap(after(g_far, fwd[2]), 1, z_size)]
    mid, n2 = mid_call(index, [after(atts[0], gs[3])] + atts[1:], wo_all, tokens_in, gains)

    n2_near = z_swap(n2, 1, z_size)
    n2_far = z_swap(n2, 2, z_size)
    n2s = [n2, n2_near, n2_far, z_swap(after(n2_far, n2_near), 1, z_size)]
    hg, gg, ug, logit_grad, router_part = units_call(place, n2s, gs, sel, router, experts_w, unit)
    ngs = product_call([gg, ug], (0, 1), experts_w, z_size, [logit_grad, router], "normed_two_grads")
    passed = z_swap(ngs[3], 1, z_size)
    outs = product_call([after(hg, ngs[0])], (2,), experts_w, z_size, [], "expert_out")
    both = (ngs[2].astype(F32) + after(passed, outs[0]).astype(F32)).astype(BF)
    far = z_swap(both, 2, z_size)
    ng_near = z_swap(after(ngs[1], passed), 1, z_size)
    weight_grads = wgrad_call(experts_w.shape[0], [after(hg, both, *outs), gg, ug], n2s, gs)
    resid = resid_call(index, [after(ngs[0], weight_grads), ng_near, far], mid, out_grad, gains, wo_all)
    resid_grad, aog, gain_two = resid[:3]
    weight_grads = after(weight_grads, aog)
    if direct:
        expert_grads = lax.psum_scatter(weight_grads, "dp", scatter_dimension=0, tiled=False)
    else:
        expert_grads = lax.psum_scatter(weight_grads[0], "dp", scatter_dimension=2, tiled=True)
    out_passed = z_swap(after(outs[3], aog), 1, z_size)
    dos = z_direct(resid[3:], z_size)
    count = experts_w.shape[0]
    wo_keep, wo_send = wo_grad_call(slots, atts, aog, count)
    out_both = (outs[2].astype(F32) + out_passed.astype(F32)).astype(BF)
    dos[0] = after(dos[0], wo_keep, out_both)
    out_far = z_swap(out_both, 2, z_size)
    out_near = z_swap(after(outs[1], out_both), 1, z_size)
    if direct:
        wo_grads = dp_fold(wo_keep, after(wo_send, *dos), 1)
    dq, dk, dv, diag = attn_bwd(place, dos, chances, q, k, v, kt, ot)
    if direct:
        wo_grads = dp_fold(*halves(wo_grads), 2)
        dq = after(dq, wo_grads)
    dq = after(dq, out_far, out_near)
    proj = proj_call(index, place, dq, dk, dv, pack, gain_two, router_part, toks)

    diag_at = (
        BLOCK * np.arange(total // BLOCK + 1)[:, None] - (BLOCK * (total // BLOCK - 2) + 1) - np.arange(2 * BLOCK)[None, :]
    )
    table = jnp.einsum("hbt,btk->hk", diag, jnp.asarray(onehot_of(diag_at)), precision=PRECISE)
    n1_passed = z_swap(proj[3], 1, z_size)
    if direct:
        table_rows = jnp.pad(table.reshape(1, -1), ((0, 7), (0, 0)))
        smalls = z_direct([proj[z_size]] * z_size, z_size)
        wo_grads = dp_fold(*halves(wo_grads), 4)[0]
        attn_keep, attn_send = attn_weights_call(slots, n1, dq, dk, dv, after(table_rows, wo_grads), smalls, 8)
        attn_grads = dp_fold(attn_keep, attn_send, 1)
        n1_passed = after(n1_passed, attn_grads)
    n1_both = (proj[2].astype(F32) + n1_passed.astype(F32)).astype(BF)
    n1_far = z_swap(n1_both, 2, z_size)
    n1_near = z_swap(after(proj[1], n1_both), 1, z_size)
    in_grad = final_call([proj[0], n1_near, n1_far], tokens_in, resid_grad, gains)
    out_parts = [outs[0], out_near, out_far]
    out_rows = (mid + functools.reduce(jnp.add, [p.astype(F32) for p in out_parts])).astype(BF)

    if direct:
        attn_grads = dp_fold(*halves(after(attn_grads, n1_both)), 2)
        attn_grads = dp_fold(*halves(after(attn_grads, n1_far, n1_near)), 4)
        attn_grads = attn_grads[0].astype(F32)
        per = width // 128
        cut = attn_grads[: 3 * per * share].reshape(3, per, share, 128)
        cut = jnp.swapaxes(cut, 1, 2).reshape(3, share, width)
        smalls = attn_grads[3 * per * share :]
        grad_table = smalls[8, : heads * BUCKETS].reshape(heads, BUCKETS)
        mine = z_rank
        grad_wo = after(wo_grads, n1_near)
    else:
        cut = jnp.stack([jnp.dot(n1.T, d, preferred_element_type=F32) for d in (dq, dk, dv)])
        cut = lax.psum_scatter(cut, "dp", scatter_dimension=1, tiled=True)
        smalls = lax.psum(proj[z_size], ("dp", "tensor"))
        grad_table = lax.psum(table, "dp")
        mine = dp_rank * z_size + z_rank
        grad_wo = lax.psum_scatter(wo_keep[0], "dp", scatter_dimension=1, tiled=True)
    wo_parts = z_direct([grad_wo[width * c : width * (c + 1)] for c in range(z_size)], z_size)
    grad_wo = functools.reduce(jnp.add, [p.astype(F32) for p in wo_parts])
    per_device = depth // (dp_size * z_size)
    own = lax.dynamic_slice_in_dim(smalls, mine * per_device, per_device, 1)

    wide = expert_grads.astype(F32).reshape(3, EXPERTS, unit, share)
    return (
        out_rows,
        in_grad,
        own[0],
        cut[0],
        cut[1],
        cut[2],
        grad_wo,
        grad_table,
        own[1],
        own[2 : 2 + EXPERTS].T,
        jnp.swapaxes(wide[0], 1, 2),
        jnp.swapaxes(wide[1], 1, 2),
        wide[2],
    )


def solution(mesh):
    rows = P(("dp", "tensor"), None)
    grid = P("dp", "tensor")
    flat = P(("dp", "tensor"))
    weights = (P(None, "dp", "tensor"), P(None, "dp", "tensor"), P(None, "tensor", "dp"))
    in_specs = (rows, rows, P("dp"), grid, grid, grid, P("tensor", "dp"), P("tensor", None), P("dp"), P("dp", None))
    out_specs = (rows, rows, flat, grid, grid, grid, P("tensor", "dp"), P("tensor", None), flat, rows)
    return jax.shard_map(
        on_device,
        mesh=mesh,
        in_specs=in_specs + weights + (P("dp", None), P("dp", None)),
        out_specs=out_specs + weights,
        check_vma=False,
    )
```

```python
import functools

import jax
import jax.numpy as jnp
import numpy as np
from jax import lax
from jax.experimental import pallas as pl
from jax.experimental.pallas import tpu as pltpu
from jax.sharding import PartitionSpec as P

EXPERTS = 4
PIECE = 256
CAP = 640
BUCKETS = 32
EPSILON = 1e-06
PRECISE = lax.Precision.HIGHEST
LIMITS = (12, 16, 23, 32, 46, 64, 91)
MASKED = -1e30
BF = jnp.bfloat16
F32 = jnp.float32
BLOCK = 256
VMEM_LIMIT = 56 * 1024 * 1024


def params(semantics=None):
    return pltpu.CompilerParams(dimension_semantics=semantics, vmem_limit_bytes=VMEM_LIMIT)


def dot_nn(a, b):
    return lax.dot_general(a, b, (((1,), (0,)), ((), ())), preferred_element_type=F32)


def dot_nt(a, b):
    return lax.dot_general(a, b, (((1,), (1,)), ((), ())), preferred_element_type=F32)


def dot_tn(a, b):
    return lax.dot_general(a, b, (((0,), (0,)), ((), ())), preferred_element_type=F32)


def bucket_of(offsets):
    distance = np.abs(offsets)
    far = np.full_like(distance, 8)
    for bound in LIMITS:
        far = far + (distance >= bound)
    return np.where(distance < 8, distance, far) + np.where(offsets > 0, 16, 0)


def onehot_of(offsets):
    return (bucket_of(offsets)[..., None] == np.arange(BUCKETS)).astype(np.float32)


def cost(flops, nbytes):
    return pl.CostEstimate(flops=int(flops), bytes_accessed=int(nbytes), transcendentals=0)


def vspec():
    return pl.BlockSpec(memory_space=pltpu.VMEM)


def sspec():
    return pl.BlockSpec(memory_space=pltpu.SMEM)


def z_swap(x, mask, size):
    return lax.ppermute(x, "tensor", [(i, i ^ mask) for i in range(size)])


def z_gather(x, size):
    near = z_swap(x, 1, size)
    far = z_swap(x, 2, size)
    return [x, near, far, z_swap(far, 1, size)]


def z_direct(parts, size):
    return [parts[0]] + [z_swap(parts[mask], mask, size) for mask in range(1, size)]


def z_reduce(parts, size):
    passed = z_swap(parts[3], 1, size)
    far = z_swap((parts[2].astype(F32) + passed.astype(F32)).astype(BF), 2, size)
    return [parts[0], z_swap(parts[1], 1, size), far]


def after(x, *others):
    return lax.optimization_barrier((x,) + others)[0]


def dp_slots(ranks):
    return ((ranks >> 1) & 3) | ((ranks & 1) << 2)


def dp_step(x, bit):
    other = lax.ppermute(x, "dp", [(i, i ^ bit) for i in range(8)])
    return jnp.concatenate([x, other], 0)


def dp_fold(keep, send, bit):
    other = lax.ppermute(send, "dp", [(i, i ^ bit) for i in range(8)])
    return (keep.astype(F32) + other.astype(F32)).astype(keep.dtype)


def halves(x):
    return x[: x.shape[0] // 2], x[x.shape[0] // 2 :]


def dp_scatter_slots(ranks):
    return ((ranks >> 2) & 1) | (((ranks >> 1) & 1) << 1) | ((ranks & 1) << 2)


def parted(keep_ref, send_ref, order_ref):
    half = keep_ref.shape[0]
    for j in range(2 * half if half > 1 else 1):
        yield (keep_ref if j < half else send_ref), j % half, order_ref[j]


def join_rows(ref, index_ref, count, rows):
    if count == 1:
        return ref[0, 0:rows, :]
    return jnp.concatenate([ref[index_ref[c], 0:rows, :] for c in range(count)], 0)


def qkv_body(count, chunks, rows, index_ref, place_ref, *refs):
    toks = refs[:chunks]
    pack_ref, small_ref = refs[chunks : chunks + 2]
    n1_ref, q_ref, k_ref, v_ref, kt_ref, vt_ref, gains_ref, router_ref = refs[chunks + 2 :]
    depth = n1_ref.shape[1] // count
    weights = join_rows(pack_ref, index_ref, count, depth)
    width = q_ref.shape[1]
    if count == 1:
        small = [small_ref[r : r + 1, :] for r in range(2 + EXPERTS)]
    else:
        lines = [small_ref[index_ref[d], depth : depth + 1, :].astype(F32) for d in range(count)]
        small = [
            jnp.concatenate([x[:, depth * r : depth * (r + 1)] for x in lines], 1) for r in range(2 + EXPERTS)
        ]
    small = jnp.concatenate([x.astype(F32) for x in small] + [jnp.zeros((2, depth * count), F32)], 0)
    gains_ref[...] = small
    routers = jnp.concatenate([small[2:], jnp.zeros((10, depth * count), F32)], 0)
    router_ref[...] = jnp.zeros_like(router_ref)
    router_ref[0:16, :] = routers.astype(BF)
    gain = small[0:1, :]
    for c in range(chunks):
        at = pl.ds(pl.multiple_of(place_ref[c] * rows, rows), rows)
        x = toks[c][...].astype(F32)
        scale = lax.rsqrt(jnp.mean(x * x, axis=1, keepdims=True) + EPSILON)
        normed = (x * scale * gain).astype(BF)
        n1_ref[at, :] = normed
        out = dot_nn(normed, weights)
        q_ref[at, :] = (out[:, :width].astype(BF).astype(F32) * 0.125).astype(BF)
        key = out[:, width : 2 * width]
        value = out[:, 2 * width :]
        k_ref[at, :] = key.astype(BF)
        v_ref[at, :] = value.astype(BF)
        kt_ref[:, at] = jnp.transpose(key).astype(BF)
        vt_ref[:, at] = jnp.transpose(value).astype(BF)


def qkv_call(index, place, toks, pack, small, width):
    chunks, rows, depth = len(toks), toks[0].shape[0], toks[0].shape[1]
    total = chunks * rows
    shapes = [(total, depth)] + [(total, width)] * 3 + [(width, total)] * 2
    return pl.pallas_call(
        functools.partial(qkv_body, pack.shape[0], chunks, rows),
        in_specs=[sspec(), sspec()] + [vspec()] * (chunks + 2),
        out_specs=[vspec()] * 8,
        out_shape=[jax.ShapeDtypeStruct(s, BF) for s in shapes]
        + [jax.ShapeDtypeStruct((8, depth), F32), jax.ShapeDtypeStruct((128, depth), BF)],
        compiler_params=params(),
        cost_estimate=cost(2 * total * depth * 3 * width, 8 * total * depth),
        name="norm_qkv",
    )(index, place, *toks, pack, small)


def extents(total):
    blocks = total // BLOCK
    return [(i, min(BLOCK * (i + 2), total)) for i in range(blocks)]


def fwd_body(total, chunks, starts_ref, place_ref, q_ref, k_ref, vt_ref, line_ref, p_ref, ot_ref, *refs):
    atts = refs[:chunks]
    strip_ref, mask_ref, all_ref = refs[chunks:]
    head = pl.program_id(0)
    heads = pl.num_programs(0)
    blocks = total // BLOCK
    width = q_ref.shape[1]
    dim = width // 4

    @pl.when(head == 0)
    def _():
        def label(pos):
            first = (pos >= starts_ref[0, 0]) & (pos < starts_ref[0, 0] + PIECE)
            second = (pos >= starts_ref[0, 1]) & (pos < starts_ref[0, 1] + PIECE)
            return first, second

        for i in range(blocks):
            for j in (i, i + 1):
                if j >= blocks:
                    continue
                kpos = lax.broadcasted_iota(jnp.int32, (BLOCK, BLOCK), 0) + BLOCK * j
                qpos = lax.broadcasted_iota(jnp.int32, (BLOCK, BLOCK), 1) + BLOCK * i
                k1, k2 = label(kpos)
                q1, q2 = label(qpos)
                seen = (kpos <= qpos) | (k1 & q1) | (k2 & q2)
                mask_ref[2 * i + j - i] = jnp.where(seen, 0.0, MASKED)

    for beta in range(blocks + 1):
        start = BLOCK * (blocks - beta)
        window = line_ref[0, 0:1, start : start + 2 * BLOCK]
        spread = jnp.broadcast_to(window, (BLOCK, 2 * BLOCK))
        rolled = pltpu.roll(spread, BLOCK + 1, 1, stride=1, stride_axis=0)
        strip_ref[BLOCK * beta : BLOCK * (beta + 1), :] = rolled[:, :BLOCK]

    lanes = lax.broadcasted_iota(jnp.int32, (BLOCK, width), 1)
    own = (lanes >= head * dim) & (lanes < (head + 1) * dim)
    at_head = pl.ds(pl.multiple_of(head * dim, dim), dim)
    for i, extent in extents(total):
        q_rows = q_ref[BLOCK * i : BLOCK * (i + 1), :]
        q_own = jnp.where(own, q_rows, jnp.zeros_like(q_rows))
        base = BLOCK * (blocks - 1 - i)
        scores = dot_nt(k_ref[0:extent, :], q_own) + strip_ref[base : base + extent, :]
        parts = [scores[BLOCK * j : BLOCK * (j + 1)] for j in range(extent // BLOCK)]
        for j in (i, i + 1):
            if j < blocks:
                parts[j] = parts[j] + mask_ref[2 * i + j - i]
        top = functools.reduce(jnp.maximum, parts)
        top = jnp.max(top, axis=0, keepdims=True)
        parts = [jnp.exp(part - top) for part in parts]
        total_sum = jnp.sum(functools.reduce(jnp.add, parts), axis=0, keepdims=True)
        inverse = 1.0 / total_sum
        chances = jnp.concatenate([(part * inverse).astype(BF) for part in parts], 0)
        p_ref[0, 0:extent, BLOCK * i : BLOCK * (i + 1)] = chances
        ot_ref[at_head, BLOCK * i : BLOCK * (i + 1)] = dot_nn(vt_ref[at_head, 0:extent], chances)

    @pl.when(head == heads - 1)
    def _():
        mixed = ot_ref[...]
        all_ref[...] = jnp.transpose(mixed).astype(BF)
        rows = total // chunks
        for c in range(chunks):
            at = pl.ds(pl.multiple_of(place_ref[c] * rows, rows), rows)
            atts[c][...] = all_ref[at, :]


def attn_fwd(starts, place, chunks, q, k, vt, line):
    total, width = q.shape
    heads = line.shape[0]
    blocks = total // BLOCK
    whole = lambda shape: pl.BlockSpec(shape, lambda h: (0,) * len(shape))
    return pl.pallas_call(
        functools.partial(fwd_body, total, chunks),
        grid=(heads,),
        in_specs=[
            sspec(),
            sspec(),
            whole((total, width)),
            whole((total, width)),
            whole((width, total)),
            pl.BlockSpec((1, 1, line.shape[2]), lambda h: (h, 0, 0)),
        ],
        out_specs=[
            pl.BlockSpec((1, total, total), lambda h: (h, 0, 0)),
            whole((width, total)),
        ]
        + [whole((total // chunks, width))] * chunks,
        out_shape=[
            jax.ShapeDtypeStruct((heads, total, total), BF),
            jax.ShapeDtypeStruct((width, total), F32),
        ]
        + [jax.ShapeDtypeStruct((total // chunks, width), BF)] * chunks,
        scratch_shapes=[
            pltpu.VMEM((BLOCK * (blocks + 1), BLOCK), F32),
            pltpu.VMEM((2 * blocks, BLOCK, BLOCK), F32),
            pltpu.VMEM((total, width), BF),
        ],
        compiler_params=params(("arbitrary",)),
        cost_estimate=cost(heads * 4 * total * total * width, 10 * total * total),
        name="attn_forward",
    )(starts, place, q, k, vt, line)


def diagonal_sums(acc):
    half = BLOCK // 2
    low, high = acc[:half], acc[half:]
    rows = jnp.concatenate(
        [high[:, :half], high[:, half:] + low[:, :half], low[:, half:], jnp.zeros((half, half), F32)], 1
    )
    step = half // 2
    while step >= 8:
        rows = rows[step:] + pltpu.roll(rows[:step], step, 1)
        step //= 2
    index = lax.broadcasted_iota(jnp.int32, rows.shape, 0)
    for step in (4, 2, 1):
        rows = jnp.where((index & step) == 0, pltpu.roll(rows, step, 1), rows)
    return jnp.sum(rows, axis=0, keepdims=True)


def bwd_body(total, chunks, place_ref, *refs):
    grads = refs[:chunks]
    p_ref, q_ref, k_ref, v_ref, kt_ref, ot_ref = refs[chunks : chunks + 6]
    dq_ref, dk_ref, dv_ref, diag_ref = refs[chunks + 6 : chunks + 10]
    do_ref, dot_ref, dqt_ref, dka_ref, dva_ref, ds_ref, acc_ref = refs[chunks + 10 :]
    head = pl.program_id(0)
    heads = pl.num_programs(0)
    blocks = total // BLOCK
    rows = total // chunks
    width = q_ref.shape[1]
    dim = width // 4

    @pl.when(head == 0)
    def _():
        for c in range(chunks):
            at = pl.ds(pl.multiple_of(place_ref[c] * rows, rows), rows)
            do_ref[at, :] = grads[c][...]
        dot_ref[...] = jnp.transpose(do_ref[...].astype(F32))
        dka_ref[...] = jnp.zeros_like(dka_ref)
        dva_ref[...] = jnp.zeros_like(dva_ref)

    at_head = pl.ds(pl.multiple_of(head * dim, dim), dim)
    inner = jnp.sum(dot_ref[at_head, :] * ot_ref[at_head, :], axis=0, keepdims=True)
    lanes = lax.broadcasted_iota(jnp.int32, (total, width), 1)
    own = (lanes >= head * dim) & (lanes < (head + 1) * dim)
    q_own = jnp.where(own, q_ref[...], jnp.zeros_like(q_ref))
    do_own = jnp.where(own, do_ref[...], jnp.zeros_like(do_ref))
    written = 0
    for i, extent in reversed(extents(total)):
        cols = slice(BLOCK * i, BLOCK * (i + 1))
        chance_grad = dot_nt(v_ref[0:extent, :], do_own[cols, :])
        chances = p_ref[0, 0:extent, cols].astype(F32)
        score_grad = (chances * (chance_grad - inner[:, cols])).astype(BF)
        ds_ref[0:extent, cols] = score_grad
        dqt_ref[at_head, cols] = dot_nn(kt_ref[at_head, 0:extent], score_grad)
        base = BLOCK * (blocks - 1 - i)
        wide = score_grad.astype(F32)
        if i == blocks - 1:
            acc_ref[0:extent, :] = wide
            written = extent
        else:
            old = written - base
            acc_ref[base:written, :] += wide[:old]
            if base + extent > written:
                acc_ref[written : base + extent, :] = wide[old:]
                written = base + extent
    for j in range(blocks):
        first = max(0, BLOCK * (j - 1))
        keys = slice(BLOCK * j, BLOCK * (j + 1))
        dka_ref[keys, :] += dot_nn(ds_ref[keys, first:], q_own[first:, :])
        dva_ref[keys, :] += dot_nn(p_ref[0, keys, first:], do_own[first:, :])
    for beta in range(blocks + 1):
        diag_ref[0, beta : beta + 1, :] = diagonal_sums(acc_ref[BLOCK * beta : BLOCK * (beta + 1), :])

    @pl.when(head == heads - 1)
    def _():
        dq_ref[...] = (jnp.transpose(dqt_ref[...]) * 0.125).astype(BF)
        dk_ref[...] = dka_ref[...].astype(BF)
        dv_ref[...] = dva_ref[...].astype(BF)


def attn_bwd(place, grads, chances, q, k, v, kt, ot):
    total, width = q.shape
    heads = chances.shape[0]
    blocks = total // BLOCK
    chunks = len(grads)
    whole = lambda shape: pl.BlockSpec(shape, lambda h: (0,) * len(shape))
    return pl.pallas_call(
        functools.partial(bwd_body, total, chunks),
        grid=(heads,),
        in_specs=[sspec()]
        + [whole(grads[0].shape)] * chunks
        + [pl.BlockSpec((1, total, total), lambda h: (h, 0, 0))]
        + [whole((total, width))] * 3
        + [whole((width, total))] * 2,
        out_specs=[whole((total, width))] * 3 + [pl.BlockSpec((1, blocks + 1, 2 * BLOCK), lambda h: (h, 0, 0))],
        out_shape=[jax.ShapeDtypeStruct((total, width), BF)] * 3
        + [jax.ShapeDtypeStruct((heads, blocks + 1, 2 * BLOCK), F32)],
        scratch_shapes=[
            pltpu.VMEM((total, width), BF),
            pltpu.VMEM((width, total), F32),
            pltpu.VMEM((width, total), F32),
            pltpu.VMEM((total, width), F32),
            pltpu.VMEM((total, width), F32),
            pltpu.VMEM((total, total), BF),
            pltpu.VMEM((BLOCK * (blocks + 1), BLOCK), F32),
        ],
        compiler_params=params(("arbitrary",)),
        cost_estimate=cost(heads * 160 * total * total * width, 10 * total * total),
        name="attn_backward",
    )(place, *grads, chances, q, k, v, kt, ot)


def join_lanes(ref, index_ref, count, slot):
    if count == 1:
        return ref[0, slot]
    return jnp.concatenate([ref[index_ref[c], slot] for c in range(count)], 1)


def mid_body(count, chunks, index_ref, *refs):
    atts = refs[:chunks]
    w_ref, tok_ref, gain_ref, mid_ref, n2_ref = refs[chunks:]
    u = tok_ref[...].astype(F32)
    for c in range(chunks):
        u = u + dot_nn(atts[c][...], join_lanes(w_ref, index_ref, count, c))
    mid_ref[...] = u
    scale = lax.rsqrt(jnp.mean(u * u, axis=1, keepdims=True) + EPSILON)
    n2_ref[...] = (u * scale * gain_ref[1:2, :]).astype(BF)


def mid_call(index, atts, w_out, tok, gains):
    chunks = len(atts)
    return pl.pallas_call(
        functools.partial(mid_body, w_out.shape[0], chunks),
        in_specs=[sspec()] + [vspec()] * (chunks + 3),
        out_specs=[vspec()] * 2,
        out_shape=[jax.ShapeDtypeStruct(tok.shape, F32), jax.ShapeDtypeStruct(tok.shape, BF)],
        compiler_params=params(),
        cost_estimate=cost(2 * tok.shape[0] * tok.shape[1] ** 2, 4 * tok.shape[1] ** 2),
        name="out_projection_norm",
    )(index, *atts, w_out, tok, gains)


def split_dot(a, b, dot):
    high = a.astype(BF)
    low = (a - high.astype(F32)).astype(BF)
    return dot(high, b) + dot(low, b)


def joined(ref, which):
    if ref.shape[0] == 1:
        return ref[0, which]
    return jnp.concatenate([ref[d, which] for d in range(ref.shape[0])], 1)


def units_body(chunks, unit, place_ref, *refs):
    n2s = refs[:chunks]
    gs = refs[chunks : 2 * chunks]
    sel_ref, rout_ref, w_ref = refs[2 * chunks : 2 * chunks + 3]
    hg_ref, gg_ref, ug_ref, lg_ref, rpart_ref = refs[2 * chunks + 3 : 2 * chunks + 8]
    n2_ref, g_ref, gate_ref, sum_ref, prob_ref, pick_ref = refs[2 * chunks + 8 :]
    step = pl.program_id(0)
    steps = pl.num_programs(0)
    rows = n2s[0].shape[0]
    tokens = chunks * rows
    lane = lax.broadcasted_iota(jnp.int32, (tokens, 128), 1)

    @pl.when(step == 0)
    def _():
        for c in range(chunks):
            n2_ref[rows * c : rows * (c + 1), :] = n2s[c][...]
            g_ref[rows * c : rows * (c + 1), :] = gs[c][...]
        logits = dot_nt(n2_ref[...], rout_ref[...])
        logits = jnp.where(lane < EXPERTS, logits, MASKED)
        raised = jnp.exp(logits - jnp.max(logits, axis=1, keepdims=True))
        prob_ref[...] = raised / jnp.sum(raised, axis=1, keepdims=True)
        for c in range(chunks):
            at = pl.ds(pl.multiple_of(place_ref[c] * rows, rows), rows)
            pick_ref[rows * c : rows * (c + 1), :] = sel_ref[at, :]
        gates = prob_ref[...] * pick_ref[...]
        for e in range(EXPERTS):
            one = jnp.sum(jnp.where(lane == e, gates, 0.0), axis=1, keepdims=True)
            gate_ref[e] = jnp.broadcast_to(one, (tokens, 128))
        sum_ref[...] = jnp.zeros_like(sum_ref)

    wg, wu, wd = joined(w_ref, 0), joined(w_ref, 1), joined(w_ref, 2)
    pre = dot_nt(n2_ref[...], jnp.concatenate([wg, wu], 0))
    gate_pre, up_pre = pre[:, : wg.shape[0]], pre[:, wg.shape[0] :]
    raw = dot_nt(g_ref[...], wd)
    c0 = float(np.sqrt(2.0 / np.pi))
    square = gate_pre * gate_pre
    th = jnp.tanh(gate_pre * (c0 + (c0 * 0.044715) * square))
    half = 0.5 + 0.5 * th
    act = gate_pre * half
    slope = half + gate_pre * (0.5 * c0 + (1.5 * c0 * 0.044715) * square) * (1.0 - th * th)
    hidden = act * up_pre
    prod = raw * hidden
    width = hg_ref.shape[1]
    e_low = (step * width) // unit
    e_high = (step * width + width - 1) // unit
    bound = jnp.where(e_high > e_low, unit * e_high - step * width, width)
    lows, highs = [], []
    for m in range(width // 128):
        is_low = lane + 128 * m < bound
        part = slice(128 * m, 128 * (m + 1))
        gate = jnp.where(is_low, gate_ref[e_low], gate_ref[e_high])
        lows.append(jnp.where(is_low, prod[:, part], 0.0))
        highs.append(prod[:, part] - lows[m])
        hg_ref[:, part] = (gate * hidden[:, part]).astype(BF)
        hidden_grad = gate * raw[:, part]
        gg_ref[:, part] = (hidden_grad * up_pre[:, part] * slope[:, part]).astype(BF)
        ug_ref[:, part] = (hidden_grad * act[:, part]).astype(BF)
    sum_ref[e_low] += functools.reduce(jnp.add, lows)

    @pl.when(e_high > e_low)
    def _():
        sum_ref[e_high] += functools.reduce(jnp.add, highs)

    @pl.when(step == steps - 1)
    def _():
        grad = jnp.zeros((tokens, 128), F32)
        for e in range(EXPERTS):
            grad = grad + jnp.where(lane == e, jnp.sum(sum_ref[e], axis=1, keepdims=True), 0.0)
        grad = grad * pick_ref[...]
        probs = prob_ref[...]
        logit_grad = probs * (grad - jnp.sum(probs * grad, axis=1, keepdims=True))
        lg_ref[...] = logit_grad
        rpart_ref[...] = split_dot(logit_grad, n2_ref[...], dot_tn)[0:8, :]


def units_call(place, n2s, gs, sel, router, weights, unit):
    chunks, rows, depth = len(n2s), n2s[0].shape[0], n2s[0].shape[1]
    count, _, ff, part = weights.shape
    tokens = chunks * rows
    whole = lambda shape: pl.BlockSpec(shape, lambda s: (0,) * len(shape))
    return pl.pallas_call(
        functools.partial(units_body, chunks, unit),
        grid=(ff // BLOCK,),
        in_specs=[sspec()]
        + [whole((rows, depth))] * (2 * chunks)
        + [whole(sel.shape), whole(router.shape), pl.BlockSpec((count, 3, BLOCK, part), lambda s: (0, 0, s, 0))],
        out_specs=[pl.BlockSpec((tokens, BLOCK), lambda s: (0, s))] * 3 + [whole((tokens, 128)), whole((8, depth))],
        out_shape=[jax.ShapeDtypeStruct((tokens, ff), BF)] * 3
        + [jax.ShapeDtypeStruct((tokens, 128), F32), jax.ShapeDtypeStruct((8, depth), F32)],
        scratch_shapes=[
            pltpu.VMEM((tokens, depth), BF),
            pltpu.VMEM((tokens, depth), BF),
            pltpu.VMEM((EXPERTS, tokens, 128), F32),
            pltpu.VMEM((EXPERTS, tokens, 128), F32),
            pltpu.VMEM((tokens, 128), F32),
            pltpu.VMEM((tokens, 128), F32),
        ],
        compiler_params=params(("arbitrary",)),
        cost_estimate=cost(6 * tokens * depth * ff, 6 * depth * ff + 12 * tokens * depth),
        name="expert_units",
    )(place, *n2s, *gs, sel, router, weights)


def product_body(terms, chunks, extra, *refs):
    xs = refs[:terms]
    ws = refs[terms : 2 * terms]
    at = 2 * terms + (2 if extra else 0)
    outs = refs[at : at + chunks]
    total = None
    for x, w in zip(xs, ws):
        term = dot_nn(x[...], joined(w, 0))
        total = term if total is None else total + term
    if extra:
        lg_ref, rout_ref = refs[2 * terms : 2 * terms + 2]
        total = total + split_dot(lg_ref[...], rout_ref[...], dot_nn)
    rows = outs[0].shape[0]
    for c in range(chunks):
        outs[c][...] = total[rows * c : rows * (c + 1)].astype(BF)


def product_call(xs, picks, weights, chunks, extra, name):
    tokens, ff = xs[0].shape
    count, _, _, part = weights.shape
    depth = count * part
    rows = tokens // chunks
    per = max(1, BLOCK // part)
    wide = min(part * per, BLOCK)
    whole = lambda shape: pl.BlockSpec(shape, lambda s: (0,) * len(shape))
    place_at = (lambda i, s: (s, i, 0, 0)) if count > 1 else (lambda i, s: (0, i, 0, s))
    w_specs = [pl.BlockSpec((min(per, count), 1, ff, wide // min(per, count)), functools.partial(place_at, i)) for i in picks]
    return pl.pallas_call(
        functools.partial(product_body, len(xs), chunks, bool(extra)),
        grid=(depth // wide,),
        in_specs=[whole((tokens, ff))] * len(xs)
        + w_specs
        + ([whole(extra[0].shape), pl.BlockSpec((128, wide), lambda s: (0, s))] if extra else []),
        out_specs=[pl.BlockSpec((rows, wide), lambda s: (0, s))] * chunks,
        out_shape=[jax.ShapeDtypeStruct((rows, depth), BF)] * chunks,
        compiler_params=params(("arbitrary",)),
        cost_estimate=cost(2 * len(xs) * tokens * depth * ff, 4 * len(xs) * depth * ff),
        name=name,
    )(*xs, *([weights] * len(xs)), *extra)


def wgrad_body(count, chunks, *refs):
    hg_ref, gg_ref, ug_ref = refs[:3]
    n2s = refs[3 : 3 + chunks]
    gs = refs[3 + chunks : 3 + 2 * chunks]
    out_ref, n2_ref, g_ref = refs[3 + 2 * chunks :]
    part = out_ref.shape[3]
    rows = n2s[0].shape[0]

    @pl.when(pl.program_id(0) == 0)
    def _():
        for c in range(chunks):
            n2_ref[rows * c : rows * (c + 1), :] = n2s[c][...]
            g_ref[rows * c : rows * (c + 1), :] = gs[c][...]

    width = hg_ref.shape[1]
    pair = dot_tn(jnp.concatenate([gg_ref[...], ug_ref[...]], 1), n2_ref[...]).astype(BF)
    down = dot_tn(hg_ref[...], g_ref[...]).astype(BF)
    for which, total in enumerate((pair[:width], pair[width:], down)):
        for d in range(count):
            out_ref[d, which] = total[:, part * d : part * (d + 1)]


def wgrad_call(count, kept, n2s, gs):
    tokens, ff = kept[0].shape
    chunks, rows, depth = len(n2s), n2s[0].shape[0], n2s[0].shape[1]
    whole = lambda shape: pl.BlockSpec(shape, lambda s: (0,) * len(shape))
    return pl.pallas_call(
        functools.partial(wgrad_body, count, chunks),
        grid=(ff // BLOCK,),
        in_specs=[pl.BlockSpec((tokens, BLOCK), lambda s: (0, s))] * 3 + [whole((rows, depth))] * (2 * chunks),
        out_specs=pl.BlockSpec((count, 3, BLOCK, depth // count), lambda s: (0, 0, s, 0)),
        out_shape=jax.ShapeDtypeStruct((count, 3, ff, depth // count), BF),
        scratch_shapes=[pltpu.VMEM((tokens, depth), BF), pltpu.VMEM((tokens, depth), BF)],
        compiler_params=params(("arbitrary",)),
        cost_estimate=cost(6 * tokens * depth * ff, 12 * depth * ff),
        name="expert_weight_grads",
    )(*kept, *n2s, *gs)


def norm_back(grad, u, gain):
    scale = lax.rsqrt(jnp.mean(u * u, axis=1, keepdims=True) + EPSILON)
    m = grad * gain
    back = scale * m - u * (scale * scale * scale) * jnp.mean(u * m, axis=1, keepdims=True)
    return back, jnp.sum(grad * u * scale, axis=0, keepdims=True)


def resid_body(count, chunks, terms, index_ref, *refs):
    parts = refs[:terms]
    mid_ref, g_ref, gains_ref, w_ref = refs[terms : terms + 4]
    rest = refs[terms + 4 :]
    resid_ref, aog_ref, gain_ref = rest[:3]
    dos = rest[3:]
    grad = functools.reduce(jnp.add, [p[...].astype(F32) for p in parts])
    back, gain_part = norm_back(grad, mid_ref[...], gains_ref[1:2, :])
    resid = g_ref[...].astype(F32) + back
    resid_ref[...] = resid
    low = resid.astype(BF)
    aog_ref[...] = low
    gain_ref[...] = jnp.broadcast_to(gain_part, gain_ref.shape)
    for c in range(chunks):
        dos[c][...] = dot_nt(low, join_lanes(w_ref, index_ref, count, c)).astype(BF)


def resid_call(index, parts, mid, grad, gains, w_out):
    chunks, terms = w_out.shape[1], len(parts)
    shape = mid.shape
    width = w_out.shape[2]
    return pl.pallas_call(
        functools.partial(resid_body, w_out.shape[0], chunks, terms),
        in_specs=[sspec()] + [vspec()] * (terms + 4),
        out_specs=[vspec()] * (3 + chunks),
        out_shape=[
            jax.ShapeDtypeStruct(shape, F32),
            jax.ShapeDtypeStruct(shape, BF),
            jax.ShapeDtypeStruct((8, shape[1]), F32),
        ]
        + [jax.ShapeDtypeStruct((shape[0], width), BF)] * chunks,
        compiler_params=params(),
        cost_estimate=cost(2 * shape[0] * shape[1] ** 2, 4 * shape[1] ** 2),
        name="resid_grad",
    )(index, *parts, mid, grad, gains, w_out)


def final_body(chunks, *refs):
    parts = refs[:chunks]
    tok_ref, resid_ref, gains_ref, out_ref = refs[chunks:]
    grad = functools.reduce(jnp.add, [p[...].astype(F32) for p in parts])
    back, _ = norm_back(grad, tok_ref[...].astype(F32), gains_ref[0:1, :])
    out_ref[...] = resid_ref[...] + back


def final_call(parts, tok, resid, gains):
    return pl.pallas_call(
        functools.partial(final_body, len(parts)),
        in_specs=[vspec()] * (len(parts) + 3),
        out_specs=vspec(),
        out_shape=jax.ShapeDtypeStruct(tok.shape, F32),
        compiler_params=params(),
        cost_estimate=cost(20 * tok.size, 12 * tok.size),
        name="in_grad",
    )(*parts, tok, resid, gains)


def proj_body(count, chunks, rows, index_ref, place_ref, dq_ref, dk_ref, dv_ref, pack_ref, two_ref, router_ref, *refs):
    toks = refs[:chunks]
    outs = refs[chunks : 2 * chunks]
    gain_ref = refs[2 * chunks]
    depth = outs[0].shape[1]
    width = dq_ref.shape[1]
    weights = join_rows(pack_ref, index_ref, count, depth // count)
    gain = jnp.zeros((1, depth), F32)
    for c in range(chunks):
        at = pl.ds(pl.multiple_of(place_ref[c] * rows, rows), rows)
        grad = dot_nt(dq_ref[at, :], weights[:, :width])
        grad = grad + dot_nt(dk_ref[at, :], weights[:, width : 2 * width])
        grad = grad + dot_nt(dv_ref[at, :], weights[:, 2 * width :])
        outs[c][...] = grad.astype(BF)
        x = toks[c][...].astype(F32)
        scale = lax.rsqrt(jnp.mean(x * x, axis=1, keepdims=True) + EPSILON)
        gain = gain + jnp.sum(grad * x * scale, axis=0, keepdims=True)
    blank = jnp.zeros((6 - EXPERTS, depth), F32)
    gain_ref[...] = jnp.concatenate([gain, two_ref[0:1, :], router_ref[0:EXPERTS, :], blank], 0)


def proj_call(index, place, dq, dk, dv, pack, gain_two, router_part, toks):
    chunks, rows, depth = len(toks), toks[0].shape[0], toks[0].shape[1]
    return pl.pallas_call(
        functools.partial(proj_body, pack.shape[0], chunks, rows),
        in_specs=[sspec(), sspec()] + [vspec()] * (6 + chunks),
        out_specs=[vspec()] * (chunks + 1),
        out_shape=[jax.ShapeDtypeStruct((rows, depth), BF)] * chunks + [jax.ShapeDtypeStruct((8, depth), F32)],
        compiler_params=params(),
        cost_estimate=cost(6 * chunks * rows * depth * dq.shape[1], 8 * chunks * rows * depth),
        name="projection_grads",
    )(index, place, dq, dk, dv, pack, gain_two, router_part, *toks)


def attn_weights_body(count, smalls, slot_ref, n1_ref, dq_ref, dk_ref, dv_ref, table_ref, *refs):
    keep_ref, send_ref, small_ref, *grad_refs = refs[smalls:]
    small_ref[...] = functools.reduce(jnp.add, [r[...] for r in refs[:smalls]])
    depth = n1_ref.shape[1]
    width = dq_ref.shape[1]
    part = depth // count
    normed = n1_ref[...]
    pieces = width // 128
    for ref, grad_ref in zip((dq_ref, dk_ref, dv_ref), grad_refs):
        grad_ref[...] = dot_tn(normed, ref[...]).astype(BF)
    for out_ref, slot, d in parted(keep_ref, send_ref, slot_ref):
        rows = pl.ds(pl.multiple_of(d * part, 128), part)
        for m, grad_ref in enumerate(grad_refs):
            for piece in range(pieces):
                at = (m * pieces + piece) * part
                out_ref[slot, at : at + part, :] = grad_ref[rows, 128 * piece : 128 * (piece + 1)]
        at = 3 * pieces * part
        value = jnp.concatenate([small_ref[:, rows], table_ref[...]], 0).astype(BF)
        out_ref[slot, at : at + 16, :] = value


def attn_weights_call(slots, n1, dq, dk, dv, table, smalls, count):
    total, depth = n1.shape
    width = dq.shape[1]
    part = depth // count
    return pl.pallas_call(
        functools.partial(attn_weights_body, count, len(smalls)),
        in_specs=[sspec()] + [vspec()] * (5 + len(smalls)),
        out_specs=[vspec()] * 2,
        out_shape=[jax.ShapeDtypeStruct((count // 2, 3 * width * part // 128 + 16, 128), BF)] * 2,
        scratch_shapes=[pltpu.VMEM((8, depth), F32)] + [pltpu.VMEM((depth, width), BF)] * 3,
        compiler_params=params(),
        cost_estimate=cost(6 * total * depth * width, 8 * total * depth),
        name="attn_weight_grads",
    )(slots, n1, dq, dk, dv, table, *smalls)


def wo_grad_body(count, chunks, slot_ref, *refs):
    atts = refs[:chunks]
    aog_ref, keep_ref, send_ref, grad_ref = refs[chunks:]
    width = atts[0].shape[1]
    part = grad_ref.shape[1] // count
    for c in range(chunks):
        at = slice(c * width, (c + 1) * width)
        grad_ref[at, :] = dot_tn(atts[c][...], aog_ref[...]).astype(BF)
    for out_ref, slot, d in parted(keep_ref, send_ref, slot_ref):
        out_ref[slot] = grad_ref[:, pl.ds(pl.multiple_of(d * part, 128), part)]


def wo_grad_call(slots, atts, aog, count):
    chunks, width = len(atts), atts[0].shape[1]
    rows, depth = aog.shape
    return pl.pallas_call(
        functools.partial(wo_grad_body, count, chunks),
        in_specs=[sspec()] + [vspec()] * (chunks + 1),
        out_specs=[vspec()] * 2,
        out_shape=[jax.ShapeDtypeStruct((max(1, count // 2), chunks * width, depth // count), BF)] * 2,
        scratch_shapes=[pltpu.VMEM((chunks * width, depth), BF)],
        compiler_params=params(),
        cost_estimate=cost(2 * rows * depth * chunks * width, 4 * depth * chunks * width),
        name="w_output_grad",
    )(slots, *atts, aog)


def kept_choices(ids):
    lanes = jnp.arange(128, dtype=jnp.int32)[None, :]
    expert_range = jnp.arange(EXPERTS, dtype=jnp.int32)[None, :]
    first = (ids[:, 0:1] == expert_range).astype(jnp.int32)
    second = (ids[:, 1:2] == expert_range).astype(jnp.int32)
    runs = jnp.cumsum(jnp.concatenate([first, second], 1), axis=0)
    first_run = runs[:, :EXPERTS]
    second_run = runs[:, EXPERTS:] + first_run[-1][None, :]
    place_one = jnp.sum(first_run * first, axis=1, keepdims=True) - 1
    place_two = jnp.sum(second_run * second, axis=1, keepdims=True) - 1
    kept = ((ids[:, 0:1] == lanes) & (place_one < CAP)) | ((ids[:, 1:2] == lanes) & (place_two < CAP))
    return kept.astype(F32)


def on_device(
    tokens_in,
    out_grad,
    attn_gain,
    w_query,
    w_key,
    w_value,
    w_output,
    rel_table,
    moe_gain,
    w_router,
    w_gate,
    w_up,
    down_weight,
    expert_ids,
    piece_starts,
):
    rows, depth = tokens_in.shape
    width = w_query.shape[1]
    z_size = lax.axis_size("tensor")
    dp_size = lax.axis_size("dp")
    z_rank = lax.axis_index("tensor").astype(jnp.int32)
    dp_rank = lax.axis_index("dp").astype(jnp.int32)
    total = rows * z_size
    share = depth // dp_size
    unit = w_gate.shape[2]
    ff = EXPERTS * unit
    heads = rel_table.shape[0]
    direct = dp_size == 8 and share == 128
    place = z_rank ^ jnp.arange(z_size, dtype=jnp.int32)

    near = z_swap(tokens_in, 1, z_size)
    far = z_swap(tokens_in, 2, z_size)
    line_at = 2 * BLOCK - 1 - np.arange(total + 2 * BLOCK)
    line = jnp.dot(rel_table, jnp.asarray(onehot_of(line_at).T), precision=PRECISE)[:, None, :]
    sel = kept_choices(expert_ids)
    toks = [tokens_in, near, far, z_swap(after(far, near, sel, line), 1, z_size)]
    w_output_late = after(w_output, far)
    small = jnp.concatenate([attn_gain, moe_gain, w_router.T.reshape(-1)])[None, :]
    packed = jnp.concatenate([w_query, w_key, w_value], 1)
    wo_slots = jnp.stack(z_direct([w_output_late] * z_size, z_size))[None]
    ranks = dp_rank ^ jnp.arange(8, dtype=jnp.int32)
    if direct:
        index = dp_slots(ranks)
        slots = dp_rank ^ dp_scatter_slots(jnp.arange(8, dtype=jnp.int32))
        pad = jnp.zeros((15, packed.shape[1]), BF)
        pack = dp_step(jnp.concatenate([packed, small, pad], 0)[None], 2)
        pack = dp_step(after(pack, near), 4)
        wo_half = dp_step(after(wo_slots, near, far), 2)
        pack = dp_step(after(pack, toks[3], wo_half), 1)
        small_all = pack
    else:
        index = slots = jnp.zeros((1,), jnp.int32)
        pack = lax.all_gather(packed, "dp", axis=0, tiled=True)[None]
        small_all = lax.all_gather(small[0], "dp", axis=0).reshape(dp_size, 2 + EXPERTS, share)
        small_all = jnp.swapaxes(small_all, 0, 1).reshape(2 + EXPERTS, depth)
        small_all = jnp.concatenate([small_all, jnp.zeros((2, depth), BF)], 0)
        wo_all = lax.all_gather(wo_slots[0], "dp", axis=2, tiled=True)[None]

    local = jnp.stack(
        [
            jnp.swapaxes(w_gate, 1, 2).reshape(ff, share),
            jnp.swapaxes(w_up, 1, 2).reshape(ff, share),
            down_weight.reshape(ff, share),
        ]
    )
    if direct:
        experts_w = lax.all_gather(local, "dp", axis=0)
    else:
        experts_w = lax.all_gather(local, "dp", axis=2, tiled=True)[None]

    n1, q, k, v, kt, vt, gains, router = qkv_call(index, place, toks, pack, small_all, width)
    g_near = z_swap(after(out_grad, toks[3]), 1, z_size)
    g_far = z_swap(after(out_grad, toks[3]), 2, z_size)
    fwd = attn_fwd(piece_starts, place, z_size, q, k, vt, line)
    chances, ot = fwd[:2]
    atts = z_direct([after(fwd[2], g_near, g_far)] + [after(x, g_near, g_far) for x in fwd[3:]], z_size)
    if direct:
        wo_all = dp_step(after(dp_step(after(wo_half, n1), 4), atts[1]), 1)
    gs = [out_grad, g_near, g_far, z_swap(after(g_far, fwd[2]), 1, z_size)]
    mid, n2 = mid_call(index, [after(atts[0], gs[3])] + atts[1:], wo_all, tokens_in, gains)

    n2_near = z_swap(n2, 1, z_size)
    n2_far = z_swap(n2, 2, z_size)
    n2s = [n2, n2_near, n2_far, z_swap(after(n2_far, n2_near), 1, z_size)]
    hg, gg, ug, logit_grad, router_part = units_call(place, n2s, gs, sel, router, experts_w, unit)
    ngs = product_call([gg, ug], (0, 1), experts_w, z_size, [logit_grad, router], "normed_two_grads")
    passed = z_swap(ngs[3], 1, z_size)
    outs = product_call([after(hg, ngs[0])], (2,), experts_w, z_size, [], "expert_out")
    both = (ngs[2].astype(F32) + after(passed, outs[0]).astype(F32)).astype(BF)
    far = z_swap(both, 2, z_size)
    ng_near = z_swap(after(ngs[1], passed), 1, z_size)
    count = experts_w.shape[0]
    weight_grads = wgrad_call(experts_w.shape[0], [after(hg, both, *outs), gg, ug], n2s, gs)
    resid = resid_call(index, [after(ngs[0], weight_grads), ng_near, far], mid, out_grad, gains, wo_all)
    resid_grad, aog, gain_two = resid[:3]
    weight_grads = after(weight_grads, far, ng_near)
    if direct:
        expert_grads = lax.psum_scatter(weight_grads, "dp", scatter_dimension=0, tiled=False)
    else:
        expert_grads = lax.psum_scatter(weight_grads[0], "dp", scatter_dimension=2, tiled=True)
    out_passed = z_swap(after(outs[3], aog), 1, z_size)
    dos = z_direct(resid[3:], z_size)
    wo_keep, wo_send = wo_grad_call(slots, atts, aog, count)
    out_both = (outs[2].astype(F32) + out_passed.astype(F32)).astype(BF)
    dos[0] = after(dos[0], wo_keep, out_both)
    out_far = z_swap(out_both, 2, z_size)
    out_near = z_swap(after(outs[1], out_both), 1, z_size)
    if direct:
        wo_grads = dp_fold(wo_keep, after(wo_send, *dos), 1)
    dq, dk, dv, diag = attn_bwd(place, dos, chances, q, k, v, kt, ot)
    if direct:
        wo_grads = dp_fold(*halves(wo_grads), 2)
        dq = after(dq, wo_grads)
    dq = after(dq, out_far, out_near)
    proj = proj_call(index, place, dq, dk, dv, pack, gain_two, router_part, toks)

    diag_at = (
        BLOCK * np.arange(total // BLOCK + 1)[:, None] - (BLOCK * (total // BLOCK - 2) + 1) - np.arange(2 * BLOCK)[None, :]
    )
    table = jnp.einsum("hbt,btk->hk", diag, jnp.asarray(onehot_of(diag_at)), precision=PRECISE)
    n1_passed = z_swap(proj[3], 1, z_size)
    if direct:
        table_rows = jnp.pad(table.reshape(1, -1), ((0, 7), (0, 0)))
        smalls = z_direct([proj[z_size]] * z_size, z_size)
        wo_grads = dp_fold(*halves(wo_grads), 4)[0]
        attn_keep, attn_send = attn_weights_call(slots, n1, dq, dk, dv, after(table_rows, wo_grads), smalls, 8)
        n1_passed = after(n1_passed, attn_keep)
    n1_both = (proj[2].astype(F32) + n1_passed.astype(F32)).astype(BF)
    n1_far = z_swap(n1_both, 2, z_size)
    n1_near = z_swap(after(proj[1], n1_both), 1, z_size)
    in_grad = final_call([proj[0], n1_near, n1_far], tokens_in, resid_grad, gains)
    out_parts = [outs[0], out_near, out_far]
    out_rows = (mid + functools.reduce(jnp.add, [p.astype(F32) for p in out_parts])).astype(BF)

    if direct:
        attn_grads = dp_fold(attn_keep, after(attn_send, n1_both), 1)
        attn_grads = dp_fold(*halves(attn_grads), 2)
        attn_grads = dp_fold(*halves(after(attn_grads, n1_far, n1_near)), 4)
        attn_grads = attn_grads[0].astype(F32)
        per = width // 128
        cut = attn_grads[: 3 * per * share].reshape(3, per, share, 128)
        cut = jnp.swapaxes(cut, 1, 2).reshape(3, share, width)
        smalls = attn_grads[3 * per * share :]
        grad_table = smalls[8, : heads * BUCKETS].reshape(heads, BUCKETS)
        mine = z_rank
        grad_wo = after(wo_grads, n1_near)
    else:
        cut = jnp.stack([jnp.dot(n1.T, d, preferred_element_type=F32) for d in (dq, dk, dv)])
        cut = lax.psum_scatter(cut, "dp", scatter_dimension=1, tiled=True)
        smalls = lax.psum(proj[z_size], ("dp", "tensor"))
        grad_table = lax.psum(table, "dp")
        mine = dp_rank * z_size + z_rank
        grad_wo = lax.psum_scatter(wo_keep[0], "dp", scatter_dimension=1, tiled=True)
    wo_parts = z_direct([grad_wo[width * c : width * (c + 1)] for c in range(z_size)], z_size)
    grad_wo = functools.reduce(jnp.add, [p.astype(F32) for p in wo_parts])
    per_device = depth // (dp_size * z_size)
    own = lax.dynamic_slice_in_dim(smalls, mine * per_device, per_device, 1)

    wide = expert_grads.astype(F32).reshape(3, EXPERTS, unit, share)
    return (
        out_rows,
        in_grad,
        own[0],
        cut[0],
        cut[1],
        cut[2],
        grad_wo,
        grad_table,
        own[1],
        own[2 : 2 + EXPERTS].T,
        jnp.swapaxes(wide[0], 1, 2),
        jnp.swapaxes(wide[1], 1, 2),
        wide[2],
    )


def solution(mesh):
    rows = P(("dp", "tensor"), None)
    grid = P("dp", "tensor")
    flat = P(("dp", "tensor"))
    weights = (P(None, "dp", "tensor"), P(None, "dp", "tensor"), P(None, "tensor", "dp"))
    in_specs = (rows, rows, P("dp"), grid, grid, grid, P("tensor", "dp"), P("tensor", None), P("dp"), P("dp", None))
    out_specs = (rows, rows, flat, grid, grid, grid, P("tensor", "dp"), P("tensor", None), flat, rows)
    return jax.shard_map(
        on_device,
        mesh=mesh,
        in_specs=in_specs + weights + (P("dp", None), P("dp", None)),
        out_specs=out_specs + weights,
        check_vma=False,
    )
```

```python
import functools

import jax
import jax.numpy as jnp
import numpy as np
from jax import lax
from jax.experimental import pallas as pl
from jax.experimental.pallas import tpu as pltpu
from jax.sharding import PartitionSpec as P

EXPERTS = 4
PIECE = 256
CAP = 640
BUCKETS = 32
EPSILON = 1e-06
PRECISE = lax.Precision.HIGHEST
LIMITS = (12, 16, 23, 32, 46, 64, 91)
MASKED = -1e30
BF = jnp.bfloat16
F32 = jnp.float32
BLOCK = 256
VMEM_LIMIT = 56 * 1024 * 1024


def params(semantics=None):
    return pltpu.CompilerParams(dimension_semantics=semantics, vmem_limit_bytes=VMEM_LIMIT)


def dot_nn(a, b):
    return lax.dot_general(a, b, (((1,), (0,)), ((), ())), preferred_element_type=F32)


def dot_nt(a, b):
    return lax.dot_general(a, b, (((1,), (1,)), ((), ())), preferred_element_type=F32)


def dot_tn(a, b):
    return lax.dot_general(a, b, (((0,), (0,)), ((), ())), preferred_element_type=F32)


def bucket_of(offsets):
    distance = np.abs(offsets)
    far = np.full_like(distance, 8)
    for bound in LIMITS:
        far = far + (distance >= bound)
    return np.where(distance < 8, distance, far) + np.where(offsets > 0, 16, 0)


def onehot_of(offsets):
    return (bucket_of(offsets)[..., None] == np.arange(BUCKETS)).astype(np.float32)


def cost(flops, nbytes):
    return pl.CostEstimate(flops=int(flops), bytes_accessed=int(nbytes), transcendentals=0)


def vspec():
    return pl.BlockSpec(memory_space=pltpu.VMEM)


def sspec():
    return pl.BlockSpec(memory_space=pltpu.SMEM)


def z_swap(x, mask, size):
    return lax.ppermute(x, "tensor", [(i, i ^ mask) for i in range(size)])


def z_gather(x, size):
    near = z_swap(x, 1, size)
    far = z_swap(x, 2, size)
    return [x, near, far, z_swap(far, 1, size)]


def z_direct(parts, size):
    return [parts[0]] + [z_swap(parts[mask], mask, size) for mask in range(1, size)]


def z_reduce(parts, size):
    passed = z_swap(parts[3], 1, size)
    far = z_swap((parts[2].astype(F32) + passed.astype(F32)).astype(BF), 2, size)
    return [parts[0], z_swap(parts[1], 1, size), far]


def after(x, *others):
    return lax.optimization_barrier((x,) + others)[0]


def dp_slots(ranks):
    x, y, core = (ranks >> 1) & 1, (ranks >> 2) & 1, ranks & 1
    return jnp.concatenate([x | (y << 1) | (core << 2), y | (x << 1) | (core << 2)])


def dp_step(x, bit):
    other = lax.ppermute(x, "dp", [(i, i ^ bit) for i in range(8)])
    return jnp.concatenate([x, other], 0)


def dp_fold(keep, send, bit):
    other = lax.ppermute(send, "dp", [(i, i ^ bit) for i in range(8)])
    return (keep.astype(F32) + other.astype(F32)).astype(keep.dtype)


def halves(x):
    return x[: x.shape[0] // 2], x[x.shape[0] // 2 :]


def dp_scatter_slots(ranks):
    return ((ranks >> 2) & 1) | (((ranks >> 1) & 1) << 1) | ((ranks & 1) << 2)


def parted(keep_ref, send_ref, order_ref):
    half = keep_ref.shape[0]
    for j in range(2 * half if half > 1 else 1):
        yield (keep_ref if j < half else send_ref), j % half, order_ref[j]


def join_rows(first_ref, last_ref, index_ref, count, rows):
    split = first_ref.shape[1]
    pieces = []
    for c in range(count):
        pieces.append(first_ref[index_ref[c], :, :])
        pieces.append(last_ref[index_ref[count + c], 0 : rows - split, :])
    return jnp.concatenate(pieces, 0)


def qkv_body(count, chunks, rows, index_ref, place_ref, *refs):
    toks = refs[:chunks]
    first_ref, last_ref, small_ref = refs[chunks : chunks + 3]
    n1_ref, q_ref, k_ref, v_ref, kt_ref, vt_ref, gains_ref, router_ref = refs[chunks + 3 :]
    depth = n1_ref.shape[1] // count
    weights = join_rows(first_ref, last_ref, index_ref, count, depth)
    width = q_ref.shape[1]
    if count == 1:
        small = [small_ref[r : r + 1, :] for r in range(2 + EXPERTS)]
    else:
        row = depth - first_ref.shape[1]
        lines = [small_ref[index_ref[count + d], row : row + 1, :].astype(F32) for d in range(count)]
        small = [
            jnp.concatenate([x[:, depth * r : depth * (r + 1)] for x in lines], 1) for r in range(2 + EXPERTS)
        ]
    small = jnp.concatenate([x.astype(F32) for x in small] + [jnp.zeros((2, depth * count), F32)], 0)
    gains_ref[...] = small
    routers = jnp.concatenate([small[2:], jnp.zeros((10, depth * count), F32)], 0)
    router_ref[...] = jnp.zeros_like(router_ref)
    router_ref[0:16, :] = routers.astype(BF)
    gain = small[0:1, :]
    for c in range(chunks):
        at = pl.ds(pl.multiple_of(place_ref[c] * rows, rows), rows)
        x = toks[c][...].astype(F32)
        scale = lax.rsqrt(jnp.mean(x * x, axis=1, keepdims=True) + EPSILON)
        normed = (x * scale * gain).astype(BF)
        n1_ref[at, :] = normed
        out = dot_nn(normed, weights)
        q_ref[at, :] = (out[:, :width].astype(BF).astype(F32) * 0.125).astype(BF)
        key = out[:, width : 2 * width]
        value = out[:, 2 * width :]
        k_ref[at, :] = key.astype(BF)
        v_ref[at, :] = value.astype(BF)
        kt_ref[:, at] = jnp.transpose(key).astype(BF)
        vt_ref[:, at] = jnp.transpose(value).astype(BF)


def qkv_call(index, place, toks, pack, small, width):
    chunks, rows, depth = len(toks), toks[0].shape[0], toks[0].shape[1]
    total = chunks * rows
    shapes = [(total, depth)] + [(total, width)] * 3 + [(width, total)] * 2
    return pl.pallas_call(
        functools.partial(qkv_body, pack[0].shape[0], chunks, rows),
        in_specs=[sspec(), sspec()] + [vspec()] * (chunks + 3),
        out_specs=[vspec()] * 8,
        out_shape=[jax.ShapeDtypeStruct(s, BF) for s in shapes]
        + [jax.ShapeDtypeStruct((8, depth), F32), jax.ShapeDtypeStruct((128, depth), BF)],
        compiler_params=params(),
        cost_estimate=cost(2 * total * depth * 3 * width, 8 * total * depth),
        name="norm_qkv",
    )(index, place, *toks, *pack, small)


def extents(total):
    blocks = total // BLOCK
    return [(i, min(BLOCK * (i + 2), total)) for i in range(blocks)]


def fwd_body(total, chunks, starts_ref, place_ref, q_ref, k_ref, vt_ref, line_ref, p_ref, ot_ref, *refs):
    atts = refs[:chunks]
    strip_ref, mask_ref, all_ref = refs[chunks:]
    head = pl.program_id(0)
    heads = pl.num_programs(0)
    blocks = total // BLOCK
    width = q_ref.shape[1]
    dim = width // 4

    @pl.when(head == 0)
    def _():
        def label(pos):
            first = (pos >= starts_ref[0, 0]) & (pos < starts_ref[0, 0] + PIECE)
            second = (pos >= starts_ref[0, 1]) & (pos < starts_ref[0, 1] + PIECE)
            return first, second

        for i in range(blocks):
            for j in (i, i + 1):
                if j >= blocks:
                    continue
                kpos = lax.broadcasted_iota(jnp.int32, (BLOCK, BLOCK), 0) + BLOCK * j
                qpos = lax.broadcasted_iota(jnp.int32, (BLOCK, BLOCK), 1) + BLOCK * i
                k1, k2 = label(kpos)
                q1, q2 = label(qpos)
                seen = (kpos <= qpos) | (k1 & q1) | (k2 & q2)
                mask_ref[2 * i + j - i] = jnp.where(seen, 0.0, MASKED)

    for beta in range(blocks + 1):
        start = BLOCK * (blocks - beta)
        window = line_ref[0, 0:1, start : start + 2 * BLOCK]
        spread = jnp.broadcast_to(window, (BLOCK, 2 * BLOCK))
        rolled = pltpu.roll(spread, BLOCK + 1, 1, stride=1, stride_axis=0)
        strip_ref[BLOCK * beta : BLOCK * (beta + 1), :] = rolled[:, :BLOCK]

    lanes = lax.broadcasted_iota(jnp.int32, (BLOCK, width), 1)
    own = (lanes >= head * dim) & (lanes < (head + 1) * dim)
    at_head = pl.ds(pl.multiple_of(head * dim, dim), dim)
    for i, extent in extents(total):
        q_rows = q_ref[BLOCK * i : BLOCK * (i + 1), :]
        q_own = jnp.where(own, q_rows, jnp.zeros_like(q_rows))
        base = BLOCK * (blocks - 1 - i)
        scores = dot_nt(k_ref[0:extent, :], q_own) + strip_ref[base : base + extent, :]
        parts = [scores[BLOCK * j : BLOCK * (j + 1)] for j in range(extent // BLOCK)]
        for j in (i, i + 1):
            if j < blocks:
                parts[j] = parts[j] + mask_ref[2 * i + j - i]
        top = functools.reduce(jnp.maximum, parts)
        top = jnp.max(top, axis=0, keepdims=True)
        parts = [jnp.exp(part - top) for part in parts]
        total_sum = jnp.sum(functools.reduce(jnp.add, parts), axis=0, keepdims=True)
        inverse = 1.0 / total_sum
        chances = jnp.concatenate([(part * inverse).astype(BF) for part in parts], 0)
        p_ref[0, 0:extent, BLOCK * i : BLOCK * (i + 1)] = chances
        ot_ref[at_head, BLOCK * i : BLOCK * (i + 1)] = dot_nn(vt_ref[at_head, 0:extent], chances)

    @pl.when(head == heads - 1)
    def _():
        mixed = ot_ref[...]
        all_ref[...] = jnp.transpose(mixed).astype(BF)
        rows = total // chunks
        for c in range(chunks):
            at = pl.ds(pl.multiple_of(place_ref[c] * rows, rows), rows)
            atts[c][...] = all_ref[at, :]


def attn_fwd(starts, place, chunks, q, k, vt, line):
    total, width = q.shape
    heads = line.shape[0]
    blocks = total // BLOCK
    whole = lambda shape: pl.BlockSpec(shape, lambda h: (0,) * len(shape))
    return pl.pallas_call(
        functools.partial(fwd_body, total, chunks),
        grid=(heads,),
        in_specs=[
            sspec(),
            sspec(),
            whole((total, width)),
            whole((total, width)),
            whole((width, total)),
            pl.BlockSpec((1, 1, line.shape[2]), lambda h: (h, 0, 0)),
        ],
        out_specs=[
            pl.BlockSpec((1, total, total), lambda h: (h, 0, 0)),
            whole((width, total)),
        ]
        + [whole((total // chunks, width))] * chunks,
        out_shape=[
            jax.ShapeDtypeStruct((heads, total, total), BF),
            jax.ShapeDtypeStruct((width, total), F32),
        ]
        + [jax.ShapeDtypeStruct((total // chunks, width), BF)] * chunks,
        scratch_shapes=[
            pltpu.VMEM((BLOCK * (blocks + 1), BLOCK), F32),
            pltpu.VMEM((2 * blocks, BLOCK, BLOCK), F32),
            pltpu.VMEM((total, width), BF),
        ],
        compiler_params=params(("arbitrary",)),
        cost_estimate=cost(heads * 4 * total * total * width, 10 * total * total),
        name="attn_forward",
    )(starts, place, q, k, vt, line)


def diagonal_sums(acc):
    half = BLOCK // 2
    low, high = acc[:half], acc[half:]
    rows = jnp.concatenate(
        [high[:, :half], high[:, half:] + low[:, :half], low[:, half:], jnp.zeros((half, half), F32)], 1
    )
    step = half // 2
    while step >= 8:
        rows = rows[step:] + pltpu.roll(rows[:step], step, 1)
        step //= 2
    index = lax.broadcasted_iota(jnp.int32, rows.shape, 0)
    for step in (4, 2, 1):
        rows = jnp.where((index & step) == 0, pltpu.roll(rows, step, 1), rows)
    return jnp.sum(rows, axis=0, keepdims=True)


def bwd_body(total, chunks, place_ref, *refs):
    grads = refs[:chunks]
    p_ref, q_ref, k_ref, v_ref, kt_ref, ot_ref = refs[chunks : chunks + 6]
    dq_ref, dk_ref, dv_ref, diag_ref = refs[chunks + 6 : chunks + 10]
    do_ref, dot_ref, dqt_ref, dka_ref, dva_ref, ds_ref, acc_ref = refs[chunks + 10 :]
    head = pl.program_id(0)
    heads = pl.num_programs(0)
    blocks = total // BLOCK
    rows = total // chunks
    width = q_ref.shape[1]
    dim = width // 4

    @pl.when(head == 0)
    def _():
        for c in range(chunks):
            at = pl.ds(pl.multiple_of(place_ref[c] * rows, rows), rows)
            do_ref[at, :] = grads[c][...]
        dot_ref[...] = jnp.transpose(do_ref[...].astype(F32))
        dka_ref[...] = jnp.zeros_like(dka_ref)
        dva_ref[...] = jnp.zeros_like(dva_ref)

    at_head = pl.ds(pl.multiple_of(head * dim, dim), dim)
    inner = jnp.sum(dot_ref[at_head, :] * ot_ref[at_head, :], axis=0, keepdims=True)
    lanes = lax.broadcasted_iota(jnp.int32, (total, width), 1)
    own = (lanes >= head * dim) & (lanes < (head + 1) * dim)
    q_own = jnp.where(own, q_ref[...], jnp.zeros_like(q_ref))
    do_own = jnp.where(own, do_ref[...], jnp.zeros_like(do_ref))
    written = 0
    for i, extent in reversed(extents(total)):
        cols = slice(BLOCK * i, BLOCK * (i + 1))
        chance_grad = dot_nt(v_ref[0:extent, :], do_own[cols, :])
        chances = p_ref[0, 0:extent, cols].astype(F32)
        score_grad = (chances * (chance_grad - inner[:, cols])).astype(BF)
        ds_ref[0:extent, cols] = score_grad
        dqt_ref[at_head, cols] = dot_nn(kt_ref[at_head, 0:extent], score_grad)
        base = BLOCK * (blocks - 1 - i)
        wide = score_grad.astype(F32)
        if i == blocks - 1:
            acc_ref[0:extent, :] = wide
            written = extent
        else:
            old = written - base
            acc_ref[base:written, :] += wide[:old]
            if base + extent > written:
                acc_ref[written : base + extent, :] = wide[old:]
                written = base + extent
    for j in range(blocks):
        first = max(0, BLOCK * (j - 1))
        keys = slice(BLOCK * j, BLOCK * (j + 1))
        dka_ref[keys, :] += dot_nn(ds_ref[keys, first:], q_own[first:, :])
        dva_ref[keys, :] += dot_nn(p_ref[0, keys, first:], do_own[first:, :])
    for beta in range(blocks + 1):
        diag_ref[0, beta : beta + 1, :] = diagonal_sums(acc_ref[BLOCK * beta : BLOCK * (beta + 1), :])

    @pl.when(head == heads - 1)
    def _():
        dq_ref[...] = (jnp.transpose(dqt_ref[...]) * 0.125).astype(BF)
        dk_ref[...] = dka_ref[...].astype(BF)
        dv_ref[...] = dva_ref[...].astype(BF)


def attn_bwd(place, grads, chances, q, k, v, kt, ot):
    total, width = q.shape
    heads = chances.shape[0]
    blocks = total // BLOCK
    chunks = len(grads)
    whole = lambda shape: pl.BlockSpec(shape, lambda h: (0,) * len(shape))
    return pl.pallas_call(
        functools.partial(bwd_body, total, chunks),
        grid=(heads,),
        in_specs=[sspec()]
        + [whole(grads[0].shape)] * chunks
        + [pl.BlockSpec((1, total, total), lambda h: (h, 0, 0))]
        + [whole((total, width))] * 3
        + [whole((width, total))] * 2,
        out_specs=[whole((total, width))] * 3 + [pl.BlockSpec((1, blocks + 1, 2 * BLOCK), lambda h: (h, 0, 0))],
        out_shape=[jax.ShapeDtypeStruct((total, width), BF)] * 3
        + [jax.ShapeDtypeStruct((heads, blocks + 1, 2 * BLOCK), F32)],
        scratch_shapes=[
            pltpu.VMEM((total, width), BF),
            pltpu.VMEM((width, total), F32),
            pltpu.VMEM((width, total), F32),
            pltpu.VMEM((total, width), F32),
            pltpu.VMEM((total, width), F32),
            pltpu.VMEM((total, total), BF),
            pltpu.VMEM((BLOCK * (blocks + 1), BLOCK), F32),
        ],
        compiler_params=params(("arbitrary",)),
        cost_estimate=cost(heads * 160 * total * total * width, 10 * total * total),
        name="attn_backward",
    )(place, *grads, chances, q, k, v, kt, ot)


def join_lanes(low_ref, high_ref, index_ref, count, slot):
    low = [low_ref[index_ref[c], slot] for c in range(count)]
    high = [high_ref[index_ref[count + c], slot] for c in range(count)]
    return jnp.concatenate([jnp.concatenate(low, 1), jnp.concatenate(high, 1)], 0)


def mid_body(count, chunks, index_ref, *refs):
    atts = refs[:chunks]
    low_ref, high_ref, tok_ref, gain_ref, mid_ref, n2_ref = refs[chunks:]
    u = tok_ref[...].astype(F32)
    for c in range(chunks):
        u = u + dot_nn(atts[c][...], join_lanes(low_ref, high_ref, index_ref, count, c))
    mid_ref[...] = u
    scale = lax.rsqrt(jnp.mean(u * u, axis=1, keepdims=True) + EPSILON)
    n2_ref[...] = (u * scale * gain_ref[1:2, :]).astype(BF)


def mid_call(index, atts, w_out, tok, gains):
    chunks = len(atts)
    return pl.pallas_call(
        functools.partial(mid_body, w_out[0].shape[0], chunks),
        in_specs=[sspec()] + [vspec()] * (chunks + 4),
        out_specs=[vspec()] * 2,
        out_shape=[jax.ShapeDtypeStruct(tok.shape, F32), jax.ShapeDtypeStruct(tok.shape, BF)],
        compiler_params=params(),
        cost_estimate=cost(2 * tok.shape[0] * tok.shape[1] ** 2, 4 * tok.shape[1] ** 2),
        name="out_projection_norm",
    )(index, *atts, *w_out, tok, gains)


def split_dot(a, b, dot):
    high = a.astype(BF)
    low = (a - high.astype(F32)).astype(BF)
    return dot(high, b) + dot(low, b)


def joined(ref, which):
    if ref.shape[0] == 1:
        return ref[0, which]
    return jnp.concatenate([ref[d, which] for d in range(ref.shape[0])], 1)


def units_body(chunks, unit, place_ref, *refs):
    n2s = refs[:chunks]
    gs = refs[chunks : 2 * chunks]
    sel_ref, rout_ref, w_ref = refs[2 * chunks : 2 * chunks + 3]
    hg_ref, gg_ref, ug_ref, lg_ref, rpart_ref = refs[2 * chunks + 3 : 2 * chunks + 8]
    n2_ref, g_ref, gate_ref, sum_ref, prob_ref, pick_ref = refs[2 * chunks + 8 :]
    step = pl.program_id(0)
    steps = pl.num_programs(0)
    rows = n2s[0].shape[0]
    tokens = chunks * rows
    lane = lax.broadcasted_iota(jnp.int32, (tokens, 128), 1)

    @pl.when(step == 0)
    def _():
        for c in range(chunks):
            n2_ref[rows * c : rows * (c + 1), :] = n2s[c][...]
            g_ref[rows * c : rows * (c + 1), :] = gs[c][...]
        logits = dot_nt(n2_ref[...], rout_ref[...])
        logits = jnp.where(lane < EXPERTS, logits, MASKED)
        raised = jnp.exp(logits - jnp.max(logits, axis=1, keepdims=True))
        prob_ref[...] = raised / jnp.sum(raised, axis=1, keepdims=True)
        for c in range(chunks):
            at = pl.ds(pl.multiple_of(place_ref[c] * rows, rows), rows)
            pick_ref[rows * c : rows * (c + 1), :] = sel_ref[at, :]
        gates = prob_ref[...] * pick_ref[...]
        for e in range(EXPERTS):
            one = jnp.sum(jnp.where(lane == e, gates, 0.0), axis=1, keepdims=True)
            gate_ref[e] = jnp.broadcast_to(one, (tokens, 128))
        sum_ref[...] = jnp.zeros_like(sum_ref)

    wg, wu, wd = joined(w_ref, 0), joined(w_ref, 1), joined(w_ref, 2)
    pre = dot_nt(n2_ref[...], jnp.concatenate([wg, wu], 0))
    gate_pre, up_pre = pre[:, : wg.shape[0]], pre[:, wg.shape[0] :]
    raw = dot_nt(g_ref[...], wd)
    c0 = float(np.sqrt(2.0 / np.pi))
    square = gate_pre * gate_pre
    th = jnp.tanh(gate_pre * (c0 + (c0 * 0.044715) * square))
    half = 0.5 + 0.5 * th
    act = gate_pre * half
    slope = half + gate_pre * (0.5 * c0 + (1.5 * c0 * 0.044715) * square) * (1.0 - th * th)
    hidden = act * up_pre
    prod = raw * hidden
    width = hg_ref.shape[1]
    e_low = (step * width) // unit
    e_high = (step * width + width - 1) // unit
    bound = jnp.where(e_high > e_low, unit * e_high - step * width, width)
    lows, highs = [], []
    for m in range(width // 128):
        is_low = lane + 128 * m < bound
        part = slice(128 * m, 128 * (m + 1))
        gate = jnp.where(is_low, gate_ref[e_low], gate_ref[e_high])
        lows.append(jnp.where(is_low, prod[:, part], 0.0))
        highs.append(prod[:, part] - lows[m])
        hg_ref[:, part] = (gate * hidden[:, part]).astype(BF)
        hidden_grad = gate * raw[:, part]
        gg_ref[:, part] = (hidden_grad * up_pre[:, part] * slope[:, part]).astype(BF)
        ug_ref[:, part] = (hidden_grad * act[:, part]).astype(BF)
    sum_ref[e_low] += functools.reduce(jnp.add, lows)

    @pl.when(e_high > e_low)
    def _():
        sum_ref[e_high] += functools.reduce(jnp.add, highs)

    @pl.when(step == steps - 1)
    def _():
        grad = jnp.zeros((tokens, 128), F32)
        for e in range(EXPERTS):
            grad = grad + jnp.where(lane == e, jnp.sum(sum_ref[e], axis=1, keepdims=True), 0.0)
        grad = grad * pick_ref[...]
        probs = prob_ref[...]
        logit_grad = probs * (grad - jnp.sum(probs * grad, axis=1, keepdims=True))
        lg_ref[...] = logit_grad
        rpart_ref[...] = split_dot(logit_grad, n2_ref[...], dot_tn)[0:8, :]


def units_call(place, n2s, gs, sel, router, weights, unit):
    chunks, rows, depth = len(n2s), n2s[0].shape[0], n2s[0].shape[1]
    count, _, ff, part = weights.shape
    tokens = chunks * rows
    whole = lambda shape: pl.BlockSpec(shape, lambda s: (0,) * len(shape))
    return pl.pallas_call(
        functools.partial(units_body, chunks, unit),
        grid=(ff // BLOCK,),
        in_specs=[sspec()]
        + [whole((rows, depth))] * (2 * chunks)
        + [whole(sel.shape), whole(router.shape), pl.BlockSpec((count, 3, BLOCK, part), lambda s: (0, 0, s, 0))],
        out_specs=[pl.BlockSpec((tokens, BLOCK), lambda s: (0, s))] * 3 + [whole((tokens, 128)), whole((8, depth))],
        out_shape=[jax.ShapeDtypeStruct((tokens, ff), BF)] * 3
        + [jax.ShapeDtypeStruct((tokens, 128), F32), jax.ShapeDtypeStruct((8, depth), F32)],
        scratch_shapes=[
            pltpu.VMEM((tokens, depth), BF),
            pltpu.VMEM((tokens, depth), BF),
            pltpu.VMEM((EXPERTS, tokens, 128), F32),
            pltpu.VMEM((EXPERTS, tokens, 128), F32),
            pltpu.VMEM((tokens, 128), F32),
            pltpu.VMEM((tokens, 128), F32),
        ],
        compiler_params=params(("arbitrary",)),
        cost_estimate=cost(6 * tokens * depth * ff, 6 * depth * ff + 12 * tokens * depth),
        name="expert_units",
    )(place, *n2s, *gs, sel, router, weights)


def product_body(terms, chunks, extra, *refs):
    xs = refs[:terms]
    ws = refs[terms : 2 * terms]
    at = 2 * terms + (2 if extra else 0)
    outs = refs[at : at + chunks]
    total = None
    for x, w in zip(xs, ws):
        term = dot_nn(x[...], joined(w, 0))
        total = term if total is None else total + term
    if extra:
        lg_ref, rout_ref = refs[2 * terms : 2 * terms + 2]
        total = total + split_dot(lg_ref[...], rout_ref[...], dot_nn)
    rows = outs[0].shape[0]
    for c in range(chunks):
        outs[c][...] = total[rows * c : rows * (c + 1)].astype(BF)


def product_call(xs, picks, weights, chunks, extra, name):
    tokens, ff = xs[0].shape
    count, _, _, part = weights.shape
    depth = count * part
    rows = tokens // chunks
    per = max(1, BLOCK // part)
    wide = min(part * per, BLOCK)
    whole = lambda shape: pl.BlockSpec(shape, lambda s: (0,) * len(shape))
    place_at = (lambda i, s: (s, i, 0, 0)) if count > 1 else (lambda i, s: (0, i, 0, s))
    w_specs = [pl.BlockSpec((min(per, count), 1, ff, wide // min(per, count)), functools.partial(place_at, i)) for i in picks]
    return pl.pallas_call(
        functools.partial(product_body, len(xs), chunks, bool(extra)),
        grid=(depth // wide,),
        in_specs=[whole((tokens, ff))] * len(xs)
        + w_specs
        + ([whole(extra[0].shape), pl.BlockSpec((128, wide), lambda s: (0, s))] if extra else []),
        out_specs=[pl.BlockSpec((rows, wide), lambda s: (0, s))] * chunks,
        out_shape=[jax.ShapeDtypeStruct((rows, depth), BF)] * chunks,
        compiler_params=params(("arbitrary",)),
        cost_estimate=cost(2 * len(xs) * tokens * depth * ff, 4 * len(xs) * depth * ff),
        name=name,
    )(*xs, *([weights] * len(xs)), *extra)


def wgrad_body(count, chunks, *refs):
    hg_ref, gg_ref, ug_ref = refs[:3]
    n2s = refs[3 : 3 + chunks]
    gs = refs[3 + chunks : 3 + 2 * chunks]
    out_ref, n2_ref, g_ref = refs[3 + 2 * chunks :]
    part = out_ref.shape[3]
    rows = n2s[0].shape[0]

    @pl.when(pl.program_id(0) == 0)
    def _():
        for c in range(chunks):
            n2_ref[rows * c : rows * (c + 1), :] = n2s[c][...]
            g_ref[rows * c : rows * (c + 1), :] = gs[c][...]

    width = hg_ref.shape[1]
    pair = dot_tn(jnp.concatenate([gg_ref[...], ug_ref[...]], 1), n2_ref[...]).astype(BF)
    down = dot_tn(hg_ref[...], g_ref[...]).astype(BF)
    for which, total in enumerate((pair[:width], pair[width:], down)):
        for d in range(count):
            out_ref[d, which] = total[:, part * d : part * (d + 1)]


def wgrad_call(count, kept, n2s, gs):
    tokens, ff = kept[0].shape
    chunks, rows, depth = len(n2s), n2s[0].shape[0], n2s[0].shape[1]
    whole = lambda shape: pl.BlockSpec(shape, lambda s: (0,) * len(shape))
    return pl.pallas_call(
        functools.partial(wgrad_body, count, chunks),
        grid=(ff // BLOCK,),
        in_specs=[pl.BlockSpec((tokens, BLOCK), lambda s: (0, s))] * 3 + [whole((rows, depth))] * (2 * chunks),
        out_specs=pl.BlockSpec((count, 3, BLOCK, depth // count), lambda s: (0, 0, s, 0)),
        out_shape=jax.ShapeDtypeStruct((count, 3, ff, depth // count), BF),
        scratch_shapes=[pltpu.VMEM((tokens, depth), BF), pltpu.VMEM((tokens, depth), BF)],
        compiler_params=params(("arbitrary",)),
        cost_estimate=cost(6 * tokens * depth * ff, 12 * depth * ff),
        name="expert_weight_grads",
    )(*kept, *n2s, *gs)


def norm_back(grad, u, gain):
    scale = lax.rsqrt(jnp.mean(u * u, axis=1, keepdims=True) + EPSILON)
    m = grad * gain
    back = scale * m - u * (scale * scale * scale) * jnp.mean(u * m, axis=1, keepdims=True)
    return back, jnp.sum(grad * u * scale, axis=0, keepdims=True)


def resid_body(count, chunks, terms, index_ref, *refs):
    parts = refs[:terms]
    mid_ref, g_ref, gains_ref, low_ref, high_ref = refs[terms : terms + 5]
    rest = refs[terms + 5 :]
    resid_ref, aog_ref, gain_ref = rest[:3]
    dos = rest[3:]
    grad = functools.reduce(jnp.add, [p[...].astype(F32) for p in parts])
    back, gain_part = norm_back(grad, mid_ref[...], gains_ref[1:2, :])
    resid = g_ref[...].astype(F32) + back
    resid_ref[...] = resid
    low = resid.astype(BF)
    aog_ref[...] = low
    gain_ref[...] = jnp.broadcast_to(gain_part, gain_ref.shape)
    for c in range(chunks):
        dos[c][...] = dot_nt(low, join_lanes(low_ref, high_ref, index_ref, count, c)).astype(BF)


def resid_call(index, parts, mid, grad, gains, w_out):
    chunks, terms = w_out[0].shape[1], len(parts)
    shape = mid.shape
    width = 2 * w_out[0].shape[2]
    return pl.pallas_call(
        functools.partial(resid_body, w_out[0].shape[0], chunks, terms),
        in_specs=[sspec()] + [vspec()] * (terms + 5),
        out_specs=[vspec()] * (3 + chunks),
        out_shape=[
            jax.ShapeDtypeStruct(shape, F32),
            jax.ShapeDtypeStruct(shape, BF),
            jax.ShapeDtypeStruct((8, shape[1]), F32),
        ]
        + [jax.ShapeDtypeStruct((shape[0], width), BF)] * chunks,
        compiler_params=params(),
        cost_estimate=cost(2 * shape[0] * shape[1] ** 2, 4 * shape[1] ** 2),
        name="resid_grad",
    )(index, *parts, mid, grad, gains, *w_out)


def final_body(chunks, *refs):
    parts = refs[:chunks]
    tok_ref, resid_ref, gains_ref, out_ref = refs[chunks:]
    grad = functools.reduce(jnp.add, [p[...].astype(F32) for p in parts])
    back, _ = norm_back(grad, tok_ref[...].astype(F32), gains_ref[0:1, :])
    out_ref[...] = resid_ref[...] + back


def final_call(parts, tok, resid, gains):
    return pl.pallas_call(
        functools.partial(final_body, len(parts)),
        in_specs=[vspec()] * (len(parts) + 3),
        out_specs=vspec(),
        out_shape=jax.ShapeDtypeStruct(tok.shape, F32),
        compiler_params=params(),
        cost_estimate=cost(20 * tok.size, 12 * tok.size),
        name="in_grad",
    )(*parts, tok, resid, gains)


def proj_body(count, chunks, rows, index_ref, place_ref, dq_ref, dk_ref, dv_ref, first_ref, last_ref, two_ref, router_ref, *refs):
    toks = refs[:chunks]
    outs = refs[chunks : 2 * chunks]
    gain_ref = refs[2 * chunks]
    depth = outs[0].shape[1]
    width = dq_ref.shape[1]
    weights = join_rows(first_ref, last_ref, index_ref, count, depth // count)
    gain = jnp.zeros((1, depth), F32)
    for c in range(chunks):
        at = pl.ds(pl.multiple_of(place_ref[c] * rows, rows), rows)
        grad = dot_nt(dq_ref[at, :], weights[:, :width])
        grad = grad + dot_nt(dk_ref[at, :], weights[:, width : 2 * width])
        grad = grad + dot_nt(dv_ref[at, :], weights[:, 2 * width :])
        outs[c][...] = grad.astype(BF)
        x = toks[c][...].astype(F32)
        scale = lax.rsqrt(jnp.mean(x * x, axis=1, keepdims=True) + EPSILON)
        gain = gain + jnp.sum(grad * x * scale, axis=0, keepdims=True)
    blank = jnp.zeros((6 - EXPERTS, depth), F32)
    gain_ref[...] = jnp.concatenate([gain, two_ref[0:1, :], router_ref[0:EXPERTS, :], blank], 0)


def proj_call(index, place, dq, dk, dv, pack, gain_two, router_part, toks):
    chunks, rows, depth = len(toks), toks[0].shape[0], toks[0].shape[1]
    return pl.pallas_call(
        functools.partial(proj_body, pack[0].shape[0], chunks, rows),
        in_specs=[sspec(), sspec()] + [vspec()] * (7 + chunks),
        out_specs=[vspec()] * (chunks + 1),
        out_shape=[jax.ShapeDtypeStruct((rows, depth), BF)] * chunks + [jax.ShapeDtypeStruct((8, depth), F32)],
        compiler_params=params(),
        cost_estimate=cost(6 * chunks * rows * depth * dq.shape[1], 8 * chunks * rows * depth),
        name="projection_grads",
    )(index, place, dq, dk, dv, *pack, gain_two, router_part, *toks)


def attn_weights_body(count, smalls, slot_ref, n1_ref, dq_ref, dk_ref, dv_ref, table_ref, *refs):
    keep_ref, send_ref, small_ref, *grad_refs = refs[smalls:]
    small_ref[...] = functools.reduce(jnp.add, [r[...] for r in refs[:smalls]])
    depth = n1_ref.shape[1]
    width = dq_ref.shape[1]
    part = depth // count
    normed = n1_ref[...]
    pieces = width // 128
    for ref, grad_ref in zip((dq_ref, dk_ref, dv_ref), grad_refs):
        grad_ref[...] = dot_tn(normed, ref[...]).astype(BF)
    for out_ref, slot, d in parted(keep_ref, send_ref, slot_ref):
        rows = pl.ds(pl.multiple_of(d * part, 128), part)
        for m, grad_ref in enumerate(grad_refs):
            for piece in range(pieces):
                at = (m * pieces + piece) * part
                out_ref[slot, at : at + part, :] = grad_ref[rows, 128 * piece : 128 * (piece + 1)]
        at = 3 * pieces * part
        value = jnp.concatenate([small_ref[:, rows], table_ref[...]], 0).astype(BF)
        out_ref[slot, at : at + 16, :] = value


def attn_weights_call(slots, n1, dq, dk, dv, table, smalls, count):
    total, depth = n1.shape
    width = dq.shape[1]
    part = depth // count
    return pl.pallas_call(
        functools.partial(attn_weights_body, count, len(smalls)),
        in_specs=[sspec()] + [vspec()] * (5 + len(smalls)),
        out_specs=[vspec()] * 2,
        out_shape=[jax.ShapeDtypeStruct((count // 2, 3 * width * part // 128 + 16, 128), BF)] * 2,
        scratch_shapes=[pltpu.VMEM((8, depth), F32)] + [pltpu.VMEM((depth, width), BF)] * 3,
        compiler_params=params(),
        cost_estimate=cost(6 * total * depth * width, 8 * total * depth),
        name="attn_weight_grads",
    )(slots, n1, dq, dk, dv, table, *smalls)


def wo_grad_body(count, chunks, slot_ref, *refs):
    atts = refs[:chunks]
    aog_ref, keep_ref, send_ref, grad_ref = refs[chunks:]
    width = atts[0].shape[1]
    part = grad_ref.shape[1] // count
    for c in range(chunks):
        at = slice(c * width, (c + 1) * width)
        grad_ref[at, :] = dot_tn(atts[c][...], aog_ref[...]).astype(BF)
    for out_ref, slot, d in parted(keep_ref, send_ref, slot_ref):
        out_ref[slot] = grad_ref[:, pl.ds(pl.multiple_of(d * part, 128), part)]


def wo_grad_call(slots, atts, aog, count):
    chunks, width = len(atts), atts[0].shape[1]
    rows, depth = aog.shape
    return pl.pallas_call(
        functools.partial(wo_grad_body, count, chunks),
        in_specs=[sspec()] + [vspec()] * (chunks + 1),
        out_specs=[vspec()] * 2,
        out_shape=[jax.ShapeDtypeStruct((max(1, count // 2), chunks * width, depth // count), BF)] * 2,
        scratch_shapes=[pltpu.VMEM((chunks * width, depth), BF)],
        compiler_params=params(),
        cost_estimate=cost(2 * rows * depth * chunks * width, 4 * depth * chunks * width),
        name="w_output_grad",
    )(slots, *atts, aog)


def kept_choices(ids):
    lanes = jnp.arange(128, dtype=jnp.int32)[None, :]
    expert_range = jnp.arange(EXPERTS, dtype=jnp.int32)[None, :]
    first = (ids[:, 0:1] == expert_range).astype(jnp.int32)
    second = (ids[:, 1:2] == expert_range).astype(jnp.int32)
    runs = jnp.cumsum(jnp.concatenate([first, second], 1), axis=0)
    first_run = runs[:, :EXPERTS]
    second_run = runs[:, EXPERTS:] + first_run[-1][None, :]
    place_one = jnp.sum(first_run * first, axis=1, keepdims=True) - 1
    place_two = jnp.sum(second_run * second, axis=1, keepdims=True) - 1
    kept = ((ids[:, 0:1] == lanes) & (place_one < CAP)) | ((ids[:, 1:2] == lanes) & (place_two < CAP))
    return kept.astype(F32)


def on_device(
    tokens_in,
    out_grad,
    attn_gain,
    w_query,
    w_key,
    w_value,
    w_output,
    rel_table,
    moe_gain,
    w_router,
    w_gate,
    w_up,
    down_weight,
    expert_ids,
    piece_starts,
):
    rows, depth = tokens_in.shape
    width = w_query.shape[1]
    z_size = lax.axis_size("tensor")
    dp_size = lax.axis_size("dp")
    z_rank = lax.axis_index("tensor").astype(jnp.int32)
    dp_rank = lax.axis_index("dp").astype(jnp.int32)
    total = rows * z_size
    share = depth // dp_size
    unit = w_gate.shape[2]
    ff = EXPERTS * unit
    heads = rel_table.shape[0]
    direct = dp_size == 8 and share == 128
    place = z_rank ^ jnp.arange(z_size, dtype=jnp.int32)

    near = z_swap(tokens_in, 1, z_size)
    far = z_swap(tokens_in, 2, z_size)
    line_at = 2 * BLOCK - 1 - np.arange(total + 2 * BLOCK)
    line = jnp.dot(rel_table, jnp.asarray(onehot_of(line_at).T), precision=PRECISE)[:, None, :]
    sel = kept_choices(expert_ids)
    toks = [tokens_in, near, far, z_swap(after(far, near, sel, line), 1, z_size)]
    w_output_late = after(w_output, far)
    small = jnp.concatenate([attn_gain, moe_gain, w_router.T.reshape(-1)])[None, :]
    packed = jnp.concatenate([w_query, w_key, w_value], 1)
    wo_slots = jnp.stack(z_direct([w_output_late] * z_size, z_size))[None]
    ranks = dp_rank ^ jnp.arange(8, dtype=jnp.int32)
    half = wo_slots.shape[2] // 2
    if direct:
        index = dp_slots(ranks)
        slots = dp_rank ^ dp_scatter_slots(jnp.arange(8, dtype=jnp.int32))
        first = dp_step(packed[:80][None], 2)
        last = dp_step(jnp.concatenate([packed[80:], small, jnp.zeros((15, packed.shape[1]), BF)], 0)[None], 4)
        first, last = dp_step(after(first, near), 4), dp_step(after(last, near), 2)
        wo_low = dp_step(after(wo_slots[:, :, :half], near, far), 2)
        wo_high = dp_step(after(wo_slots[:, :, half:], near, far), 4)
        first = dp_step(after(first, toks[3], wo_low, wo_high), 1)
        last = dp_step(after(last, toks[3], wo_low, wo_high), 1)
        pack, small_all = [first, last], last
    else:
        slots = jnp.zeros((1,), jnp.int32)
        index = jnp.zeros((2,), jnp.int32)
        pack = lax.all_gather(packed, "dp", axis=0, tiled=True)[None]
        pack = [pack[:, : depth // 2], pack[:, depth // 2 :]]
        small_all = lax.all_gather(small[0], "dp", axis=0).reshape(dp_size, 2 + EXPERTS, share)
        small_all = jnp.swapaxes(small_all, 0, 1).reshape(2 + EXPERTS, depth)
        small_all = jnp.concatenate([small_all, jnp.zeros((2, depth), BF)], 0)
        wo_all = lax.all_gather(wo_slots[0], "dp", axis=2, tiled=True)[None]
        wo_all = [wo_all[:, :, :half], wo_all[:, :, half:]]

    local = jnp.stack(
        [
            jnp.swapaxes(w_gate, 1, 2).reshape(ff, share),
            jnp.swapaxes(w_up, 1, 2).reshape(ff, share),
            down_weight.reshape(ff, share),
        ]
    )
    if direct:
        experts_w = lax.all_gather(local, "dp", axis=0)
    else:
        experts_w = lax.all_gather(local, "dp", axis=2, tiled=True)[None]

    n1, q, k, v, kt, vt, gains, router = qkv_call(index, place, toks, pack, small_all, width)
    g_near = z_swap(after(out_grad, toks[3]), 1, z_size)
    g_far = z_swap(after(out_grad, toks[3]), 2, z_size)
    fwd = attn_fwd(piece_starts, place, z_size, q, k, vt, line)
    chances, ot = fwd[:2]
    atts = z_direct([after(fwd[2], g_near, g_far)] + [after(x, g_near, g_far) for x in fwd[3:]], z_size)
    if direct:
        wo_low, wo_high = dp_step(after(wo_low, n1), 4), dp_step(after(wo_high, n1), 2)
        wo_all = [dp_step(after(x, atts[1]), 1) for x in (wo_low, wo_high)]
    gs = [out_grad, g_near, g_far, z_swap(after(g_far, fwd[2]), 1, z_size)]
    mid, n2 = mid_call(index, [after(atts[0], gs[3])] + atts[1:], wo_all, tokens_in, gains)

    n2_near = z_swap(n2, 1, z_size)
    n2_far = z_swap(n2, 2, z_size)
    n2s = [n2, n2_near, n2_far, z_swap(after(n2_far, n2_near), 1, z_size)]
    hg, gg, ug, logit_grad, router_part = units_call(place, n2s, gs, sel, router, experts_w, unit)
    ngs = product_call([gg, ug], (0, 1), experts_w, z_size, [logit_grad, router], "normed_two_grads")
    passed = z_swap(ngs[3], 1, z_size)
    outs = product_call([after(hg, ngs[0])], (2,), experts_w, z_size, [], "expert_out")
    both = (ngs[2].astype(F32) + after(passed, outs[0]).astype(F32)).astype(BF)
    far = z_swap(both, 2, z_size)
    ng_near = z_swap(after(ngs[1], passed), 1, z_size)
    count = experts_w.shape[0]
    weight_grads = wgrad_call(experts_w.shape[0], [after(hg, both, *outs), gg, ug], n2s, gs)
    resid = resid_call(index, [after(ngs[0], weight_grads), ng_near, far], mid, out_grad, gains, wo_all)
    resid_grad, aog, gain_two = resid[:3]
    weight_grads = after(weight_grads, far, ng_near)
    if direct:
        expert_grads = lax.psum_scatter(weight_grads, "dp", scatter_dimension=0, tiled=False)
    else:
        expert_grads = lax.psum_scatter(weight_grads[0], "dp", scatter_dimension=2, tiled=True)
    out_passed = z_swap(after(outs[3], aog), 1, z_size)
    dos = z_direct(resid[3:], z_size)
    wo_keep, wo_send = wo_grad_call(slots, atts, aog, count)
    out_both = (outs[2].astype(F32) + out_passed.astype(F32)).astype(BF)
    dos[0] = after(dos[0], wo_keep, out_both)
    out_far = z_swap(out_both, 2, z_size)
    out_near = z_swap(after(outs[1], out_both), 1, z_size)
    if direct:
        wo_grads = dp_fold(wo_keep, after(wo_send, *dos), 1)
    dq, dk, dv, diag = attn_bwd(place, dos, chances, q, k, v, kt, ot)
    if direct:
        wo_grads = dp_fold(*halves(wo_grads), 2)
        dq = after(dq, wo_grads)
    dq = after(dq, out_far, out_near)
    proj = proj_call(index, place, dq, dk, dv, pack, gain_two, router_part, toks)

    diag_at = (
        BLOCK * np.arange(total // BLOCK + 1)[:, None] - (BLOCK * (total // BLOCK - 2) + 1) - np.arange(2 * BLOCK)[None, :]
    )
    table = jnp.einsum("hbt,btk->hk", diag, jnp.asarray(onehot_of(diag_at)), precision=PRECISE)
    n1_passed = z_swap(proj[3], 1, z_size)
    if direct:
        table_rows = jnp.pad(table.reshape(1, -1), ((0, 7), (0, 0)))
        smalls = z_direct([proj[z_size]] * z_size, z_size)
        wo_grads = dp_fold(*halves(wo_grads), 4)[0]
        attn_keep, attn_send = attn_weights_call(slots, n1, dq, dk, dv, after(table_rows, wo_grads), smalls, 8)
        n1_passed = after(n1_passed, attn_keep)
    n1_both = (proj[2].astype(F32) + n1_passed.astype(F32)).astype(BF)
    n1_far = z_swap(n1_both, 2, z_size)
    n1_near = z_swap(after(proj[1], n1_both), 1, z_size)
    in_grad = final_call([proj[0], n1_near, n1_far], tokens_in, resid_grad, gains)
    out_parts = [outs[0], out_near, out_far]
    out_rows = (mid + functools.reduce(jnp.add, [p.astype(F32) for p in out_parts])).astype(BF)

    if direct:
        attn_grads = dp_fold(attn_keep, after(attn_send, n1_both), 1)
        attn_grads = dp_fold(*halves(attn_grads), 2)
        attn_grads = dp_fold(*halves(after(attn_grads, n1_far, n1_near)), 4)
        attn_grads = attn_grads[0].astype(F32)
        per = width // 128
        cut = attn_grads[: 3 * per * share].reshape(3, per, share, 128)
        cut = jnp.swapaxes(cut, 1, 2).reshape(3, share, width)
        smalls = attn_grads[3 * per * share :]
        grad_table = smalls[8, : heads * BUCKETS].reshape(heads, BUCKETS)
        mine = z_rank
        grad_wo = after(wo_grads, n1_near)
    else:
        cut = jnp.stack([jnp.dot(n1.T, d, preferred_element_type=F32) for d in (dq, dk, dv)])
        cut = lax.psum_scatter(cut, "dp", scatter_dimension=1, tiled=True)
        smalls = lax.psum(proj[z_size], ("dp", "tensor"))
        grad_table = lax.psum(table, "dp")
        mine = dp_rank * z_size + z_rank
        grad_wo = lax.psum_scatter(wo_keep[0], "dp", scatter_dimension=1, tiled=True)
    wo_parts = z_direct([grad_wo[width * c : width * (c + 1)] for c in range(z_size)], z_size)
    grad_wo = functools.reduce(jnp.add, [p.astype(F32) for p in wo_parts])
    per_device = depth // (dp_size * z_size)
    own = lax.dynamic_slice_in_dim(smalls, mine * per_device, per_device, 1)

    wide = expert_grads.astype(F32).reshape(3, EXPERTS, unit, share)
    return (
        out_rows,
        in_grad,
        own[0],
        cut[0],
        cut[1],
        cut[2],
        grad_wo,
        grad_table,
        own[1],
        own[2 : 2 + EXPERTS].T,
        jnp.swapaxes(wide[0], 1, 2),
        jnp.swapaxes(wide[1], 1, 2),
        wide[2],
    )


def solution(mesh):
    rows = P(("dp", "tensor"), None)
    grid = P("dp", "tensor")
    flat = P(("dp", "tensor"))
    weights = (P(None, "dp", "tensor"), P(None, "dp", "tensor"), P(None, "tensor", "dp"))
    in_specs = (rows, rows, P("dp"), grid, grid, grid, P("tensor", "dp"), P("tensor", None), P("dp"), P("dp", None))
    out_specs = (rows, rows, flat, grid, grid, grid, P("tensor", "dp"), P("tensor", None), flat, rows)
    return jax.shard_map(
        on_device,
        mesh=mesh,
        in_specs=in_specs + weights + (P("dp", None), P("dp", None)),
        out_specs=out_specs + weights,
        check_vma=False,
    )
```

```python
import functools

import jax
import jax.numpy as jnp
import numpy as np
from jax import lax
from jax.experimental import pallas as pl
from jax.experimental.pallas import tpu as pltpu
from jax.sharding import PartitionSpec as P

EXPERTS = 4
PIECE = 256
CAP = 640
BUCKETS = 32
EPSILON = 1e-06
PRECISE = lax.Precision.HIGHEST
LIMITS = (12, 16, 23, 32, 46, 64, 91)
MASKED = -1e30
BF = jnp.bfloat16
F32 = jnp.float32
BLOCK = 256
VMEM_LIMIT = 56 * 1024 * 1024


def params(semantics=None):
    return pltpu.CompilerParams(dimension_semantics=semantics, vmem_limit_bytes=VMEM_LIMIT)


def dot_nn(a, b):
    return lax.dot_general(a, b, (((1,), (0,)), ((), ())), preferred_element_type=F32)


def dot_nt(a, b):
    return lax.dot_general(a, b, (((1,), (1,)), ((), ())), preferred_element_type=F32)


def dot_tn(a, b):
    return lax.dot_general(a, b, (((0,), (0,)), ((), ())), preferred_element_type=F32)


def bucket_of(offsets):
    distance = np.abs(offsets)
    far = np.full_like(distance, 8)
    for bound in LIMITS:
        far = far + (distance >= bound)
    return np.where(distance < 8, distance, far) + np.where(offsets > 0, 16, 0)


def onehot_of(offsets):
    return (bucket_of(offsets)[..., None] == np.arange(BUCKETS)).astype(np.float32)


def cost(flops, nbytes):
    return pl.CostEstimate(flops=int(flops), bytes_accessed=int(nbytes), transcendentals=0)


def vspec():
    return pl.BlockSpec(memory_space=pltpu.VMEM)


def sspec():
    return pl.BlockSpec(memory_space=pltpu.SMEM)


def z_swap(x, mask, size):
    return lax.ppermute(x, "tensor", [(i, i ^ mask) for i in range(size)])


def z_gather(x, size):
    near = z_swap(x, 1, size)
    far = z_swap(x, 2, size)
    return [x, near, far, z_swap(far, 1, size)]


def z_direct(parts, size):
    return [parts[0]] + [z_swap(parts[mask], mask, size) for mask in range(1, size)]


def z_reduce(parts, size):
    passed = z_swap(parts[3], 1, size)
    far = z_swap((parts[2].astype(F32) + passed.astype(F32)).astype(BF), 2, size)
    return [parts[0], z_swap(parts[1], 1, size), far]


def after(x, *others):
    return lax.optimization_barrier((x,) + others)[0]


def dp_slots(ranks):
    x, y, core = (ranks >> 1) & 1, (ranks >> 2) & 1, ranks & 1
    return jnp.concatenate([x | (y << 1) | (core << 2), y | (x << 1) | (core << 2)])


def dp_step(x, bit):
    other = lax.ppermute(x, "dp", [(i, i ^ bit) for i in range(8)])
    return jnp.concatenate([x, other], 0)


def dp_fold(keep, send, bit):
    other = lax.ppermute(send, "dp", [(i, i ^ bit) for i in range(8)])
    return (keep.astype(F32) + other.astype(F32)).astype(keep.dtype)


def halves(x):
    return x[: x.shape[0] // 2], x[x.shape[0] // 2 :]


def dp_scatter_slots(ranks):
    return ((ranks >> 2) & 1) | (((ranks >> 1) & 1) << 1) | ((ranks & 1) << 2)


def parted(keep_ref, send_ref, order_ref):
    half = keep_ref.shape[0]
    for j in range(2 * half if half > 1 else 1):
        yield (keep_ref if j < half else send_ref), j % half, order_ref[j]


def join_rows(first_ref, last_ref, index_ref, count, rows):
    split = first_ref.shape[1]
    pieces = []
    for c in range(count):
        pieces.append(first_ref[index_ref[c], :, :])
        pieces.append(last_ref[index_ref[count + c], 0 : rows - split, :])
    return jnp.concatenate(pieces, 0)


def qkv_body(count, chunks, rows, index_ref, place_ref, *refs):
    toks = refs[:chunks]
    first_ref, last_ref, small_ref = refs[chunks : chunks + 3]
    n1_ref, q_ref, k_ref, v_ref, kt_ref, vt_ref, gains_ref, router_ref = refs[chunks + 3 :]
    depth = n1_ref.shape[1] // count
    weights = join_rows(first_ref, last_ref, index_ref, count, depth)
    width = q_ref.shape[1]
    if count == 1:
        small = [small_ref[r : r + 1, :] for r in range(2 + EXPERTS)]
    else:
        row = depth - first_ref.shape[1]
        lines = [small_ref[index_ref[count + d], row : row + 1, :].astype(F32) for d in range(count)]
        small = [
            jnp.concatenate([x[:, depth * r : depth * (r + 1)] for x in lines], 1) for r in range(2 + EXPERTS)
        ]
    small = jnp.concatenate([x.astype(F32) for x in small] + [jnp.zeros((2, depth * count), F32)], 0)
    gains_ref[...] = small
    routers = jnp.concatenate([small[2:], jnp.zeros((10, depth * count), F32)], 0)
    router_ref[...] = jnp.zeros_like(router_ref)
    router_ref[0:16, :] = routers.astype(BF)
    gain = small[0:1, :]
    for c in range(chunks):
        at = pl.ds(pl.multiple_of(place_ref[c] * rows, rows), rows)
        x = toks[c][...].astype(F32)
        scale = lax.rsqrt(jnp.mean(x * x, axis=1, keepdims=True) + EPSILON)
        normed = (x * scale * gain).astype(BF)
        n1_ref[at, :] = normed
        out = dot_nn(normed, weights)
        q_ref[at, :] = (out[:, :width].astype(BF).astype(F32) * 0.125).astype(BF)
        key = out[:, width : 2 * width]
        value = out[:, 2 * width :]
        k_ref[at, :] = key.astype(BF)
        v_ref[at, :] = value.astype(BF)
        kt_ref[:, at] = jnp.transpose(key).astype(BF)
        vt_ref[:, at] = jnp.transpose(value).astype(BF)


def qkv_call(index, place, toks, pack, small, width):
    chunks, rows, depth = len(toks), toks[0].shape[0], toks[0].shape[1]
    total = chunks * rows
    shapes = [(total, depth)] + [(total, width)] * 3 + [(width, total)] * 2
    return pl.pallas_call(
        functools.partial(qkv_body, pack[0].shape[0], chunks, rows),
        in_specs=[sspec(), sspec()] + [vspec()] * (chunks + 3),
        out_specs=[vspec()] * 8,
        out_shape=[jax.ShapeDtypeStruct(s, BF) for s in shapes]
        + [jax.ShapeDtypeStruct((8, depth), F32), jax.ShapeDtypeStruct((128, depth), BF)],
        compiler_params=params(),
        cost_estimate=cost(2 * total * depth * 3 * width, 8 * total * depth),
        name="norm_qkv",
    )(index, place, *toks, *pack, small)


def extent_of(i, total):
    return min(BLOCK * (i + 2), total)


def fwd_body(total, chunks, starts_ref, place_ref, q_ref, k_ref, vt_ref, line_ref, p_ref, ot_ref, *refs):
    atts = refs[:chunks]
    strip_ref, mask_ref, all_ref = refs[chunks:]
    head = pl.program_id(0)
    heads = pl.num_programs(0)
    blocks = total // BLOCK
    width = q_ref.shape[1]
    dim = width // 4

    @pl.when(head == 0)
    def _():
        def label(pos):
            first = (pos >= starts_ref[0, 0]) & (pos < starts_ref[0, 0] + PIECE)
            second = (pos >= starts_ref[0, 1]) & (pos < starts_ref[0, 1] + PIECE)
            return first, second

        for i in range(blocks):
            for j in (i, i + 1):
                if j >= blocks:
                    continue
                kpos = lax.broadcasted_iota(jnp.int32, (BLOCK, BLOCK), 0) + BLOCK * j
                qpos = lax.broadcasted_iota(jnp.int32, (BLOCK, BLOCK), 1) + BLOCK * i
                k1, k2 = label(kpos)
                q1, q2 = label(qpos)
                seen = (kpos <= qpos) | (k1 & q1) | (k2 & q2)
                mask_ref[2 * i + j - i] = jnp.where(seen, 0.0, MASKED)

    for beta in range(blocks + 1):
        start = BLOCK * (blocks - beta)
        window = line_ref[0, 0:1, start : start + 2 * BLOCK]
        spread = jnp.broadcast_to(window, (BLOCK, 2 * BLOCK))
        rolled = pltpu.roll(spread, BLOCK + 1, 1, stride=1, stride_axis=0)
        strip_ref[BLOCK * beta : BLOCK * (beta + 1), :] = rolled[:, :BLOCK]

    lanes = lax.broadcasted_iota(jnp.int32, (2 * BLOCK, width), 1)
    own = (lanes >= head * dim) & (lanes < (head + 1) * dim)
    at_head = pl.ds(pl.multiple_of(head * dim, dim), dim)
    for pair in range(0, blocks, 2):
        both = slice(BLOCK * pair, BLOCK * (pair + 2))
        reach = extent_of(pair + 1, total)
        q_rows = q_ref[both, :]
        q_own = jnp.where(own, q_rows, jnp.zeros_like(q_rows))
        raw = dot_nt(k_ref[0:reach, :], q_own)
        for i in (pair, pair + 1):
            extent = extent_of(i, total)
            cols = slice(BLOCK * i, BLOCK * (i + 1))
            base = BLOCK * (blocks - 1 - i)
            scores = raw[0:extent, BLOCK * (i - pair) : BLOCK * (i - pair + 1)] + strip_ref[base : base + extent, :]
            parts = [scores[BLOCK * j : BLOCK * (j + 1)] for j in range(extent // BLOCK)]
            for j in (i, i + 1):
                if j < blocks:
                    parts[j] = parts[j] + mask_ref[2 * i + j - i]
            top = functools.reduce(jnp.maximum, parts)
            top = jnp.max(top, axis=0, keepdims=True)
            parts = [jnp.exp(part - top) for part in parts]
            total_sum = jnp.sum(functools.reduce(jnp.add, parts), axis=0, keepdims=True)
            inverse = 1.0 / total_sum
            p_ref[0, 0:extent, cols] = jnp.concatenate([(part * inverse).astype(BF) for part in parts], 0)
            if extent < total:
                p_ref[0, extent : extent + BLOCK, cols] = jnp.zeros((BLOCK, BLOCK), BF)
        ot_ref[at_head, both] = dot_nn(vt_ref[at_head, 0:reach], p_ref[0, 0:reach, both])

    @pl.when(head == heads - 1)
    def _():
        mixed = ot_ref[...]
        all_ref[...] = jnp.transpose(mixed).astype(BF)
        rows = total // chunks
        for c in range(chunks):
            at = pl.ds(pl.multiple_of(place_ref[c] * rows, rows), rows)
            atts[c][...] = all_ref[at, :]


def attn_fwd(starts, place, chunks, q, k, vt, line):
    total, width = q.shape
    heads = line.shape[0]
    blocks = total // BLOCK
    whole = lambda shape: pl.BlockSpec(shape, lambda h: (0,) * len(shape))
    return pl.pallas_call(
        functools.partial(fwd_body, total, chunks),
        grid=(heads,),
        in_specs=[
            sspec(),
            sspec(),
            whole((total, width)),
            whole((total, width)),
            whole((width, total)),
            pl.BlockSpec((1, 1, line.shape[2]), lambda h: (h, 0, 0)),
        ],
        out_specs=[
            pl.BlockSpec((1, total, total), lambda h: (h, 0, 0)),
            whole((width, total)),
        ]
        + [whole((total // chunks, width))] * chunks,
        out_shape=[
            jax.ShapeDtypeStruct((heads, total, total), BF),
            jax.ShapeDtypeStruct((width, total), F32),
        ]
        + [jax.ShapeDtypeStruct((total // chunks, width), BF)] * chunks,
        scratch_shapes=[
            pltpu.VMEM((BLOCK * (blocks + 1), BLOCK), F32),
            pltpu.VMEM((2 * blocks, BLOCK, BLOCK), F32),
            pltpu.VMEM((total, width), BF),
        ],
        compiler_params=params(("arbitrary",)),
        cost_estimate=cost(heads * 4 * total * total * width, 10 * total * total),
        name="attn_forward",
    )(starts, place, q, k, vt, line)


def diagonal_sums(acc):
    half = BLOCK // 2
    low, high = acc[:half], acc[half:]
    rows = jnp.concatenate(
        [high[:, :half], high[:, half:] + low[:, :half], low[:, half:], jnp.zeros((half, half), F32)], 1
    )
    step = half // 2
    while step >= 8:
        rows = rows[step:] + pltpu.roll(rows[:step], step, 1)
        step //= 2
    index = lax.broadcasted_iota(jnp.int32, rows.shape, 0)
    for step in (4, 2, 1):
        rows = jnp.where((index & step) == 0, pltpu.roll(rows, step, 1), rows)
    return jnp.sum(rows, axis=0, keepdims=True)


def bwd_body(total, chunks, place_ref, *refs):
    grads = refs[:chunks]
    p_ref, q_ref, k_ref, v_ref, kt_ref, ot_ref = refs[chunks : chunks + 6]
    dq_ref, dk_ref, dv_ref, diag_ref = refs[chunks + 6 : chunks + 10]
    do_ref, dot_ref, dqt_ref, dka_ref, dva_ref, ds_ref, acc_ref = refs[chunks + 10 :]
    head = pl.program_id(0)
    heads = pl.num_programs(0)
    blocks = total // BLOCK
    rows = total // chunks
    width = q_ref.shape[1]
    dim = width // 4

    @pl.when(head == 0)
    def _():
        for c in range(chunks):
            at = pl.ds(pl.multiple_of(place_ref[c] * rows, rows), rows)
            do_ref[at, :] = grads[c][...]
        dot_ref[...] = jnp.transpose(do_ref[...].astype(F32))
        ds_ref[...] = jnp.zeros_like(ds_ref)
        dka_ref[...] = jnp.zeros_like(dka_ref)
        dva_ref[...] = jnp.zeros_like(dva_ref)

    at_head = pl.ds(pl.multiple_of(head * dim, dim), dim)
    inner = jnp.sum(dot_ref[at_head, :] * ot_ref[at_head, :], axis=0, keepdims=True)
    lanes = lax.broadcasted_iota(jnp.int32, (total, width), 1)
    own = (lanes >= head * dim) & (lanes < (head + 1) * dim)
    q_own = jnp.where(own, q_ref[...], jnp.zeros_like(q_ref))
    do_own = jnp.where(own, do_ref[...], jnp.zeros_like(do_ref))
    written = 0
    for pair in range(blocks - 2, -1, -2):
        both = slice(BLOCK * pair, BLOCK * (pair + 2))
        reach = extent_of(pair + 1, total)
        pair_grad = dot_nt(v_ref[0:reach, :], do_own[both, :])
        for i in (pair + 1, pair):
            extent = extent_of(i, total)
            cols = slice(BLOCK * i, BLOCK * (i + 1))
            chance_grad = pair_grad[0:extent, BLOCK * (i - pair) : BLOCK * (i - pair + 1)]
            chances = p_ref[0, 0:extent, cols].astype(F32)
            score_grad = (chances * (chance_grad - inner[:, cols])).astype(BF)
            ds_ref[0:extent, cols] = score_grad
            base = BLOCK * (blocks - 1 - i)
            wide = score_grad.astype(F32)
            if i == blocks - 1:
                acc_ref[0:extent, :] = wide
                written = extent
            else:
                old = written - base
                acc_ref[base:written, :] += wide[:old]
                if base + extent > written:
                    acc_ref[written : base + extent, :] = wide[old:]
                    written = base + extent
        dqt_ref[at_head, both] = dot_nn(kt_ref[at_head, 0:reach], ds_ref[0:reach, both])
    for pair in range(0, blocks, 2):
        first = max(0, BLOCK * (pair - 1))
        keys = slice(BLOCK * pair, BLOCK * (pair + 2))
        dka_ref[keys, :] += dot_nn(ds_ref[keys, first:], q_own[first:, :])
        dva_ref[keys, :] += dot_nn(p_ref[0, keys, first:], do_own[first:, :])
    for beta in range(blocks + 1):
        diag_ref[0, beta : beta + 1, :] = diagonal_sums(acc_ref[BLOCK * beta : BLOCK * (beta + 1), :])

    @pl.when(head == heads - 1)
    def _():
        dq_ref[...] = (jnp.transpose(dqt_ref[...]) * 0.125).astype(BF)
        dk_ref[...] = dka_ref[...].astype(BF)
        dv_ref[...] = dva_ref[...].astype(BF)


def attn_bwd(place, grads, chances, q, k, v, kt, ot):
    total, width = q.shape
    heads = chances.shape[0]
    blocks = total // BLOCK
    chunks = len(grads)
    whole = lambda shape: pl.BlockSpec(shape, lambda h: (0,) * len(shape))
    return pl.pallas_call(
        functools.partial(bwd_body, total, chunks),
        grid=(heads,),
        in_specs=[sspec()]
        + [whole(grads[0].shape)] * chunks
        + [pl.BlockSpec((1, total, total), lambda h: (h, 0, 0))]
        + [whole((total, width))] * 3
        + [whole((width, total))] * 2,
        out_specs=[whole((total, width))] * 3 + [pl.BlockSpec((1, blocks + 1, 2 * BLOCK), lambda h: (h, 0, 0))],
        out_shape=[jax.ShapeDtypeStruct((total, width), BF)] * 3
        + [jax.ShapeDtypeStruct((heads, blocks + 1, 2 * BLOCK), F32)],
        scratch_shapes=[
            pltpu.VMEM((total, width), BF),
            pltpu.VMEM((width, total), F32),
            pltpu.VMEM((width, total), F32),
            pltpu.VMEM((total, width), F32),
            pltpu.VMEM((total, width), F32),
            pltpu.VMEM((total, total), BF),
            pltpu.VMEM((BLOCK * (blocks + 1), BLOCK), F32),
        ],
        compiler_params=params(("arbitrary",)),
        cost_estimate=cost(heads * 160 * total * total * width, 10 * total * total),
        name="attn_backward",
    )(place, *grads, chances, q, k, v, kt, ot)


def join_lanes(low_ref, high_ref, index_ref, count, slot):
    low = [low_ref[index_ref[c], slot] for c in range(count)]
    high = [high_ref[index_ref[count + c], slot] for c in range(count)]
    return jnp.concatenate([jnp.concatenate(low, 1), jnp.concatenate(high, 1)], 0)


def mid_body(count, chunks, index_ref, *refs):
    atts = refs[:chunks]
    low_ref, high_ref, tok_ref, gain_ref, mid_ref, n2_ref = refs[chunks:]
    u = tok_ref[...].astype(F32)
    for c in range(chunks):
        u = u + dot_nn(atts[c][...], join_lanes(low_ref, high_ref, index_ref, count, c))
    mid_ref[...] = u
    scale = lax.rsqrt(jnp.mean(u * u, axis=1, keepdims=True) + EPSILON)
    n2_ref[...] = (u * scale * gain_ref[1:2, :]).astype(BF)


def mid_call(index, atts, w_out, tok, gains):
    chunks = len(atts)
    return pl.pallas_call(
        functools.partial(mid_body, w_out[0].shape[0], chunks),
        in_specs=[sspec()] + [vspec()] * (chunks + 4),
        out_specs=[vspec()] * 2,
        out_shape=[jax.ShapeDtypeStruct(tok.shape, F32), jax.ShapeDtypeStruct(tok.shape, BF)],
        compiler_params=params(),
        cost_estimate=cost(2 * tok.shape[0] * tok.shape[1] ** 2, 4 * tok.shape[1] ** 2),
        name="out_projection_norm",
    )(index, *atts, *w_out, tok, gains)


def split_dot(a, b, dot):
    high = a.astype(BF)
    low = (a - high.astype(F32)).astype(BF)
    return dot(high, b) + dot(low, b)


def joined(ref, which):
    if ref.shape[0] == 1:
        return ref[0, which]
    return jnp.concatenate([ref[d, which] for d in range(ref.shape[0])], 1)


def units_body(chunks, unit, place_ref, *refs):
    n2s = refs[:chunks]
    gs = refs[chunks : 2 * chunks]
    sel_ref, rout_ref, w_ref = refs[2 * chunks : 2 * chunks + 3]
    hg_ref, gg_ref, ug_ref, lg_ref, rpart_ref = refs[2 * chunks + 3 : 2 * chunks + 8]
    n2_ref, g_ref, gate_ref, sum_ref, prob_ref, pick_ref = refs[2 * chunks + 8 :]
    step = pl.program_id(0)
    steps = pl.num_programs(0)
    rows = n2s[0].shape[0]
    tokens = chunks * rows
    lane = lax.broadcasted_iota(jnp.int32, (tokens, 128), 1)

    @pl.when(step == 0)
    def _():
        for c in range(chunks):
            n2_ref[rows * c : rows * (c + 1), :] = n2s[c][...]
            g_ref[rows * c : rows * (c + 1), :] = gs[c][...]
        logits = dot_nt(n2_ref[...], rout_ref[...])
        logits = jnp.where(lane < EXPERTS, logits, MASKED)
        raised = jnp.exp(logits - jnp.max(logits, axis=1, keepdims=True))
        prob_ref[...] = raised / jnp.sum(raised, axis=1, keepdims=True)
        for c in range(chunks):
            at = pl.ds(pl.multiple_of(place_ref[c] * rows, rows), rows)
            pick_ref[rows * c : rows * (c + 1), :] = sel_ref[at, :]
        gates = prob_ref[...] * pick_ref[...]
        for e in range(EXPERTS):
            one = jnp.sum(jnp.where(lane == e, gates, 0.0), axis=1, keepdims=True)
            gate_ref[e] = jnp.broadcast_to(one, (tokens, 128))
        sum_ref[...] = jnp.zeros_like(sum_ref)

    wg, wu, wd = joined(w_ref, 0), joined(w_ref, 1), joined(w_ref, 2)
    pre = dot_nt(n2_ref[...], jnp.concatenate([wg, wu], 0))
    gate_pre, up_pre = pre[:, : wg.shape[0]], pre[:, wg.shape[0] :]
    raw = dot_nt(g_ref[...], wd)
    c0 = float(np.sqrt(2.0 / np.pi))
    square = gate_pre * gate_pre
    th = jnp.tanh(gate_pre * (c0 + (c0 * 0.044715) * square))
    half = 0.5 + 0.5 * th
    act = gate_pre * half
    slope = half + gate_pre * (0.5 * c0 + (1.5 * c0 * 0.044715) * square) * (1.0 - th * th)
    hidden = act * up_pre
    prod = raw * hidden
    width = hg_ref.shape[1]
    e_low = (step * width) // unit
    e_high = (step * width + width - 1) // unit
    bound = jnp.where(e_high > e_low, unit * e_high - step * width, width)
    lows, highs = [], []
    for m in range(width // 128):
        is_low = lane + 128 * m < bound
        part = slice(128 * m, 128 * (m + 1))
        gate = jnp.where(is_low, gate_ref[e_low], gate_ref[e_high])
        lows.append(jnp.where(is_low, prod[:, part], 0.0))
        highs.append(prod[:, part] - lows[m])
        hg_ref[:, part] = (gate * hidden[:, part]).astype(BF)
        hidden_grad = gate * raw[:, part]
        gg_ref[:, part] = (hidden_grad * up_pre[:, part] * slope[:, part]).astype(BF)
        ug_ref[:, part] = (hidden_grad * act[:, part]).astype(BF)
    sum_ref[e_low] += functools.reduce(jnp.add, lows)

    @pl.when(e_high > e_low)
    def _():
        sum_ref[e_high] += functools.reduce(jnp.add, highs)

    @pl.when(step == steps - 1)
    def _():
        grad = jnp.zeros((tokens, 128), F32)
        for e in range(EXPERTS):
            grad = grad + jnp.where(lane == e, jnp.sum(sum_ref[e], axis=1, keepdims=True), 0.0)
        grad = grad * pick_ref[...]
        probs = prob_ref[...]
        logit_grad = probs * (grad - jnp.sum(probs * grad, axis=1, keepdims=True))
        lg_ref[...] = logit_grad
        rpart_ref[...] = split_dot(logit_grad, n2_ref[...], dot_tn)[0:8, :]


def units_call(place, n2s, gs, sel, router, weights, unit):
    chunks, rows, depth = len(n2s), n2s[0].shape[0], n2s[0].shape[1]
    count, _, ff, part = weights.shape
    tokens = chunks * rows
    whole = lambda shape: pl.BlockSpec(shape, lambda s: (0,) * len(shape))
    return pl.pallas_call(
        functools.partial(units_body, chunks, unit),
        grid=(ff // BLOCK,),
        in_specs=[sspec()]
        + [whole((rows, depth))] * (2 * chunks)
        + [whole(sel.shape), whole(router.shape), pl.BlockSpec((count, 3, BLOCK, part), lambda s: (0, 0, s, 0))],
        out_specs=[pl.BlockSpec((tokens, BLOCK), lambda s: (0, s))] * 3 + [whole((tokens, 128)), whole((8, depth))],
        out_shape=[jax.ShapeDtypeStruct((tokens, ff), BF)] * 3
        + [jax.ShapeDtypeStruct((tokens, 128), F32), jax.ShapeDtypeStruct((8, depth), F32)],
        scratch_shapes=[
            pltpu.VMEM((tokens, depth), BF),
            pltpu.VMEM((tokens, depth), BF),
            pltpu.VMEM((EXPERTS, tokens, 128), F32),
            pltpu.VMEM((EXPERTS, tokens, 128), F32),
            pltpu.VMEM((tokens, 128), F32),
            pltpu.VMEM((tokens, 128), F32),
        ],
        compiler_params=params(("arbitrary",)),
        cost_estimate=cost(6 * tokens * depth * ff, 6 * depth * ff + 12 * tokens * depth),
        name="expert_units",
    )(place, *n2s, *gs, sel, router, weights)


def product_body(terms, chunks, extra, *refs):
    xs = refs[:terms]
    ws = refs[terms : 2 * terms]
    at = 2 * terms + (2 if extra else 0)
    outs = refs[at : at + chunks]
    total = None
    for x, w in zip(xs, ws):
        term = dot_nn(x[...], joined(w, 0))
        total = term if total is None else total + term
    if extra:
        lg_ref, rout_ref = refs[2 * terms : 2 * terms + 2]
        total = total + split_dot(lg_ref[...], rout_ref[...], dot_nn)
    rows = outs[0].shape[0]
    for c in range(chunks):
        outs[c][...] = total[rows * c : rows * (c + 1)].astype(BF)


def product_call(xs, picks, weights, chunks, extra, name):
    tokens, ff = xs[0].shape
    count, _, _, part = weights.shape
    depth = count * part
    rows = tokens // chunks
    per = max(1, BLOCK // part)
    wide = min(part * per, BLOCK)
    whole = lambda shape: pl.BlockSpec(shape, lambda s: (0,) * len(shape))
    place_at = (lambda i, s: (s, i, 0, 0)) if count > 1 else (lambda i, s: (0, i, 0, s))
    w_specs = [pl.BlockSpec((min(per, count), 1, ff, wide // min(per, count)), functools.partial(place_at, i)) for i in picks]
    return pl.pallas_call(
        functools.partial(product_body, len(xs), chunks, bool(extra)),
        grid=(depth // wide,),
        in_specs=[whole((tokens, ff))] * len(xs)
        + w_specs
        + ([whole(extra[0].shape), pl.BlockSpec((128, wide), lambda s: (0, s))] if extra else []),
        out_specs=[pl.BlockSpec((rows, wide), lambda s: (0, s))] * chunks,
        out_shape=[jax.ShapeDtypeStruct((rows, depth), BF)] * chunks,
        compiler_params=params(("arbitrary",)),
        cost_estimate=cost(2 * len(xs) * tokens * depth * ff, 4 * len(xs) * depth * ff),
        name=name,
    )(*xs, *([weights] * len(xs)), *extra)


def wgrad_body(count, chunks, *refs):
    hg_ref, gg_ref, ug_ref = refs[:3]
    n2s = refs[3 : 3 + chunks]
    gs = refs[3 + chunks : 3 + 2 * chunks]
    out_ref, n2_ref, g_ref = refs[3 + 2 * chunks :]
    part = out_ref.shape[3]
    rows = n2s[0].shape[0]

    @pl.when(pl.program_id(0) == 0)
    def _():
        for c in range(chunks):
            n2_ref[rows * c : rows * (c + 1), :] = n2s[c][...]
            g_ref[rows * c : rows * (c + 1), :] = gs[c][...]

    width = hg_ref.shape[1]
    pair = dot_tn(jnp.concatenate([gg_ref[...], ug_ref[...]], 1), n2_ref[...]).astype(BF)
    down = dot_tn(hg_ref[...], g_ref[...]).astype(BF)
    for which, total in enumerate((pair[:width], pair[width:], down)):
        for d in range(count):
            out_ref[d, which] = total[:, part * d : part * (d + 1)]


def wgrad_call(count, kept, n2s, gs):
    tokens, ff = kept[0].shape
    chunks, rows, depth = len(n2s), n2s[0].shape[0], n2s[0].shape[1]
    whole = lambda shape: pl.BlockSpec(shape, lambda s: (0,) * len(shape))
    return pl.pallas_call(
        functools.partial(wgrad_body, count, chunks),
        grid=(ff // BLOCK,),
        in_specs=[pl.BlockSpec((tokens, BLOCK), lambda s: (0, s))] * 3 + [whole((rows, depth))] * (2 * chunks),
        out_specs=pl.BlockSpec((count, 3, BLOCK, depth // count), lambda s: (0, 0, s, 0)),
        out_shape=jax.ShapeDtypeStruct((count, 3, ff, depth // count), BF),
        scratch_shapes=[pltpu.VMEM((tokens, depth), BF), pltpu.VMEM((tokens, depth), BF)],
        compiler_params=params(("arbitrary",)),
        cost_estimate=cost(6 * tokens * depth * ff, 12 * depth * ff),
        name="expert_weight_grads",
    )(*kept, *n2s, *gs)


def norm_back(grad, u, gain):
    scale = lax.rsqrt(jnp.mean(u * u, axis=1, keepdims=True) + EPSILON)
    m = grad * gain
    back = scale * m - u * (scale * scale * scale) * jnp.mean(u * m, axis=1, keepdims=True)
    return back, jnp.sum(grad * u * scale, axis=0, keepdims=True)


def resid_body(count, chunks, terms, index_ref, *refs):
    parts = refs[:terms]
    mid_ref, g_ref, gains_ref, low_ref, high_ref = refs[terms : terms + 5]
    rest = refs[terms + 5 :]
    resid_ref, aog_ref, gain_ref = rest[:3]
    dos = rest[3:]
    grad = functools.reduce(jnp.add, [p[...].astype(F32) for p in parts])
    back, gain_part = norm_back(grad, mid_ref[...], gains_ref[1:2, :])
    resid = g_ref[...].astype(F32) + back
    resid_ref[...] = resid
    low = resid.astype(BF)
    aog_ref[...] = low
    gain_ref[...] = jnp.broadcast_to(gain_part, gain_ref.shape)
    for c in range(chunks):
        dos[c][...] = dot_nt(low, join_lanes(low_ref, high_ref, index_ref, count, c)).astype(BF)


def resid_call(index, parts, mid, grad, gains, w_out):
    chunks, terms = w_out[0].shape[1], len(parts)
    shape = mid.shape
    width = 2 * w_out[0].shape[2]
    return pl.pallas_call(
        functools.partial(resid_body, w_out[0].shape[0], chunks, terms),
        in_specs=[sspec()] + [vspec()] * (terms + 5),
        out_specs=[vspec()] * (3 + chunks),
        out_shape=[
            jax.ShapeDtypeStruct(shape, F32),
            jax.ShapeDtypeStruct(shape, BF),
            jax.ShapeDtypeStruct((8, shape[1]), F32),
        ]
        + [jax.ShapeDtypeStruct((shape[0], width), BF)] * chunks,
        compiler_params=params(),
        cost_estimate=cost(2 * shape[0] * shape[1] ** 2, 4 * shape[1] ** 2),
        name="resid_grad",
    )(index, *parts, mid, grad, gains, *w_out)


def final_body(chunks, *refs):
    parts = refs[:chunks]
    tok_ref, resid_ref, gains_ref, out_ref = refs[chunks:]
    grad = functools.reduce(jnp.add, [p[...].astype(F32) for p in parts])
    back, _ = norm_back(grad, tok_ref[...].astype(F32), gains_ref[0:1, :])
    out_ref[...] = resid_ref[...] + back


def final_call(parts, tok, resid, gains):
    return pl.pallas_call(
        functools.partial(final_body, len(parts)),
        in_specs=[vspec()] * (len(parts) + 3),
        out_specs=vspec(),
        out_shape=jax.ShapeDtypeStruct(tok.shape, F32),
        compiler_params=params(),
        cost_estimate=cost(20 * tok.size, 12 * tok.size),
        name="in_grad",
    )(*parts, tok, resid, gains)


def proj_body(count, chunks, rows, index_ref, place_ref, dq_ref, dk_ref, dv_ref, first_ref, last_ref, two_ref, router_ref, *refs):
    toks = refs[:chunks]
    outs = refs[chunks : 2 * chunks]
    gain_ref = refs[2 * chunks]
    depth = outs[0].shape[1]
    width = dq_ref.shape[1]
    weights = join_rows(first_ref, last_ref, index_ref, count, depth // count)
    gain = jnp.zeros((1, depth), F32)
    for c in range(chunks):
        at = pl.ds(pl.multiple_of(place_ref[c] * rows, rows), rows)
        grad = dot_nt(dq_ref[at, :], weights[:, :width])
        grad = grad + dot_nt(dk_ref[at, :], weights[:, width : 2 * width])
        grad = grad + dot_nt(dv_ref[at, :], weights[:, 2 * width :])
        outs[c][...] = grad.astype(BF)
        x = toks[c][...].astype(F32)
        scale = lax.rsqrt(jnp.mean(x * x, axis=1, keepdims=True) + EPSILON)
        gain = gain + jnp.sum(grad * x * scale, axis=0, keepdims=True)
    blank = jnp.zeros((6 - EXPERTS, depth), F32)
    gain_ref[...] = jnp.concatenate([gain, two_ref[0:1, :], router_ref[0:EXPERTS, :], blank], 0)


def proj_call(index, place, dq, dk, dv, pack, gain_two, router_part, toks):
    chunks, rows, depth = len(toks), toks[0].shape[0], toks[0].shape[1]
    return pl.pallas_call(
        functools.partial(proj_body, pack[0].shape[0], chunks, rows),
        in_specs=[sspec(), sspec()] + [vspec()] * (7 + chunks),
        out_specs=[vspec()] * (chunks + 1),
        out_shape=[jax.ShapeDtypeStruct((rows, depth), BF)] * chunks + [jax.ShapeDtypeStruct((8, depth), F32)],
        compiler_params=params(),
        cost_estimate=cost(6 * chunks * rows * depth * dq.shape[1], 8 * chunks * rows * depth),
        name="projection_grads",
    )(index, place, dq, dk, dv, *pack, gain_two, router_part, *toks)


def attn_weights_body(count, smalls, slot_ref, n1_ref, dq_ref, dk_ref, dv_ref, table_ref, *refs):
    keep_ref, send_ref, small_ref, *grad_refs = refs[smalls:]
    small_ref[...] = functools.reduce(jnp.add, [r[...] for r in refs[:smalls]])
    depth = n1_ref.shape[1]
    width = dq_ref.shape[1]
    part = depth // count
    normed = n1_ref[...]
    pieces = width // 128
    for ref, grad_ref in zip((dq_ref, dk_ref, dv_ref), grad_refs):
        grad_ref[...] = dot_tn(normed, ref[...]).astype(BF)
    for out_ref, slot, d in parted(keep_ref, send_ref, slot_ref):
        rows = pl.ds(pl.multiple_of(d * part, 128), part)
        for m, grad_ref in enumerate(grad_refs):
            for piece in range(pieces):
                at = (m * pieces + piece) * part
                out_ref[slot, at : at + part, :] = grad_ref[rows, 128 * piece : 128 * (piece + 1)]
        at = 3 * pieces * part
        value = jnp.concatenate([small_ref[:, rows], table_ref[...]], 0).astype(BF)
        out_ref[slot, at : at + 16, :] = value


def attn_weights_call(slots, n1, dq, dk, dv, table, smalls, count):
    total, depth = n1.shape
    width = dq.shape[1]
    part = depth // count
    return pl.pallas_call(
        functools.partial(attn_weights_body, count, len(smalls)),
        in_specs=[sspec()] + [vspec()] * (5 + len(smalls)),
        out_specs=[vspec()] * 2,
        out_shape=[jax.ShapeDtypeStruct((count // 2, 3 * width * part // 128 + 16, 128), BF)] * 2,
        scratch_shapes=[pltpu.VMEM((8, depth), F32)] + [pltpu.VMEM((depth, width), BF)] * 3,
        compiler_params=params(),
        cost_estimate=cost(6 * total * depth * width, 8 * total * depth),
        name="attn_weight_grads",
    )(slots, n1, dq, dk, dv, table, *smalls)


def wo_grad_body(count, chunks, slot_ref, *refs):
    atts = refs[:chunks]
    aog_ref, keep_ref, send_ref, grad_ref = refs[chunks:]
    width = atts[0].shape[1]
    part = grad_ref.shape[1] // count
    for c in range(chunks):
        at = slice(c * width, (c + 1) * width)
        grad_ref[at, :] = dot_tn(atts[c][...], aog_ref[...]).astype(BF)
    for out_ref, slot, d in parted(keep_ref, send_ref, slot_ref):
        out_ref[slot] = grad_ref[:, pl.ds(pl.multiple_of(d * part, 128), part)]


def wo_grad_call(slots, atts, aog, count):
    chunks, width = len(atts), atts[0].shape[1]
    rows, depth = aog.shape
    return pl.pallas_call(
        functools.partial(wo_grad_body, count, chunks),
        in_specs=[sspec()] + [vspec()] * (chunks + 1),
        out_specs=[vspec()] * 2,
        out_shape=[jax.ShapeDtypeStruct((max(1, count // 2), chunks * width, depth // count), BF)] * 2,
        scratch_shapes=[pltpu.VMEM((chunks * width, depth), BF)],
        compiler_params=params(),
        cost_estimate=cost(2 * rows * depth * chunks * width, 4 * depth * chunks * width),
        name="w_output_grad",
    )(slots, *atts, aog)


def kept_choices(ids):
    lanes = jnp.arange(128, dtype=jnp.int32)[None, :]
    expert_range = jnp.arange(EXPERTS, dtype=jnp.int32)[None, :]
    first = (ids[:, 0:1] == expert_range).astype(jnp.int32)
    second = (ids[:, 1:2] == expert_range).astype(jnp.int32)
    runs = jnp.cumsum(jnp.concatenate([first, second], 1), axis=0)
    first_run = runs[:, :EXPERTS]
    second_run = runs[:, EXPERTS:] + first_run[-1][None, :]
    place_one = jnp.sum(first_run * first, axis=1, keepdims=True) - 1
    place_two = jnp.sum(second_run * second, axis=1, keepdims=True) - 1
    kept = ((ids[:, 0:1] == lanes) & (place_one < CAP)) | ((ids[:, 1:2] == lanes) & (place_two < CAP))
    return kept.astype(F32)


def on_device(
    tokens_in,
    out_grad,
    attn_gain,
    w_query,
    w_key,
    w_value,
    w_output,
    rel_table,
    moe_gain,
    w_router,
    w_gate,
    w_up,
    down_weight,
    expert_ids,
    piece_starts,
):
    rows, depth = tokens_in.shape
    width = w_query.shape[1]
    z_size = lax.axis_size("tensor")
    dp_size = lax.axis_size("dp")
    z_rank = lax.axis_index("tensor").astype(jnp.int32)
    dp_rank = lax.axis_index("dp").astype(jnp.int32)
    total = rows * z_size
    share = depth // dp_size
    unit = w_gate.shape[2]
    ff = EXPERTS * unit
    heads = rel_table.shape[0]
    direct = dp_size == 8 and share == 128
    place = z_rank ^ jnp.arange(z_size, dtype=jnp.int32)

    near = z_swap(tokens_in, 1, z_size)
    far = z_swap(tokens_in, 2, z_size)
    line_at = 2 * BLOCK - 1 - np.arange(total + 2 * BLOCK)
    line = jnp.dot(rel_table, jnp.asarray(onehot_of(line_at).T), precision=PRECISE)[:, None, :]
    sel = kept_choices(expert_ids)
    toks = [tokens_in, near, far, z_swap(after(far, near, sel, line), 1, z_size)]
    w_output_late = after(w_output, far)
    small = jnp.concatenate([attn_gain, moe_gain, w_router.T.reshape(-1)])[None, :]
    packed = jnp.concatenate([w_query, w_key, w_value], 1)
    wo_slots = jnp.stack(z_direct([w_output_late] * z_size, z_size))[None]
    ranks = dp_rank ^ jnp.arange(8, dtype=jnp.int32)
    half = wo_slots.shape[2] // 2
    if direct:
        index = dp_slots(ranks)
        slots = dp_rank ^ dp_scatter_slots(jnp.arange(8, dtype=jnp.int32))
        first = dp_step(packed[:80][None], 2)
        last = dp_step(jnp.concatenate([packed[80:], small, jnp.zeros((15, packed.shape[1]), BF)], 0)[None], 4)
        first, last = dp_step(after(first, near), 4), dp_step(after(last, near), 2)
        wo_low = dp_step(after(wo_slots[:, :, :half], near, far), 2)
        wo_high = dp_step(after(wo_slots[:, :, half:], near, far), 4)
        first = dp_step(after(first, toks[3], wo_low, wo_high), 1)
        last = dp_step(after(last, toks[3], wo_low, wo_high), 1)
        pack, small_all = [first, last], last
    else:
        slots = jnp.zeros((1,), jnp.int32)
        index = jnp.zeros((2,), jnp.int32)
        pack = lax.all_gather(packed, "dp", axis=0, tiled=True)[None]
        pack = [pack[:, : depth // 2], pack[:, depth // 2 :]]
        small_all = lax.all_gather(small[0], "dp", axis=0).reshape(dp_size, 2 + EXPERTS, share)
        small_all = jnp.swapaxes(small_all, 0, 1).reshape(2 + EXPERTS, depth)
        small_all = jnp.concatenate([small_all, jnp.zeros((2, depth), BF)], 0)
        wo_all = lax.all_gather(wo_slots[0], "dp", axis=2, tiled=True)[None]
        wo_all = [wo_all[:, :, :half], wo_all[:, :, half:]]

    local = jnp.stack(
        [
            jnp.swapaxes(w_gate, 1, 2).reshape(ff, share),
            jnp.swapaxes(w_up, 1, 2).reshape(ff, share),
            down_weight.reshape(ff, share),
        ]
    )
    if direct:
        experts_w = lax.all_gather(local, "dp", axis=0)
    else:
        experts_w = lax.all_gather(local, "dp", axis=2, tiled=True)[None]

    n1, q, k, v, kt, vt, gains, router = qkv_call(index, place, toks, pack, small_all, width)
    g_near = z_swap(after(out_grad, toks[3]), 1, z_size)
    g_far = z_swap(after(out_grad, toks[3]), 2, z_size)
    fwd = attn_fwd(piece_starts, place, z_size, q, k, vt, line)
    chances, ot = fwd[:2]
    atts = z_direct([after(fwd[2], g_near, g_far)] + [after(x, g_near, g_far) for x in fwd[3:]], z_size)
    if direct:
        wo_low, wo_high = dp_step(after(wo_low, n1), 4), dp_step(after(wo_high, n1), 2)
        wo_all = [dp_step(after(x, atts[1]), 1) for x in (wo_low, wo_high)]
    gs = [out_grad, g_near, g_far, z_swap(after(g_far, fwd[2]), 1, z_size)]
    mid, n2 = mid_call(index, [after(atts[0], gs[3])] + atts[1:], wo_all, tokens_in, gains)

    n2_near = z_swap(n2, 1, z_size)
    n2_far = z_swap(n2, 2, z_size)
    n2s = [n2, n2_near, n2_far, z_swap(after(n2_far, n2_near), 1, z_size)]
    hg, gg, ug, logit_grad, router_part = units_call(place, n2s, gs, sel, router, experts_w, unit)
    ngs = product_call([gg, ug], (0, 1), experts_w, z_size, [logit_grad, router], "normed_two_grads")
    passed = z_swap(ngs[3], 1, z_size)
    outs = product_call([after(hg, ngs[0])], (2,), experts_w, z_size, [], "expert_out")
    both = (ngs[2].astype(F32) + after(passed, outs[0]).astype(F32)).astype(BF)
    far = z_swap(both, 2, z_size)
    ng_near = z_swap(after(ngs[1], passed), 1, z_size)
    count = experts_w.shape[0]
    weight_grads = wgrad_call(experts_w.shape[0], [after(hg, both, *outs), gg, ug], n2s, gs)
    resid = resid_call(index, [after(ngs[0], weight_grads), ng_near, far], mid, out_grad, gains, wo_all)
    resid_grad, aog, gain_two = resid[:3]
    weight_grads = after(weight_grads, far, ng_near)
    if direct:
        expert_grads = lax.psum_scatter(weight_grads, "dp", scatter_dimension=0, tiled=False)
    else:
        expert_grads = lax.psum_scatter(weight_grads[0], "dp", scatter_dimension=2, tiled=True)
    out_passed = z_swap(after(outs[3], aog), 1, z_size)
    dos = z_direct(resid[3:], z_size)
    wo_keep, wo_send = wo_grad_call(slots, atts, aog, count)
    out_both = (outs[2].astype(F32) + out_passed.astype(F32)).astype(BF)
    dos[0] = after(dos[0], wo_keep, out_both)
    out_far = z_swap(out_both, 2, z_size)
    out_near = z_swap(after(outs[1], out_both), 1, z_size)
    if direct:
        wo_grads = dp_fold(wo_keep, after(wo_send, *dos), 1)
    dq, dk, dv, diag = attn_bwd(place, dos, chances, q, k, v, kt, ot)
    if direct:
        wo_grads = dp_fold(*halves(wo_grads), 2)
        dq = after(dq, wo_grads)
    dq = after(dq, out_far, out_near)
    proj = proj_call(index, place, dq, dk, dv, pack, gain_two, router_part, toks)

    diag_at = (
        BLOCK * np.arange(total // BLOCK + 1)[:, None] - (BLOCK * (total // BLOCK - 2) + 1) - np.arange(2 * BLOCK)[None, :]
    )
    table = jnp.einsum("hbt,btk->hk", diag, jnp.asarray(onehot_of(diag_at)), precision=PRECISE)
    n1_passed = z_swap(proj[3], 1, z_size)
    if direct:
        table_rows = jnp.pad(table.reshape(1, -1), ((0, 7), (0, 0)))
        smalls = z_direct([proj[z_size]] * z_size, z_size)
        wo_grads = dp_fold(*halves(wo_grads), 4)[0]
        attn_keep, attn_send = attn_weights_call(slots, n1, dq, dk, dv, after(table_rows, wo_grads), smalls, 8)
        n1_passed = after(n1_passed, attn_keep)
    n1_both = (proj[2].astype(F32) + n1_passed.astype(F32)).astype(BF)
    n1_far = z_swap(n1_both, 2, z_size)
    n1_near = z_swap(after(proj[1], n1_both), 1, z_size)
    in_grad = final_call([proj[0], n1_near, n1_far], tokens_in, resid_grad, gains)
    out_parts = [outs[0], out_near, out_far]
    out_rows = (mid + functools.reduce(jnp.add, [p.astype(F32) for p in out_parts])).astype(BF)

    if direct:
        attn_grads = dp_fold(attn_keep, after(attn_send, n1_both), 1)
        attn_grads = dp_fold(*halves(attn_grads), 2)
        attn_grads = dp_fold(*halves(after(attn_grads, n1_far, n1_near)), 4)
        attn_grads = attn_grads[0].astype(F32)
        per = width // 128
        cut = attn_grads[: 3 * per * share].reshape(3, per, share, 128)
        cut = jnp.swapaxes(cut, 1, 2).reshape(3, share, width)
        smalls = attn_grads[3 * per * share :]
        grad_table = smalls[8, : heads * BUCKETS].reshape(heads, BUCKETS)
        mine = z_rank
        grad_wo = after(wo_grads, n1_near)
    else:
        cut = jnp.stack([jnp.dot(n1.T, d, preferred_element_type=F32) for d in (dq, dk, dv)])
        cut = lax.psum_scatter(cut, "dp", scatter_dimension=1, tiled=True)
        smalls = lax.psum(proj[z_size], ("dp", "tensor"))
        grad_table = lax.psum(table, "dp")
        mine = dp_rank * z_size + z_rank
        grad_wo = lax.psum_scatter(wo_keep[0], "dp", scatter_dimension=1, tiled=True)
    wo_parts = z_direct([grad_wo[width * c : width * (c + 1)] for c in range(z_size)], z_size)
    grad_wo = functools.reduce(jnp.add, [p.astype(F32) for p in wo_parts])
    per_device = depth // (dp_size * z_size)
    own = lax.dynamic_slice_in_dim(smalls, mine * per_device, per_device, 1)

    wide = expert_grads.astype(F32).reshape(3, EXPERTS, unit, share)
    return (
        out_rows,
        in_grad,
        own[0],
        cut[0],
        cut[1],
        cut[2],
        grad_wo,
        grad_table,
        own[1],
        own[2 : 2 + EXPERTS].T,
        jnp.swapaxes(wide[0], 1, 2),
        jnp.swapaxes(wide[1], 1, 2),
        wide[2],
    )


def solution(mesh):
    rows = P(("dp", "tensor"), None)
    grid = P("dp", "tensor")
    flat = P(("dp", "tensor"))
    weights = (P(None, "dp", "tensor"), P(None, "dp", "tensor"), P(None, "tensor", "dp"))
    in_specs = (rows, rows, P("dp"), grid, grid, grid, P("tensor", "dp"), P("tensor", None), P("dp"), P("dp", None))
    out_specs = (rows, rows, flat, grid, grid, grid, P("tensor", "dp"), P("tensor", None), flat, rows)
    return jax.shard_map(
        on_device,
        mesh=mesh,
        in_specs=in_specs + weights + (P("dp", None), P("dp", None)),
        out_specs=out_specs + weights,
        check_vma=False,
    )
```

```python
import functools

import jax
import jax.numpy as jnp
import numpy as np
from jax import lax
from jax.experimental import pallas as pl
from jax.experimental.pallas import tpu as pltpu
from jax.sharding import PartitionSpec as P

EXPERTS = 4
PIECE = 256
CAP = 640
BUCKETS = 32
EPSILON = 1e-06
PRECISE = lax.Precision.HIGHEST
LIMITS = (12, 16, 23, 32, 46, 64, 91)
MASKED = -1e30
BF = jnp.bfloat16
F32 = jnp.float32
BLOCK = 256
VMEM_LIMIT = 56 * 1024 * 1024


def params(semantics=None):
    return pltpu.CompilerParams(dimension_semantics=semantics, vmem_limit_bytes=VMEM_LIMIT)


def dot_nn(a, b):
    return lax.dot_general(a, b, (((1,), (0,)), ((), ())), preferred_element_type=F32)


def dot_nt(a, b):
    return lax.dot_general(a, b, (((1,), (1,)), ((), ())), preferred_element_type=F32)


def dot_tn(a, b):
    return lax.dot_general(a, b, (((0,), (0,)), ((), ())), preferred_element_type=F32)


def bucket_of(offsets):
    distance = np.abs(offsets)
    far = np.full_like(distance, 8)
    for bound in LIMITS:
        far = far + (distance >= bound)
    return np.where(distance < 8, distance, far) + np.where(offsets > 0, 16, 0)


def onehot_of(offsets):
    return (bucket_of(offsets)[..., None] == np.arange(BUCKETS)).astype(np.float32)


def cost(flops, nbytes):
    return pl.CostEstimate(flops=int(flops), bytes_accessed=int(nbytes), transcendentals=0)


def vspec():
    return pl.BlockSpec(memory_space=pltpu.VMEM)


def sspec():
    return pl.BlockSpec(memory_space=pltpu.SMEM)


def z_swap(x, mask, size):
    return lax.ppermute(x, "tensor", [(i, i ^ mask) for i in range(size)])


def z_gather(x, size):
    near = z_swap(x, 1, size)
    far = z_swap(x, 2, size)
    return [x, near, far, z_swap(far, 1, size)]


def z_direct(parts, size):
    return [parts[0]] + [z_swap(parts[mask], mask, size) for mask in range(1, size)]


def z_reduce(parts, size):
    passed = z_swap(parts[3], 1, size)
    far = z_swap((parts[2].astype(F32) + passed.astype(F32)).astype(BF), 2, size)
    return [parts[0], z_swap(parts[1], 1, size), far]


def after(x, *others):
    return lax.optimization_barrier((x,) + others)[0]


def dp_slots(ranks):
    x, y, core = (ranks >> 1) & 1, (ranks >> 2) & 1, ranks & 1
    return jnp.concatenate([x | (y << 1) | (core << 2), y | (x << 1) | (core << 2)])


def dp_step(x, bit):
    other = lax.ppermute(x, "dp", [(i, i ^ bit) for i in range(8)])
    return jnp.concatenate([x, other], 0)


def dp_fold(keep, send, bit):
    other = lax.ppermute(send, "dp", [(i, i ^ bit) for i in range(8)])
    return (keep.astype(F32) + other.astype(F32)).astype(keep.dtype)


def halves(x):
    return x[: x.shape[0] // 2], x[x.shape[0] // 2 :]


def dp_scatter_slots(ranks):
    return ((ranks >> 2) & 1) | (((ranks >> 1) & 1) << 1) | ((ranks & 1) << 2)


def parted(keep_ref, send_ref, order_ref):
    half = keep_ref.shape[0]
    for j in range(2 * half if half > 1 else 1):
        yield (keep_ref if j < half else send_ref), j % half, order_ref[j]


def join_rows(first_ref, last_ref, index_ref, count, rows):
    split = first_ref.shape[1]
    pieces = []
    for c in range(count):
        pieces.append(first_ref[index_ref[c], :, :])
        pieces.append(last_ref[index_ref[count + c], 0 : rows - split, :])
    return jnp.concatenate(pieces, 0)


def qkv_body(count, chunks, rows, index_ref, place_ref, *refs):
    toks = refs[:chunks]
    first_ref, last_ref, small_ref = refs[chunks : chunks + 3]
    n1_ref, q_ref, k_ref, v_ref, kt_ref, vt_ref, gains_ref, router_ref = refs[chunks + 3 :]
    depth = n1_ref.shape[1] // count
    weights = join_rows(first_ref, last_ref, index_ref, count, depth)
    width = q_ref.shape[1]
    if count == 1:
        small = [small_ref[r : r + 1, :] for r in range(2 + EXPERTS)]
    else:
        row = depth - first_ref.shape[1]
        lines = [small_ref[index_ref[count + d], row : row + 1, :].astype(F32) for d in range(count)]
        small = [
            jnp.concatenate([x[:, depth * r : depth * (r + 1)] for x in lines], 1) for r in range(2 + EXPERTS)
        ]
    small = jnp.concatenate([x.astype(F32) for x in small] + [jnp.zeros((2, depth * count), F32)], 0)
    gains_ref[...] = small
    routers = jnp.concatenate([small[2:], jnp.zeros((10, depth * count), F32)], 0)
    router_ref[...] = jnp.zeros_like(router_ref)
    router_ref[0:16, :] = routers.astype(BF)
    gain = small[0:1, :]
    for c in range(chunks):
        at = pl.ds(pl.multiple_of(place_ref[c] * rows, rows), rows)
        x = toks[c][...].astype(F32)
        scale = lax.rsqrt(jnp.mean(x * x, axis=1, keepdims=True) + EPSILON)
        normed = (x * scale * gain).astype(BF)
        n1_ref[at, :] = normed
        out = dot_nn(normed, weights)
        q_ref[at, :] = (out[:, :width].astype(BF).astype(F32) * 0.125).astype(BF)
        key = out[:, width : 2 * width]
        value = out[:, 2 * width :]
        k_ref[at, :] = key.astype(BF)
        v_ref[at, :] = value.astype(BF)
        kt_ref[:, at] = jnp.transpose(key).astype(BF)
        vt_ref[:, at] = jnp.transpose(value).astype(BF)


def qkv_call(index, place, toks, pack, small, width):
    chunks, rows, depth = len(toks), toks[0].shape[0], toks[0].shape[1]
    total = chunks * rows
    shapes = [(total, depth)] + [(total, width)] * 3 + [(width, total)] * 2
    return pl.pallas_call(
        functools.partial(qkv_body, pack[0].shape[0], chunks, rows),
        in_specs=[sspec(), sspec()] + [vspec()] * (chunks + 3),
        out_specs=[vspec()] * 8,
        out_shape=[jax.ShapeDtypeStruct(s, BF) for s in shapes]
        + [jax.ShapeDtypeStruct((8, depth), F32), jax.ShapeDtypeStruct((128, depth), BF)],
        compiler_params=params(),
        cost_estimate=cost(2 * total * depth * 3 * width, 8 * total * depth),
        name="norm_qkv",
    )(index, place, *toks, *pack, small)


def extent_of(i, total):
    return min(BLOCK * (i + 2), total)


def fwd_body(total, chunks, starts_ref, place_ref, q_ref, k_ref, vt_ref, line_ref, p_ref, ot_ref, *refs):
    atts = refs[:chunks]
    strip_ref, mask_ref, all_ref = refs[chunks:]
    head = pl.program_id(0)
    heads = pl.num_programs(0)
    blocks = total // BLOCK
    width = q_ref.shape[1]
    dim = width // 4

    @pl.when(head == 0)
    def _():
        def label(pos):
            first = (pos >= starts_ref[0, 0]) & (pos < starts_ref[0, 0] + PIECE)
            second = (pos >= starts_ref[0, 1]) & (pos < starts_ref[0, 1] + PIECE)
            return first, second

        for i in range(blocks):
            for j in (i, i + 1):
                if j >= blocks:
                    continue
                kpos = lax.broadcasted_iota(jnp.int32, (BLOCK, BLOCK), 0) + BLOCK * j
                qpos = lax.broadcasted_iota(jnp.int32, (BLOCK, BLOCK), 1) + BLOCK * i
                k1, k2 = label(kpos)
                q1, q2 = label(qpos)
                seen = (kpos <= qpos) | (k1 & q1) | (k2 & q2)
                mask_ref[2 * i + j - i] = jnp.where(seen, 0.0, MASKED)

    for beta in range(blocks + 1):
        start = BLOCK * (blocks - beta)
        window = line_ref[0, 0:1, start : start + 2 * BLOCK]
        spread = jnp.broadcast_to(window, (BLOCK, 2 * BLOCK))
        rolled = pltpu.roll(spread, BLOCK + 1, 1, stride=1, stride_axis=0)
        strip_ref[BLOCK * beta : BLOCK * (beta + 1), :] = rolled[:, :BLOCK]

    lanes = lax.broadcasted_iota(jnp.int32, (2 * BLOCK, width), 1)
    own = (lanes >= head * dim) & (lanes < (head + 1) * dim)
    at_head = pl.ds(pl.multiple_of(head * dim, dim), dim)
    for pair in range(0, blocks, 2):
        both = slice(BLOCK * pair, BLOCK * (pair + 2))
        reach = extent_of(pair + 1, total)
        q_rows = q_ref[both, :]
        q_own = jnp.where(own, q_rows, jnp.zeros_like(q_rows))
        raw = dot_nt(k_ref[0:reach, :], q_own)
        for i in (pair, pair + 1):
            extent = extent_of(i, total)
            cols = slice(BLOCK * i, BLOCK * (i + 1))
            base = BLOCK * (blocks - 1 - i)
            scores = raw[0:extent, BLOCK * (i - pair) : BLOCK * (i - pair + 1)] + strip_ref[base : base + extent, :]
            parts = [scores[BLOCK * j : BLOCK * (j + 1)] for j in range(extent // BLOCK)]
            for j in (i, i + 1):
                if j < blocks:
                    parts[j] = parts[j] + mask_ref[2 * i + j - i]
            top = functools.reduce(jnp.maximum, parts)
            top = jnp.max(top, axis=0, keepdims=True)
            parts = [jnp.exp(part - top) for part in parts]
            total_sum = jnp.sum(functools.reduce(jnp.add, parts), axis=0, keepdims=True)
            inverse = 1.0 / total_sum
            p_ref[0, 0:extent, cols] = jnp.concatenate([(part * inverse).astype(BF) for part in parts], 0)
            if extent < total:
                p_ref[0, extent : extent + BLOCK, cols] = jnp.zeros((BLOCK, BLOCK), BF)
        ot_ref[at_head, both] = dot_nn(vt_ref[at_head, 0:reach], p_ref[0, 0:reach, both])

    @pl.when(head == heads - 1)
    def _():
        mixed = ot_ref[...]
        all_ref[...] = jnp.transpose(mixed).astype(BF)
        rows = total // chunks
        for c in range(chunks):
            at = pl.ds(pl.multiple_of(place_ref[c] * rows, rows), rows)
            atts[c][...] = all_ref[at, :]


def attn_fwd(starts, place, chunks, q, k, vt, line):
    total, width = q.shape
    heads = line.shape[0]
    blocks = total // BLOCK
    whole = lambda shape: pl.BlockSpec(shape, lambda h: (0,) * len(shape))
    return pl.pallas_call(
        functools.partial(fwd_body, total, chunks),
        grid=(heads,),
        in_specs=[
            sspec(),
            sspec(),
            whole((total, width)),
            whole((total, width)),
            whole((width, total)),
            pl.BlockSpec((1, 1, line.shape[2]), lambda h: (h, 0, 0)),
        ],
        out_specs=[
            pl.BlockSpec((1, total, total), lambda h: (h, 0, 0)),
            whole((width, total)),
        ]
        + [whole((total // chunks, width))] * chunks,
        out_shape=[
            jax.ShapeDtypeStruct((heads, total, total), BF),
            jax.ShapeDtypeStruct((width, total), F32),
        ]
        + [jax.ShapeDtypeStruct((total // chunks, width), BF)] * chunks,
        scratch_shapes=[
            pltpu.VMEM((BLOCK * (blocks + 1), BLOCK), F32),
            pltpu.VMEM((2 * blocks, BLOCK, BLOCK), F32),
            pltpu.VMEM((total, width), BF),
        ],
        compiler_params=params(("arbitrary",)),
        cost_estimate=cost(heads * 4 * total * total * width, 10 * total * total),
        name="attn_forward",
    )(starts, place, q, k, vt, line)


def diagonal_sums(acc):
    half = BLOCK // 2
    low, high = acc[:half], acc[half:]
    rows = jnp.concatenate(
        [high[:, :half], high[:, half:] + low[:, :half], low[:, half:], jnp.zeros((half, half), F32)], 1
    )
    step = half // 2
    while step >= 8:
        rows = rows[step:] + pltpu.roll(rows[:step], step, 1)
        step //= 2
    index = lax.broadcasted_iota(jnp.int32, rows.shape, 0)
    for step in (4, 2, 1):
        rows = jnp.where((index & step) == 0, pltpu.roll(rows, step, 1), rows)
    return jnp.sum(rows, axis=0, keepdims=True)


def bwd_body(total, chunks, place_ref, *refs):
    grads = refs[:chunks]
    p_ref, q_ref, k_ref, v_ref, kt_ref, ot_ref = refs[chunks : chunks + 6]
    dq_ref, dk_ref, dv_ref, diag_ref = refs[chunks + 6 : chunks + 10]
    do_ref, dot_ref, dqt_ref, dka_ref, dva_ref, ds_ref, acc_ref = refs[chunks + 10 :]
    head = pl.program_id(0)
    heads = pl.num_programs(0)
    blocks = total // BLOCK
    rows = total // chunks
    width = q_ref.shape[1]
    dim = width // 4

    @pl.when(head == 0)
    def _():
        for c in range(chunks):
            at = pl.ds(pl.multiple_of(place_ref[c] * rows, rows), rows)
            do_ref[at, :] = grads[c][...]
        dot_ref[...] = jnp.transpose(do_ref[...].astype(F32))
        ds_ref[...] = jnp.zeros_like(ds_ref)
        dka_ref[...] = jnp.zeros_like(dka_ref)
        dva_ref[...] = jnp.zeros_like(dva_ref)

    at_head = pl.ds(pl.multiple_of(head * dim, dim), dim)
    inner = jnp.sum(dot_ref[at_head, :] * ot_ref[at_head, :], axis=0, keepdims=True)
    lanes = lax.broadcasted_iota(jnp.int32, (total, width), 1)
    own = (lanes >= head * dim) & (lanes < (head + 1) * dim)
    q_own = jnp.where(own, q_ref[...], jnp.zeros_like(q_ref))
    do_own = jnp.where(own, do_ref[...], jnp.zeros_like(do_ref))
    written = 0
    for pair in range(blocks - 2, -1, -2):
        both = slice(BLOCK * pair, BLOCK * (pair + 2))
        reach = extent_of(pair + 1, total)
        pair_grad = dot_nt(v_ref[0:reach, :], do_own[both, :])
        for i in (pair + 1, pair):
            extent = extent_of(i, total)
            cols = slice(BLOCK * i, BLOCK * (i + 1))
            chance_grad = pair_grad[0:extent, BLOCK * (i - pair) : BLOCK * (i - pair + 1)]
            chances = p_ref[0, 0:extent, cols].astype(F32)
            score_grad = (chances * (chance_grad - inner[:, cols])).astype(BF)
            ds_ref[0:extent, cols] = score_grad
            base = BLOCK * (blocks - 1 - i)
            wide = score_grad.astype(F32)
            if i == blocks - 1:
                acc_ref[0:extent, :] = wide
                written = extent
            else:
                old = written - base
                acc_ref[base:written, :] += wide[:old]
                if base + extent > written:
                    acc_ref[written : base + extent, :] = wide[old:]
                    written = base + extent
        dqt_ref[at_head, both] = dot_nn(kt_ref[at_head, 0:reach], ds_ref[0:reach, both])
    for pair in range(0, blocks, 2):
        first = max(0, BLOCK * (pair - 1))
        keys = slice(BLOCK * pair, BLOCK * (pair + 2))
        dka_ref[keys, :] += dot_nn(ds_ref[keys, first:], q_own[first:, :])
        dva_ref[keys, :] += dot_nn(p_ref[0, keys, first:], do_own[first:, :])
    for beta in range(blocks + 1):
        diag_ref[0, beta : beta + 1, :] = diagonal_sums(acc_ref[BLOCK * beta : BLOCK * (beta + 1), :])

    @pl.when(head == heads - 1)
    def _():
        dq_ref[...] = (jnp.transpose(dqt_ref[...]) * 0.125).astype(BF)
        dk_ref[...] = dka_ref[...].astype(BF)
        dv_ref[...] = dva_ref[...].astype(BF)


def attn_bwd(place, grads, chances, q, k, v, kt, ot):
    total, width = q.shape
    heads = chances.shape[0]
    blocks = total // BLOCK
    chunks = len(grads)
    whole = lambda shape: pl.BlockSpec(shape, lambda h: (0,) * len(shape))
    return pl.pallas_call(
        functools.partial(bwd_body, total, chunks),
        grid=(heads,),
        in_specs=[sspec()]
        + [whole(grads[0].shape)] * chunks
        + [pl.BlockSpec((1, total, total), lambda h: (h, 0, 0))]
        + [whole((total, width))] * 3
        + [whole((width, total))] * 2,
        out_specs=[whole((total, width))] * 3 + [pl.BlockSpec((1, blocks + 1, 2 * BLOCK), lambda h: (h, 0, 0))],
        out_shape=[jax.ShapeDtypeStruct((total, width), BF)] * 3
        + [jax.ShapeDtypeStruct((heads, blocks + 1, 2 * BLOCK), F32)],
        scratch_shapes=[
            pltpu.VMEM((total, width), BF),
            pltpu.VMEM((width, total), F32),
            pltpu.VMEM((width, total), F32),
            pltpu.VMEM((total, width), F32),
            pltpu.VMEM((total, width), F32),
            pltpu.VMEM((total, total), BF),
            pltpu.VMEM((BLOCK * (blocks + 1), BLOCK), F32),
        ],
        compiler_params=params(("arbitrary",)),
        cost_estimate=cost(heads * 160 * total * total * width, 10 * total * total),
        name="attn_backward",
    )(place, *grads, chances, q, k, v, kt, ot)


def join_lanes(low_ref, high_ref, index_ref, count, slot):
    low = [low_ref[index_ref[c], slot] for c in range(count)]
    high = [high_ref[index_ref[count + c], slot] for c in range(count)]
    return jnp.concatenate([jnp.concatenate(low, 1), jnp.concatenate(high, 1)], 0)


def mid_body(count, chunks, index_ref, *refs):
    atts = refs[:chunks]
    low_ref, high_ref, tok_ref, gain_ref, mid_ref, n2_ref = refs[chunks:]
    u = tok_ref[...].astype(F32)
    for c in range(chunks):
        u = u + dot_nn(atts[c][...], join_lanes(low_ref, high_ref, index_ref, count, c))
    mid_ref[...] = u
    scale = lax.rsqrt(jnp.mean(u * u, axis=1, keepdims=True) + EPSILON)
    n2_ref[...] = (u * scale * gain_ref[1:2, :]).astype(BF)


def mid_call(index, atts, w_out, tok, gains):
    chunks = len(atts)
    return pl.pallas_call(
        functools.partial(mid_body, w_out[0].shape[0], chunks),
        in_specs=[sspec()] + [vspec()] * (chunks + 4),
        out_specs=[vspec()] * 2,
        out_shape=[jax.ShapeDtypeStruct(tok.shape, F32), jax.ShapeDtypeStruct(tok.shape, BF)],
        compiler_params=params(),
        cost_estimate=cost(2 * tok.shape[0] * tok.shape[1] ** 2, 4 * tok.shape[1] ** 2),
        name="out_projection_norm",
    )(index, *atts, *w_out, tok, gains)


def split_dot(a, b, dot):
    high = a.astype(BF)
    low = (a - high.astype(F32)).astype(BF)
    return dot(high, b) + dot(low, b)


def joined(ref, which):
    if ref.shape[0] == 1:
        return ref[0, which]
    return jnp.concatenate([ref[d, which] for d in range(ref.shape[0])], 1)


def units_body(chunks, unit, place_ref, *refs):
    n2s = refs[:chunks]
    gs = refs[chunks : 2 * chunks]
    sel_ref, rout_ref, w_ref = refs[2 * chunks : 2 * chunks + 3]
    hg_ref, gg_ref, ug_ref, lg_ref, rpart_ref = refs[2 * chunks + 3 : 2 * chunks + 8]
    n2_ref, g_ref, gate_ref, sum_ref, prob_ref, pick_ref = refs[2 * chunks + 8 :]
    step = pl.program_id(0)
    steps = pl.num_programs(0)
    rows = n2s[0].shape[0]
    tokens = chunks * rows
    lane = lax.broadcasted_iota(jnp.int32, (tokens, 128), 1)

    @pl.when(step == 0)
    def _():
        for c in range(chunks):
            n2_ref[rows * c : rows * (c + 1), :] = n2s[c][...]
            g_ref[rows * c : rows * (c + 1), :] = gs[c][...]
        logits = dot_nt(n2_ref[...], rout_ref[...])
        logits = jnp.where(lane < EXPERTS, logits, MASKED)
        raised = jnp.exp(logits - jnp.max(logits, axis=1, keepdims=True))
        prob_ref[...] = raised / jnp.sum(raised, axis=1, keepdims=True)
        for c in range(chunks):
            at = pl.ds(pl.multiple_of(place_ref[c] * rows, rows), rows)
            pick_ref[rows * c : rows * (c + 1), :] = sel_ref[at, :]
        gates = prob_ref[...] * pick_ref[...]
        for e in range(EXPERTS):
            one = jnp.sum(jnp.where(lane == e, gates, 0.0), axis=1, keepdims=True)
            gate_ref[e] = jnp.broadcast_to(one, (tokens, 128))
        sum_ref[...] = jnp.zeros_like(sum_ref)

    wg, wu, wd = joined(w_ref, 0), joined(w_ref, 1), joined(w_ref, 2)
    pre = dot_nt(n2_ref[...], jnp.concatenate([wg, wu], 0))
    gate_pre, up_pre = pre[:, : wg.shape[0]], pre[:, wg.shape[0] :]
    raw = dot_nt(g_ref[...], wd)
    c0 = float(np.sqrt(2.0 / np.pi))
    square = gate_pre * gate_pre
    th = jnp.tanh(gate_pre * (c0 + (c0 * 0.044715) * square))
    half = 0.5 + 0.5 * th
    act = gate_pre * half
    slope = half + gate_pre * (0.5 * c0 + (1.5 * c0 * 0.044715) * square) * (1.0 - th * th)
    hidden = act * up_pre
    prod = raw * hidden
    width = hg_ref.shape[1]
    e_low = (step * width) // unit
    e_high = (step * width + width - 1) // unit
    bound = jnp.where(e_high > e_low, unit * e_high - step * width, width)
    lows, highs = [], []
    for m in range(width // 128):
        is_low = lane + 128 * m < bound
        part = slice(128 * m, 128 * (m + 1))
        gate = jnp.where(is_low, gate_ref[e_low], gate_ref[e_high])
        lows.append(jnp.where(is_low, prod[:, part], 0.0))
        highs.append(prod[:, part] - lows[m])
        hg_ref[:, part] = (gate * hidden[:, part]).astype(BF)
        hidden_grad = gate * raw[:, part]
        gg_ref[:, part] = (hidden_grad * up_pre[:, part] * slope[:, part]).astype(BF)
        ug_ref[:, part] = (hidden_grad * act[:, part]).astype(BF)
    sum_ref[e_low] += functools.reduce(jnp.add, lows)

    @pl.when(e_high > e_low)
    def _():
        sum_ref[e_high] += functools.reduce(jnp.add, highs)

    @pl.when(step == steps - 1)
    def _():
        grad = jnp.zeros((tokens, 128), F32)
        for e in range(EXPERTS):
            grad = grad + jnp.where(lane == e, jnp.sum(sum_ref[e], axis=1, keepdims=True), 0.0)
        grad = grad * pick_ref[...]
        probs = prob_ref[...]
        logit_grad = probs * (grad - jnp.sum(probs * grad, axis=1, keepdims=True))
        lg_ref[...] = logit_grad
        rpart_ref[...] = split_dot(logit_grad, n2_ref[...], dot_tn)[0:8, :]


def units_call(place, n2s, gs, sel, router, weights, unit):
    chunks, rows, depth = len(n2s), n2s[0].shape[0], n2s[0].shape[1]
    count, _, ff, part = weights.shape
    tokens = chunks * rows
    whole = lambda shape: pl.BlockSpec(shape, lambda s: (0,) * len(shape))
    return pl.pallas_call(
        functools.partial(units_body, chunks, unit),
        grid=(ff // BLOCK,),
        in_specs=[sspec()]
        + [whole((rows, depth))] * (2 * chunks)
        + [whole(sel.shape), whole(router.shape), pl.BlockSpec((count, 3, BLOCK, part), lambda s: (0, 0, s, 0))],
        out_specs=[pl.BlockSpec((tokens, BLOCK), lambda s: (0, s))] * 3 + [whole((tokens, 128)), whole((8, depth))],
        out_shape=[jax.ShapeDtypeStruct((tokens, ff), BF)] * 3
        + [jax.ShapeDtypeStruct((tokens, 128), F32), jax.ShapeDtypeStruct((8, depth), F32)],
        scratch_shapes=[
            pltpu.VMEM((tokens, depth), BF),
            pltpu.VMEM((tokens, depth), BF),
            pltpu.VMEM((EXPERTS, tokens, 128), F32),
            pltpu.VMEM((EXPERTS, tokens, 128), F32),
            pltpu.VMEM((tokens, 128), F32),
            pltpu.VMEM((tokens, 128), F32),
        ],
        compiler_params=params(("arbitrary",)),
        cost_estimate=cost(6 * tokens * depth * ff, 6 * depth * ff + 12 * tokens * depth),
        name="expert_units",
    )(place, *n2s, *gs, sel, router, weights)


def product_body(terms, chunks, extra, *refs):
    xs = refs[:terms]
    ws = refs[terms : 2 * terms]
    at = 2 * terms + (2 if extra else 0)
    outs = refs[at : at + chunks]
    total = None
    for x, w in zip(xs, ws):
        term = dot_nn(x[...], joined(w, 0))
        total = term if total is None else total + term
    if extra:
        lg_ref, rout_ref = refs[2 * terms : 2 * terms + 2]
        total = total + split_dot(lg_ref[...], rout_ref[...], dot_nn)
    rows = outs[0].shape[0]
    for c in range(chunks):
        outs[c][...] = total[rows * c : rows * (c + 1)].astype(BF)


def product_call(xs, picks, weights, chunks, extra, name):
    tokens, ff = xs[0].shape
    count, _, _, part = weights.shape
    depth = count * part
    rows = tokens // chunks
    per = max(1, BLOCK // part)
    wide = min(part * per, BLOCK)
    whole = lambda shape: pl.BlockSpec(shape, lambda s: (0,) * len(shape))
    place_at = (lambda i, s: (s, i, 0, 0)) if count > 1 else (lambda i, s: (0, i, 0, s))
    w_specs = [pl.BlockSpec((min(per, count), 1, ff, wide // min(per, count)), functools.partial(place_at, i)) for i in picks]
    return pl.pallas_call(
        functools.partial(product_body, len(xs), chunks, bool(extra)),
        grid=(depth // wide,),
        in_specs=[whole((tokens, ff))] * len(xs)
        + w_specs
        + ([whole(extra[0].shape), pl.BlockSpec((128, wide), lambda s: (0, s))] if extra else []),
        out_specs=[pl.BlockSpec((rows, wide), lambda s: (0, s))] * chunks,
        out_shape=[jax.ShapeDtypeStruct((rows, depth), BF)] * chunks,
        compiler_params=params(("arbitrary",)),
        cost_estimate=cost(2 * len(xs) * tokens * depth * ff, 4 * len(xs) * depth * ff),
        name=name,
    )(*xs, *([weights] * len(xs)), *extra)


def wgrad_body(count, chunks, *refs):
    hg_ref, gg_ref, ug_ref = refs[:3]
    n2s = refs[3 : 3 + chunks]
    gs = refs[3 + chunks : 3 + 2 * chunks]
    out_ref, n2_ref, g_ref = refs[3 + 2 * chunks :]
    part = out_ref.shape[3]
    rows = n2s[0].shape[0]

    @pl.when(pl.program_id(0) == 0)
    def _():
        for c in range(chunks):
            n2_ref[rows * c : rows * (c + 1), :] = n2s[c][...]
            g_ref[rows * c : rows * (c + 1), :] = gs[c][...]

    width = hg_ref.shape[1]
    pair = dot_tn(jnp.concatenate([gg_ref[...], ug_ref[...]], 1), n2_ref[...]).astype(BF)
    down = dot_tn(hg_ref[...], g_ref[...]).astype(BF)
    for which, total in enumerate((pair[:width], pair[width:], down)):
        for d in range(count):
            out_ref[d, which] = total[:, part * d : part * (d + 1)]


def wgrad_call(count, kept, n2s, gs):
    tokens, ff = kept[0].shape
    chunks, rows, depth = len(n2s), n2s[0].shape[0], n2s[0].shape[1]
    whole = lambda shape: pl.BlockSpec(shape, lambda s: (0,) * len(shape))
    return pl.pallas_call(
        functools.partial(wgrad_body, count, chunks),
        grid=(ff // BLOCK,),
        in_specs=[pl.BlockSpec((tokens, BLOCK), lambda s: (0, s))] * 3 + [whole((rows, depth))] * (2 * chunks),
        out_specs=pl.BlockSpec((count, 3, BLOCK, depth // count), lambda s: (0, 0, s, 0)),
        out_shape=jax.ShapeDtypeStruct((count, 3, ff, depth // count), BF),
        scratch_shapes=[pltpu.VMEM((tokens, depth), BF), pltpu.VMEM((tokens, depth), BF)],
        compiler_params=params(("arbitrary",)),
        cost_estimate=cost(6 * tokens * depth * ff, 12 * depth * ff),
        name="expert_weight_grads",
    )(*kept, *n2s, *gs)


def norm_back(grad, u, gain):
    scale = lax.rsqrt(jnp.mean(u * u, axis=1, keepdims=True) + EPSILON)
    m = grad * gain
    back = scale * m - u * (scale * scale * scale) * jnp.mean(u * m, axis=1, keepdims=True)
    return back, jnp.sum(grad * u * scale, axis=0, keepdims=True)


def resid_body(count, chunks, terms, index_ref, *refs):
    parts = refs[:terms]
    mid_ref, g_ref, gains_ref, low_ref, high_ref = refs[terms : terms + 5]
    rest = refs[terms + 5 :]
    resid_ref, aog_ref, gain_ref = rest[:3]
    dos = rest[3:]
    grad = functools.reduce(jnp.add, [p[...].astype(F32) for p in parts])
    back, gain_part = norm_back(grad, mid_ref[...], gains_ref[1:2, :])
    resid = g_ref[...].astype(F32) + back
    resid_ref[...] = resid
    low = resid.astype(BF)
    aog_ref[...] = low
    gain_ref[...] = jnp.broadcast_to(gain_part, gain_ref.shape)
    for c in range(chunks):
        dos[c][...] = dot_nt(low, join_lanes(low_ref, high_ref, index_ref, count, c)).astype(BF)


def resid_call(index, parts, mid, grad, gains, w_out):
    chunks, terms = w_out[0].shape[1], len(parts)
    shape = mid.shape
    width = 2 * w_out[0].shape[2]
    return pl.pallas_call(
        functools.partial(resid_body, w_out[0].shape[0], chunks, terms),
        in_specs=[sspec()] + [vspec()] * (terms + 5),
        out_specs=[vspec()] * (3 + chunks),
        out_shape=[
            jax.ShapeDtypeStruct(shape, F32),
            jax.ShapeDtypeStruct(shape, BF),
            jax.ShapeDtypeStruct((8, shape[1]), F32),
        ]
        + [jax.ShapeDtypeStruct((shape[0], width), BF)] * chunks,
        compiler_params=params(),
        cost_estimate=cost(2 * shape[0] * shape[1] ** 2, 4 * shape[1] ** 2),
        name="resid_grad",
    )(index, *parts, mid, grad, gains, *w_out)


def final_body(chunks, *refs):
    parts = refs[:chunks]
    tok_ref, resid_ref, gains_ref, out_ref = refs[chunks:]
    grad = functools.reduce(jnp.add, [p[...].astype(F32) for p in parts])
    back, _ = norm_back(grad, tok_ref[...].astype(F32), gains_ref[0:1, :])
    out_ref[...] = resid_ref[...] + back


def final_call(parts, tok, resid, gains):
    return pl.pallas_call(
        functools.partial(final_body, len(parts)),
        in_specs=[vspec()] * (len(parts) + 3),
        out_specs=vspec(),
        out_shape=jax.ShapeDtypeStruct(tok.shape, F32),
        compiler_params=params(),
        cost_estimate=cost(20 * tok.size, 12 * tok.size),
        name="in_grad",
    )(*parts, tok, resid, gains)


def proj_body(count, chunks, rows, index_ref, place_ref, dq_ref, dk_ref, dv_ref, first_ref, last_ref, two_ref, router_ref, *refs):
    toks = refs[:chunks]
    outs = refs[chunks : 2 * chunks]
    gain_ref = refs[2 * chunks]
    depth = outs[0].shape[1]
    width = dq_ref.shape[1]
    weights = join_rows(first_ref, last_ref, index_ref, count, depth // count)
    gain = jnp.zeros((1, depth), F32)
    for c in range(chunks):
        at = pl.ds(pl.multiple_of(place_ref[c] * rows, rows), rows)
        grad = dot_nt(dq_ref[at, :], weights[:, :width])
        grad = grad + dot_nt(dk_ref[at, :], weights[:, width : 2 * width])
        grad = grad + dot_nt(dv_ref[at, :], weights[:, 2 * width :])
        outs[c][...] = grad.astype(BF)
        x = toks[c][...].astype(F32)
        scale = lax.rsqrt(jnp.mean(x * x, axis=1, keepdims=True) + EPSILON)
        gain = gain + jnp.sum(grad * x * scale, axis=0, keepdims=True)
    blank = jnp.zeros((6 - EXPERTS, depth), F32)
    gain_ref[...] = jnp.concatenate([gain, two_ref[0:1, :], router_ref[0:EXPERTS, :], blank], 0)


def proj_call(index, place, dq, dk, dv, pack, gain_two, router_part, toks):
    chunks, rows, depth = len(toks), toks[0].shape[0], toks[0].shape[1]
    return pl.pallas_call(
        functools.partial(proj_body, pack[0].shape[0], chunks, rows),
        in_specs=[sspec(), sspec()] + [vspec()] * (7 + chunks),
        out_specs=[vspec()] * (chunks + 1),
        out_shape=[jax.ShapeDtypeStruct((rows, depth), BF)] * chunks + [jax.ShapeDtypeStruct((8, depth), F32)],
        compiler_params=params(),
        cost_estimate=cost(6 * chunks * rows * depth * dq.shape[1], 8 * chunks * rows * depth),
        name="projection_grads",
    )(index, place, dq, dk, dv, *pack, gain_two, router_part, *toks)


def attn_weights_body(count, smalls, slot_ref, n1_ref, dq_ref, dk_ref, dv_ref, table_ref, *refs):
    keep_ref, send_ref, small_ref, *grad_refs = refs[smalls:]
    small_ref[...] = functools.reduce(jnp.add, [r[...] for r in refs[:smalls]])
    depth = n1_ref.shape[1]
    width = dq_ref.shape[1]
    part = depth // count
    normed = n1_ref[...]
    pieces = width // 128
    for ref, grad_ref in zip((dq_ref, dk_ref, dv_ref), grad_refs):
        grad_ref[...] = dot_tn(normed, ref[...]).astype(BF)
    for out_ref, slot, d in parted(keep_ref, send_ref, slot_ref):
        rows = pl.ds(pl.multiple_of(d * part, 128), part)
        for m, grad_ref in enumerate(grad_refs):
            for piece in range(pieces):
                at = (m * pieces + piece) * part
                out_ref[slot, at : at + part, :] = grad_ref[rows, 128 * piece : 128 * (piece + 1)]
        at = 3 * pieces * part
        value = jnp.concatenate([small_ref[:, rows], table_ref[...]], 0).astype(BF)
        out_ref[slot, at : at + 16, :] = value


def attn_weights_call(slots, n1, dq, dk, dv, table, smalls, count):
    total, depth = n1.shape
    width = dq.shape[1]
    part = depth // count
    return pl.pallas_call(
        functools.partial(attn_weights_body, count, len(smalls)),
        in_specs=[sspec()] + [vspec()] * (5 + len(smalls)),
        out_specs=[vspec()] * 2,
        out_shape=[jax.ShapeDtypeStruct((count // 2, 3 * width * part // 128 + 16, 128), BF)] * 2,
        scratch_shapes=[pltpu.VMEM((8, depth), F32)] + [pltpu.VMEM((depth, width), BF)] * 3,
        compiler_params=params(),
        cost_estimate=cost(6 * total * depth * width, 8 * total * depth),
        name="attn_weight_grads",
    )(slots, n1, dq, dk, dv, table, *smalls)


def wo_grad_body(count, chunks, slot_ref, *refs):
    atts = refs[:chunks]
    aog_ref, keep_ref, send_ref, grad_ref = refs[chunks:]
    width = atts[0].shape[1]
    part = grad_ref.shape[1] // count
    for c in range(chunks):
        at = slice(c * width, (c + 1) * width)
        grad_ref[at, :] = dot_tn(atts[c][...], aog_ref[...]).astype(BF)
    for out_ref, slot, d in parted(keep_ref, send_ref, slot_ref):
        out_ref[slot] = grad_ref[:, pl.ds(pl.multiple_of(d * part, 128), part)]


def wo_grad_call(slots, atts, aog, count):
    chunks, width = len(atts), atts[0].shape[1]
    rows, depth = aog.shape
    return pl.pallas_call(
        functools.partial(wo_grad_body, count, chunks),
        in_specs=[sspec()] + [vspec()] * (chunks + 1),
        out_specs=[vspec()] * 2,
        out_shape=[jax.ShapeDtypeStruct((max(1, count // 2), chunks * width, depth // count), BF)] * 2,
        scratch_shapes=[pltpu.VMEM((chunks * width, depth), BF)],
        compiler_params=params(),
        cost_estimate=cost(2 * rows * depth * chunks * width, 4 * depth * chunks * width),
        name="w_output_grad",
    )(slots, *atts, aog)


def kept_choices(ids):
    lanes = jnp.arange(128, dtype=jnp.int32)[None, :]
    expert_range = jnp.arange(EXPERTS, dtype=jnp.int32)[None, :]
    first = (ids[:, 0:1] == expert_range).astype(jnp.int32)
    second = (ids[:, 1:2] == expert_range).astype(jnp.int32)
    runs = jnp.cumsum(jnp.concatenate([first, second], 1), axis=0)
    first_run = runs[:, :EXPERTS]
    second_run = runs[:, EXPERTS:] + first_run[-1][None, :]
    place_one = jnp.sum(first_run * first, axis=1, keepdims=True) - 1
    place_two = jnp.sum(second_run * second, axis=1, keepdims=True) - 1
    kept = ((ids[:, 0:1] == lanes) & (place_one < CAP)) | ((ids[:, 1:2] == lanes) & (place_two < CAP))
    return kept.astype(F32)


def on_device(
    tokens_in,
    out_grad,
    attn_gain,
    w_query,
    w_key,
    w_value,
    w_output,
    rel_table,
    moe_gain,
    w_router,
    w_gate,
    w_up,
    down_weight,
    expert_ids,
    piece_starts,
):
    rows, depth = tokens_in.shape
    width = w_query.shape[1]
    z_size = lax.axis_size("tensor")
    dp_size = lax.axis_size("dp")
    z_rank = lax.axis_index("tensor").astype(jnp.int32)
    dp_rank = lax.axis_index("dp").astype(jnp.int32)
    total = rows * z_size
    share = depth // dp_size
    unit = w_gate.shape[2]
    ff = EXPERTS * unit
    heads = rel_table.shape[0]
    direct = dp_size == 8 and share == 128
    place = z_rank ^ jnp.arange(z_size, dtype=jnp.int32)

    near = z_swap(tokens_in, 1, z_size)
    far = z_swap(tokens_in, 2, z_size)
    line_at = 2 * BLOCK - 1 - np.arange(total + 2 * BLOCK)
    line = jnp.dot(rel_table, jnp.asarray(onehot_of(line_at).T), precision=PRECISE)[:, None, :]
    sel = kept_choices(expert_ids)
    toks = [tokens_in, near, far, z_swap(after(far, near, sel, line), 1, z_size)]
    w_output_late = after(w_output, far)
    small = jnp.concatenate([attn_gain, moe_gain, w_router.T.reshape(-1)])[None, :]
    packed = jnp.concatenate([w_query, w_key, w_value], 1)
    wo_slots = jnp.stack(z_direct([w_output_late] * z_size, z_size))[None]
    ranks = dp_rank ^ jnp.arange(8, dtype=jnp.int32)
    half = wo_slots.shape[2] // 2
    if direct:
        index = dp_slots(ranks)
        slots = dp_rank ^ dp_scatter_slots(jnp.arange(8, dtype=jnp.int32))
        first = dp_step(packed[:80][None], 2)
        last = dp_step(jnp.concatenate([packed[80:], small, jnp.zeros((15, packed.shape[1]), BF)], 0)[None], 4)
        first, last = dp_step(after(first, near), 4), dp_step(after(last, near), 2)
        wo_low = dp_step(after(wo_slots[:, :, :half], near, far), 2)
        wo_high = dp_step(after(wo_slots[:, :, half:], near, far), 4)
        first = dp_step(after(first, toks[3], wo_low, wo_high), 1)
        last = dp_step(after(last, toks[3], wo_low, wo_high), 1)
        pack, small_all = [first, last], last
    else:
        slots = jnp.zeros((1,), jnp.int32)
        index = jnp.zeros((2,), jnp.int32)
        pack = lax.all_gather(packed, "dp", axis=0, tiled=True)[None]
        pack = [pack[:, : depth // 2], pack[:, depth // 2 :]]
        small_all = lax.all_gather(small[0], "dp", axis=0).reshape(dp_size, 2 + EXPERTS, share)
        small_all = jnp.swapaxes(small_all, 0, 1).reshape(2 + EXPERTS, depth)
        small_all = jnp.concatenate([small_all, jnp.zeros((2, depth), BF)], 0)
        wo_all = lax.all_gather(wo_slots[0], "dp", axis=2, tiled=True)[None]
        wo_all = [wo_all[:, :, :half], wo_all[:, :, half:]]

    local = jnp.stack(
        [
            jnp.swapaxes(w_gate, 1, 2).reshape(ff, share),
            jnp.swapaxes(w_up, 1, 2).reshape(ff, share),
            down_weight.reshape(ff, share),
        ]
    )
    if direct:
        experts_w = lax.all_gather(local, "dp", axis=0)
    else:
        experts_w = lax.all_gather(local, "dp", axis=2, tiled=True)[None]

    n1, q, k, v, kt, vt, gains, router = qkv_call(index, place, toks, pack, small_all, width)
    g_near = z_swap(after(out_grad, toks[3]), 1, z_size)
    g_far = z_swap(after(out_grad, toks[3]), 2, z_size)
    fwd = attn_fwd(piece_starts, place, z_size, q, k, vt, line)
    chances, ot = fwd[:2]
    atts = z_direct([after(fwd[2], g_near, g_far)] + [after(x, g_near, g_far) for x in fwd[3:]], z_size)
    if direct:
        wo_low, wo_high = dp_step(after(wo_low, n1), 4), dp_step(after(wo_high, n1), 2)
        wo_all = [dp_step(after(x, atts[1]), 1) for x in (wo_low, wo_high)]
    gs = [out_grad, g_near, g_far, z_swap(after(g_far, fwd[2]), 1, z_size)]
    mid, n2 = mid_call(index, [after(atts[0], gs[3])] + atts[1:], wo_all, tokens_in, gains)

    n2_near = z_swap(n2, 1, z_size)
    n2_far = z_swap(n2, 2, z_size)
    n2s = [n2, n2_near, n2_far, z_swap(after(n2_far, n2_near), 1, z_size)]
    hg, gg, ug, logit_grad, router_part = units_call(place, n2s, gs, sel, router, experts_w, unit)
    ngs = product_call([gg, ug], (0, 1), experts_w, z_size, [logit_grad, router], "normed_two_grads")
    passed = z_swap(ngs[3], 1, z_size)
    outs = product_call([after(hg, ngs[0])], (2,), experts_w, z_size, [], "expert_out")
    both = (ngs[2].astype(F32) + after(passed, outs[0]).astype(F32)).astype(BF)
    far = z_swap(both, 2, z_size)
    ng_near = z_swap(after(ngs[1], passed), 1, z_size)
    count = experts_w.shape[0]
    weight_grads = wgrad_call(experts_w.shape[0], [after(hg, both, *outs), gg, ug], n2s, gs)
    resid = resid_call(index, [after(ngs[0], weight_grads), ng_near, far], mid, out_grad, gains, wo_all)
    resid_grad, aog, gain_two = resid[:3]
    weight_grads = after(weight_grads, far, ng_near)
    if direct:
        expert_grads = lax.psum_scatter(weight_grads, "dp", scatter_dimension=0, tiled=False)
    else:
        expert_grads = lax.psum_scatter(weight_grads[0], "dp", scatter_dimension=2, tiled=True)
    out_passed = z_swap(after(outs[3], far), 1, z_size)
    dos = z_direct(resid[3:], z_size)
    wo_keep, wo_send = wo_grad_call(slots, atts, aog, count)
    out_both = (outs[2].astype(F32) + out_passed.astype(F32)).astype(BF)
    dos[0] = after(dos[0], wo_keep, out_both)
    out_far = z_swap(out_both, 2, z_size)
    out_near = z_swap(after(outs[1], out_both), 1, z_size)
    if direct:
        wo_grads = dp_fold(wo_keep, after(wo_send, *dos), 1)
    dq, dk, dv, diag = attn_bwd(place, dos, chances, q, k, v, kt, ot)
    if direct:
        wo_grads = dp_fold(*halves(wo_grads), 2)
        dq = after(dq, wo_grads)
    dq = after(dq, out_far, out_near)
    proj = proj_call(index, place, dq, dk, dv, pack, gain_two, router_part, toks)

    diag_at = (
        BLOCK * np.arange(total // BLOCK + 1)[:, None] - (BLOCK * (total // BLOCK - 2) + 1) - np.arange(2 * BLOCK)[None, :]
    )
    table = jnp.einsum("hbt,btk->hk", diag, jnp.asarray(onehot_of(diag_at)), precision=PRECISE)
    n1_passed = z_swap(proj[3], 1, z_size)
    if direct:
        table_rows = jnp.pad(table.reshape(1, -1), ((0, 7), (0, 0)))
        smalls = z_direct([proj[z_size]] * z_size, z_size)
        wo_grads = dp_fold(*halves(wo_grads), 4)[0]
        attn_keep, attn_send = attn_weights_call(slots, n1, dq, dk, dv, after(table_rows, wo_grads), smalls, 8)
        n1_passed = after(n1_passed, attn_keep)
    n1_both = (proj[2].astype(F32) + n1_passed.astype(F32)).astype(BF)
    n1_far = z_swap(n1_both, 2, z_size)
    n1_near = z_swap(after(proj[1], n1_both), 1, z_size)
    in_grad = final_call([proj[0], n1_near, n1_far], tokens_in, resid_grad, gains)
    out_parts = [outs[0], out_near, out_far]
    out_rows = (mid + functools.reduce(jnp.add, [p.astype(F32) for p in out_parts])).astype(BF)

    if direct:
        attn_grads = dp_fold(attn_keep, after(attn_send, n1_both), 1)
        attn_grads = dp_fold(*halves(attn_grads), 2)
        attn_grads = dp_fold(*halves(after(attn_grads, n1_far, n1_near)), 4)
        attn_grads = attn_grads[0].astype(F32)
        per = width // 128
        cut = attn_grads[: 3 * per * share].reshape(3, per, share, 128)
        cut = jnp.swapaxes(cut, 1, 2).reshape(3, share, width)
        smalls = attn_grads[3 * per * share :]
        grad_table = smalls[8, : heads * BUCKETS].reshape(heads, BUCKETS)
        mine = z_rank
        grad_wo = after(wo_grads, n1_near)
    else:
        cut = jnp.stack([jnp.dot(n1.T, d, preferred_element_type=F32) for d in (dq, dk, dv)])
        cut = lax.psum_scatter(cut, "dp", scatter_dimension=1, tiled=True)
        smalls = lax.psum(proj[z_size], ("dp", "tensor"))
        grad_table = lax.psum(table, "dp")
        mine = dp_rank * z_size + z_rank
        grad_wo = lax.psum_scatter(wo_keep[0], "dp", scatter_dimension=1, tiled=True)
    wo_parts = z_direct([grad_wo[width * c : width * (c + 1)] for c in range(z_size)], z_size)
    grad_wo = functools.reduce(jnp.add, [p.astype(F32) for p in wo_parts])
    per_device = depth // (dp_size * z_size)
    own = lax.dynamic_slice_in_dim(smalls, mine * per_device, per_device, 1)

    wide = expert_grads.astype(F32).reshape(3, EXPERTS, unit, share)
    return (
        out_rows,
        in_grad,
        own[0],
        cut[0],
        cut[1],
        cut[2],
        grad_wo,
        grad_table,
        own[1],
        own[2 : 2 + EXPERTS].T,
        jnp.swapaxes(wide[0], 1, 2),
        jnp.swapaxes(wide[1], 1, 2),
        wide[2],
    )


def solution(mesh):
    rows = P(("dp", "tensor"), None)
    grid = P("dp", "tensor")
    flat = P(("dp", "tensor"))
    weights = (P(None, "dp", "tensor"), P(None, "dp", "tensor"), P(None, "tensor", "dp"))
    in_specs = (rows, rows, P("dp"), grid, grid, grid, P("tensor", "dp"), P("tensor", None), P("dp"), P("dp", None))
    out_specs = (rows, rows, flat, grid, grid, grid, P("tensor", "dp"), P("tensor", None), flat, rows)
    return jax.shard_map(
        on_device,
        mesh=mesh,
        in_specs=in_specs + weights + (P("dp", None), P("dp", None)),
        out_specs=out_specs + weights,
        check_vma=False,
    )
```

```python
import functools

import jax
import jax.numpy as jnp
import numpy as np
from jax import lax
from jax.experimental import pallas as pl
from jax.experimental.pallas import tpu as pltpu
from jax.sharding import PartitionSpec as P

EXPERTS = 4
PIECE = 256
CAP = 640
BUCKETS = 32
EPSILON = 1e-06
PRECISE = lax.Precision.HIGHEST
LIMITS = (12, 16, 23, 32, 46, 64, 91)
MASKED = -1e30
BF = jnp.bfloat16
F32 = jnp.float32
BLOCK = 256
VMEM_LIMIT = 56 * 1024 * 1024


def params(semantics=None):
    return pltpu.CompilerParams(dimension_semantics=semantics, vmem_limit_bytes=VMEM_LIMIT)


def dot_nn(a, b):
    return lax.dot_general(a, b, (((1,), (0,)), ((), ())), preferred_element_type=F32)


def dot_nt(a, b):
    return lax.dot_general(a, b, (((1,), (1,)), ((), ())), preferred_element_type=F32)


def dot_tn(a, b):
    return lax.dot_general(a, b, (((0,), (0,)), ((), ())), preferred_element_type=F32)


def bucket_of(offsets):
    distance = np.abs(offsets)
    far = np.full_like(distance, 8)
    for bound in LIMITS:
        far = far + (distance >= bound)
    return np.where(distance < 8, distance, far) + np.where(offsets > 0, 16, 0)


def onehot_of(offsets):
    return (bucket_of(offsets)[..., None] == np.arange(BUCKETS)).astype(np.float32)


def cost(flops, nbytes):
    return pl.CostEstimate(flops=int(flops), bytes_accessed=int(nbytes), transcendentals=0)


def vspec():
    return pl.BlockSpec(memory_space=pltpu.VMEM)


def sspec():
    return pl.BlockSpec(memory_space=pltpu.SMEM)


def z_swap(x, mask, size):
    return lax.ppermute(x, "tensor", [(i, i ^ mask) for i in range(size)])


def z_gather(x, size):
    near = z_swap(x, 1, size)
    far = z_swap(x, 2, size)
    return [x, near, far, z_swap(far, 1, size)]


def z_direct(parts, size):
    return [parts[0]] + [z_swap(parts[mask], mask, size) for mask in range(1, size)]


def z_reduce(parts, size):
    passed = z_swap(parts[3], 1, size)
    far = z_swap((parts[2].astype(F32) + passed.astype(F32)).astype(BF), 2, size)
    return [parts[0], z_swap(parts[1], 1, size), far]


def after(x, *others):
    return lax.optimization_barrier((x,) + others)[0]


def dp_slots(ranks):
    x, y, core = (ranks >> 1) & 1, (ranks >> 2) & 1, ranks & 1
    return jnp.concatenate([x | (y << 1) | (core << 2), y | (x << 1) | (core << 2)])


def dp_step(x, bit):
    other = lax.ppermute(x, "dp", [(i, i ^ bit) for i in range(8)])
    return jnp.concatenate([x, other], 0)


def dp_fold(keep, send, bit):
    other = lax.ppermute(send, "dp", [(i, i ^ bit) for i in range(8)])
    return (keep.astype(F32) + other.astype(F32)).astype(keep.dtype)


def halves(x):
    return x[: x.shape[0] // 2], x[x.shape[0] // 2 :]


def dp_scatter_slots(ranks):
    return ((ranks >> 2) & 1) | (((ranks >> 1) & 1) << 1) | ((ranks & 1) << 2)


def parted(keep_ref, send_ref, order_ref):
    half = keep_ref.shape[0]
    for j in range(2 * half if half > 1 else 1):
        yield (keep_ref if j < half else send_ref), j % half, order_ref[j]


def join_rows(first_ref, last_ref, index_ref, count, rows):
    split = first_ref.shape[1]
    pieces = []
    for c in range(count):
        pieces.append(first_ref[index_ref[c], :, :])
        pieces.append(last_ref[index_ref[count + c], 0 : rows - split, :])
    return jnp.concatenate(pieces, 0)


def qkv_body(count, chunks, rows, index_ref, place_ref, *refs):
    toks = refs[:chunks]
    first_ref, last_ref, small_ref = refs[chunks : chunks + 3]
    n1_ref, q_ref, k_ref, v_ref, kt_ref, vt_ref, gains_ref, router_ref = refs[chunks + 3 :]
    depth = n1_ref.shape[1] // count
    weights = join_rows(first_ref, last_ref, index_ref, count, depth)
    width = q_ref.shape[1]
    if count == 1:
        small = [small_ref[r : r + 1, :] for r in range(2 + EXPERTS)]
    else:
        row = depth - first_ref.shape[1]
        lines = [small_ref[index_ref[count + d], row : row + 16, :].astype(F32)[0:1] for d in range(count)]
        small = [
            jnp.concatenate([x[:, depth * r : depth * (r + 1)] for x in lines], 1) for r in range(2 + EXPERTS)
        ]
    small = jnp.concatenate([x.astype(F32) for x in small] + [jnp.zeros((2, depth * count), F32)], 0)
    gains_ref[...] = small
    routers = jnp.concatenate([small[2:], jnp.zeros((10, depth * count), F32)], 0)
    router_ref[...] = jnp.zeros_like(router_ref)
    router_ref[0:16, :] = routers.astype(BF)
    gain = small[0:1, :]
    for c in range(chunks):
        at = pl.ds(pl.multiple_of(place_ref[c] * rows, rows), rows)
        x = toks[c][...].astype(F32)
        scale = lax.rsqrt(jnp.mean(x * x, axis=1, keepdims=True) + EPSILON)
        normed = (x * scale * gain).astype(BF)
        n1_ref[at, :] = normed
        out = dot_nn(normed, weights)
        q_ref[at, :] = (out[:, :width].astype(BF).astype(F32) * 0.125).astype(BF)
        key = out[:, width : 2 * width]
        value = out[:, 2 * width :]
        k_ref[at, :] = key.astype(BF)
        v_ref[at, :] = value.astype(BF)
        kt_ref[:, at] = jnp.transpose(key).astype(BF)
        vt_ref[:, at] = jnp.transpose(value).astype(BF)


def qkv_call(index, place, toks, pack, small, width):
    chunks, rows, depth = len(toks), toks[0].shape[0], toks[0].shape[1]
    total = chunks * rows
    shapes = [(total, depth)] + [(total, width)] * 3 + [(width, total)] * 2
    return pl.pallas_call(
        functools.partial(qkv_body, pack[0].shape[0], chunks, rows),
        in_specs=[sspec(), sspec()] + [vspec()] * (chunks + 3),
        out_specs=[vspec()] * 8,
        out_shape=[jax.ShapeDtypeStruct(s, BF) for s in shapes]
        + [jax.ShapeDtypeStruct((8, depth), F32), jax.ShapeDtypeStruct((128, depth), BF)],
        compiler_params=params(),
        cost_estimate=cost(2 * total * depth * 3 * width, 8 * total * depth),
        name="norm_qkv",
    )(index, place, *toks, *pack, small)


def extent_of(i, total):
    return min(BLOCK * (i + 2), total)


def fwd_body(total, chunks, starts_ref, place_ref, q_ref, k_ref, vt_ref, line_ref, p_ref, ot_ref, *refs):
    atts = refs[:chunks]
    strip_ref, mask_ref, all_ref = refs[chunks:]
    head = pl.program_id(0)
    heads = pl.num_programs(0)
    blocks = total // BLOCK
    width = q_ref.shape[1]
    dim = width // 4

    @pl.when(head == 0)
    def _():
        def label(pos):
            first = (pos >= starts_ref[0, 0]) & (pos < starts_ref[0, 0] + PIECE)
            second = (pos >= starts_ref[0, 1]) & (pos < starts_ref[0, 1] + PIECE)
            return first, second

        for i in range(blocks):
            for j in (i, i + 1):
                if j >= blocks:
                    continue
                kpos = lax.broadcasted_iota(jnp.int32, (BLOCK, BLOCK), 0) + BLOCK * j
                qpos = lax.broadcasted_iota(jnp.int32, (BLOCK, BLOCK), 1) + BLOCK * i
                k1, k2 = label(kpos)
                q1, q2 = label(qpos)
                seen = (kpos <= qpos) | (k1 & q1) | (k2 & q2)
                mask_ref[2 * i + j - i] = jnp.where(seen, 0.0, MASKED)

    for beta in range(blocks + 1):
        start = BLOCK * (blocks - beta)
        window = line_ref[0, 0:1, start : start + 2 * BLOCK]
        spread = jnp.broadcast_to(window, (BLOCK, 2 * BLOCK))
        rolled = pltpu.roll(spread, BLOCK + 1, 1, stride=1, stride_axis=0)
        strip_ref[BLOCK * beta : BLOCK * (beta + 1), :] = rolled[:, :BLOCK]

    lanes = lax.broadcasted_iota(jnp.int32, (2 * BLOCK, width), 1)
    own = (lanes >= head * dim) & (lanes < (head + 1) * dim)
    at_head = pl.ds(pl.multiple_of(head * dim, dim), dim)
    for pair in range(0, blocks, 2):
        both = slice(BLOCK * pair, BLOCK * (pair + 2))
        reach = extent_of(pair + 1, total)
        q_rows = q_ref[both, :]
        q_own = jnp.where(own, q_rows, jnp.zeros_like(q_rows))
        raw = dot_nt(k_ref[0:reach, :], q_own)
        for i in (pair, pair + 1):
            extent = extent_of(i, total)
            cols = slice(BLOCK * i, BLOCK * (i + 1))
            base = BLOCK * (blocks - 1 - i)
            scores = raw[0:extent, BLOCK * (i - pair) : BLOCK * (i - pair + 1)] + strip_ref[base : base + extent, :]
            parts = [scores[BLOCK * j : BLOCK * (j + 1)] for j in range(extent // BLOCK)]
            for j in (i, i + 1):
                if j < blocks:
                    parts[j] = parts[j] + mask_ref[2 * i + j - i]
            top = functools.reduce(jnp.maximum, parts)
            top = jnp.max(top, axis=0, keepdims=True)
            parts = [jnp.exp(part - top) for part in parts]
            total_sum = jnp.sum(functools.reduce(jnp.add, parts), axis=0, keepdims=True)
            inverse = 1.0 / total_sum
            p_ref[0, 0:extent, cols] = jnp.concatenate([(part * inverse).astype(BF) for part in parts], 0)
            if extent < total:
                p_ref[0, extent : extent + BLOCK, cols] = jnp.zeros((BLOCK, BLOCK), BF)
        ot_ref[at_head, both] = dot_nn(vt_ref[at_head, 0:reach], p_ref[0, 0:reach, both])

    @pl.when(head == heads - 1)
    def _():
        mixed = ot_ref[...]
        all_ref[...] = jnp.transpose(mixed).astype(BF)
        rows = total // chunks
        for c in range(chunks):
            at = pl.ds(pl.multiple_of(place_ref[c] * rows, rows), rows)
            atts[c][...] = all_ref[at, :]


def attn_fwd(starts, place, chunks, q, k, vt, line):
    total, width = q.shape
    heads = line.shape[0]
    blocks = total // BLOCK
    whole = lambda shape: pl.BlockSpec(shape, lambda h: (0,) * len(shape))
    return pl.pallas_call(
        functools.partial(fwd_body, total, chunks),
        grid=(heads,),
        in_specs=[
            sspec(),
            sspec(),
            whole((total, width)),
            whole((total, width)),
            whole((width, total)),
            pl.BlockSpec((1, 1, line.shape[2]), lambda h: (h, 0, 0)),
        ],
        out_specs=[
            pl.BlockSpec((1, total, total), lambda h: (h, 0, 0)),
            whole((width, total)),
        ]
        + [whole((total // chunks, width))] * chunks,
        out_shape=[
            jax.ShapeDtypeStruct((heads, total, total), BF),
            jax.ShapeDtypeStruct((width, total), F32),
        ]
        + [jax.ShapeDtypeStruct((total // chunks, width), BF)] * chunks,
        scratch_shapes=[
            pltpu.VMEM((BLOCK * (blocks + 1), BLOCK), F32),
            pltpu.VMEM((2 * blocks, BLOCK, BLOCK), F32),
            pltpu.VMEM((total, width), BF),
        ],
        compiler_params=params(("arbitrary",)),
        cost_estimate=cost(heads * 4 * total * total * width, 10 * total * total),
        name="attn_forward",
    )(starts, place, q, k, vt, line)


def diagonal_sums(acc):
    half = BLOCK // 2
    low, high = acc[:half], acc[half:]
    rows = jnp.concatenate(
        [high[:, :half], high[:, half:] + low[:, :half], low[:, half:], jnp.zeros((half, half), F32)], 1
    )
    step = half // 2
    while step >= 8:
        rows = rows[step:] + pltpu.roll(rows[:step], step, 1)
        step //= 2
    index = lax.broadcasted_iota(jnp.int32, rows.shape, 0)
    for step in (4, 2, 1):
        rows = jnp.where((index & step) == 0, pltpu.roll(rows, step, 1), rows)
    return jnp.sum(rows, axis=0, keepdims=True)


def bwd_body(total, chunks, place_ref, *refs):
    grads = refs[:chunks]
    p_ref, q_ref, k_ref, v_ref, kt_ref, ot_ref = refs[chunks : chunks + 6]
    dq_ref, dk_ref, dv_ref, diag_ref = refs[chunks + 6 : chunks + 10]
    do_ref, dot_ref, dqt_ref, dka_ref, dva_ref, ds_ref, acc_ref = refs[chunks + 10 :]
    head = pl.program_id(0)
    heads = pl.num_programs(0)
    blocks = total // BLOCK
    rows = total // chunks
    width = q_ref.shape[1]
    dim = width // 4

    @pl.when(head == 0)
    def _():
        for c in range(chunks):
            at = pl.ds(pl.multiple_of(place_ref[c] * rows, rows), rows)
            do_ref[at, :] = grads[c][...]
        dot_ref[...] = jnp.transpose(do_ref[...].astype(F32))
        ds_ref[...] = jnp.zeros_like(ds_ref)
        dka_ref[...] = jnp.zeros_like(dka_ref)
        dva_ref[...] = jnp.zeros_like(dva_ref)

    at_head = pl.ds(pl.multiple_of(head * dim, dim), dim)
    inner = jnp.sum(dot_ref[at_head, :] * ot_ref[at_head, :], axis=0, keepdims=True)
    lanes = lax.broadcasted_iota(jnp.int32, (total, width), 1)
    own = (lanes >= head * dim) & (lanes < (head + 1) * dim)
    q_own = jnp.where(own, q_ref[...], jnp.zeros_like(q_ref))
    do_own = jnp.where(own, do_ref[...], jnp.zeros_like(do_ref))
    written = 0
    for pair in range(blocks - 2, -1, -2):
        both = slice(BLOCK * pair, BLOCK * (pair + 2))
        reach = extent_of(pair + 1, total)
        pair_grad = dot_nt(v_ref[0:reach, :], do_own[both, :])
        for i in (pair + 1, pair):
            extent = extent_of(i, total)
            cols = slice(BLOCK * i, BLOCK * (i + 1))
            chance_grad = pair_grad[0:extent, BLOCK * (i - pair) : BLOCK * (i - pair + 1)]
            chances = p_ref[0, 0:extent, cols].astype(F32)
            score_grad = (chances * (chance_grad - inner[:, cols])).astype(BF)
            ds_ref[0:extent, cols] = score_grad
            base = BLOCK * (blocks - 1 - i)
            wide = score_grad.astype(F32)
            if i == blocks - 1:
                acc_ref[0:extent, :] = wide
                written = extent
            else:
                old = written - base
                acc_ref[base:written, :] += wide[:old]
                if base + extent > written:
                    acc_ref[written : base + extent, :] = wide[old:]
                    written = base + extent
        dqt_ref[at_head, both] = dot_nn(kt_ref[at_head, 0:reach], ds_ref[0:reach, both])
    for pair in range(0, blocks, 2):
        first = max(0, BLOCK * (pair - 1))
        keys = slice(BLOCK * pair, BLOCK * (pair + 2))
        dka_ref[keys, :] += dot_nn(ds_ref[keys, first:], q_own[first:, :])
        dva_ref[keys, :] += dot_nn(p_ref[0, keys, first:], do_own[first:, :])
    for beta in range(blocks + 1):
        diag_ref[0, beta : beta + 1, :] = diagonal_sums(acc_ref[BLOCK * beta : BLOCK * (beta + 1), :])

    @pl.when(head == heads - 1)
    def _():
        dq_ref[...] = (jnp.transpose(dqt_ref[...]) * 0.125).astype(BF)
        dk_ref[...] = dka_ref[...].astype(BF)
        dv_ref[...] = dva_ref[...].astype(BF)


def attn_bwd(place, grads, chances, q, k, v, kt, ot):
    total, width = q.shape
    heads = chances.shape[0]
    blocks = total // BLOCK
    chunks = len(grads)
    whole = lambda shape: pl.BlockSpec(shape, lambda h: (0,) * len(shape))
    return pl.pallas_call(
        functools.partial(bwd_body, total, chunks),
        grid=(heads,),
        in_specs=[sspec()]
        + [whole(grads[0].shape)] * chunks
        + [pl.BlockSpec((1, total, total), lambda h: (h, 0, 0))]
        + [whole((total, width))] * 3
        + [whole((width, total))] * 2,
        out_specs=[whole((total, width))] * 3 + [pl.BlockSpec((1, blocks + 1, 2 * BLOCK), lambda h: (h, 0, 0))],
        out_shape=[jax.ShapeDtypeStruct((total, width), BF)] * 3
        + [jax.ShapeDtypeStruct((heads, blocks + 1, 2 * BLOCK), F32)],
        scratch_shapes=[
            pltpu.VMEM((total, width), BF),
            pltpu.VMEM((width, total), F32),
            pltpu.VMEM((width, total), F32),
            pltpu.VMEM((total, width), F32),
            pltpu.VMEM((total, width), F32),
            pltpu.VMEM((total, total), BF),
            pltpu.VMEM((BLOCK * (blocks + 1), BLOCK), F32),
        ],
        compiler_params=params(("arbitrary",)),
        cost_estimate=cost(heads * 160 * total * total * width, 10 * total * total),
        name="attn_backward",
    )(place, *grads, chances, q, k, v, kt, ot)


def join_lanes(low_ref, high_ref, index_ref, count, slot):
    low = [low_ref[index_ref[c], slot] for c in range(count)]
    high = [high_ref[index_ref[count + c], slot] for c in range(count)]
    return jnp.concatenate([jnp.concatenate(low, 1), jnp.concatenate(high, 1)], 0)


def mid_body(count, chunks, index_ref, *refs):
    atts = refs[:chunks]
    low_ref, high_ref, tok_ref, gain_ref, mid_ref, n2_ref = refs[chunks:]
    u = tok_ref[...].astype(F32)
    for c in range(chunks):
        u = u + dot_nn(atts[c][...], join_lanes(low_ref, high_ref, index_ref, count, c))
    mid_ref[...] = u
    scale = lax.rsqrt(jnp.mean(u * u, axis=1, keepdims=True) + EPSILON)
    n2_ref[...] = (u * scale * gain_ref[1:2, :]).astype(BF)


def mid_call(index, atts, w_out, tok, gains):
    chunks = len(atts)
    return pl.pallas_call(
        functools.partial(mid_body, w_out[0].shape[0], chunks),
        in_specs=[sspec()] + [vspec()] * (chunks + 4),
        out_specs=[vspec()] * 2,
        out_shape=[jax.ShapeDtypeStruct(tok.shape, F32), jax.ShapeDtypeStruct(tok.shape, BF)],
        compiler_params=params(),
        cost_estimate=cost(2 * tok.shape[0] * tok.shape[1] ** 2, 4 * tok.shape[1] ** 2),
        name="out_projection_norm",
    )(index, *atts, *w_out, tok, gains)


def split_dot(a, b, dot):
    high = a.astype(BF)
    low = (a - high.astype(F32)).astype(BF)
    return dot(high, b) + dot(low, b)


def joined(ref, which):
    if ref.shape[0] == 1:
        return ref[0, which]
    return jnp.concatenate([ref[d, which] for d in range(ref.shape[0])], 1)


def units_body(chunks, unit, place_ref, *refs):
    n2s = refs[:chunks]
    gs = refs[chunks : 2 * chunks]
    sel_ref, rout_ref, w_ref = refs[2 * chunks : 2 * chunks + 3]
    hg_ref, gg_ref, ug_ref, lg_ref, rpart_ref = refs[2 * chunks + 3 : 2 * chunks + 8]
    n2_ref, g_ref, gate_ref, sum_ref, prob_ref, pick_ref = refs[2 * chunks + 8 :]
    step = pl.program_id(0)
    steps = pl.num_programs(0)
    rows = n2s[0].shape[0]
    tokens = chunks * rows
    lane = lax.broadcasted_iota(jnp.int32, (tokens, 128), 1)

    @pl.when(step == 0)
    def _():
        for c in range(chunks):
            n2_ref[rows * c : rows * (c + 1), :] = n2s[c][...]
            g_ref[rows * c : rows * (c + 1), :] = gs[c][...]
        logits = dot_nt(n2_ref[...], rout_ref[...])
        logits = jnp.where(lane < EXPERTS, logits, MASKED)
        raised = jnp.exp(logits - jnp.max(logits, axis=1, keepdims=True))
        prob_ref[...] = raised / jnp.sum(raised, axis=1, keepdims=True)
        for c in range(chunks):
            at = pl.ds(pl.multiple_of(place_ref[c] * rows, rows), rows)
            pick_ref[rows * c : rows * (c + 1), :] = sel_ref[at, :]
        gates = prob_ref[...] * pick_ref[...]
        for e in range(EXPERTS):
            one = jnp.sum(jnp.where(lane == e, gates, 0.0), axis=1, keepdims=True)
            gate_ref[e] = jnp.broadcast_to(one, (tokens, 128))
        sum_ref[...] = jnp.zeros_like(sum_ref)

    wg, wu, wd = joined(w_ref, 0), joined(w_ref, 1), joined(w_ref, 2)
    pre = dot_nt(n2_ref[...], jnp.concatenate([wg, wu], 0))
    gate_pre, up_pre = pre[:, : wg.shape[0]], pre[:, wg.shape[0] :]
    raw = dot_nt(g_ref[...], wd)
    c0 = float(np.sqrt(2.0 / np.pi))
    square = gate_pre * gate_pre
    th = jnp.tanh(gate_pre * (c0 + (c0 * 0.044715) * square))
    half = 0.5 + 0.5 * th
    act = gate_pre * half
    slope = half + gate_pre * (0.5 * c0 + (1.5 * c0 * 0.044715) * square) * (1.0 - th * th)
    hidden = act * up_pre
    prod = raw * hidden
    width = hg_ref.shape[1]
    e_low = (step * width) // unit
    e_high = (step * width + width - 1) // unit
    bound = jnp.where(e_high > e_low, unit * e_high - step * width, width)
    lows = []
    for m in range(width // 128):
        is_low = lane + 128 * m < bound
        part = slice(128 * m, 128 * (m + 1))
        gate = jnp.where(is_low, gate_ref[e_low], gate_ref[e_high])
        lows.append(jnp.where(is_low, prod[:, part], 0.0))
        hg_ref[:, part] = (gate * hidden[:, part]).astype(BF)
        hidden_grad = gate * raw[:, part]
        gg_ref[:, part] = (hidden_grad * up_pre[:, part] * slope[:, part]).astype(BF)
        ug_ref[:, part] = (hidden_grad * act[:, part]).astype(BF)
    sum_ref[e_low] += functools.reduce(jnp.add, lows)

    @pl.when(e_high > e_low)
    def _():
        every = [prod[:, 128 * m : 128 * (m + 1)] - lows[m] for m in range(width // 128)]
        sum_ref[e_high] += functools.reduce(jnp.add, every)

    @pl.when(step == steps - 1)
    def _():
        grad = jnp.zeros((tokens, 128), F32)
        for e in range(EXPERTS):
            grad = grad + jnp.where(lane == e, jnp.sum(sum_ref[e], axis=1, keepdims=True), 0.0)
        grad = grad * pick_ref[...]
        probs = prob_ref[...]
        logit_grad = probs * (grad - jnp.sum(probs * grad, axis=1, keepdims=True))
        lg_ref[...] = logit_grad
        rpart_ref[...] = split_dot(logit_grad, n2_ref[...], dot_tn)[0:8, :]


def units_call(place, n2s, gs, sel, router, weights, unit):
    chunks, rows, depth = len(n2s), n2s[0].shape[0], n2s[0].shape[1]
    count, _, ff, part = weights.shape
    tokens = chunks * rows
    whole = lambda shape: pl.BlockSpec(shape, lambda s: (0,) * len(shape))
    return pl.pallas_call(
        functools.partial(units_body, chunks, unit),
        grid=(ff // BLOCK,),
        in_specs=[sspec()]
        + [whole((rows, depth))] * (2 * chunks)
        + [whole(sel.shape), whole(router.shape), pl.BlockSpec((count, 3, BLOCK, part), lambda s: (0, 0, s, 0))],
        out_specs=[pl.BlockSpec((tokens, BLOCK), lambda s: (0, s))] * 3 + [whole((tokens, 128)), whole((8, depth))],
        out_shape=[jax.ShapeDtypeStruct((tokens, ff), BF)] * 3
        + [jax.ShapeDtypeStruct((tokens, 128), F32), jax.ShapeDtypeStruct((8, depth), F32)],
        scratch_shapes=[
            pltpu.VMEM((tokens, depth), BF),
            pltpu.VMEM((tokens, depth), BF),
            pltpu.VMEM((EXPERTS, tokens, 128), F32),
            pltpu.VMEM((EXPERTS, tokens, 128), F32),
            pltpu.VMEM((tokens, 128), F32),
            pltpu.VMEM((tokens, 128), F32),
        ],
        compiler_params=params(("arbitrary",)),
        cost_estimate=cost(6 * tokens * depth * ff, 6 * depth * ff + 12 * tokens * depth),
        name="expert_units",
    )(place, *n2s, *gs, sel, router, weights)


def product_body(terms, chunks, extra, *refs):
    xs = refs[:terms]
    ws = refs[terms : 2 * terms]
    at = 2 * terms + (2 if extra else 0)
    outs = refs[at : at + chunks]
    total = None
    for x, w in zip(xs, ws):
        term = dot_nn(x[...], joined(w, 0))
        total = term if total is None else total + term
    if extra:
        lg_ref, rout_ref = refs[2 * terms : 2 * terms + 2]
        total = total + split_dot(lg_ref[...], rout_ref[...], dot_nn)
    rows = outs[0].shape[0]
    for c in range(chunks):
        outs[c][...] = total[rows * c : rows * (c + 1)].astype(BF)


def product_call(xs, picks, weights, chunks, extra, name):
    tokens, ff = xs[0].shape
    count, _, _, part = weights.shape
    depth = count * part
    rows = tokens // chunks
    per = max(1, BLOCK // part)
    wide = min(part * per, BLOCK)
    whole = lambda shape: pl.BlockSpec(shape, lambda s: (0,) * len(shape))
    place_at = (lambda i, s: (s, i, 0, 0)) if count > 1 else (lambda i, s: (0, i, 0, s))
    w_specs = [pl.BlockSpec((min(per, count), 1, ff, wide // min(per, count)), functools.partial(place_at, i)) for i in picks]
    return pl.pallas_call(
        functools.partial(product_body, len(xs), chunks, bool(extra)),
        grid=(depth // wide,),
        in_specs=[whole((tokens, ff))] * len(xs)
        + w_specs
        + ([whole(extra[0].shape), pl.BlockSpec((128, wide), lambda s: (0, s))] if extra else []),
        out_specs=[pl.BlockSpec((rows, wide), lambda s: (0, s))] * chunks,
        out_shape=[jax.ShapeDtypeStruct((rows, depth), BF)] * chunks,
        compiler_params=params(("arbitrary",)),
        cost_estimate=cost(2 * len(xs) * tokens * depth * ff, 4 * len(xs) * depth * ff),
        name=name,
    )(*xs, *([weights] * len(xs)), *extra)


def wgrad_body(count, chunks, *refs):
    hg_ref, gg_ref, ug_ref = refs[:3]
    n2s = refs[3 : 3 + chunks]
    gs = refs[3 + chunks : 3 + 2 * chunks]
    out_ref, n2_ref, g_ref = refs[3 + 2 * chunks :]
    part = out_ref.shape[3]
    rows = n2s[0].shape[0]

    @pl.when(pl.program_id(0) == 0)
    def _():
        for c in range(chunks):
            n2_ref[rows * c : rows * (c + 1), :] = n2s[c][...]
            g_ref[rows * c : rows * (c + 1), :] = gs[c][...]

    width = hg_ref.shape[1]
    pair = dot_tn(jnp.concatenate([gg_ref[...], ug_ref[...]], 1), n2_ref[...]).astype(BF)
    down = dot_tn(hg_ref[...], g_ref[...]).astype(BF)
    for which, total in enumerate((pair[:width], pair[width:], down)):
        for d in range(count):
            out_ref[d, which] = total[:, part * d : part * (d + 1)]


def wgrad_call(count, kept, n2s, gs):
    tokens, ff = kept[0].shape
    chunks, rows, depth = len(n2s), n2s[0].shape[0], n2s[0].shape[1]
    whole = lambda shape: pl.BlockSpec(shape, lambda s: (0,) * len(shape))
    return pl.pallas_call(
        functools.partial(wgrad_body, count, chunks),
        grid=(ff // BLOCK,),
        in_specs=[pl.BlockSpec((tokens, BLOCK), lambda s: (0, s))] * 3 + [whole((rows, depth))] * (2 * chunks),
        out_specs=pl.BlockSpec((count, 3, BLOCK, depth // count), lambda s: (0, 0, s, 0)),
        out_shape=jax.ShapeDtypeStruct((count, 3, ff, depth // count), BF),
        scratch_shapes=[pltpu.VMEM((tokens, depth), BF), pltpu.VMEM((tokens, depth), BF)],
        compiler_params=params(("arbitrary",)),
        cost_estimate=cost(6 * tokens * depth * ff, 12 * depth * ff),
        name="expert_weight_grads",
    )(*kept, *n2s, *gs)


def norm_back(grad, u, gain):
    scale = lax.rsqrt(jnp.mean(u * u, axis=1, keepdims=True) + EPSILON)
    m = grad * gain
    back = scale * m - u * (scale * scale * scale) * jnp.mean(u * m, axis=1, keepdims=True)
    return back, jnp.sum(grad * u * scale, axis=0, keepdims=True)


def resid_body(count, chunks, terms, index_ref, *refs):
    parts = refs[:terms]
    mid_ref, g_ref, gains_ref, low_ref, high_ref = refs[terms : terms + 5]
    rest = refs[terms + 5 :]
    resid_ref, aog_ref, gain_ref = rest[:3]
    dos = rest[3:]
    grad = functools.reduce(jnp.add, [p[...].astype(F32) for p in parts])
    back, gain_part = norm_back(grad, mid_ref[...], gains_ref[1:2, :])
    resid = g_ref[...].astype(F32) + back
    resid_ref[...] = resid
    low = resid.astype(BF)
    aog_ref[...] = low
    gain_ref[...] = jnp.broadcast_to(gain_part, gain_ref.shape)
    for c in range(chunks):
        dos[c][...] = dot_nt(low, join_lanes(low_ref, high_ref, index_ref, count, c)).astype(BF)


def resid_call(index, parts, mid, grad, gains, w_out):
    chunks, terms = w_out[0].shape[1], len(parts)
    shape = mid.shape
    width = 2 * w_out[0].shape[2]
    return pl.pallas_call(
        functools.partial(resid_body, w_out[0].shape[0], chunks, terms),
        in_specs=[sspec()] + [vspec()] * (terms + 5),
        out_specs=[vspec()] * (3 + chunks),
        out_shape=[
            jax.ShapeDtypeStruct(shape, F32),
            jax.ShapeDtypeStruct(shape, BF),
            jax.ShapeDtypeStruct((8, shape[1]), F32),
        ]
        + [jax.ShapeDtypeStruct((shape[0], width), BF)] * chunks,
        compiler_params=params(),
        cost_estimate=cost(2 * shape[0] * shape[1] ** 2, 4 * shape[1] ** 2),
        name="resid_grad",
    )(index, *parts, mid, grad, gains, *w_out)


def final_body(chunks, *refs):
    parts = refs[:chunks]
    tok_ref, resid_ref, gains_ref, out_ref = refs[chunks:]
    grad = functools.reduce(jnp.add, [p[...].astype(F32) for p in parts])
    back, _ = norm_back(grad, tok_ref[...].astype(F32), gains_ref[0:1, :])
    out_ref[...] = resid_ref[...] + back


def final_call(parts, tok, resid, gains):
    return pl.pallas_call(
        functools.partial(final_body, len(parts)),
        in_specs=[vspec()] * (len(parts) + 3),
        out_specs=vspec(),
        out_shape=jax.ShapeDtypeStruct(tok.shape, F32),
        compiler_params=params(),
        cost_estimate=cost(20 * tok.size, 12 * tok.size),
        name="in_grad",
    )(*parts, tok, resid, gains)


def proj_body(count, chunks, rows, index_ref, place_ref, dq_ref, dk_ref, dv_ref, first_ref, last_ref, two_ref, router_ref, *refs):
    toks = refs[:chunks]
    outs = refs[chunks : 2 * chunks]
    gain_ref = refs[2 * chunks]
    depth = outs[0].shape[1]
    width = dq_ref.shape[1]
    weights = join_rows(first_ref, last_ref, index_ref, count, depth // count)
    gain = jnp.zeros((1, depth), F32)
    for c in range(chunks):
        at = pl.ds(pl.multiple_of(place_ref[c] * rows, rows), rows)
        grad = dot_nt(dq_ref[at, :], weights[:, :width])
        grad = grad + dot_nt(dk_ref[at, :], weights[:, width : 2 * width])
        grad = grad + dot_nt(dv_ref[at, :], weights[:, 2 * width :])
        outs[c][...] = grad.astype(BF)
        x = toks[c][...].astype(F32)
        scale = lax.rsqrt(jnp.mean(x * x, axis=1, keepdims=True) + EPSILON)
        gain = gain + jnp.sum(grad * x * scale, axis=0, keepdims=True)
    blank = jnp.zeros((6 - EXPERTS, depth), F32)
    gain_ref[...] = jnp.concatenate([gain, two_ref[0:1, :], router_ref[0:EXPERTS, :], blank], 0)


def proj_call(index, place, dq, dk, dv, pack, gain_two, router_part, toks):
    chunks, rows, depth = len(toks), toks[0].shape[0], toks[0].shape[1]
    return pl.pallas_call(
        functools.partial(proj_body, pack[0].shape[0], chunks, rows),
        in_specs=[sspec(), sspec()] + [vspec()] * (7 + chunks),
        out_specs=[vspec()] * (chunks + 1),
        out_shape=[jax.ShapeDtypeStruct((rows, depth), BF)] * chunks + [jax.ShapeDtypeStruct((8, depth), F32)],
        compiler_params=params(),
        cost_estimate=cost(6 * chunks * rows * depth * dq.shape[1], 8 * chunks * rows * depth),
        name="projection_grads",
    )(index, place, dq, dk, dv, *pack, gain_two, router_part, *toks)


def attn_weights_body(count, smalls, slot_ref, n1_ref, dq_ref, dk_ref, dv_ref, table_ref, *refs):
    keep_ref, send_ref, small_ref, *grad_refs = refs[smalls:]
    small_ref[...] = functools.reduce(jnp.add, [r[...] for r in refs[:smalls]])
    depth = n1_ref.shape[1]
    width = dq_ref.shape[1]
    part = depth // count
    normed = n1_ref[...]
    pieces = width // 128
    for ref, grad_ref in zip((dq_ref, dk_ref, dv_ref), grad_refs):
        grad_ref[...] = dot_tn(normed, ref[...]).astype(BF)
    for out_ref, slot, d in parted(keep_ref, send_ref, slot_ref):
        rows = pl.ds(pl.multiple_of(d * part, 128), part)
        for m, grad_ref in enumerate(grad_refs):
            for piece in range(pieces):
                at = (m * pieces + piece) * part
                out_ref[slot, at : at + part, :] = grad_ref[rows, 128 * piece : 128 * (piece + 1)]
        at = 3 * pieces * part
        value = jnp.concatenate([small_ref[:, rows], table_ref[...]], 0).astype(BF)
        out_ref[slot, at : at + 16, :] = value


def attn_weights_call(slots, n1, dq, dk, dv, table, smalls, count):
    total, depth = n1.shape
    width = dq.shape[1]
    part = depth // count
    return pl.pallas_call(
        functools.partial(attn_weights_body, count, len(smalls)),
        in_specs=[sspec()] + [vspec()] * (5 + len(smalls)),
        out_specs=[vspec()] * 2,
        out_shape=[jax.ShapeDtypeStruct((count // 2, 3 * width * part // 128 + 16, 128), BF)] * 2,
        scratch_shapes=[pltpu.VMEM((8, depth), F32)] + [pltpu.VMEM((depth, width), BF)] * 3,
        compiler_params=params(),
        cost_estimate=cost(6 * total * depth * width, 8 * total * depth),
        name="attn_weight_grads",
    )(slots, n1, dq, dk, dv, table, *smalls)


def wo_grad_body(count, chunks, slot_ref, *refs):
    atts = refs[:chunks]
    aog_ref, keep_ref, send_ref, grad_ref = refs[chunks:]
    width = atts[0].shape[1]
    part = grad_ref.shape[1] // count
    for c in range(chunks):
        at = slice(c * width, (c + 1) * width)
        grad_ref[at, :] = dot_tn(atts[c][...], aog_ref[...]).astype(BF)
    for out_ref, slot, d in parted(keep_ref, send_ref, slot_ref):
        out_ref[slot] = grad_ref[:, pl.ds(pl.multiple_of(d * part, 128), part)]


def wo_grad_call(slots, atts, aog, count):
    chunks, width = len(atts), atts[0].shape[1]
    rows, depth = aog.shape
    return pl.pallas_call(
        functools.partial(wo_grad_body, count, chunks),
        in_specs=[sspec()] + [vspec()] * (chunks + 1),
        out_specs=[vspec()] * 2,
        out_shape=[jax.ShapeDtypeStruct((max(1, count // 2), chunks * width, depth // count), BF)] * 2,
        scratch_shapes=[pltpu.VMEM((chunks * width, depth), BF)],
        compiler_params=params(),
        cost_estimate=cost(2 * rows * depth * chunks * width, 4 * depth * chunks * width),
        name="w_output_grad",
    )(slots, *atts, aog)


def kept_choices(ids):
    lanes = jnp.arange(128, dtype=jnp.int32)[None, :]
    expert_range = jnp.arange(EXPERTS, dtype=jnp.int32)[None, :]
    first = (ids[:, 0:1] == expert_range).astype(jnp.int32)
    second = (ids[:, 1:2] == expert_range).astype(jnp.int32)
    runs = jnp.cumsum(jnp.concatenate([first, second], 1), axis=0)
    first_run = runs[:, :EXPERTS]
    second_run = runs[:, EXPERTS:] + first_run[-1][None, :]
    place_one = jnp.sum(first_run * first, axis=1, keepdims=True) - 1
    place_two = jnp.sum(second_run * second, axis=1, keepdims=True) - 1
    kept = ((ids[:, 0:1] == lanes) & (place_one < CAP)) | ((ids[:, 1:2] == lanes) & (place_two < CAP))
    return kept.astype(F32)


def on_device(
    tokens_in,
    out_grad,
    attn_gain,
    w_query,
    w_key,
    w_value,
    w_output,
    rel_table,
    moe_gain,
    w_router,
    w_gate,
    w_up,
    down_weight,
    expert_ids,
    piece_starts,
):
    rows, depth = tokens_in.shape
    width = w_query.shape[1]
    z_size = lax.axis_size("tensor")
    dp_size = lax.axis_size("dp")
    z_rank = lax.axis_index("tensor").astype(jnp.int32)
    dp_rank = lax.axis_index("dp").astype(jnp.int32)
    total = rows * z_size
    share = depth // dp_size
    unit = w_gate.shape[2]
    ff = EXPERTS * unit
    heads = rel_table.shape[0]
    direct = dp_size == 8 and share == 128
    place = z_rank ^ jnp.arange(z_size, dtype=jnp.int32)

    near = z_swap(tokens_in, 1, z_size)
    far = z_swap(tokens_in, 2, z_size)
    line_at = 2 * BLOCK - 1 - np.arange(total + 2 * BLOCK)
    line = jnp.dot(rel_table, jnp.asarray(onehot_of(line_at).T), precision=PRECISE)[:, None, :]
    sel = kept_choices(expert_ids)
    toks = [tokens_in, near, far, z_swap(after(far, near, sel, line), 1, z_size)]
    w_output_late = after(w_output, far)
    small = jnp.concatenate([attn_gain, moe_gain, w_router.T.reshape(-1)])[None, :]
    packed = jnp.concatenate([w_query, w_key, w_value], 1)
    wo_slots = jnp.stack(z_direct([w_output_late] * z_size, z_size))[None]
    ranks = dp_rank ^ jnp.arange(8, dtype=jnp.int32)
    half = wo_slots.shape[2] // 2
    if direct:
        index = dp_slots(ranks)
        slots = dp_rank ^ dp_scatter_slots(jnp.arange(8, dtype=jnp.int32))
        first = dp_step(packed[:80][None], 2)
        last = dp_step(jnp.concatenate([packed[80:], small, jnp.zeros((15, packed.shape[1]), BF)], 0)[None], 4)
        first, last = dp_step(after(first, near), 4), dp_step(after(last, near), 2)
        wo_low = dp_step(after(wo_slots[:, :, :half], near, far), 2)
        wo_high = dp_step(after(wo_slots[:, :, half:], near, far), 4)
        first = dp_step(after(first, toks[3], wo_low, wo_high), 1)
        last = dp_step(after(last, toks[3], wo_low, wo_high), 1)
        pack, small_all = [first, last], last
    else:
        slots = jnp.zeros((1,), jnp.int32)
        index = jnp.zeros((2,), jnp.int32)
        pack = lax.all_gather(packed, "dp", axis=0, tiled=True)[None]
        pack = [pack[:, : depth // 2], pack[:, depth // 2 :]]
        small_all = lax.all_gather(small[0], "dp", axis=0).reshape(dp_size, 2 + EXPERTS, share)
        small_all = jnp.swapaxes(small_all, 0, 1).reshape(2 + EXPERTS, depth)
        small_all = jnp.concatenate([small_all, jnp.zeros((2, depth), BF)], 0)
        wo_all = lax.all_gather(wo_slots[0], "dp", axis=2, tiled=True)[None]
        wo_all = [wo_all[:, :, :half], wo_all[:, :, half:]]

    local = jnp.stack(
        [
            jnp.swapaxes(w_gate, 1, 2).reshape(ff, share),
            jnp.swapaxes(w_up, 1, 2).reshape(ff, share),
            down_weight.reshape(ff, share),
        ]
    )
    if direct:
        experts_w = lax.all_gather(local, "dp", axis=0)
    else:
        experts_w = lax.all_gather(local, "dp", axis=2, tiled=True)[None]

    n1, q, k, v, kt, vt, gains, router = qkv_call(index, place, toks, pack, small_all, width)
    g_near = z_swap(after(out_grad, toks[3]), 1, z_size)
    g_far = z_swap(after(out_grad, toks[3]), 2, z_size)
    fwd = attn_fwd(piece_starts, place, z_size, q, k, vt, line)
    chances, ot = fwd[:2]
    atts = z_direct([after(fwd[2], g_near, g_far)] + [after(x, g_near, g_far) for x in fwd[3:]], z_size)
    if direct:
        wo_low, wo_high = dp_step(after(wo_low, n1), 4), dp_step(after(wo_high, n1), 2)
        wo_all = [dp_step(after(x, atts[1]), 1) for x in (wo_low, wo_high)]
    gs = [out_grad, g_near, g_far, z_swap(after(g_far, fwd[2]), 1, z_size)]
    mid, n2 = mid_call(index, [after(atts[0], gs[3])] + atts[1:], wo_all, tokens_in, gains)

    n2_near = z_swap(n2, 1, z_size)
    n2_far = z_swap(n2, 2, z_size)
    n2s = [n2, n2_near, n2_far, z_swap(after(n2_far, n2_near), 1, z_size)]
    hg, gg, ug, logit_grad, router_part = units_call(place, n2s, gs, sel, router, experts_w, unit)
    ngs = product_call([gg, ug], (0, 1), experts_w, z_size, [logit_grad, router], "normed_two_grads")
    passed = z_swap(ngs[3], 1, z_size)
    outs = product_call([after(hg, ngs[0])], (2,), experts_w, z_size, [], "expert_out")
    both = (ngs[2].astype(F32) + after(passed, outs[0]).astype(F32)).astype(BF)
    far = z_swap(both, 2, z_size)
    ng_near = z_swap(after(ngs[1], passed), 1, z_size)
    count = experts_w.shape[0]
    weight_grads = wgrad_call(experts_w.shape[0], [after(hg, both, *outs), gg, ug], n2s, gs)
    resid = resid_call(index, [after(ngs[0], weight_grads), ng_near, far], mid, out_grad, gains, wo_all)
    resid_grad, aog, gain_two = resid[:3]
    weight_grads = after(weight_grads, far, ng_near)
    if direct:
        expert_grads = lax.psum_scatter(weight_grads, "dp", scatter_dimension=0, tiled=False)
    else:
        expert_grads = lax.psum_scatter(weight_grads[0], "dp", scatter_dimension=2, tiled=True)
    out_passed = z_swap(after(outs[3], far), 1, z_size)
    dos = z_direct(resid[3:], z_size)
    wo_keep, wo_send = wo_grad_call(slots, atts, aog, count)
    out_both = (outs[2].astype(F32) + out_passed.astype(F32)).astype(BF)
    dos[0] = after(dos[0], wo_keep, out_both)
    out_far = z_swap(out_both, 2, z_size)
    out_near = z_swap(after(outs[1], out_both), 1, z_size)
    if direct:
        wo_grads = dp_fold(wo_keep, after(wo_send, *dos), 1)
    dq, dk, dv, diag = attn_bwd(place, dos, chances, q, k, v, kt, ot)
    if direct:
        wo_grads = dp_fold(*halves(wo_grads), 2)
        dq = after(dq, wo_grads)
    dq = after(dq, out_far, out_near)
    proj = proj_call(index, place, dq, dk, dv, pack, gain_two, router_part, toks)

    diag_at = (
        BLOCK * np.arange(total // BLOCK + 1)[:, None] - (BLOCK * (total // BLOCK - 2) + 1) - np.arange(2 * BLOCK)[None, :]
    )
    table = jnp.einsum("hbt,btk->hk", diag, jnp.asarray(onehot_of(diag_at)), precision=PRECISE)
    n1_passed = z_swap(proj[3], 1, z_size)
    if direct:
        table_rows = jnp.pad(table.reshape(1, -1), ((0, 7), (0, 0)))
        smalls = z_direct([proj[z_size]] * z_size, z_size)
        wo_grads = dp_fold(*halves(wo_grads), 4)[0]
        attn_keep, attn_send = attn_weights_call(slots, n1, dq, dk, dv, after(table_rows, wo_grads), smalls, 8)
        n1_passed = after(n1_passed, attn_keep)
    n1_both = (proj[2].astype(F32) + n1_passed.astype(F32)).astype(BF)
    n1_far = z_swap(n1_both, 2, z_size)
    n1_near = z_swap(after(proj[1], n1_both), 1, z_size)
    in_grad = final_call([proj[0], n1_near, n1_far], tokens_in, resid_grad, gains)
    out_parts = [outs[0], out_near, out_far]
    out_rows = (mid + functools.reduce(jnp.add, [p.astype(F32) for p in out_parts])).astype(BF)

    if direct:
        attn_grads = dp_fold(attn_keep, after(attn_send, n1_both), 1)
        attn_grads = dp_fold(*halves(attn_grads), 2)
        attn_grads = dp_fold(*halves(after(attn_grads, n1_far, n1_near)), 4)
        attn_grads = attn_grads[0].astype(F32)
        per = width // 128
        cut = attn_grads[: 3 * per * share].reshape(3, per, share, 128)
        cut = jnp.swapaxes(cut, 1, 2).reshape(3, share, width)
        smalls = attn_grads[3 * per * share :]
        grad_table = smalls[8, : heads * BUCKETS].reshape(heads, BUCKETS)
        mine = z_rank
        grad_wo = after(wo_grads, n1_near)
    else:
        cut = jnp.stack([jnp.dot(n1.T, d, preferred_element_type=F32) for d in (dq, dk, dv)])
        cut = lax.psum_scatter(cut, "dp", scatter_dimension=1, tiled=True)
        smalls = lax.psum(proj[z_size], ("dp", "tensor"))
        grad_table = lax.psum(table, "dp")
        mine = dp_rank * z_size + z_rank
        grad_wo = lax.psum_scatter(wo_keep[0], "dp", scatter_dimension=1, tiled=True)
    wo_parts = z_direct([grad_wo[width * c : width * (c + 1)] for c in range(z_size)], z_size)
    grad_wo = functools.reduce(jnp.add, [p.astype(F32) for p in wo_parts])
    per_device = depth // (dp_size * z_size)
    own = lax.dynamic_slice_in_dim(smalls, mine * per_device, per_device, 1)

    wide = expert_grads.astype(F32).reshape(3, EXPERTS, unit, share)
    return (
        out_rows,
        in_grad,
        own[0],
        cut[0],
        cut[1],
        cut[2],
        grad_wo,
        grad_table,
        own[1],
        own[2 : 2 + EXPERTS].T,
        jnp.swapaxes(wide[0], 1, 2),
        jnp.swapaxes(wide[1], 1, 2),
        wide[2],
    )


def solution(mesh):
    rows = P(("dp", "tensor"), None)
    grid = P("dp", "tensor")
    flat = P(("dp", "tensor"))
    weights = (P(None, "dp", "tensor"), P(None, "dp", "tensor"), P(None, "tensor", "dp"))
    in_specs = (rows, rows, P("dp"), grid, grid, grid, P("tensor", "dp"), P("tensor", None), P("dp"), P("dp", None))
    out_specs = (rows, rows, flat, grid, grid, grid, P("tensor", "dp"), P("tensor", None), flat, rows)
    return jax.shard_map(
        on_device,
        mesh=mesh,
        in_specs=in_specs + weights + (P("dp", None), P("dp", None)),
        out_specs=out_specs + weights,
        check_vma=False,
    )
```

```python
import functools

import jax
import jax.numpy as jnp
import numpy as np
from jax import lax
from jax.experimental import pallas as pl
from jax.experimental.pallas import tpu as pltpu
from jax.sharding import PartitionSpec as P

EXPERTS = 4
PIECE = 256
CAP = 640
BUCKETS = 32
EPSILON = 1e-06
PRECISE = lax.Precision.HIGHEST
LIMITS = (12, 16, 23, 32, 46, 64, 91)
MASKED = -1e30
BF = jnp.bfloat16
F32 = jnp.float32
BLOCK = 256
VMEM_LIMIT = 56 * 1024 * 1024


def params(semantics=None):
    return pltpu.CompilerParams(dimension_semantics=semantics, vmem_limit_bytes=VMEM_LIMIT)


def dot_nn(a, b):
    return lax.dot_general(a, b, (((1,), (0,)), ((), ())), preferred_element_type=F32)


def dot_nt(a, b):
    return lax.dot_general(a, b, (((1,), (1,)), ((), ())), preferred_element_type=F32)


def dot_tn(a, b):
    return lax.dot_general(a, b, (((0,), (0,)), ((), ())), preferred_element_type=F32)


def bucket_of(offsets):
    distance = np.abs(offsets)
    far = np.full_like(distance, 8)
    for bound in LIMITS:
        far = far + (distance >= bound)
    return np.where(distance < 8, distance, far) + np.where(offsets > 0, 16, 0)


def onehot_of(offsets):
    return (bucket_of(offsets)[..., None] == np.arange(BUCKETS)).astype(np.float32)


def cost(flops, nbytes):
    return pl.CostEstimate(flops=int(flops), bytes_accessed=int(nbytes), transcendentals=0)


def vspec():
    return pl.BlockSpec(memory_space=pltpu.VMEM)


def sspec():
    return pl.BlockSpec(memory_space=pltpu.SMEM)


def z_swap(x, mask, size):
    return lax.ppermute(x, "tensor", [(i, i ^ mask) for i in range(size)])


def z_gather(x, size):
    near = z_swap(x, 1, size)
    far = z_swap(x, 2, size)
    return [x, near, far, z_swap(far, 1, size)]


def z_direct(parts, size):
    return [parts[0]] + [z_swap(parts[mask], mask, size) for mask in range(1, size)]


def z_reduce(parts, size):
    passed = z_swap(parts[3], 1, size)
    far = z_swap((parts[2].astype(F32) + passed.astype(F32)).astype(BF), 2, size)
    return [parts[0], z_swap(parts[1], 1, size), far]


def after(x, *others):
    return lax.optimization_barrier((x,) + others)[0]


def dp_slots(ranks):
    x, y, core = (ranks >> 1) & 1, (ranks >> 2) & 1, ranks & 1
    return jnp.concatenate([x | (y << 1) | (core << 2), y | (x << 1) | (core << 2)])


def dp_step(x, bit):
    other = lax.ppermute(x, "dp", [(i, i ^ bit) for i in range(8)])
    return jnp.concatenate([x, other], 0)


def dp_fold(keep, send, bit):
    other = lax.ppermute(send, "dp", [(i, i ^ bit) for i in range(8)])
    return (keep.astype(F32) + other.astype(F32)).astype(keep.dtype)


def halves(x):
    return x[: x.shape[0] // 2], x[x.shape[0] // 2 :]


def dp_scatter_slots(ranks):
    return ((ranks >> 2) & 1) | (((ranks >> 1) & 1) << 1) | ((ranks & 1) << 2)


def parted(keep_ref, send_ref, order_ref):
    half = keep_ref.shape[0]
    for j in range(2 * half if half > 1 else 1):
        yield (keep_ref if j < half else send_ref), j % half, order_ref[j]


def join_rows(first_ref, last_ref, index_ref, count, rows):
    split = first_ref.shape[1]
    pieces = []
    for c in range(count):
        pieces.append(first_ref[index_ref[c], :, :])
        pieces.append(last_ref[index_ref[count + c], 0 : rows - split, :])
    return jnp.concatenate(pieces, 0)


def qkv_body(count, chunks, rows, index_ref, place_ref, *refs):
    toks = refs[:chunks]
    first_ref, last_ref, small_ref = refs[chunks : chunks + 3]
    n1_ref, q_ref, k_ref, v_ref, kt_ref, vt_ref, gains_ref, router_ref = refs[chunks + 3 :]
    depth = n1_ref.shape[1] // count
    weights = join_rows(first_ref, last_ref, index_ref, count, depth)
    width = q_ref.shape[1]
    if count == 1:
        small = [small_ref[r : r + 1, :] for r in range(2 + EXPERTS)]
    else:
        row = depth - first_ref.shape[1]
        lines = [small_ref[index_ref[count + d], row : row + 16, :].astype(F32)[0:1] for d in range(count)]
        small = [
            jnp.concatenate([x[:, depth * r : depth * (r + 1)] for x in lines], 1) for r in range(2 + EXPERTS)
        ]
    small = jnp.concatenate([x.astype(F32) for x in small] + [jnp.zeros((2, depth * count), F32)], 0)
    gains_ref[...] = small
    routers = jnp.concatenate([small[2:], jnp.zeros((10, depth * count), F32)], 0)
    router_ref[...] = jnp.zeros_like(router_ref)
    router_ref[0:16, :] = routers.astype(BF)
    gain = small[0:1, :]
    for c in range(chunks):
        at = pl.ds(pl.multiple_of(place_ref[c] * rows, rows), rows)
        x = toks[c][...].astype(F32)
        scale = lax.rsqrt(jnp.mean(x * x, axis=1, keepdims=True) + EPSILON)
        normed = (x * scale * gain).astype(BF)
        n1_ref[at, :] = normed
        out = dot_nn(normed, weights)
        q_ref[at, :] = (out[:, :width].astype(BF).astype(F32) * 0.125).astype(BF)
        key = out[:, width : 2 * width]
        value = out[:, 2 * width :]
        k_ref[at, :] = key.astype(BF)
        v_ref[at, :] = value.astype(BF)
        kt_ref[:, at] = jnp.transpose(key).astype(BF)
        vt_ref[:, at] = jnp.transpose(value).astype(BF)


def qkv_call(index, place, toks, pack, small, width):
    chunks, rows, depth = len(toks), toks[0].shape[0], toks[0].shape[1]
    total = chunks * rows
    shapes = [(total, depth)] + [(total, width)] * 3 + [(width, total)] * 2
    return pl.pallas_call(
        functools.partial(qkv_body, pack[0].shape[0], chunks, rows),
        in_specs=[sspec(), sspec()] + [vspec()] * (chunks + 3),
        out_specs=[vspec()] * 8,
        out_shape=[jax.ShapeDtypeStruct(s, BF) for s in shapes]
        + [jax.ShapeDtypeStruct((8, depth), F32), jax.ShapeDtypeStruct((128, depth), BF)],
        compiler_params=params(),
        cost_estimate=cost(2 * total * depth * 3 * width, 8 * total * depth),
        name="norm_qkv",
    )(index, place, *toks, *pack, small)


def extent_of(i, total):
    return min(BLOCK * (i + 2), total)


def fwd_body(total, chunks, starts_ref, place_ref, q_ref, k_ref, vt_ref, line_ref, p_ref, ot_ref, *refs):
    atts = refs[:chunks]
    strip_ref, mask_ref, all_ref = refs[chunks:]
    head = pl.program_id(0)
    heads = pl.num_programs(0)
    blocks = total // BLOCK
    width = q_ref.shape[1]
    dim = width // 4

    @pl.when(head == 0)
    def _():
        def label(pos):
            first = (pos >= starts_ref[0, 0]) & (pos < starts_ref[0, 0] + PIECE)
            second = (pos >= starts_ref[0, 1]) & (pos < starts_ref[0, 1] + PIECE)
            return first, second

        for i in range(blocks):
            for j in (i, i + 1):
                if j >= blocks:
                    continue
                kpos = lax.broadcasted_iota(jnp.int32, (BLOCK, BLOCK), 0) + BLOCK * j
                qpos = lax.broadcasted_iota(jnp.int32, (BLOCK, BLOCK), 1) + BLOCK * i
                k1, k2 = label(kpos)
                q1, q2 = label(qpos)
                seen = (kpos <= qpos) | (k1 & q1) | (k2 & q2)
                mask_ref[2 * i + j - i] = jnp.where(seen, 0.0, MASKED)

    for beta in range(blocks + 1):
        start = BLOCK * (blocks - beta)
        window = line_ref[0, 0:1, start : start + 2 * BLOCK]
        spread = jnp.broadcast_to(window, (BLOCK, 2 * BLOCK))
        rolled = pltpu.roll(spread, BLOCK + 1, 1, stride=1, stride_axis=0)
        strip_ref[BLOCK * beta : BLOCK * (beta + 1), :] = rolled[:, :BLOCK]

    lanes = lax.broadcasted_iota(jnp.int32, (2 * BLOCK, width), 1)
    own = (lanes >= head * dim) & (lanes < (head + 1) * dim)
    at_head = pl.ds(pl.multiple_of(head * dim, dim), dim)
    for pair in range(0, blocks, 2):
        both = slice(BLOCK * pair, BLOCK * (pair + 2))
        reach = extent_of(pair + 1, total)
        q_rows = q_ref[both, :]
        q_own = jnp.where(own, q_rows, jnp.zeros_like(q_rows))
        raw = dot_nt(k_ref[0:reach, :], q_own)
        for i in (pair, pair + 1):
            extent = extent_of(i, total)
            cols = slice(BLOCK * i, BLOCK * (i + 1))
            base = BLOCK * (blocks - 1 - i)
            scores = raw[0:extent, BLOCK * (i - pair) : BLOCK * (i - pair + 1)] + strip_ref[base : base + extent, :]
            parts = [scores[BLOCK * j : BLOCK * (j + 1)] for j in range(extent // BLOCK)]
            for j in (i, i + 1):
                if j < blocks:
                    parts[j] = parts[j] + mask_ref[2 * i + j - i]
            top = functools.reduce(jnp.maximum, parts)
            top = jnp.max(top, axis=0, keepdims=True)
            parts = [jnp.exp(part - top) for part in parts]
            total_sum = jnp.sum(functools.reduce(jnp.add, parts), axis=0, keepdims=True)
            inverse = 1.0 / total_sum
            p_ref[0, 0:extent, cols] = jnp.concatenate([(part * inverse).astype(BF) for part in parts], 0)
            if extent < total:
                p_ref[0, extent : extent + BLOCK, cols] = jnp.zeros((BLOCK, BLOCK), BF)
        ot_ref[at_head, both] = dot_nn(vt_ref[at_head, 0:reach], p_ref[0, 0:reach, both])

    @pl.when(head == heads - 1)
    def _():
        mixed = ot_ref[...]
        all_ref[...] = jnp.transpose(mixed).astype(BF)
        rows = total // chunks
        for c in range(chunks):
            at = pl.ds(pl.multiple_of(place_ref[c] * rows, rows), rows)
            atts[c][...] = all_ref[at, :]


def attn_fwd(starts, place, chunks, q, k, vt, line):
    total, width = q.shape
    heads = line.shape[0]
    blocks = total // BLOCK
    whole = lambda shape: pl.BlockSpec(shape, lambda h: (0,) * len(shape))
    return pl.pallas_call(
        functools.partial(fwd_body, total, chunks),
        grid=(heads,),
        in_specs=[
            sspec(),
            sspec(),
            whole((total, width)),
            whole((total, width)),
            whole((width, total)),
            pl.BlockSpec((1, 1, line.shape[2]), lambda h: (h, 0, 0)),
        ],
        out_specs=[
            pl.BlockSpec((1, total, total), lambda h: (h, 0, 0)),
            whole((width, total)),
        ]
        + [whole((total // chunks, width))] * chunks,
        out_shape=[
            jax.ShapeDtypeStruct((heads, total, total), BF),
            jax.ShapeDtypeStruct((width, total), F32),
        ]
        + [jax.ShapeDtypeStruct((total // chunks, width), BF)] * chunks,
        scratch_shapes=[
            pltpu.VMEM((BLOCK * (blocks + 1), BLOCK), F32),
            pltpu.VMEM((2 * blocks, BLOCK, BLOCK), F32),
            pltpu.VMEM((total, width), BF),
        ],
        compiler_params=params(("arbitrary",)),
        cost_estimate=cost(heads * 4 * total * total * width, 10 * total * total),
        name="attn_forward",
    )(starts, place, q, k, vt, line)


def diagonal_sums(acc):
    half = BLOCK // 2
    low, high = acc[:half], acc[half:]
    rows = jnp.concatenate(
        [high[:, :half], high[:, half:] + low[:, :half], low[:, half:], jnp.zeros((half, half), F32)], 1
    )
    step = half // 2
    while step >= 8:
        rows = rows[step:] + pltpu.roll(rows[:step], step, 1)
        step //= 2
    index = lax.broadcasted_iota(jnp.int32, rows.shape, 0)
    for step in (4, 2, 1):
        rows = jnp.where((index & step) == 0, pltpu.roll(rows, step, 1), rows)
    return jnp.sum(rows, axis=0, keepdims=True)


def bwd_body(total, chunks, place_ref, *refs):
    grads = refs[:chunks]
    p_ref, q_ref, k_ref, v_ref, kt_ref, ot_ref = refs[chunks : chunks + 6]
    dq_ref, dk_ref, dv_ref, diag_ref = refs[chunks + 6 : chunks + 10]
    do_ref, dot_ref, dqt_ref, dka_ref, dva_ref, ds_ref, acc_ref = refs[chunks + 10 :]
    head = pl.program_id(0)
    heads = pl.num_programs(0)
    blocks = total // BLOCK
    rows = total // chunks
    width = q_ref.shape[1]
    dim = width // 4

    @pl.when(head == 0)
    def _():
        for c in range(chunks):
            at = pl.ds(pl.multiple_of(place_ref[c] * rows, rows), rows)
            do_ref[at, :] = grads[c][...]
        dot_ref[...] = jnp.transpose(do_ref[...].astype(F32))
        ds_ref[...] = jnp.zeros_like(ds_ref)
        dka_ref[...] = jnp.zeros_like(dka_ref)
        dva_ref[...] = jnp.zeros_like(dva_ref)

    at_head = pl.ds(pl.multiple_of(head * dim, dim), dim)
    inner = jnp.sum(dot_ref[at_head, :] * ot_ref[at_head, :], axis=0, keepdims=True)
    lanes = lax.broadcasted_iota(jnp.int32, (total, width), 1)
    own = (lanes >= head * dim) & (lanes < (head + 1) * dim)
    q_own = jnp.where(own, q_ref[...], jnp.zeros_like(q_ref))
    do_own = jnp.where(own, do_ref[...], jnp.zeros_like(do_ref))
    written = 0
    for pair in range(blocks - 2, -1, -2):
        both = slice(BLOCK * pair, BLOCK * (pair + 2))
        reach = extent_of(pair + 1, total)
        pair_grad = dot_nt(v_ref[0:reach, :], do_own[both, :])
        for i in (pair + 1, pair):
            extent = extent_of(i, total)
            cols = slice(BLOCK * i, BLOCK * (i + 1))
            chance_grad = pair_grad[0:extent, BLOCK * (i - pair) : BLOCK * (i - pair + 1)]
            chances = p_ref[0, 0:extent, cols].astype(F32)
            score_grad = (chances * (chance_grad - inner[:, cols])).astype(BF)
            ds_ref[0:extent, cols] = score_grad
            base = BLOCK * (blocks - 1 - i)
            wide = score_grad.astype(F32)
            if i == blocks - 1:
                acc_ref[0:extent, :] = wide
                written = extent
            else:
                old = written - base
                acc_ref[base:written, :] += wide[:old]
                if base + extent > written:
                    acc_ref[written : base + extent, :] = wide[old:]
                    written = base + extent
        dqt_ref[at_head, both] = dot_nn(kt_ref[at_head, 0:reach], ds_ref[0:reach, both])
    for pair in range(0, blocks, 2):
        first = max(0, BLOCK * (pair - 1))
        keys = slice(BLOCK * pair, BLOCK * (pair + 2))
        dka_ref[keys, :] += dot_nn(ds_ref[keys, first:], q_own[first:, :])
        dva_ref[keys, :] += dot_nn(p_ref[0, keys, first:], do_own[first:, :])
    for beta in range(blocks + 1):
        diag_ref[0, beta : beta + 1, :] = diagonal_sums(acc_ref[BLOCK * beta : BLOCK * (beta + 1), :])

    @pl.when(head == heads - 1)
    def _():
        dq_ref[...] = (jnp.transpose(dqt_ref[...]) * 0.125).astype(BF)
        dk_ref[...] = dka_ref[...].astype(BF)
        dv_ref[...] = dva_ref[...].astype(BF)


def attn_bwd(place, grads, chances, q, k, v, kt, ot):
    total, width = q.shape
    heads = chances.shape[0]
    blocks = total // BLOCK
    chunks = len(grads)
    whole = lambda shape: pl.BlockSpec(shape, lambda h: (0,) * len(shape))
    return pl.pallas_call(
        functools.partial(bwd_body, total, chunks),
        grid=(heads,),
        in_specs=[sspec()]
        + [whole(grads[0].shape)] * chunks
        + [pl.BlockSpec((1, total, total), lambda h: (h, 0, 0))]
        + [whole((total, width))] * 3
        + [whole((width, total))] * 2,
        out_specs=[whole((total, width))] * 3 + [pl.BlockSpec((1, blocks + 1, 2 * BLOCK), lambda h: (h, 0, 0))],
        out_shape=[jax.ShapeDtypeStruct((total, width), BF)] * 3
        + [jax.ShapeDtypeStruct((heads, blocks + 1, 2 * BLOCK), F32)],
        scratch_shapes=[
            pltpu.VMEM((total, width), BF),
            pltpu.VMEM((width, total), F32),
            pltpu.VMEM((width, total), F32),
            pltpu.VMEM((total, width), F32),
            pltpu.VMEM((total, width), F32),
            pltpu.VMEM((total, total), BF),
            pltpu.VMEM((BLOCK * (blocks + 1), BLOCK), F32),
        ],
        compiler_params=params(("arbitrary",)),
        cost_estimate=cost(heads * 160 * total * total * width, 10 * total * total),
        name="attn_backward",
    )(place, *grads, chances, q, k, v, kt, ot)


def join_lanes(low_ref, high_ref, index_ref, count, slot):
    low = [low_ref[index_ref[c], slot] for c in range(count)]
    high = [high_ref[index_ref[count + c], slot] for c in range(count)]
    return jnp.concatenate([jnp.concatenate(low, 1), jnp.concatenate(high, 1)], 0)


def mid_body(count, chunks, index_ref, *refs):
    atts = refs[:chunks]
    low_ref, high_ref, tok_ref, gain_ref, mid_ref, n2_ref = refs[chunks:]
    u = tok_ref[...].astype(F32)
    for c in range(chunks):
        u = u + dot_nn(atts[c][...], join_lanes(low_ref, high_ref, index_ref, count, c))
    mid_ref[...] = u
    scale = lax.rsqrt(jnp.mean(u * u, axis=1, keepdims=True) + EPSILON)
    n2_ref[...] = (u * scale * gain_ref[1:2, :]).astype(BF)


def mid_call(index, atts, w_out, tok, gains):
    chunks = len(atts)
    return pl.pallas_call(
        functools.partial(mid_body, w_out[0].shape[0], chunks),
        in_specs=[sspec()] + [vspec()] * (chunks + 4),
        out_specs=[vspec()] * 2,
        out_shape=[jax.ShapeDtypeStruct(tok.shape, F32), jax.ShapeDtypeStruct(tok.shape, BF)],
        compiler_params=params(),
        cost_estimate=cost(2 * tok.shape[0] * tok.shape[1] ** 2, 4 * tok.shape[1] ** 2),
        name="out_projection_norm",
    )(index, *atts, *w_out, tok, gains)


def split_dot(a, b, dot):
    high = a.astype(BF)
    low = (a - high.astype(F32)).astype(BF)
    return dot(high, b) + dot(low, b)


def joined(ref, which):
    if ref.shape[0] == 1:
        return ref[0, which]
    return jnp.concatenate([ref[d, which] for d in range(ref.shape[0])], 1)


def units_body(chunks, unit, place_ref, *refs):
    n2s = refs[:chunks]
    gs = refs[chunks : 2 * chunks]
    sel_ref, rout_ref, w_ref = refs[2 * chunks : 2 * chunks + 3]
    hg_ref, gg_ref, ug_ref, lg_ref, rpart_ref = refs[2 * chunks + 3 : 2 * chunks + 8]
    n2_ref, g_ref, gate_ref, sum_ref, prob_ref, pick_ref = refs[2 * chunks + 8 :]
    step = pl.program_id(0)
    steps = pl.num_programs(0)
    rows = n2s[0].shape[0]
    tokens = chunks * rows
    lane = lax.broadcasted_iota(jnp.int32, (tokens, 128), 1)

    @pl.when(step == 0)
    def _():
        for c in range(chunks):
            n2_ref[rows * c : rows * (c + 1), :] = n2s[c][...]
            g_ref[rows * c : rows * (c + 1), :] = gs[c][...]
        logits = dot_nt(n2_ref[...], rout_ref[...])
        logits = jnp.where(lane < EXPERTS, logits, MASKED)
        raised = jnp.exp(logits - jnp.max(logits, axis=1, keepdims=True))
        prob_ref[...] = raised / jnp.sum(raised, axis=1, keepdims=True)
        for c in range(chunks):
            at = pl.ds(pl.multiple_of(place_ref[c] * rows, rows), rows)
            pick_ref[rows * c : rows * (c + 1), :] = sel_ref[at, :]
        gates = prob_ref[...] * pick_ref[...]
        for e in range(EXPERTS):
            one = jnp.sum(jnp.where(lane == e, gates, 0.0), axis=1, keepdims=True)
            gate_ref[e] = jnp.broadcast_to(one, (tokens, 128))
        sum_ref[...] = jnp.zeros_like(sum_ref)

    wg, wu, wd = joined(w_ref, 0), joined(w_ref, 1), joined(w_ref, 2)
    pre = dot_nt(n2_ref[...], jnp.concatenate([wg, wu], 0))
    gate_pre, up_pre = pre[:, : wg.shape[0]], pre[:, wg.shape[0] :]
    raw = dot_nt(g_ref[...], wd)
    c0 = float(np.sqrt(2.0 / np.pi))
    square = gate_pre * gate_pre
    th = jnp.tanh(gate_pre * (c0 + (c0 * 0.044715) * square))
    half = 0.5 + 0.5 * th
    act = gate_pre * half
    slope = half + gate_pre * (0.5 * c0 + (1.5 * c0 * 0.044715) * square) * (1.0 - th * th)
    hidden = act * up_pre
    prod = raw * hidden
    width = hg_ref.shape[1]
    e_low = (step * width) // unit
    e_high = (step * width + width - 1) // unit
    bound = jnp.where(e_high > e_low, unit * e_high - step * width, width)
    lows = []
    for m in range(width // 128):
        is_low = lane + 128 * m < bound
        part = slice(128 * m, 128 * (m + 1))
        gate = jnp.where(is_low, gate_ref[e_low], gate_ref[e_high])
        lows.append(jnp.where(is_low, prod[:, part], 0.0))
        hg_ref[:, part] = (gate * hidden[:, part]).astype(BF)
        hidden_grad = gate * raw[:, part]
        gg_ref[:, part] = (hidden_grad * up_pre[:, part] * slope[:, part]).astype(BF)
        ug_ref[:, part] = (hidden_grad * act[:, part]).astype(BF)
    sum_ref[e_low] += functools.reduce(jnp.add, lows)

    @pl.when(e_high > e_low)
    def _():
        every = [prod[:, 128 * m : 128 * (m + 1)] - lows[m] for m in range(width // 128)]
        sum_ref[e_high] += functools.reduce(jnp.add, every)

    @pl.when(step == steps - 1)
    def _():
        grad = jnp.zeros((tokens, 128), F32)
        for e in range(EXPERTS):
            grad = grad + jnp.where(lane == e, jnp.sum(sum_ref[e], axis=1, keepdims=True), 0.0)
        grad = grad * pick_ref[...]
        probs = prob_ref[...]
        logit_grad = probs * (grad - jnp.sum(probs * grad, axis=1, keepdims=True))
        lg_ref[...] = logit_grad
        rpart_ref[...] = split_dot(logit_grad, n2_ref[...], dot_tn)[0:8, :]


def units_call(place, n2s, gs, sel, router, weights, unit):
    chunks, rows, depth = len(n2s), n2s[0].shape[0], n2s[0].shape[1]
    count, _, ff, part = weights.shape
    tokens = chunks * rows
    whole = lambda shape: pl.BlockSpec(shape, lambda s: (0,) * len(shape))
    return pl.pallas_call(
        functools.partial(units_body, chunks, unit),
        grid=(ff // BLOCK,),
        in_specs=[sspec()]
        + [whole((rows, depth))] * (2 * chunks)
        + [whole(sel.shape), whole(router.shape), pl.BlockSpec((count, 3, BLOCK, part), lambda s: (0, 0, s, 0))],
        out_specs=[pl.BlockSpec((tokens, BLOCK), lambda s: (0, s))] * 3 + [whole((tokens, 128)), whole((8, depth))],
        out_shape=[jax.ShapeDtypeStruct((tokens, ff), BF)] * 3
        + [jax.ShapeDtypeStruct((tokens, 128), F32), jax.ShapeDtypeStruct((8, depth), F32)],
        scratch_shapes=[
            pltpu.VMEM((tokens, depth), BF),
            pltpu.VMEM((tokens, depth), BF),
            pltpu.VMEM((EXPERTS, tokens, 128), F32),
            pltpu.VMEM((EXPERTS, tokens, 128), F32),
            pltpu.VMEM((tokens, 128), F32),
            pltpu.VMEM((tokens, 128), F32),
        ],
        compiler_params=params(("arbitrary",)),
        cost_estimate=cost(6 * tokens * depth * ff, 6 * depth * ff + 12 * tokens * depth),
        name="expert_units",
    )(place, *n2s, *gs, sel, router, weights)


def product_body(terms, chunks, extra, *refs):
    xs = refs[:terms]
    ws = refs[terms : 2 * terms]
    at = 2 * terms + (2 if extra else 0)
    outs = refs[at : at + chunks]
    total = None
    for x, w in zip(xs, ws):
        term = dot_nn(x[...], joined(w, 0))
        total = term if total is None else total + term
    if extra:
        lg_ref, rout_ref = refs[2 * terms : 2 * terms + 2]
        total = total + split_dot(lg_ref[...], rout_ref[...], dot_nn)
    rows = outs[0].shape[0]
    for c in range(chunks):
        outs[c][...] = total[rows * c : rows * (c + 1)].astype(BF)


def product_call(xs, picks, weights, chunks, extra, name):
    tokens, ff = xs[0].shape
    count, _, _, part = weights.shape
    depth = count * part
    rows = tokens // chunks
    per = max(1, BLOCK // part)
    wide = min(part * per, BLOCK)
    whole = lambda shape: pl.BlockSpec(shape, lambda s: (0,) * len(shape))
    place_at = (lambda i, s: (s, i, 0, 0)) if count > 1 else (lambda i, s: (0, i, 0, s))
    w_specs = [pl.BlockSpec((min(per, count), 1, ff, wide // min(per, count)), functools.partial(place_at, i)) for i in picks]
    return pl.pallas_call(
        functools.partial(product_body, len(xs), chunks, bool(extra)),
        grid=(depth // wide,),
        in_specs=[whole((tokens, ff))] * len(xs)
        + w_specs
        + ([whole(extra[0].shape), pl.BlockSpec((128, wide), lambda s: (0, s))] if extra else []),
        out_specs=[pl.BlockSpec((rows, wide), lambda s: (0, s))] * chunks,
        out_shape=[jax.ShapeDtypeStruct((rows, depth), BF)] * chunks,
        compiler_params=params(("arbitrary",)),
        cost_estimate=cost(2 * len(xs) * tokens * depth * ff, 4 * len(xs) * depth * ff),
        name=name,
    )(*xs, *([weights] * len(xs)), *extra)


def wgrad_body(count, chunks, *refs):
    hg_ref, gg_ref, ug_ref = refs[:3]
    n2s = refs[3 : 3 + chunks]
    gs = refs[3 + chunks : 3 + 2 * chunks]
    out_ref, n2_ref, g_ref = refs[3 + 2 * chunks :]
    part = out_ref.shape[3]
    rows = n2s[0].shape[0]

    @pl.when(pl.program_id(0) == 0)
    def _():
        for c in range(chunks):
            n2_ref[rows * c : rows * (c + 1), :] = n2s[c][...]
            g_ref[rows * c : rows * (c + 1), :] = gs[c][...]

    width = hg_ref.shape[1]
    pair = dot_tn(jnp.concatenate([gg_ref[...], ug_ref[...]], 1), n2_ref[...]).astype(BF)
    down = dot_tn(hg_ref[...], g_ref[...]).astype(BF)
    for which, total in enumerate((pair[:width], pair[width:], down)):
        for d in range(count):
            out_ref[d, which] = total[:, part * d : part * (d + 1)]


def wgrad_call(count, kept, n2s, gs):
    tokens, ff = kept[0].shape
    chunks, rows, depth = len(n2s), n2s[0].shape[0], n2s[0].shape[1]
    whole = lambda shape: pl.BlockSpec(shape, lambda s: (0,) * len(shape))
    return pl.pallas_call(
        functools.partial(wgrad_body, count, chunks),
        grid=(ff // BLOCK,),
        in_specs=[pl.BlockSpec((tokens, BLOCK), lambda s: (0, s))] * 3 + [whole((rows, depth))] * (2 * chunks),
        out_specs=pl.BlockSpec((count, 3, BLOCK, depth // count), lambda s: (0, 0, s, 0)),
        out_shape=jax.ShapeDtypeStruct((count, 3, ff, depth // count), BF),
        scratch_shapes=[pltpu.VMEM((tokens, depth), BF), pltpu.VMEM((tokens, depth), BF)],
        compiler_params=params(("arbitrary",)),
        cost_estimate=cost(6 * tokens * depth * ff, 12 * depth * ff),
        name="expert_weight_grads",
    )(*kept, *n2s, *gs)


def norm_back(grad, u, gain):
    scale = lax.rsqrt(jnp.mean(u * u, axis=1, keepdims=True) + EPSILON)
    m = grad * gain
    back = scale * m - u * (scale * scale * scale) * jnp.mean(u * m, axis=1, keepdims=True)
    return back, jnp.sum(grad * u * scale, axis=0, keepdims=True)


def resid_body(count, chunks, terms, index_ref, *refs):
    parts = refs[:terms]
    mid_ref, g_ref, gains_ref, low_ref, high_ref = refs[terms : terms + 5]
    rest = refs[terms + 5 :]
    resid_ref, aog_ref, gain_ref = rest[:3]
    dos = rest[3:]
    grad = functools.reduce(jnp.add, [p[...].astype(F32) for p in parts])
    back, gain_part = norm_back(grad, mid_ref[...], gains_ref[1:2, :])
    resid = g_ref[...].astype(F32) + back
    resid_ref[...] = resid
    low = resid.astype(BF)
    aog_ref[...] = low
    gain_ref[...] = jnp.broadcast_to(gain_part, gain_ref.shape)
    for c in range(chunks):
        dos[c][...] = dot_nt(low, join_lanes(low_ref, high_ref, index_ref, count, c)).astype(BF)


def resid_call(index, parts, mid, grad, gains, w_out):
    chunks, terms = w_out[0].shape[1], len(parts)
    shape = mid.shape
    width = 2 * w_out[0].shape[2]
    return pl.pallas_call(
        functools.partial(resid_body, w_out[0].shape[0], chunks, terms),
        in_specs=[sspec()] + [vspec()] * (terms + 5),
        out_specs=[vspec()] * (3 + chunks),
        out_shape=[
            jax.ShapeDtypeStruct(shape, F32),
            jax.ShapeDtypeStruct(shape, BF),
            jax.ShapeDtypeStruct((8, shape[1]), F32),
        ]
        + [jax.ShapeDtypeStruct((shape[0], width), BF)] * chunks,
        compiler_params=params(),
        cost_estimate=cost(2 * shape[0] * shape[1] ** 2, 4 * shape[1] ** 2),
        name="resid_grad",
    )(index, *parts, mid, grad, gains, *w_out)


def final_body(chunks, *refs):
    parts = refs[:chunks]
    tok_ref, resid_ref, gains_ref, out_ref = refs[chunks:]
    grad = functools.reduce(jnp.add, [p[...].astype(F32) for p in parts])
    back, _ = norm_back(grad, tok_ref[...].astype(F32), gains_ref[0:1, :])
    out_ref[...] = resid_ref[...] + back


def final_call(parts, tok, resid, gains):
    return pl.pallas_call(
        functools.partial(final_body, len(parts)),
        in_specs=[vspec()] * (len(parts) + 3),
        out_specs=vspec(),
        out_shape=jax.ShapeDtypeStruct(tok.shape, F32),
        compiler_params=params(),
        cost_estimate=cost(20 * tok.size, 12 * tok.size),
        name="in_grad",
    )(*parts, tok, resid, gains)


def proj_body(count, chunks, rows, index_ref, place_ref, dq_ref, dk_ref, dv_ref, first_ref, last_ref, two_ref, router_ref, *refs):
    toks = refs[:chunks]
    outs = refs[chunks : 2 * chunks]
    gain_ref = refs[2 * chunks]
    depth = outs[0].shape[1]
    width = dq_ref.shape[1]
    weights = join_rows(first_ref, last_ref, index_ref, count, depth // count)
    gain = jnp.zeros((1, depth), F32)
    for c in range(chunks):
        at = pl.ds(pl.multiple_of(place_ref[c] * rows, rows), rows)
        grad = dot_nt(dq_ref[at, :], weights[:, :width])
        grad = grad + dot_nt(dk_ref[at, :], weights[:, width : 2 * width])
        grad = grad + dot_nt(dv_ref[at, :], weights[:, 2 * width :])
        outs[c][...] = grad.astype(BF)
        x = toks[c][...].astype(F32)
        scale = lax.rsqrt(jnp.mean(x * x, axis=1, keepdims=True) + EPSILON)
        gain = gain + jnp.sum(grad * x * scale, axis=0, keepdims=True)
    blank = jnp.zeros((6 - EXPERTS, depth), F32)
    gain_ref[...] = jnp.concatenate([gain, two_ref[0:1, :], router_ref[0:EXPERTS, :], blank], 0)


def proj_call(index, place, dq, dk, dv, pack, gain_two, router_part, toks):
    chunks, rows, depth = len(toks), toks[0].shape[0], toks[0].shape[1]
    return pl.pallas_call(
        functools.partial(proj_body, pack[0].shape[0], chunks, rows),
        in_specs=[sspec(), sspec()] + [vspec()] * (7 + chunks),
        out_specs=[vspec()] * (chunks + 1),
        out_shape=[jax.ShapeDtypeStruct((rows, depth), BF)] * chunks + [jax.ShapeDtypeStruct((8, depth), F32)],
        compiler_params=params(),
        cost_estimate=cost(6 * chunks * rows * depth * dq.shape[1], 8 * chunks * rows * depth),
        name="projection_grads",
    )(index, place, dq, dk, dv, *pack, gain_two, router_part, *toks)


def attn_weights_body(count, smalls, slot_ref, n1_ref, dq_ref, dk_ref, dv_ref, table_ref, *refs):
    keep_ref, send_ref, small_ref, *grad_refs = refs[smalls:]
    small_ref[...] = functools.reduce(jnp.add, [r[...] for r in refs[:smalls]])
    depth = n1_ref.shape[1]
    width = dq_ref.shape[1]
    part = depth // count
    normed = n1_ref[...]
    pieces = width // 128
    for ref, grad_ref in zip((dq_ref, dk_ref, dv_ref), grad_refs):
        grad_ref[...] = dot_tn(normed, ref[...]).astype(BF)
    for out_ref, slot, d in parted(keep_ref, send_ref, slot_ref):
        rows = pl.ds(pl.multiple_of(d * part, 128), part)
        for m, grad_ref in enumerate(grad_refs):
            for piece in range(pieces):
                at = (m * pieces + piece) * part
                out_ref[slot, at : at + part, :] = grad_ref[rows, 128 * piece : 128 * (piece + 1)]
        at = 3 * pieces * part
        value = jnp.concatenate([small_ref[:, rows], table_ref[...]], 0).astype(BF)
        out_ref[slot, at : at + 16, :] = value


def attn_weights_call(slots, n1, dq, dk, dv, table, smalls, count):
    total, depth = n1.shape
    width = dq.shape[1]
    part = depth // count
    return pl.pallas_call(
        functools.partial(attn_weights_body, count, len(smalls)),
        in_specs=[sspec()] + [vspec()] * (5 + len(smalls)),
        out_specs=[vspec()] * 2,
        out_shape=[jax.ShapeDtypeStruct((count // 2, 3 * width * part // 128 + 16, 128), BF)] * 2,
        scratch_shapes=[pltpu.VMEM((8, depth), F32)] + [pltpu.VMEM((depth, width), BF)] * 3,
        compiler_params=params(),
        cost_estimate=cost(6 * total * depth * width, 8 * total * depth),
        name="attn_weight_grads",
    )(slots, n1, dq, dk, dv, table, *smalls)


def wo_grad_body(count, chunks, slot_ref, *refs):
    atts = refs[:chunks]
    aog_ref, keep_ref, send_ref, grad_ref = refs[chunks:]
    width = atts[0].shape[1]
    part = grad_ref.shape[1] // count
    for c in range(chunks):
        at = slice(c * width, (c + 1) * width)
        grad_ref[at, :] = dot_tn(atts[c][...], aog_ref[...]).astype(BF)
    for out_ref, slot, d in parted(keep_ref, send_ref, slot_ref):
        out_ref[slot] = grad_ref[:, pl.ds(pl.multiple_of(d * part, 128), part)]


def wo_grad_call(slots, atts, aog, count):
    chunks, width = len(atts), atts[0].shape[1]
    rows, depth = aog.shape
    return pl.pallas_call(
        functools.partial(wo_grad_body, count, chunks),
        in_specs=[sspec()] + [vspec()] * (chunks + 1),
        out_specs=[vspec()] * 2,
        out_shape=[jax.ShapeDtypeStruct((max(1, count // 2), chunks * width, depth // count), BF)] * 2,
        scratch_shapes=[pltpu.VMEM((chunks * width, depth), BF)],
        compiler_params=params(),
        cost_estimate=cost(2 * rows * depth * chunks * width, 4 * depth * chunks * width),
        name="w_output_grad",
    )(slots, *atts, aog)


def kept_choices(ids):
    lanes = jnp.arange(128, dtype=jnp.int32)[None, :]
    expert_range = jnp.arange(EXPERTS, dtype=jnp.int32)[None, :]
    first = (ids[:, 0:1] == expert_range).astype(jnp.int32)
    second = (ids[:, 1:2] == expert_range).astype(jnp.int32)
    runs = jnp.cumsum(jnp.concatenate([first, second], 1), axis=0)
    first_run = runs[:, :EXPERTS]
    second_run = runs[:, EXPERTS:] + first_run[-1][None, :]
    place_one = jnp.sum(first_run * first, axis=1, keepdims=True) - 1
    place_two = jnp.sum(second_run * second, axis=1, keepdims=True) - 1
    kept = ((ids[:, 0:1] == lanes) & (place_one < CAP)) | ((ids[:, 1:2] == lanes) & (place_two < CAP))
    return kept.astype(F32)


def on_device(
    tokens_in,
    out_grad,
    attn_gain,
    w_query,
    w_key,
    w_value,
    w_output,
    rel_table,
    moe_gain,
    w_router,
    w_gate,
    w_up,
    down_weight,
    expert_ids,
    piece_starts,
):
    rows, depth = tokens_in.shape
    width = w_query.shape[1]
    z_size = lax.axis_size("tensor")
    dp_size = lax.axis_size("dp")
    z_rank = lax.axis_index("tensor").astype(jnp.int32)
    dp_rank = lax.axis_index("dp").astype(jnp.int32)
    total = rows * z_size
    share = depth // dp_size
    unit = w_gate.shape[2]
    ff = EXPERTS * unit
    heads = rel_table.shape[0]
    direct = dp_size == 8 and share == 128
    place = z_rank ^ jnp.arange(z_size, dtype=jnp.int32)

    near = z_swap(tokens_in, 1, z_size)
    far = z_swap(tokens_in, 2, z_size)
    line_at = 2 * BLOCK - 1 - np.arange(total + 2 * BLOCK)
    line = jnp.dot(rel_table, jnp.asarray(onehot_of(line_at).T), precision=PRECISE)[:, None, :]
    sel = kept_choices(expert_ids)
    toks = [tokens_in, near, far, z_swap(after(far, near, sel, line), 1, z_size)]
    w_output_late = after(w_output, far)
    small = jnp.concatenate([attn_gain, moe_gain, w_router.T.reshape(-1)])[None, :]
    packed = jnp.concatenate([w_query, w_key, w_value], 1)
    wo_slots = jnp.stack(z_direct([w_output_late] * z_size, z_size))[None]
    ranks = dp_rank ^ jnp.arange(8, dtype=jnp.int32)
    half = wo_slots.shape[2] // 2
    if direct:
        index = dp_slots(ranks)
        slots = dp_rank ^ dp_scatter_slots(jnp.arange(8, dtype=jnp.int32))
        first = dp_step(packed[:80][None], 2)
        last = dp_step(jnp.concatenate([packed[80:], small, jnp.zeros((15, packed.shape[1]), BF)], 0)[None], 4)
        first, last = dp_step(after(first, near), 4), dp_step(after(last, near), 2)
        wo_low = dp_step(after(wo_slots[:, :, :half], near, far), 2)
        wo_high = dp_step(after(wo_slots[:, :, half:], near, far), 4)
        first = dp_step(after(first, toks[3], wo_low, wo_high), 1)
        last = dp_step(after(last, toks[3], wo_low, wo_high), 1)
        pack, small_all = [first, last], last
    else:
        slots = jnp.zeros((1,), jnp.int32)
        index = jnp.zeros((2,), jnp.int32)
        pack = lax.all_gather(packed, "dp", axis=0, tiled=True)[None]
        pack = [pack[:, : depth // 2], pack[:, depth // 2 :]]
        small_all = lax.all_gather(small[0], "dp", axis=0).reshape(dp_size, 2 + EXPERTS, share)
        small_all = jnp.swapaxes(small_all, 0, 1).reshape(2 + EXPERTS, depth)
        small_all = jnp.concatenate([small_all, jnp.zeros((2, depth), BF)], 0)
        wo_all = lax.all_gather(wo_slots[0], "dp", axis=2, tiled=True)[None]
        wo_all = [wo_all[:, :, :half], wo_all[:, :, half:]]

    local = jnp.stack(
        [
            jnp.swapaxes(w_gate, 1, 2).reshape(ff, share),
            jnp.swapaxes(w_up, 1, 2).reshape(ff, share),
            down_weight.reshape(ff, share),
        ]
    )
    if direct:
        experts_w = lax.all_gather(local, "dp", axis=0)
    else:
        experts_w = lax.all_gather(local, "dp", axis=2, tiled=True)[None]

    n1, q, k, v, kt, vt, gains, router = qkv_call(index, place, toks, pack, small_all, width)
    g_near = z_swap(after(out_grad, toks[3]), 1, z_size)
    g_far = z_swap(after(out_grad, toks[3]), 2, z_size)
    fwd = attn_fwd(piece_starts, place, z_size, q, k, vt, line)
    chances, ot = fwd[:2]
    atts = z_direct([after(fwd[2], g_near, g_far)] + [after(x, g_near, g_far) for x in fwd[3:]], z_size)
    if direct:
        wo_low, wo_high = dp_step(after(wo_low, n1), 4), dp_step(after(wo_high, n1), 2)
        wo_all = [dp_step(after(x, atts[1]), 1) for x in (wo_low, wo_high)]
    gs = [out_grad, g_near, g_far, z_swap(after(g_far, fwd[2]), 1, z_size)]
    mid, n2 = mid_call(index, [after(atts[0], gs[3])] + atts[1:], wo_all, tokens_in, gains)

    n2_near = z_swap(n2, 1, z_size)
    n2_far = z_swap(n2, 2, z_size)
    n2s = [n2, n2_near, n2_far, z_swap(after(n2_far, n2_near), 1, z_size)]
    hg, gg, ug, logit_grad, router_part = units_call(place, n2s, gs, sel, router, experts_w, unit)
    ngs = product_call([gg, ug], (0, 1), experts_w, z_size, [logit_grad, router], "normed_two_grads")
    passed = z_swap(ngs[3], 1, z_size)
    outs = product_call([after(hg, ngs[0])], (2,), experts_w, z_size, [], "expert_out")
    both = (ngs[2].astype(F32) + after(passed, outs[0]).astype(F32)).astype(BF)
    far = z_swap(both, 2, z_size)
    ng_near = z_swap(after(ngs[1], passed), 1, z_size)
    count = experts_w.shape[0]
    weight_grads = wgrad_call(experts_w.shape[0], [after(hg, both, *outs), gg, ug], n2s, gs)
    resid = resid_call(index, [after(ngs[0], weight_grads), ng_near, far], mid, out_grad, gains, wo_all)
    resid_grad, aog, gain_two = resid[:3]
    weight_grads = after(weight_grads, far, ng_near)
    if direct:
        expert_grads = lax.psum_scatter(weight_grads, "dp", scatter_dimension=0, tiled=False)
    else:
        expert_grads = lax.psum_scatter(weight_grads[0], "dp", scatter_dimension=2, tiled=True)
    out_passed = z_swap(after(outs[3], far), 1, z_size)
    dos = z_direct(resid[3:], z_size)
    wo_keep, wo_send = wo_grad_call(slots, atts, aog, count)
    out_both = (outs[2].astype(F32) + out_passed.astype(F32)).astype(BF)
    dos[0] = after(dos[0], wo_keep, out_both)
    out_far = z_swap(out_both, 2, z_size)
    out_near = z_swap(after(outs[1], out_both), 1, z_size)
    if direct:
        wo_grads = dp_fold(wo_keep, after(wo_send, *dos), 1)
    dq, dk, dv, diag = attn_bwd(place, dos, chances, q, k, v, kt, ot)
    if direct:
        wo_grads = dp_fold(*halves(wo_grads), 2)
        dq = after(dq, wo_grads)
    dq = after(dq, out_far, out_near)
    proj = proj_call(index, place, dq, dk, dv, pack, gain_two, router_part, toks)

    diag_at = (
        BLOCK * np.arange(total // BLOCK + 1)[:, None] - (BLOCK * (total // BLOCK - 2) + 1) - np.arange(2 * BLOCK)[None, :]
    )
    table = jnp.einsum("hbt,btk->hk", diag, jnp.asarray(onehot_of(diag_at)), precision=PRECISE)
    n1_passed = z_swap(after(proj[3], out_far), 1, z_size)
    if direct:
        table_rows = jnp.pad(table.reshape(1, -1), ((0, 7), (0, 0)))
        smalls = z_direct([proj[z_size]] * z_size, z_size)
        wo_grads = dp_fold(*halves(wo_grads), 4)[0]
        attn_keep, attn_send = attn_weights_call(slots, n1, dq, dk, dv, after(table_rows, wo_grads), smalls, 8)
        n1_passed = after(n1_passed, attn_keep)
    n1_both = (proj[2].astype(F32) + n1_passed.astype(F32)).astype(BF)
    n1_far = z_swap(n1_both, 2, z_size)
    n1_near = z_swap(after(proj[1], n1_both), 1, z_size)
    in_grad = final_call([proj[0], n1_near, n1_far], tokens_in, resid_grad, gains)
    out_parts = [outs[0], out_near, out_far]
    out_rows = (mid + functools.reduce(jnp.add, [p.astype(F32) for p in out_parts])).astype(BF)

    if direct:
        attn_grads = dp_fold(attn_keep, after(attn_send, n1_both), 1)
        attn_grads = dp_fold(*halves(attn_grads), 2)
        attn_grads = dp_fold(*halves(after(attn_grads, n1_far, n1_near)), 4)
        attn_grads = attn_grads[0].astype(F32)
        per = width // 128
        cut = attn_grads[: 3 * per * share].reshape(3, per, share, 128)
        cut = jnp.swapaxes(cut, 1, 2).reshape(3, share, width)
        smalls = attn_grads[3 * per * share :]
        grad_table = smalls[8, : heads * BUCKETS].reshape(heads, BUCKETS)
        mine = z_rank
        grad_wo = after(wo_grads, n1_near)
    else:
        cut = jnp.stack([jnp.dot(n1.T, d, preferred_element_type=F32) for d in (dq, dk, dv)])
        cut = lax.psum_scatter(cut, "dp", scatter_dimension=1, tiled=True)
        smalls = lax.psum(proj[z_size], ("dp", "tensor"))
        grad_table = lax.psum(table, "dp")
        mine = dp_rank * z_size + z_rank
        grad_wo = lax.psum_scatter(wo_keep[0], "dp", scatter_dimension=1, tiled=True)
    wo_parts = z_direct([grad_wo[width * c : width * (c + 1)] for c in range(z_size)], z_size)
    grad_wo = functools.reduce(jnp.add, [p.astype(F32) for p in wo_parts])
    per_device = depth // (dp_size * z_size)
    own = lax.dynamic_slice_in_dim(smalls, mine * per_device, per_device, 1)

    wide = expert_grads.astype(F32).reshape(3, EXPERTS, unit, share)
    return (
        out_rows,
        in_grad,
        own[0],
        cut[0],
        cut[1],
        cut[2],
        grad_wo,
        grad_table,
        own[1],
        own[2 : 2 + EXPERTS].T,
        jnp.swapaxes(wide[0], 1, 2),
        jnp.swapaxes(wide[1], 1, 2),
        wide[2],
    )


def solution(mesh):
    rows = P(("dp", "tensor"), None)
    grid = P("dp", "tensor")
    flat = P(("dp", "tensor"))
    weights = (P(None, "dp", "tensor"), P(None, "dp", "tensor"), P(None, "tensor", "dp"))
    in_specs = (rows, rows, P("dp"), grid, grid, grid, P("tensor", "dp"), P("tensor", None), P("dp"), P("dp", None))
    out_specs = (rows, rows, flat, grid, grid, grid, P("tensor", "dp"), P("tensor", None), flat, rows)
    return jax.shard_map(
        on_device,
        mesh=mesh,
        in_specs=in_specs + weights + (P("dp", None), P("dp", None)),
        out_specs=out_specs + weights,
        check_vma=False,
    )
```
